32 devices in a mesh: seq: 8 (over z, x), mp: 4 (over y, core).
Axes of the slice: x: 2, y: 2, z: 4, core: 2. Of those that a mesh axis runs over, the one named last changes fastest.
Arguments:
- mel_frames: float32 [4096, 80], P('seq'), may hold values from -6 to 6
- noise_frames: float32 [4096, 80], P('seq'), may hold values from -6 to 6
- phone_ids: int32 [4096], P('seq'), may hold values from 0 to 127
- lengths: int32 [5], replicated, may hold values from 1 to 1600, 4096 in all
- span_start: int32 [5], replicated, may hold values from 0 to 399
- span_end: int32 [5], replicated, may hold values from 800 to 1600
- flow_times: float32 [5], replicated, may hold values from 0.05 to 1
- attention_weight: float32 [4, 1024, 1024], P(None, 'seq', 'mp'), may hold values from -0.1875 to 0.1875
- attention_first: float32 [4, 1024, 1024], P(None, 'seq', 'mp'), may hold values from -1.9073486e-06 to 1.9073486e-06
- attention_second: float32 [4, 1024, 1024], P(None, 'seq', 'mp'), may hold values from 8.830318e-14 to 3.5697029e-13
- feedforward_weight: float32 [2, 1024, 4096], P(None, 'seq', 'mp'), may hold values from -0.1875 to 0.1875
- feedforward_first: float32 [2, 1024, 4096], P(None, 'seq', 'mp'), may hold values from -1.9073486e-06 to 1.9073486e-06
- feedforward_second: float32 [2, 1024, 4096], P(None, 'seq', 'mp'), may hold values from 8.830318e-14 to 3.5697029e-13
- input_weight: float32 [160, 1024], replicated, may hold values from -0.5 to 0.5
- input_first: float32 [160, 1024], replicated, may hold values from -1.9073486e-06 to 1.9073486e-06
- input_second: float32 [160, 1024], replicated, may hold values from 8.830318e-14 to 3.5697029e-13
- phone_table: float32 [128, 1024], replicated, may hold values from -6 to 6
- phone_first: float32 [128, 1024], replicated, may hold values from -1.9073486e-06 to 1.9073486e-06
- phone_second: float32 [128, 1024], replicated, may hold values from 8.830318e-14 to 3.5697029e-13
- position_kernel: float32 [31, 1024], replicated, may hold values from -1 to 1
- position_first: float32 [31, 1024], replicated, may hold values from -1.9073486e-06 to 1.9073486e-06
- position_second: float32 [31, 1024], replicated, may hold values from 8.830318e-14 to 3.5697029e-13
- output_weight: float32 [1024, 80], replicated, may hold values from -0.1875 to 0.1875
- output_first: float32 [1024, 80], replicated, may hold values from -1.9073486e-06 to 1.9073486e-06
- output_second: float32 [1024, 80], replicated, may hold values from 8.830318e-14 to 3.5697029e-13
- layer_gains: float32 [3, 1024], replicated, may hold values from 0.5 to 1.5
- gain_first: float32 [3, 1024], replicated, may hold values from -1.9073486e-06 to 1.9073486e-06
- gain_second: float32 [3, 1024], replicated, may hold values from 8.830318e-14 to 3.5697029e-13
Outputs:
- loss: float32 [], replicated
- grad_norm: float32 [], replicated
- attention_moment: float32 [4, 1024, 1024], P(None, 'seq', 'mp')
- attention_square: float32 [4, 1024, 1024], P(None, 'seq', 'mp')
- attention_update: float32 [4, 1024, 1024], P(None, 'seq', 'mp')
- feedforward_moment: float32 [2, 1024, 4096], P(None, 'seq', 'mp')
- feedforward_square: float32 [2, 1024, 4096], P(None, 'seq', 'mp')
- feedforward_update: float32 [2, 1024, 4096], P(None, 'seq', 'mp')
- input_moment: float32 [160, 1024], replicated
- input_square: float32 [160, 1024], replicated
- input_update: float32 [160, 1024], replicated
- phone_moment: float32 [128, 1024], replicated
- phone_square: float32 [128, 1024], replicated
- phone_update: float32 [128, 1024], replicated
- position_moment: float32 [31, 1024], replicated
- position_square: float32 [31, 1024], replicated
- position_update: float32 [31, 1024], replicated
- output_moment: float32 [1024, 80], replicated
- output_square: float32 [1024, 80], replicated
- output_update: float32 [1024, 80], replicated
- gain_moment: float32 [3, 1024], replicated
- gain_square: float32 [3, 1024], replicated
- gain_update: float32 [3, 1024], replicated
The draws below stay inside these ranges and needn't reach their ends.
Inputs may be any that keep to these rules, and one draw needn't show every extreme that they name: `lengths`: the utterances fill the 4096 frames in order, summing to 4096; the longest has exactly 1600 frames. `span_end`: positions beyond an utterance's length mask nothing.
All inputs are finite; a program needn't handle non-finite values.
Results may differ from the reference program's by a relative error of at most 0.0025.
The reference program's roundings to bfloat16 on the way count: a program that leaves them out, or rounds other values in their place, can miss the bound.
Values may be sent and summed in bfloat16 or wider, within the bound.
A program may use at most 384 MiB of HBM per device.

```python
import math
import jax
import jax.numpy as jnp
import numpy as np
from jax import lax

D = 1024
HEADS = 16
HD = 64
FF = 4096
MEL = 80
PHONES = 128
KW = 31
STEP = 10
FRAMES = 4096
LONGEST = 1600
UTTS = 5
NPARAMS = 12994560


def with_ends(array, rng, smallest, largest):
    longest = array.shape.index(max(array.shape))
    spots = []
    for shift in (0, 1):
        where = [jax.random.randint(jax.random.fold_in(rng, axis), (), 0, length) for axis, length in enumerate(array.shape)]
        where[longest] = (where[longest] + shift) % array.shape[longest]
        spots.append(tuple(where))
    return array.at[spots[0]].set(smallest).at[spots[1]].set(largest)


def shard_levels(own_key, dims, pieces, smallest, largest):
    level = 1.0
    for dim, blocks in pieces:
        steps = jax.random.uniform(jax.random.fold_in(jax.random.fold_in(own_key, 6), dim), (blocks,), jnp.float32, smallest / len(pieces), largest / len(pieces))
        level = level * jnp.repeat(jnp.exp(steps), dims[dim] // blocks).reshape((-1,) + (1,) * (len(dims) - 1 - dim))
    return level


def rank_table(amount, skew):
    loads = [(1 << 20) // math.isqrt(rank ** skew) + 1 for rank in range(1, amount + 1)]
    deviation = 1 + sum(loads) // (1 << 30)
    return np.cumsum(np.array([max(1, weight // deviation) for weight in loads]))


def skewed_ids(rng, dims, number_of, lean):
    table = rank_table(number_of, lean)
    pick = jax.random.randint(jax.random.fold_in(rng, 1), dims, 0, int(table[number_of - 1]))
    rank = jnp.searchsorted(jnp.asarray(table, jnp.int32), pick, side="right")
    return jax.random.permutation(jax.random.fold_in(rng, 2), number_of)[rank].astype(jnp.int32)


def length_profile(number_of, total, limit, slope):
    weights = [(1 << 20) // math.isqrt(standing ** slope) + 1 for standing in range(2, number_of + 1)]
    surplus, given = total - limit - (number_of - 1), [1] * (number_of - 1)
    while surplus > 0:
        movable = [i for i in range(number_of - 1) if given[i] < limit]
        mass, budget = sum([weights[i] for i in movable]), surplus
        for i in movable:
            extra = min(limit - given[i], max(1, budget * weights[i] // mass), surplus)
            given[i] = given[i] + extra
            surplus = surplus - extra
    return np.array([limit] + given)


def ragged_sizes(rng, count, total, bound, lean):
    if count == 2:
        one = jax.random.randint(rng, (), max(1, total - bound), min(bound, total - 1) + 1)
        return jnp.stack([one, total - one])
    tallies = jnp.asarray(length_profile(count, total, bound, lean), jnp.int32)
    couples = (count - 1) // 2
    giver, receiver = tallies[1:1 + 2 * couples:2], tallies[2:2 + 2 * couples:2]
    room = jnp.minimum(giver - 1, bound - receiver)
    moved = jax.random.randint(jax.random.fold_in(rng, 1), (couples,), 0, 1 << 20) % (room + 1)
    tallies = tallies.at[1:1 + 2 * couples:2].set(giver - moved).at[2:2 + 2 * couples:2].set(receiver + moved)
    return tallies[jax.random.permutation(jax.random.fold_in(rng, 2), count)]


def scatter_about(key, extent, spread, limit, shards=(), dtype=jnp.bfloat16):
    level = shard_levels(key, extent, shards, -0.22, 0.18) if shards else 1.0
    array = jax.random.normal(key, extent, jnp.float32) * spread * level
    return jnp.minimum(jnp.maximum(array, -limit), limit).astype(dtype)


def setup_inputs(seed: int = 0) -> dict:
    streams_of = jax.random.split(jax.random.key(seed), 29)
    return {
        "mel_frames": scatter_about(streams_of[0], (FRAMES, MEL), 1.0, 6.0, ((0, 8),), jnp.float32),
        "noise_frames": scatter_about(streams_of[1], (FRAMES, MEL), 1.0, 6.0, ((0, 8),), jnp.float32),
        "phone_ids": with_ends(skewed_ids(streams_of[2], (FRAMES,), PHONES, 2), jax.random.fold_in(streams_of[2], 3), 0, PHONES - 1).astype(jnp.int32),
        "lengths": ragged_sizes(streams_of[3], UTTS, FRAMES, LONGEST, 1).astype(jnp.int32),
        "span_start": with_ends(jax.random.randint(streams_of[4], (UTTS,), 0, LONGEST // 4), jax.random.fold_in(streams_of[4], 1), 0, (LONGEST // 4) - 1).astype(jnp.int32),
        "span_end": with_ends(jax.random.randint(streams_of[5], (UTTS,), LONGEST // 2, LONGEST + 1), jax.random.fold_in(streams_of[5], 1), LONGEST // 2, LONGEST).astype(jnp.int32),
        "flow_times": jnp.clip(jax.random.uniform(streams_of[6], (UTTS,), jnp.float32, 0.05, 1.0), 0.05, 1.0),
        "attention_weight": scatter_about(streams_of[7], (4, D, HEADS * HD), D ** -0.5, 0.1875, ((1, 8), (2, 4)), jnp.float32),
        "attention_first": scatter_about(streams_of[8], (4, D, HEADS * HD), (0.033 / (FRAMES * NPARAMS) ** 0.5), 1.9073486328125e-06, ((1, 8), (2, 4)), jnp.float32),
        "attention_second": jnp.clip(jnp.exp(math.log(3.5697028557928057e-13) - 1.3968764 * jax.random.uniform(streams_of[9], (4, D, HEADS * HD), jnp.float32) ** shard_levels(streams_of[9], (4, D, HEADS * HD), ((1, 8), (2, 4)), -0.2, 0.2)), 8.830317797499723e-14, 3.5697028557928057e-13),
        "feedforward_weight": scatter_about(streams_of[10], (2, D, FF), D ** -0.5, 0.1875, ((1, 8), (2, 4)), jnp.float32),
        "feedforward_first": scatter_about(streams_of[11], (2, D, FF), (0.033 / (FRAMES * NPARAMS) ** 0.5), 1.9073486328125e-06, ((1, 8), (2, 4)), jnp.float32),
        "feedforward_second": jnp.clip(jnp.exp(math.log(3.5697028557928057e-13) - 1.3968764 * jax.random.uniform(streams_of[12], (2, D, FF), jnp.float32) ** shard_levels(streams_of[12], (2, D, FF), ((1, 8), (2, 4)), -0.2, 0.2)), 8.830317797499723e-14, 3.5697028557928057e-13),
        "input_weight": scatter_about(streams_of[13], (2 * MEL, D), (2 * MEL) ** -0.5, 0.5, (), jnp.float32),
        "input_first": scatter_about(streams_of[14], (2 * MEL, D), (0.033 / (FRAMES * NPARAMS) ** 0.5), 1.9073486328125e-06, (), jnp.float32),
        "input_second": jnp.clip(jnp.exp(jax.random.uniform(streams_of[15], (2 * MEL, D), jnp.float32, math.log(8.830317797499723e-14), math.log(3.5697028557928057e-13))), 8.830317797499723e-14, 3.5697028557928057e-13),
        "phone_table": scatter_about(streams_of[16], (PHONES, D), 1.0, 6.0, (), jnp.float32),
        "phone_first": scatter_about(streams_of[17], (PHONES, D), (0.033 / (FRAMES * NPARAMS) ** 0.5), 1.9073486328125e-06, (), jnp.float32),
        "phone_second": jnp.clip(jnp.exp(jax.random.uniform(streams_of[18], (PHONES, D), jnp.float32, math.log(8.830317797499723e-14), math.log(3.5697028557928057e-13))), 8.830317797499723e-14, 3.5697028557928057e-13),
        "position_kernel": scatter_about(streams_of[19], (KW, D), KW ** -0.5, 1.0, (), jnp.float32),
        "position_first": scatter_about(streams_of[20], (KW, D), (0.033 / (FRAMES * NPARAMS) ** 0.5), 1.9073486328125e-06, (), jnp.float32),
        "position_second": jnp.clip(jnp.exp(jax.random.uniform(streams_of[21], (KW, D), jnp.float32, math.log(8.830317797499723e-14), math.log(3.5697028557928057e-13))), 8.830317797499723e-14, 3.5697028557928057e-13),
        "output_weight": scatter_about(streams_of[22], (D, MEL), D ** -0.5, 0.1875, (), jnp.float32),
        "output_first": scatter_about(streams_of[23], (D, MEL), (0.033 / (FRAMES * NPARAMS) ** 0.5), 1.9073486328125e-06, (), jnp.float32),
        "output_second": jnp.clip(jnp.exp(jax.random.uniform(streams_of[24], (D, MEL), jnp.float32, math.log(8.830317797499723e-14), math.log(3.5697028557928057e-13))), 8.830317797499723e-14, 3.5697028557928057e-13),
        "layer_gains": jnp.clip(1.0 + 0.1 * jax.random.normal(streams_of[25], (3, D), jnp.float32), 0.5, 1.5),
        "gain_first": scatter_about(streams_of[26], (3, D), (0.033 / (FRAMES * NPARAMS) ** 0.5), 1.9073486328125e-06, (), jnp.float32),
        "gain_second": jnp.clip(jnp.exp(jax.random.uniform(streams_of[27], (3, D), jnp.float32, math.log(8.830317797499723e-14), math.log(3.5697028557928057e-13))), 8.830317797499723e-14, 3.5697028557928057e-13),
    }


@jax.custom_vjp
def low(v):
    return lax.optimization_barrier(v.astype(jnp.bfloat16)).astype(jnp.float32)

@jax.custom_vjp
def low_back(v):
    return v

def low_keep(v):
    return (low(v), None)

def low_pass(kept, grad):
    return (grad,)

def back_keep(v):
    return (v, None)

def back_low(kept, grad):
    return (low(grad),)
low.defvjp(low_keep, low_pass)
low_back.defvjp(back_keep, back_low)
precise = lax.Precision.HIGHEST
norm_epsilon = 1e-05
flow_sigma = 1e-05
beta_one = 0.9
beta_two = 0.95
adam_epsilon = 1e-08
weight_decay = 0.1
step_rates = (0.04, 0.04, 0.08, 1.0, 0.2, 0.04, 1.0)
decay_flags = (1.0, 1.0, 1.0, 1.0, 1.0, 1.0, 0.0)
query_block = 512

def layer_norm(inputs, gain_row):
    centre_mean = lax.optimization_barrier(jnp.mean(inputs, -1, keepdims=True))
    centered = inputs - centre_mean
    variance = lax.optimization_barrier(jnp.mean(centered * centered, -1, keepdims=True))
    return centered * lax.rsqrt(variance + norm_epsilon) * gain_row

def frame_tables(lengths, span_start, span_end, flow_times, frame_index):
    utter_ends = jnp.cumsum(lengths)
    starts = utter_ends - lengths
    member = ((frame_index[:, None] >= starts[None, :]) & (frame_index[:, None] < utter_ends[None, :])).astype(jnp.float32)
    labels = (jnp.arange(lengths.shape[0]) + 1).astype(jnp.float32)
    owners = lax.optimization_barrier(jnp.sum(member * labels[None, :], 1)) - 1.0
    position = frame_index.astype(jnp.float32) - lax.optimization_barrier(jnp.sum(member * starts.astype(jnp.float32)[None, :], 1))
    low_end = lax.optimization_barrier(jnp.sum(member * span_start.astype(jnp.float32)[None, :], 1))
    high_end = lax.optimization_barrier(jnp.sum(member * span_end.astype(jnp.float32)[None, :], 1))
    masked = ((position >= low_end) & (position < high_end)).astype(jnp.float32)
    moment = lax.optimization_barrier(jnp.sum(member * flow_times[None, :], 1))
    return (owners, masked, moment)

def mask_counts(lengths, span_start, span_end):
    span_low = jnp.minimum(span_start, lengths)
    span_high = jnp.minimum(span_end, lengths)
    covered = jnp.sum(jnp.maximum(span_high - span_low, 0)).astype(jnp.float32)
    return (covered, jnp.sum(lengths).astype(jnp.float32) - covered)

def time_features(moment, width):
    half_width = width // 2
    frequency = jnp.exp(-math.log(10000.0) * jnp.arange(half_width).astype(jnp.float32) / half_width)
    angles = moment[:, None] * 100.0 * frequency[None, :]
    return jnp.concatenate([jnp.sin(angles), jnp.cos(angles)], 1)

def head_slopes(first_head, head_count, heads_all):
    head_index = first_head + jnp.arange(head_count)
    return jnp.exp2(-8.0 * (head_index + 1).astype(jnp.float32) / heads_all)

def matmul(left, right):
    return jnp.dot(left, right, precision=precise, preferred_element_type=jnp.float32)

def conv_apply(padded, pad_owner, owners, kernel_all):
    row_count = owners.shape[0]
    running = jnp.zeros((row_count, kernel_all.shape[1]), jnp.float32)
    for offset in range(kernel_all.shape[0]):
        same_owner = (pad_owner[offset:offset + row_count] == owners).astype(jnp.float32)
        running = running + kernel_all[offset][None, :] * padded[offset:offset + row_count] * same_owner[:, None]
    return running

def forward(params, mel_frames, noise_frames, phone_ids, lengths, span_start, span_end, flow_times):
    attention_all, feedforward_all, input_all, phone_all, kernel_all, output_all, gains_all = params
    frames = mel_frames.shape[0]
    reach = kernel_all.shape[0] // 2
    tables = (lengths, span_start, span_end, flow_times)
    frame_index = jnp.arange(frames)
    owners, masked, moment = frame_tables(*tables, frame_index)
    covered, uncovered = mask_counts(lengths, span_start, span_end)
    row_weight = masked / jnp.maximum(covered, 1.0) + 0.1 * (1.0 - masked) / jnp.maximum(uncovered, 1.0)
    target = mel_frames - (1.0 - flow_sigma) * noise_frames
    noisy = (1.0 - (1.0 - flow_sigma) * moment[:, None]) * noise_frames + moment[:, None] * mel_frames
    context = mel_frames * (1.0 - masked[:, None])
    feats = low(jnp.concatenate([context, noisy], 1))
    choose = (phone_ids[:, None] == jnp.arange(phone_all.shape[0])[None, :]).astype(jnp.float32)
    start_h = matmul(feats, low(input_all)) + matmul(choose, low(phone_all))
    start_h = low_back(start_h + time_features(moment, input_all.shape[1]))
    start_low = low(start_h)
    padded = jnp.pad(start_low, ((reach, reach), (0, 0)))
    pad_owner = frame_tables(*tables, jnp.arange(frames + 2 * reach) - reach)[0]
    conv_out = low_back(conv_apply(padded, pad_owner, owners, kernel_all))
    hidden_one = start_h + jax.nn.gelu(conv_out)
    ln_one = low(layer_norm(hidden_one, gains_all[0]))
    queries = low_back(low(matmul(ln_one, low(attention_all[0])))).reshape(frames, HEADS, HD)
    keyed = low_back(low(matmul(ln_one, low(attention_all[1])))).reshape(frames, HEADS, HD)
    valued = low_back(low(matmul(ln_one, low(attention_all[2])))).reshape(frames, HEADS, HD)
    slopes = head_slopes(0, HEADS, HEADS)
    block_rows = min(query_block, frames)
    block_count = frames // block_rows

    def attend_block(query_rows, row_index, row_owner):
        product = low_back(jnp.einsum('qhd,khd->hqk', query_rows, keyed, precision=precise) * 0.125)
        distance = jnp.abs(row_index[:, None] - frame_index[None, :]).astype(jnp.float32)
        biased = product - slopes[:, None, None] * distance[None]
        biased = jnp.where((row_owner[:, None] == owners[None, :])[None], biased, -1e+30)
        probs = jax.nn.softmax(biased, -1)
        return jnp.einsum('hqk,khd->qhd', low(probs), valued, precision=precise)
    blocked = (queries.reshape(block_count, block_rows, HEADS, HD), frame_index.reshape(block_count, block_rows), owners.reshape(block_count, block_rows))
    outputs = lax.map(lambda scanned: jax.checkpoint(attend_block)(*scanned), blocked)
    attended_heads = low_back(low(outputs.reshape(frames, HEADS * HD)))
    attended = low_back(matmul(attended_heads, low(attention_all[3]).T))
    hidden_two = hidden_one + attended
    ln_two = low(layer_norm(hidden_two, gains_all[1]))
    upward = low_back(matmul(ln_two, low(feedforward_all[0])))
    gated = low(jax.nn.gelu(upward))
    downward = low_back(matmul(gated, low(feedforward_all[1]).T))
    hidden_three = hidden_two + downward
    ln_three = low(layer_norm(hidden_three, gains_all[2]))
    predicted = low_back(matmul(ln_three, low(output_all)))
    errors = predicted - target
    return jnp.sum(row_weight * lax.optimization_barrier(jnp.mean(errors * errors, 1)))

def adam_step(weight, first_old, second, gradient, step_rate, decay_on):
    first_new = beta_one * first_old + (1.0 - beta_one) * gradient
    second_new = beta_two * second + (1.0 - beta_two) * gradient * gradient
    fix_one = 1.0 - beta_one ** STEP
    fix_two = 1.0 - beta_two ** STEP
    moved = first_new / fix_one / (jnp.sqrt(second_new / fix_two) + adam_epsilon)
    return (first_new, second_new, weight - step_rate * (moved + decay_on * weight_decay * weight))

def reference(mel_frames, noise_frames, phone_ids, lengths, span_start, span_end, flow_times, attention_weight, attention_first, attention_second, feedforward_weight, feedforward_first, feedforward_second, input_weight, input_first, input_second, phone_table, phone_first, phone_second, position_kernel, position_first, position_second, output_weight, output_first, output_second, layer_gains, gain_first, gain_second):
    weights = (attention_weight, feedforward_weight, input_weight, phone_table, position_kernel, output_weight, layer_gains)
    firsts = (attention_first, feedforward_first, input_first, phone_first, position_first, output_first, gain_first)
    seconds = (attention_second, feedforward_second, input_second, phone_second, position_second, output_second, gain_second)

    def loss_of(*params):
        return forward(params, mel_frames, noise_frames, phone_ids, lengths, span_start, span_end, flow_times)
    loss, pullback = jax.vjp(loss_of, *weights)
    grads = pullback(jnp.ones_like(loss))
    squares = jnp.zeros((), jnp.float32)
    for gradient in grads:
        squares = squares + jnp.sum(gradient * gradient)
    grad_norm = jnp.sqrt(squares)
    clip_level = 0.3 / math.sqrt(FRAMES)
    factor = jnp.minimum(1.0, clip_level / grad_norm)
    results = [loss, grad_norm]
    for number in range(7):
        results.extend(adam_step(weights[number], firsts[number], seconds[number], grads[number] * factor, step_rates[number], decay_flags[number]))
    return tuple(results)
```

```python
import functools
import math

import jax
import jax.numpy as jnp
from jax import lax
from jax.experimental import pallas as pl
from jax.experimental.pallas import tpu as pltpu
from jax.sharding import PartitionSpec as P

D = 1024
HEADS = 16
HD = 64
STEP = 10
MAXLEN = 1600


norm_epsilon = 1e-05
flow_sigma = 1e-05
beta_one = 0.9
beta_two = 0.95
adam_epsilon = 1e-08
weight_decay = 0.1
step_rates = (0.04, 0.04, 0.08, 1.0, 0.2, 0.04, 1.0)
decay_flags = (1.0, 1.0, 1.0, 1.0, 1.0, 1.0, 0.0)


def padded_2(array, sides, width):
    for axis, dim in sides:
        devices, length = (lax.axis_size(axis), array.shape[dim])
        up = [(i, (i + 1) % devices) for i in range(devices - 1)]
        down = [(j, i) for i, j in up]
        last = lax.slice_in_dim(array, length - width, length, axis=dim)
        initial = lax.slice_in_dim(array, 0, width, axis=dim)
        before = lax.ppermute(last, axis, up)
        after = lax.ppermute(initial, axis, down)
        array = jnp.concatenate([before, array, after], axis=dim)
    return array


def layer_norm(inputs, gain_row):
    centre_mean = jnp.mean(inputs, -1, keepdims=True)
    centered = inputs - centre_mean
    variance = jnp.mean(centered * centered, -1, keepdims=True)
    return centered * lax.rsqrt(variance + norm_epsilon) * gain_row


def frame_tables(lengths, span_start, span_end, flow_times, frame_index):
    utter_ends = jnp.cumsum(lengths)
    starts = utter_ends - lengths
    member = (
        (frame_index[:, None] >= starts[None, :]) & (frame_index[:, None] < utter_ends[None, :])
    ).astype(jnp.float32)
    labels = (jnp.arange(lengths.shape[0]) + 1).astype(jnp.float32)
    owners = jnp.sum(member * labels[None, :], 1) - 1.0
    position = frame_index.astype(jnp.float32) - jnp.sum(
        member * starts.astype(jnp.float32)[None, :], 1
    )
    low_end = jnp.sum(member * span_start.astype(jnp.float32)[None, :], 1)
    high_end = jnp.sum(member * span_end.astype(jnp.float32)[None, :], 1)
    masked = ((position >= low_end) & (position < high_end)).astype(jnp.float32)
    moment = jnp.sum(member * flow_times[None, :], 1)
    return (owners, masked, moment)


def mask_counts(lengths, span_start, span_end):
    span_low = jnp.minimum(span_start, lengths)
    span_high = jnp.minimum(span_end, lengths)
    covered = jnp.sum(jnp.maximum(span_high - span_low, 0)).astype(jnp.float32)
    return (covered, jnp.sum(lengths).astype(jnp.float32) - covered)


def time_features(moment, width):
    half_width = width // 2
    frequency = jnp.exp(
        -math.log(10000.0) * jnp.arange(half_width).astype(jnp.float32) / half_width
    )
    angles = moment[:, None] * 100.0 * frequency[None, :]
    return jnp.concatenate([jnp.sin(angles), jnp.cos(angles)], 1)


def head_slopes(first_head, head_count, heads_all):
    head_index = first_head + jnp.arange(head_count)
    return jnp.exp2(-8.0 * (head_index + 1).astype(jnp.float32) / heads_all)


def product(left, right):
    return jnp.dot(left, right, preferred_element_type=jnp.float32)


def contract_rows(left, right):
    return lax.dot_general(
        left, right, (((0,), (0,)), ((), ())), preferred_element_type=jnp.float32
    )


def contract_cols(left, right):
    return lax.dot_general(
        left, right, (((1,), (1,)), ((), ())), preferred_element_type=jnp.float32
    )


QB=128
NEG=1e30
def _nt(a,b): return lax.dot_general(a,b,(((1,),(1,)),((),())),preferred_element_type=jnp.float32)
def _nn(a,b): return jnp.dot(a,b,preferred_element_type=jnp.float32)

def lane_half(rows):
    return lax.broadcasted_iota(jnp.int32,(rows,128),1)<64

def stack_pair(x):
    low=lane_half(x.shape[0])
    zero=jnp.zeros_like(x)
    return jnp.concatenate([jnp.where(low,x,zero),jnp.where(low,zero,x)],0)

def unstack_pair(x):
    n=x.shape[0]//2
    return jnp.where(lane_half(n),x[:n],x[n:])

def tile_distance(row0,key0,row_own,key_own,kt):
    dist=jnp.abs((row0-key0)+lax.broadcasted_iota(jnp.int32,(QB,kt),0)-lax.broadcasted_iota(jnp.int32,(QB,kt),1)).astype(jnp.float32)
    return jnp.where(row_own==key_own,dist,NEG)

def fwd_kernel(kt,bounds,slopes,q_ref,k_ref,v_ref,rown_ref,kown_ref,o_ref,ob_ref,lse_ref):
    i=pl.program_id(0)
    lo,hi=bounds[2*i],bounds[2*i+1]
    off=bounds[2*pl.num_programs(0)]
    row0=off+i*QB
    pairs=q_ref.shape[1]//128
    rown=rown_ref[...]
    qs=[stack_pair(q_ref[:,128*j:128*(j+1)])*jnp.bfloat16(0.125) for j in range(pairs)]
    def body(t,carry):
        k0=pl.multiple_of(t*kt,kt)
        dist=tile_distance(row0,k0,rown,kown_ref[:,pl.ds(k0,kt)],kt)
        out=[]
        for j in range(pairs):
            m,l,acc=carry[j]
            s=_nt(qs[j],k_ref[pl.ds(k0,kt),128*j:128*(j+1)])
            s=jnp.concatenate([s[:QB]-slopes[2*j]*dist,s[QB:]-slopes[2*j+1]*dist],0)
            mn=jnp.maximum(m,jnp.max(s,-1,keepdims=True))
            a=jnp.exp(m-mn)
            p=jnp.exp(s-mn)
            l=l*a+jnp.sum(p,-1,keepdims=True)
            acc=acc*a+_nn(p.astype(jnp.bfloat16),v_ref[pl.ds(k0,kt),128*j:128*(j+1)])
            out.append((mn,l,acc))
        return tuple(out)
    init=tuple((jnp.full((2*QB,1),-NEG,jnp.float32),jnp.zeros((2*QB,1),jnp.float32),jnp.zeros((2*QB,128),jnp.float32)) for _ in range(pairs))
    res=lax.fori_loop(lo,hi,body,init)
    lane=lax.broadcasted_iota(jnp.int32,(QB,128),1)
    lse=jnp.zeros((QB,128),jnp.float32)
    for j in range(pairs):
        m,l,acc=res[j]
        o=unstack_pair(acc/l)
        o_ref[:,128*j:128*(j+1)]=o
        ob_ref[:,128*j:128*(j+1)]=o.astype(jnp.bfloat16)
        g=m+jnp.log(l)
        lse=jnp.where(lane==2*j,g[:QB],lse)
        lse=jnp.where(lane==2*j+1,g[QB:],lse)
    lse_ref[...]=lse

def attn_fwd(q,k,v,rown,kown,bounds,slopes,kt=512):
    R,W=q.shape; N=k.shape[0]
    full=lambda shp: pl.BlockSpec(shp,lambda i,*_:(0,)*len(shp))
    blk=lambda w: pl.BlockSpec((QB,w),lambda i,*_:(i,0))
    return pl.pallas_call(functools.partial(fwd_kernel,kt),
        out_shape=(jax.ShapeDtypeStruct((R,W),jnp.float32),jax.ShapeDtypeStruct((R,W),jnp.bfloat16),jax.ShapeDtypeStruct((R,128),jnp.float32)),
        grid_spec=pltpu.PrefetchScalarGridSpec(num_scalar_prefetch=2,grid=(R//QB,),
            in_specs=[blk(W),full((N,W)),full((N,W)),blk(1),full((1,N))],
            out_specs=(blk(W),blk(W),blk(128))),
        compiler_params=pltpu.CompilerParams(vmem_limit_bytes=50<<20),name="attend_forward")(bounds,slopes,q,k,v,rown,kown)

def bwd_kernel(kt,bounds,slopes,q_ref,k_ref,v_ref,do_ref,lse_ref,del_ref,qa_ref,ka_ref,va_ref,doa_ref,lsea_ref,dela_ref,rown_ref,kown_ref,out_ref):
    i=pl.program_id(0)
    lo,hi=bounds[2*i],bounds[2*i+1]
    off=bounds[2*pl.num_programs(0)]
    row0=off+i*QB
    W=q_ref.shape[1]
    pairs=W//128
    rown=rown_ref[...]
    sl=[slice(128*j,128*(j+1)) for j in range(pairs)]
    scale=jnp.bfloat16(0.125)
    col=lambda ref,j: jnp.concatenate([ref[:,2*j:2*j+1],ref[:,2*j+1:2*j+2]],0)
    qs=[stack_pair(q_ref[:,sl[j]])*scale for j in range(pairs)]
    dos=[stack_pair(do_ref[:,sl[j]]) for j in range(pairs)]
    lses=[col(lse_ref,j) for j in range(pairs)]
    dels=[col(del_ref,j) for j in range(pairs)]
    ks=[stack_pair(k_ref[:,sl[j]])*scale for j in range(pairs)]
    vs=[stack_pair(v_ref[:,sl[j]]) for j in range(pairs)]
    def body(t,carry):
        k0=pl.multiple_of(t*kt,kt)
        win=pl.ds(k0,kt)
        dist=tile_distance(row0,k0,rown,kown_ref[:,win],kt)
        out=[]
        for j in range(pairs):
            dq,dk,dv=carry[j]
            kj,vj,qj,doj=ka_ref[win,sl[j]],va_ref[win,sl[j]],qa_ref[win,sl[j]],doa_ref[win,sl[j]]
            bias=[slopes[2*j]*dist,slopes[2*j+1]*dist]
            s=_nt(qs[j],kj)
            p=jnp.exp(jnp.concatenate([s[:QB]-bias[0],s[QB:]-bias[1]],0)-lses[j])
            ds=(p*(_nt(dos[j],vj)-dels[j])).astype(jnp.bfloat16)
            dq=dq+_nn(ds,kj)
            s=_nt(ks[j],qj)
            lr=[lsea_ref[2*j+c:2*j+c+1,win] for c in (0,1)]
            dr=[dela_ref[2*j+c:2*j+c+1,win] for c in (0,1)]
            p=jnp.exp(jnp.concatenate([s[:QB]-bias[0]-lr[0],s[QB:]-bias[1]-lr[1]],0))
            dv=dv+_nn(p.astype(jnp.bfloat16),doj)
            g=_nt(vs[j],doj)
            ds=(p*jnp.concatenate([g[:QB]-dr[0],g[QB:]-dr[1]],0)).astype(jnp.bfloat16)
            dk=dk+_nn(ds,qj)
            out.append((dq,dk,dv))
        return tuple(out)
    z=jnp.zeros((2*QB,128),jnp.float32)
    res=lax.fori_loop(lo,hi,body,tuple((z,z,z) for _ in range(pairs)))
    for j in range(pairs):
        dq,dk,dv=res[j]
        out_ref[0,:,sl[j]]=(unstack_pair(dq)*0.125).astype(jnp.bfloat16)
        out_ref[1,:,sl[j]]=(unstack_pair(dk)*0.125).astype(jnp.bfloat16)
        out_ref[2,:,sl[j]]=unstack_pair(dv).astype(jnp.bfloat16)

def attn_bwd(q,k,v,do,lse,dele,qa,ka,va,doa,lsea,dela,rown,kown,bounds,slopes,kt=512):
    R,W=q.shape; N=ka.shape[0]
    full=lambda shp: pl.BlockSpec(shp,lambda i,*_:(0,)*len(shp))
    blk=lambda w: pl.BlockSpec((QB,w),lambda i,*_:(i,0))
    return pl.pallas_call(functools.partial(bwd_kernel,kt),
        out_shape=jax.ShapeDtypeStruct((3,R,W),jnp.bfloat16),
        grid_spec=pltpu.PrefetchScalarGridSpec(num_scalar_prefetch=2,grid=(R//QB,),
            in_specs=[blk(W)]*4+[blk(128)]*2+[full((N,W))]*4+[full((8,N))]*2+[blk(1),full((1,N))],
            out_specs=pl.BlockSpec((3,QB,W),lambda i,*_:(0,i,0))),
        compiler_params=pltpu.CompilerParams(vmem_limit_bytes=50<<20),name="attend_backward")(bounds,slopes,q,k,v,do,lse,dele,qa,ka,va,doa,lsea,dela,rown,kown)
MESH=pl.DeviceIdType.MESH
VM=pl.BlockSpec(memory_space=pltpu.VMEM)

def grid_place():
    s=lax.axis_index("seq"); m=lax.axis_index("mp")
    return s,m,s//2,lax.rem(s,2)

def greet_grid():
    s,m,z,x=grid_place()
    b=pltpu.get_barrier_semaphore()
    pl.semaphore_signal(b,inc=1,device_id=(s+1-2*x,m),device_id_type=MESH)
    @pl.when(z<3)
    def _(): pl.semaphore_signal(b,inc=1,device_id=(s+2,m),device_id_type=MESH)
    @pl.when(z>0)
    def _(): pl.semaphore_signal(b,inc=1,device_id=(s-2,m),device_id_type=MESH)
    pl.semaphore_wait(b,1+(z<3).astype(jnp.int32)+(z>0).astype(jnp.int32))

def gather_copy(slot,kind,dst,sems):
    s,m,z,x=grid_place()
    dev=[(s+1-2*x,m),(s+2,m),(s-2,m)][kind]
    send,recv=sems
    return pltpu.make_async_remote_copy(src_ref=dst.at[slot],dst_ref=dst.at[slot],send_sem=send.at[kind,slot],recv_sem=recv.at[slot],device_id=dev,device_id_type=MESH)

def gather_run(chunks):
    s,m,z,x=grid_place()
    for d,q in chunks:
        gather_copy(s,0,d,q).start()
        @pl.when(z<3)
        def _(d=d,q=q): gather_copy(s,1,d,q).start()
        @pl.when(z>0)
        def _(d=d,q=q): gather_copy(s,2,d,q).start()
    for t in range(3):
        for d,q in chunks:
            lowslot=s-2*(t+1); highslot=s+2*(t+1)
            @pl.when(z-1-t>=0)
            def _(d=d,q=q):
                gather_copy(lowslot,0,d,q).wait_recv()
                gather_copy(lowslot,0,d,q).start()
                @pl.when(z<3)
                def _(): gather_copy(lowslot,1,d,q).start()
            @pl.when(z+1+t<=3)
            def _(d=d,q=q):
                gather_copy(highslot,0,d,q).wait_recv()
                gather_copy(highslot,0,d,q).start()
                @pl.when(z>0)
                def _(): gather_copy(highslot,2,d,q).start()

def gather_finish(chunks):
    s,m,z,x=grid_place()
    for d,q in chunks:
        for zz in range(4):
            gather_copy(2*zz+1-x,0,d,q).wait_recv()
        for zz in range(4):
            slot=2*zz+x
            gather_copy(slot,0,d,q).wait_send()
            @pl.when((z<3)&(z>=zz))
            def _(): gather_copy(slot,1,d,q).wait_send()
            @pl.when((z>0)&(z<=zz))
            def _(): gather_copy(slot,2,d,q).wait_send()

def gather_kernel(n,*refs):
    src,dst,sems=refs[:n],refs[n:2*n],refs[2*n:]
    s,m,z,x=grid_place()
    local=[pltpu.make_async_copy(src[i],dst[i].at[s],sems[3*i+2]) for i in range(n)]
    for c in local: c.start()
    greet_grid()
    for c in local: c.wait()
    chunks=[(dst[i],(sems[3*i],sems[3*i+1])) for i in range(n)]
    gather_run(chunks)
    gather_finish(chunks)

GATHER_SEMS=[pltpu.SemaphoreType.DMA((3,8)),pltpu.SemaphoreType.DMA((8,)),pltpu.SemaphoreType.DMA]
def seq_gather(arrays,cid):
    n=len(arrays)
    return pl.pallas_call(functools.partial(gather_kernel,n),
        out_shape=tuple(jax.ShapeDtypeStruct((8,)+a.shape,a.dtype) for a in arrays),
        in_specs=[VM]*n,out_specs=tuple([VM]*n),
        scratch_shapes=GATHER_SEMS*n,
        compiler_params=pltpu.CompilerParams(collective_id=cid,has_side_effects=True,vmem_limit_bytes=50<<20),name="seq_gather_%d"%cid)(*arrays)

KT = 512

def range_bounds(lengths, row_base, window_start, row_count):
    ends = jnp.cumsum(lengths)
    starts = ends - lengths
    first = row_base + QB * jnp.arange(row_count // QB)
    low = jnp.max(jnp.where(starts[None] <= first[:, None], starts[None], 0), 1)
    high = jnp.min(jnp.where(ends[None] >= first[:, None] + QB, ends[None], jnp.sum(lengths)), 1)
    tiles = jnp.stack([(low - window_start) // KT, (high - window_start + KT - 1) // KT], 1)
    return jnp.concatenate([tiles.reshape(-1), (row_base - window_start)[None]]).astype(jnp.int32)


def gather_window(arrays, near_count, row_count, cid):
    if lax.axis_size("seq") == 8:
        gathered = seq_gather(arrays, cid)
        return tuple(g.reshape((-1,) + g.shape[2:]) for g in gathered)
    row_base = lax.axis_index("seq") * row_count
    return tuple(
        slice_window(lax.all_gather(a, "seq", axis=0, tiled=True), row_base // row_count * a.shape[0], near_count, a.shape[0])
        for a in arrays
    )


def slice_window(full_rows, row_base, near_count, row_count):
    pad_rows = near_count * row_count
    padded = jnp.pad(full_rows, ((pad_rows, pad_rows), (0, 0)))
    return lax.dynamic_slice_in_dim(padded, row_base, (2 * near_count + 1) * row_count, 0)


def adam_step(weight, first_old, second, gradient, step_rate, decay_on):
    first_new = beta_one * first_old + (1.0 - beta_one) * gradient
    second_new = beta_two * second + (1.0 - beta_two) * gradient * gradient
    fix_one = 1.0 - beta_one**STEP
    fix_two = 1.0 - beta_two**STEP
    moved = first_new / fix_one / (jnp.sqrt(second_new / fix_two) + adam_epsilon)
    return (first_new, second_new, weight - step_rate * (moved + decay_on * weight_decay * weight))


def per_device(
    mel_frames,
    noise_frames,
    phone_ids,
    lengths,
    span_start,
    span_end,
    flow_times,
    attention_weight,
    attention_first,
    attention_second,
    feedforward_weight,
    feedforward_first,
    feedforward_second,
    input_weight,
    input_first,
    input_second,
    phone_table,
    phone_first,
    phone_second,
    position_kernel,
    position_first,
    position_second,
    output_weight,
    output_first,
    output_second,
    layer_gains,
    gain_first,
    gain_second,
):
    row_count = mel_frames.shape[0]
    frames = row_count * lax.axis_size("seq")
    row_base = lax.axis_index("seq") * row_count
    longest = min(MAXLEN, frames // 2)
    near_count = min((longest - 1 + row_count - 1) // row_count, lax.axis_size("seq") - 1)
    window_start = row_base - near_count * row_count
    reach = position_kernel.shape[0] // 2
    tables = (lengths, span_start, span_end, flow_times)
    row_index = row_base + jnp.arange(row_count)
    owners, masked, moment = frame_tables(*tables, row_index)
    covered, uncovered = mask_counts(lengths, span_start, span_end)
    row_weight = masked / jnp.maximum(covered, 1.0) + 0.1 * (1.0 - masked) / jnp.maximum(
        uncovered, 1.0
    )
    attention_full, feedforward_full = (
        lax.all_gather(attention_weight.astype(jnp.bfloat16), "seq", axis=1, tiled=True),
        lax.all_gather(feedforward_weight.astype(jnp.bfloat16), "seq", axis=1, tiled=True),
    )
    heads_local = attention_full.shape[2] // HD
    slopes = head_slopes(lax.axis_index("mp") * heads_local, heads_local, HEADS)
    target = mel_frames - (1.0 - flow_sigma) * noise_frames
    noisy = (1.0 - (1.0 - flow_sigma) * moment[:, None]) * noise_frames + moment[
        :, None
    ] * mel_frames
    context = mel_frames * (1.0 - masked[:, None])
    feats = jnp.concatenate([context, noisy], 1).astype(jnp.bfloat16)
    choose = (phone_ids[:, None] == jnp.arange(phone_table.shape[0])[None, :]).astype(jnp.bfloat16)
    start_h = product(feats, input_weight.astype(jnp.bfloat16)) + product(
        choose, phone_table.astype(jnp.bfloat16)
    )
    start_h = start_h + time_features(moment, D)
    start_low = start_h.astype(jnp.bfloat16)
    rim = padded_2(start_low, (("seq", 0),), reach)
    pad_owner = frame_tables(*tables, row_base - reach + jnp.arange(row_count + 2 * reach))[0]
    conv_raw = jnp.zeros(start_h.shape, jnp.float32)
    for offset in range(position_kernel.shape[0]):
        same_owner = (pad_owner[offset : offset + row_count] == owners).astype(jnp.float32)
        conv_raw = (
            conv_raw
            + position_kernel[offset][None, :]
            * rim[offset : offset + row_count].astype(jnp.float32)
            * same_owner[:, None]
        )
    conv_gelu, conv_back = jax.vjp(jax.nn.gelu, conv_raw)
    hidden_one = start_h + conv_gelu
    ln_one, norm_back_one = jax.vjp(layer_norm, hidden_one, layer_gains[0])
    ln_one_low = ln_one.astype(jnp.bfloat16)
    projected = jnp.einsum(
        "td,kdh->kth", ln_one_low, attention_full[:3], preferred_element_type=jnp.float32
    ).astype(jnp.bfloat16)
    queries, keyed, valued = (projected[0], projected[1], projected[2])
    window_start = jnp.where(lax.axis_size("seq") == 8, 0, window_start)
    query_all, key_all, value_all = gather_window(
        (queries, keyed, valued), near_count, row_count, 0
    )
    bounds = range_bounds(lengths, row_base, window_start, row_count)
    key_owner = frame_tables(*tables, window_start + jnp.arange(key_all.shape[0]))[0][None]
    row_owner = owners[:, None]
    out_f32, out_low, log_total = attn_fwd(
        queries, key_all, value_all, row_owner, key_owner, bounds, slopes, KT
    )
    attended = lax.psum(
        contract_cols(out_low, attention_full[3]).astype(jnp.bfloat16), "mp"
    ).astype(jnp.float32)
    hidden_two = hidden_one + attended
    ln_two, norm_back_two = jax.vjp(layer_norm, hidden_two, layer_gains[1])
    ln_two_low = ln_two.astype(jnp.bfloat16)
    upward = product(ln_two_low, feedforward_full[0])
    gated_f32, gelu_back = jax.vjp(jax.nn.gelu, upward)
    gated = gated_f32.astype(jnp.bfloat16)
    downward = lax.psum(
        contract_cols(gated, feedforward_full[1]).astype(jnp.bfloat16), "mp"
    ).astype(jnp.float32)
    hidden_three = hidden_two + downward
    ln_three, norm_back_three = jax.vjp(layer_norm, hidden_three, layer_gains[2])
    ln_three_low = ln_three.astype(jnp.bfloat16)
    output_low = output_weight.astype(jnp.bfloat16)
    predicted = product(ln_three_low, output_low)
    errors = predicted - target
    loss_local = jnp.sum(row_weight * jnp.mean(errors * errors, 1))
    loss_total = lax.psum(loss_local, "seq")
    pred_grad = (row_weight[:, None] * (2.0 / errors.shape[1]) * errors).astype(jnp.bfloat16)
    output_grad = contract_rows(ln_three_low, pred_grad)
    three_grad, gain_three = norm_back_three(contract_cols(pred_grad, output_low))
    down_low = three_grad.astype(jnp.bfloat16)
    down_wgrad = contract_rows(down_low, gated)
    up_grad = gelu_back(product(down_low, feedforward_full[1]))[0].astype(jnp.bfloat16)
    up_wgrad = contract_rows(ln_two_low, up_grad)
    two_sum = lax.psum(
        contract_cols(up_grad, feedforward_full[0]).astype(jnp.bfloat16), "mp"
    ).astype(jnp.float32)
    norm_grad, gain_two = norm_back_two(two_sum)
    two_grad = three_grad + norm_grad
    attended_low = two_grad.astype(jnp.bfloat16)
    out_wgrad = contract_rows(attended_low, out_low)
    out_heads = product(attended_low, attention_full[3]).astype(jnp.bfloat16)
    delta = jnp.sum(
        (out_heads.astype(jnp.float32) * out_f32).reshape(row_count, heads_local, HD), 2
    )
    rows8 = jnp.concatenate([log_total[:, :heads_local].T, delta.T], 0)
    pad_cols = ((0, 0), (0, 128 - heads_local))
    out_all, rows_all = gather_window((out_heads, rows8), near_count, row_count, 1)
    rows_all = rows_all.reshape(-1, 2, heads_local, row_count).transpose(1, 2, 0, 3)
    rows_all = jnp.pad(rows_all.reshape(2, heads_local, -1), ((0, 0), (0, 8 - heads_local), (0, 0)))
    proj_grad = attn_bwd(
        queries, keyed, valued, out_heads, log_total, jnp.pad(delta, pad_cols),
        query_all, key_all, value_all, out_all, rows_all[0], rows_all[1],
        row_owner, key_owner, bounds, slopes, KT,
    )
    qkv_wgrad = jnp.einsum("td,kth->kdh", ln_one_low, proj_grad, preferred_element_type=jnp.float32)
    one_part = jnp.einsum(
        "kth,kdh->td", proj_grad, attention_full[:3], preferred_element_type=jnp.float32
    )
    one_sum = lax.psum(one_part.astype(jnp.bfloat16), "mp").astype(jnp.float32)
    norm_grad, gain_one = norm_back_one(one_sum)
    one_grad = two_grad + norm_grad
    conv_grad = conv_back(one_grad)[0].astype(jnp.bfloat16)
    grad_rim = padded_2(conv_grad, (("seq", 0),), reach)
    spread = jnp.zeros(one_grad.shape, jnp.float32)
    kernel_rows = []
    conv_grad_f32 = conv_grad.astype(jnp.float32)
    for offset in range(position_kernel.shape[0]):
        back_start = 2 * reach - offset
        same_back = (pad_owner[back_start : back_start + row_count] == owners).astype(jnp.float32)
        spread = (
            spread
            + position_kernel[offset][None, :]
            * grad_rim[back_start : back_start + row_count].astype(jnp.float32)
            * same_back[:, None]
        )
        same_fore = (pad_owner[offset : offset + row_count] == owners).astype(jnp.float32)
        kernel_rows.append(
            jnp.sum(
                conv_grad_f32
                * rim[offset : offset + row_count].astype(jnp.float32)
                * same_fore[:, None],
                0,
            )
        )
    kernel_grad = jnp.stack(kernel_rows)
    start_grad = (one_grad + spread).astype(jnp.bfloat16)
    input_wgrad = contract_rows(feats, start_grad)
    phone_wgrad = contract_rows(choose, start_grad)
    gains_grad = jnp.stack([gain_one, gain_two, gain_three])
    small_sums = lax.psum((input_wgrad, phone_wgrad, kernel_grad, output_grad, gains_grad), "seq")
    attention_grad, feedforward_grad = (
        lax.psum_scatter(
            jnp.concatenate([qkv_wgrad, out_wgrad[None]], 0), "seq", scatter_dimension=1, tiled=True
        ),
        lax.psum_scatter(jnp.stack([up_wgrad, down_wgrad]), "seq", scatter_dimension=1, tiled=True),
    )
    big_squares = jnp.sum(attention_grad * attention_grad) + jnp.sum(
        feedforward_grad * feedforward_grad
    )
    small_squares = jnp.zeros((), jnp.float32)
    for gradient in small_sums:
        small_squares = small_squares + jnp.sum(gradient * gradient)
    big_total = lax.psum(big_squares, ("seq", "mp"))
    grad_norm = jnp.sqrt(big_total + small_squares)
    factor = jnp.minimum(1.0, 0.3 / math.sqrt(frames) / grad_norm)
    weights = (
        attention_weight,
        feedforward_weight,
        input_weight,
        phone_table,
        position_kernel,
        output_weight,
        layer_gains,
    )
    firsts = (
        attention_first,
        feedforward_first,
        input_first,
        phone_first,
        position_first,
        output_first,
        gain_first,
    )
    seconds = (
        attention_second,
        feedforward_second,
        input_second,
        phone_second,
        position_second,
        output_second,
        gain_second,
    )
    grads = (attention_grad, feedforward_grad) + tuple(small_sums)
    results = [loss_total, grad_norm]
    for number in range(7):
        results.extend(
            adam_step(
                weights[number],
                firsts[number],
                seconds[number],
                grads[number] * factor,
                step_rates[number],
                decay_flags[number],
            )
        )
    return tuple(results)


def solution(mesh):
    in_specs = (
        P("seq", None),
        P("seq", None),
        P("seq"),
        P(),
        P(),
        P(),
        P(),
        P(None, "seq", "mp"),
        P(None, "seq", "mp"),
        P(None, "seq", "mp"),
        P(None, "seq", "mp"),
        P(None, "seq", "mp"),
        P(None, "seq", "mp"),
        P(),
        P(),
        P(),
        P(),
        P(),
        P(),
        P(),
        P(),
        P(),
        P(),
        P(),
        P(),
        P(),
        P(),
        P(),
    )
    out_specs = (
        P(),
        P(),
        P(None, "seq", "mp"),
        P(None, "seq", "mp"),
        P(None, "seq", "mp"),
        P(None, "seq", "mp"),
        P(None, "seq", "mp"),
        P(None, "seq", "mp"),
        P(),
        P(),
        P(),
        P(),
        P(),
        P(),
        P(),
        P(),
        P(),
        P(),
        P(),
        P(),
        P(),
        P(),
        P(),
    )
    return jax.shard_map(
        per_device, mesh=mesh, in_specs=in_specs, out_specs=out_specs, check_vma=False
    )
```

```python
import functools
import math

import jax
import jax.numpy as jnp
from jax import lax
from jax.experimental import pallas as pl
from jax.experimental.pallas import tpu as pltpu
from jax.sharding import PartitionSpec as P

D = 1024
HEADS = 16
HD = 64
MEL = 80
STEP = 10
MAXLEN = 1600


norm_epsilon = 1e-05
flow_sigma = 1e-05
beta_one = 0.9
beta_two = 0.95
adam_epsilon = 1e-08
weight_decay = 0.1
step_rates = (0.04, 0.04, 0.08, 1.0, 0.2, 0.04, 1.0)
decay_flags = (1.0, 1.0, 1.0, 1.0, 1.0, 1.0, 0.0)


def padded_2(array, sides, width):
    for axis, dim in sides:
        devices, length = (lax.axis_size(axis), array.shape[dim])
        up = [(i, (i + 1) % devices) for i in range(devices - 1)]
        down = [(j, i) for i, j in up]
        last = lax.slice_in_dim(array, length - width, length, axis=dim)
        initial = lax.slice_in_dim(array, 0, width, axis=dim)
        before = lax.ppermute(last, axis, up)
        after = lax.ppermute(initial, axis, down)
        array = jnp.concatenate([before, array, after], axis=dim)
    return array


def layer_norm(inputs, gain_row):
    centre_mean = jnp.mean(inputs, -1, keepdims=True)
    centered = inputs - centre_mean
    variance = jnp.mean(centered * centered, -1, keepdims=True)
    return centered * lax.rsqrt(variance + norm_epsilon) * gain_row


def frame_tables(lengths, span_start, span_end, flow_times, frame_index):
    utter_ends = jnp.cumsum(lengths)
    starts = utter_ends - lengths
    member = (
        (frame_index[:, None] >= starts[None, :]) & (frame_index[:, None] < utter_ends[None, :])
    ).astype(jnp.float32)
    labels = (jnp.arange(lengths.shape[0]) + 1).astype(jnp.float32)
    owners = jnp.sum(member * labels[None, :], 1) - 1.0
    position = frame_index.astype(jnp.float32) - jnp.sum(
        member * starts.astype(jnp.float32)[None, :], 1
    )
    low_end = jnp.sum(member * span_start.astype(jnp.float32)[None, :], 1)
    high_end = jnp.sum(member * span_end.astype(jnp.float32)[None, :], 1)
    masked = ((position >= low_end) & (position < high_end)).astype(jnp.float32)
    moment = jnp.sum(member * flow_times[None, :], 1)
    return (owners, masked, moment)


def mask_counts(lengths, span_start, span_end):
    span_low = jnp.minimum(span_start, lengths)
    span_high = jnp.minimum(span_end, lengths)
    covered = jnp.sum(jnp.maximum(span_high - span_low, 0)).astype(jnp.float32)
    return (covered, jnp.sum(lengths).astype(jnp.float32) - covered)


def time_features(moment, width):
    half_width = width // 2
    frequency = jnp.exp(
        -math.log(10000.0) * jnp.arange(half_width).astype(jnp.float32) / half_width
    )
    angles = moment[:, None] * 100.0 * frequency[None, :]
    return jnp.concatenate([jnp.sin(angles), jnp.cos(angles)], 1)


def product(left, right):
    return jnp.dot(left, right, preferred_element_type=jnp.float32)


def contract_rows(left, right):
    return lax.dot_general(
        left, right, (((0,), (0,)), ((), ())), preferred_element_type=jnp.float32
    )


def contract_cols(left, right):
    return lax.dot_general(
        left, right, (((1,), (1,)), ((), ())), preferred_element_type=jnp.float32
    )


def slice_window(full_rows, row_base, near_count, row_count):
    pad_rows = near_count * row_count
    padded = jnp.pad(full_rows, ((pad_rows, pad_rows), (0, 0)))
    return lax.dynamic_slice_in_dim(padded, row_base, (2 * near_count + 1) * row_count, 0)


MESH = pl.DeviceIdType.MESH
VM = pl.BlockSpec(memory_space=pltpu.VMEM)
SM = pl.BlockSpec(memory_space=pltpu.SMEM)
BF = jnp.bfloat16
F32 = jnp.float32
OWN = 128
EDGE = 16


def nn(a, b):
    return jnp.dot(a, b, preferred_element_type=F32)


def nt(a, b):
    return lax.dot_general(a, b, (((1,), (1,)), ((), ())), preferred_element_type=F32)


def tn(a, b):
    return lax.dot_general(a, b, (((0,), (0,)), ((), ())), preferred_element_type=F32)


def put(src, dst, send, recv, device):
    return pltpu.make_async_remote_copy(
        src_ref=src, dst_ref=dst, send_sem=send, recv_sem=recv, device_id=device, device_id_type=MESH
    )


class Place:
    def __init__(self):
        self.s, self.m = lax.axis_index("seq"), lax.axis_index("mp")
        self.z, self.x = self.s // 2, lax.rem(self.s, 2)
        self.y, self.c = self.m // 2, lax.rem(self.m, 2)
        self.core = (self.s, self.m + 1 - 2 * self.c)
        self.across = (self.s, lax.rem(self.m + 2, 4))
        self.side = (self.s + 1 - 2 * self.x, self.m)
        self.up = (self.s + 2, self.m)
        self.down = (self.s - 2, self.m)


def greet(peers):
    barrier = pltpu.get_barrier_semaphore()
    total = 0
    for device, exists in peers:
        if exists is None:
            pl.semaphore_signal(barrier, inc=1, device_id=device, device_id_type=MESH)
            total = total + 1
        else:

            @pl.when(exists)
            def _(device=device):
                pl.semaphore_signal(barrier, inc=1, device_id=device, device_id_type=MESH)

            total = total + exists.astype(jnp.int32)
    pl.semaphore_wait(barrier, total)


def grid_peers(p):
    return [(p.side, None), (p.up, p.z < 3), (p.down, p.z > 0)]


def mp_peers(p):
    return [(p.core, None), (p.across, None)]


class Gather:
    SEMS = [pltpu.SemaphoreType.DMA((3, 8)), pltpu.SemaphoreType.DMA((8,))]

    def __init__(self, p, view, send, recv):
        self.p, self.view, self.send, self.recv = p, view, send, recv

    def copy(self, slot, kind):
        p = self.p
        device = (p.side, p.up, p.down)[kind]
        return put(
            self.view(slot), self.view(slot), self.send.at[kind, slot], self.recv.at[slot], device
        )

    def start(self):
        p = self.p
        self.copy(p.s, 0).start()

        @pl.when(p.z < 3)
        def _():
            self.copy(p.s, 1).start()

        @pl.when(p.z > 0)
        def _():
            self.copy(p.s, 2).start()

    def step(self, hop):
        p = self.p
        below, above = p.s - 2 * (hop + 1), p.s + 2 * (hop + 1)

        @pl.when(p.z - 1 - hop >= 0)
        def _():
            self.copy(below, 0).wait_recv()
            self.copy(below, 0).start()

            @pl.when(p.z < 3)
            def _():
                self.copy(below, 1).start()

        @pl.when(p.z + 1 + hop <= 3)
        def _():
            self.copy(above, 0).wait_recv()
            self.copy(above, 0).start()

            @pl.when(p.z > 0)
            def _():
                self.copy(above, 2).start()

    def finish(self):
        p = self.p
        for zz in range(4):
            self.copy(2 * zz + 1 - p.x, 0).wait_recv()
        for zz in range(4):
            slot = 2 * zz + p.x
            self.copy(slot, 0).wait_send()

            @pl.when((p.z < 3) & (p.z >= zz))
            def _(slot=slot):
                self.copy(slot, 1).wait_send()

            @pl.when((p.z > 0) & (p.z <= zz))
            def _(slot=slot):
                self.copy(slot, 2).wait_send()


class BlockGather:
    SEMS = [pltpu.SemaphoreType.DMA((3,)), pltpu.SemaphoreType.DMA((4,))]

    def __init__(self, p, full, send, recv):
        self.p, self.full, self.send, self.recv = p, full, send, recv

    def copy(self, slot, kind):
        rows = self.full.at[pl.ds(pl.multiple_of(slot * OWN, OWN), OWN)]
        device = self.p.across if kind == 0 else self.p.core
        return put(rows, rows, self.send.at[kind], self.recv.at[slot], device)

    def start(self):
        self.copy(self.p.m, 0).start()
        self.copy(self.p.m, 1).start()

    def finish(self):
        p = self.p
        far = lax.rem(p.m + 2, 4)
        self.copy(far, 0).wait_recv()
        self.copy(far, 2).start()
        self.copy(p.m + 1 - 2 * p.c, 1).wait_recv()
        self.copy(lax.rem(p.m + 3 - 2 * p.c, 4), 2).wait_recv()
        for kind in range(3):
            self.copy(p.m, kind).wait_send()


class BlockReduce:
    SEMS = [pltpu.SemaphoreType.DMA((3,)), pltpu.SemaphoreType.DMA((3,))]

    def __init__(self, p, part, from_core, pair, send, recv):
        self.p, self.part, self.from_core, self.pair = p, part, from_core, pair
        self.send, self.recv = send, recv

    def rows(self, slot):
        return pl.ds(pl.multiple_of(slot * OWN, OWN), OWN)

    def core_copy(self, i):
        p = self.p
        yy = 1 - p.y if i == 0 else p.y
        return put(
            self.part.at[self.rows(2 * yy + 1 - p.c)], self.from_core.at[i],
            self.send.at[i], self.recv.at[i], p.core,
        )

    def across_copy(self):
        return put(self.pair.at[0], self.pair.at[1], self.send.at[2], self.recv.at[2], self.p.across)

    def far_rows(self):
        return pl.ds(pl.multiple_of((1 - self.p.y) * 2 * OWN, OWN), 2 * OWN)

    def near_rows(self):
        return pl.ds(pl.multiple_of(self.p.y * 2 * OWN, OWN), 2 * OWN)

    def send_far(self):
        p = self.p
        self.core_copy(0).start()
        self.core_copy(0).wait_recv()
        mine = self.part[self.rows(2 * (1 - p.y) + p.c), :].astype(F32)
        self.pair[0] = (mine + self.from_core[0].astype(F32)).astype(BF)
        self.across_copy().start()

    def send_near(self):
        self.core_copy(1).start()

    def finish(self):
        self.core_copy(1).wait_recv()
        total = self.part[self.rows(self.p.m), :].astype(F32) + self.from_core[1].astype(F32)
        self.across_copy().wait_recv()
        total = total + self.pair[1].astype(F32)
        self.core_copy(0).wait_send()
        self.core_copy(1).wait_send()
        self.across_copy().wait_send()
        return total


def reduce_scratch():
    return [pltpu.VMEM((512, D), BF), pltpu.VMEM((2, OWN, D), BF), pltpu.VMEM((2, OWN, D), BF)]


GELU_A = math.sqrt(2.0 / math.pi)


def gelu(v):
    return 0.5 * v * (1.0 + jnp.tanh(GELU_A * (v + 0.044715 * (v * v * v))))


def gelu_slope(v):
    t = jnp.tanh(GELU_A * (v + 0.044715 * (v * v * v)))
    return 0.5 * (1.0 + t) + 0.5 * v * (1.0 - t * t) * (GELU_A * (1.0 + 3.0 * 0.044715 * v * v))


def norm_parts(v):
    mean = jnp.mean(v, -1, keepdims=True)
    centered = v - mean
    variance = jnp.mean(centered * centered, -1, keepdims=True)
    scale = lax.rsqrt(variance + norm_epsilon)
    return centered * scale, scale


def norm_back(v, gain, grad):
    unit, scale = norm_parts(v)
    gain_row = jnp.sum(grad * unit, 0, keepdims=True)
    g = grad * gain
    inner = g - jnp.mean(g, -1, keepdims=True) - unit * jnp.mean(g * unit, -1, keepdims=True)
    return scale * inner, gain_row


def frame_columns(lengths, first, rows, extra=()):
    frame = first + lax.broadcasted_iota(jnp.int32, (rows, 1), 0)
    end = jnp.int32(0)
    owner = jnp.full((rows, 1), -1, jnp.int32)
    starts = jnp.zeros((rows, 1), jnp.int32)
    ends = jnp.zeros((rows, 1), jnp.int32)
    picked = [jnp.zeros((rows, 1), e.dtype) for e in extra]
    for u in range(lengths.shape[0]):
        start = end
        end = start + lengths[u]
        inside = (frame >= start) & (frame < end)
        owner = jnp.where(inside, u, owner)
        starts = jnp.where(inside, start, starts)
        ends = jnp.where(inside, end, ends)
        picked = [jnp.where(inside, e[u], c) for e, c in zip(extra, picked)]
    return frame, owner, starts, ends, picked


def tap_masks(frame, starts, ends, mask_ref):
    low = jnp.broadcast_to(starts - frame + 15, (OWN, 128))
    high = jnp.broadcast_to(ends - frame + 15, (OWN, 128))
    for k in range(31):
        mask_ref[k] = ((low <= k) & (high > k)).astype(F32)


def front_kernel(
    lengths, span_start, span_end, flow_times, pack_ref, table_ref, win_ref, phone_ref, kern_ref,
    gain_ref, watt_ref,
    h1_ref, conv_ref, rim_ref, a_ref, q_ref, k_ref, v_ref, wqkv_ref, wout_ref, feats_ref, choose_ref,
    ext, rimf, masks, edge_send, edge_recv, ag_send, ag_recv, w_send, w_recv, o_send, o_recv,
    k_send, k_recv, v_send, v_recv,
):
    p = Place()
    group = pack_ref.shape[0]
    prior, following = (p.s - 1, p.m), (p.s + 1, p.m)
    shard = watt_ref.shape[1]
    own_w = pl.ds(pl.multiple_of(p.s * shard, shard), shard)
    for j in range(3):
        wqkv_ref[j, own_w, :] = watt_ref[j].astype(BF)
    wout_ref[own_w, :] = watt_ref[3].astype(BF)
    ext[:EDGE, :] = jnp.zeros((EDGE, 256), F32)
    ext[EDGE + group :, :] = jnp.zeros((EDGE, 256), F32)
    ext[EDGE : EDGE + group, :] = pack_ref[...]
    greet(grid_peers(p) + mp_peers(p) + [(prior, p.s > 0), (following, p.s < 7)])
    edge_up = put(ext.at[pl.ds(group, EDGE)], ext.at[pl.ds(0, EDGE)], edge_send.at[0], edge_recv.at[0], following)
    edge_down = put(ext.at[pl.ds(EDGE, EDGE)], ext.at[pl.ds(EDGE + group, EDGE)], edge_send.at[1], edge_recv.at[1], prior)

    @pl.when(p.s < 7)
    def _():
        edge_up.start()

    @pl.when(p.s > 0)
    def _():
        edge_down.start()

    def shard_rows(slot):
        return pl.ds(pl.multiple_of(slot * shard, shard), shard)

    gather_w = Gather(p, lambda slot: wqkv_ref.at[:, shard_rows(slot), :], w_send, w_recv)
    gather_o = Gather(p, lambda slot: wout_ref.at[shard_rows(slot), :], o_send, o_recv)
    gather_w.start()
    gather_o.start()

    @pl.when(p.s > 0)
    def _():
        edge_up.wait_recv()

    @pl.when(p.s < 7)
    def _():
        edge_down.wait_recv()

    first = p.s * group + p.m * OWN
    wide = OWN + 2 * EDGE
    frame, owner, starts, _, picked = frame_columns(
        lengths, first - EDGE, wide, (span_start, span_end, flow_times)
    )
    position = frame - starts
    masked = ((position >= picked[0]) & (position < picked[1]) & (owner >= 0)).astype(F32)
    moment = picked[2]
    both = ext[pl.ds(pl.multiple_of(p.m * OWN, OWN), wide), :]
    mel, noise = both[:, :128], both[:, 128:]
    lane = lax.broadcasted_iota(jnp.int32, (wide, 128), 1)
    context = (mel * (1.0 - masked)).astype(BF)
    noisy = (1.0 - (1.0 - flow_sigma) * moment) * noise + moment * mel
    noisy = jnp.where(lane < MEL, noisy, 0.0).astype(BF)
    phone = noise[:, MEL : MEL + 1]
    choose = jnp.where(phone == lane.astype(F32), 1.0, 0.0).astype(BF)
    h0 = nn(context[:, :MEL], win_ref[:MEL, :].astype(BF))
    h0 = h0 + nn(noisy[:, :MEL], win_ref[MEL:, :].astype(BF)) + nn(choose, phone_ref[...].astype(BF))
    time = jnp.zeros((wide, D), F32)
    for u in range(table_ref.shape[0]):
        time = jnp.where(owner == u, table_ref[u : u + 1, :], time)
    h0 = h0 + time
    low = h0.astype(BF)
    rim_ref[...] = low
    rimf[...] = low.astype(F32)
    h1_ref[...] = h0[EDGE : EDGE + OWN]
    feats_ref[:, :128] = context[EDGE : EDGE + OWN]
    feats_ref[:, 128:] = noisy[EDGE : EDGE + OWN]
    choose_ref[...] = choose[EDGE : EDGE + OWN]
    gather_w.step(0)
    gather_o.step(0)
    frame, _, starts, ends, _ = frame_columns(lengths, first, OWN)
    tap_masks(frame, starts, ends, masks)

    @pl.loop(0, D // 128)
    def _(t):
        lanes = pl.ds(pl.multiple_of(t * 128, 128), 128)
        total = jnp.zeros((OWN, 128), F32)
        for k in range(31):
            total = total + kern_ref[k : k + 1, lanes] * (rimf[1 + k : 1 + k + OWN, lanes] * masks[k])
        conv_ref[:, lanes] = total

    h1 = h1_ref[...] + gelu(conv_ref[...])
    h1_ref[...] = h1
    unit, _ = norm_parts(h1)
    own = pl.ds(pl.multiple_of(p.m * OWN, OWN), OWN)
    a_ref[own, :] = (unit * gain_ref[0:1, :]).astype(BF)
    gather_a = BlockGather(p, a_ref, ag_send, ag_recv)
    gather_a.start()
    gather_w.step(1)
    gather_o.step(1)
    gather_a.finish()
    gather_w.step(2)
    gather_o.step(2)
    gather_w.finish()
    rows = pl.ds(pl.multiple_of(p.s * group, group), group)

    def rows_of(slot):
        return pl.ds(pl.multiple_of(slot * group, group), group)

    gather_k = Gather(p, lambda slot: k_ref.at[rows_of(slot), :], k_send, k_recv)
    gather_v = Gather(p, lambda slot: v_ref.at[rows_of(slot), :], v_send, v_recv)
    k_ref[rows, :] = nn(a_ref[...], wqkv_ref[1]).astype(BF)
    gather_k.start()
    v_ref[rows, :] = nn(a_ref[...], wqkv_ref[2]).astype(BF)
    gather_v.start()
    q_ref[...] = nn(a_ref[...], wqkv_ref[0]).astype(BF)
    gather_o.finish()
    for hop in range(3):
        gather_k.step(hop)
        gather_v.step(hop)
    gather_k.finish()
    gather_v.finish()

    @pl.when(p.s < 7)
    def _():
        edge_up.wait_send()

    @pl.when(p.s > 0)
    def _():
        edge_down.wait_send()


def vmem_call(kernel, outs, specs, scratch, cid, name, flops=1e9):
    return pl.pallas_call(
        kernel,
        out_shape=tuple(jax.ShapeDtypeStruct(*o) for o in outs),
        in_specs=specs,
        out_specs=tuple([VM] * len(outs)),
        scratch_shapes=scratch,
        compiler_params=pltpu.CompilerParams(
            collective_id=cid, has_side_effects=True, vmem_limit_bytes=56 << 20
        ),
        cost_estimate=pl.CostEstimate(flops=int(flops), bytes_accessed=1 << 24, transcendentals=0),
        name=name,
    )


def front(lengths, span_start, span_end, flow_times, pack, table, win, phone, kern, gains, watt):
    group = pack.shape[0]
    shard, width = watt.shape[1:]
    outs = [
        ((OWN, D), F32), ((OWN, D), F32), ((OWN + 2 * EDGE, D), BF), ((group, D), BF),
        ((group, width), BF), ((8 * group, width), BF), ((8 * group, width), BF),
        ((3, 8 * shard, width), BF), ((8 * shard, width), BF), ((OWN, 256), BF), ((OWN, 128), BF),
    ]
    scratch = [
        pltpu.VMEM((group + 2 * EDGE, 256), F32), pltpu.VMEM((OWN + 2 * EDGE, D), F32),
        pltpu.VMEM((31, OWN, 128), F32), pltpu.SemaphoreType.DMA((2,)), pltpu.SemaphoreType.DMA((2,)),
    ] + BlockGather.SEMS + Gather.SEMS * 4
    return vmem_call(front_kernel, outs, [SM] * 4 + [VM] * 7, scratch, 0, "front", 2e10)(
        lengths, span_start, span_end, flow_times, pack, table, win, phone, kern, gains, watt
    )


def middle_kernel(
    lengths, span_start, span_end, pack_ref, o32_ref, o_ref, lse_ref, q_ref, h1_ref, gain_ref,
    wout_ref, wff_ref, wpred_ref,
    dh2_ref, rows_ref, outg_ref, do_ref, delta_ref, qall_ref, doall_ref, stat_ref, gff_ref, gout_ref,
    u_ref, gated, b_ref, dy_ref, du_ref, dlow, h_ref, h3_ref, dh3_ref,
    part1, core1, pair1, part2, core2, pair2, part3, core3, pair3,
    s1, r1, s2, r2, s3, r3, as1, ar1, as2, ar2, as3, ar3,
    q_send, q_recv, d_send, d_recv, t_send, t_recv,
):
    p = Place()
    group = pack_ref.shape[0]
    halves = group // 2
    first = p.s * group + p.m * OWN
    own = pl.ds(pl.multiple_of(p.m * OWN, OWN), OWN)

    def rows_of(slot):
        return pl.ds(pl.multiple_of(slot * group, group), group)

    qall_ref[rows_of(p.s), :] = q_ref[...]
    greet(grid_peers(p) + mp_peers(p))
    gather_q = Gather(p, lambda slot: qall_ref.at[rows_of(slot), :], q_send, q_recv)
    gather_d = Gather(p, lambda slot: doall_ref.at[rows_of(slot), :], d_send, d_recv)
    gather_t = Gather(p, lambda slot: stat_ref.at[slot], t_send, t_recv)
    gather_q.start()

    red = BlockReduce(p, part1, core1, pair1, s1, r1)
    for rows, send in ((red.far_rows(), red.send_far), (red.near_rows(), red.send_near)):
        part1[rows, :] = nt(o_ref[rows, :], wout_ref[...]).astype(BF)
        send()
    gather_q.step(0)
    h2 = h1_ref[...] + red.finish()
    h_ref[...] = h2
    unit, _ = norm_parts(h2)
    b_ref[own, :] = (unit * gain_ref[1:2, :]).astype(BF)
    gather_b = BlockGather(p, b_ref, as1, ar1)
    gather_b.start()
    gather_q.step(1)
    gather_b.finish()

    ff = wff_ref.shape[2]
    tile = 256

    @pl.loop(0, ff // tile)
    def _(t):
        lanes = pl.ds(pl.multiple_of(t * tile, tile), tile)
        up = nn(b_ref[...], wff_ref[0, :, lanes])
        u_ref[:, lanes] = up
        gated[:, lanes] = gelu(up).astype(BF)

    red = BlockReduce(p, part2, core2, pair2, s2, r2)
    for rows, send in ((red.far_rows(), red.send_far), (red.near_rows(), red.send_near)):

        @pl.loop(0, D // tile)
        def _(t):
            lanes = pl.ds(pl.multiple_of(t * tile, tile), tile)
            part2[rows, lanes] = nt(gated[rows, :], wff_ref[1, lanes, :]).astype(BF)

        send()
    gather_q.step(2)
    _, owner, starts, _, picked = frame_columns(lengths, first, OWN, (span_start, span_end))
    position = first + lax.broadcasted_iota(jnp.int32, (OWN, 1), 0) - starts
    masked = ((position >= picked[0]) & (position < picked[1])).astype(F32)
    covered, frames = jnp.int32(0), jnp.int32(0)
    for n in range(lengths.shape[0]):
        span = jnp.minimum(span_end[n], lengths[n]) - jnp.minimum(span_start[n], lengths[n])
        covered = covered + jnp.maximum(span, 0)
        frames = frames + lengths[n]
    count = jnp.full((OWN, 1), jnp.maximum(covered, 1), jnp.int32).astype(F32)
    rest = jnp.full((OWN, 1), jnp.maximum(frames - covered, 1), jnp.int32).astype(F32)
    weight = masked / count + 0.1 * (1.0 - masked) / rest
    both = pack_ref[own, :]
    target = (both[:, :128] - (1.0 - flow_sigma) * both[:, 128:])[:, :MEL]
    wpred = wpred_ref[...].astype(BF)

    h3 = h_ref[...] + red.finish()
    h3_ref[...] = h3
    unit, _ = norm_parts(h3)
    low = (unit * gain_ref[2:3, :]).astype(BF)
    errors = nn(low, wpred) - target
    loss = jnp.sum(weight * jnp.mean(errors * errors, 1, keepdims=True), 0, keepdims=True)
    dpred = (weight * (2.0 / MEL) * errors).astype(BF)
    outg_ref[...] = tn(dpred, low)
    dh3, gain3 = norm_back(h3, gain_ref[2:3, :], nt(dpred, wpred))
    dh3_ref[...] = dh3
    dy_ref[own, :] = dh3.astype(BF)
    gather_y = BlockGather(p, dy_ref, as2, ar2)
    gather_y.start()
    gather_q.finish()
    gather_y.finish()

    @pl.loop(0, ff // tile)
    def _(t):
        lanes = pl.ds(pl.multiple_of(t * tile, tile), tile)
        down = nn(dy_ref[...], wff_ref[1, :, lanes])
        du_ref[:, lanes] = (down * gelu_slope(u_ref[:, lanes])).astype(BF)

    red = BlockReduce(p, part3, core3, pair3, s3, r3)
    for rows, send in ((red.far_rows(), red.send_far), (red.near_rows(), red.send_near)):

        @pl.loop(0, D // tile)
        def _(t):
            lanes = pl.ds(pl.multiple_of(t * tile, tile), tile)
            part3[rows, lanes] = nt(du_ref[rows, :], wff_ref[0, lanes, :]).astype(BF)

        send()

    @pl.loop(0, D // tile)
    def _(t):
        lanes = pl.ds(pl.multiple_of(t * tile, tile), tile)
        gff_ref[1, lanes, :] = tn(dy_ref[:, lanes], gated[...])

    db = red.finish()
    norm_grad, gain2 = norm_back(h_ref[...], gain_ref[1:2, :], db)
    dh2 = dh3_ref[...] + norm_grad
    dh2_ref[...] = dh2
    dlow[own, :] = dh2.astype(BF)
    gather_h = BlockGather(p, dlow, as3, ar3)
    gather_h.start()
    rows_ref[...] = jnp.concatenate(
        [gain3, gain2, jnp.broadcast_to(loss, (1, D)), jnp.zeros((5, D), F32)], 0
    )

    @pl.loop(0, D // tile)
    def _(t):
        lanes = pl.ds(pl.multiple_of(t * tile, tile), tile)
        gff_ref[0, lanes, :] = tn(b_ref[:, lanes], du_ref[...])

    gather_h.finish()
    grad = nn(dlow[...], wout_ref[...]).astype(BF)
    do_ref[...] = grad
    doall_ref[rows_of(p.s), :] = grad
    gather_d.start()
    weighted = grad.astype(F32) * o32_ref[...]
    width = o_ref.shape[1]
    head = lax.broadcasted_iota(jnp.int32, (width, 128), 0) // HD
    pick = (head == lax.broadcasted_iota(jnp.int32, (width, 128), 1)).astype(F32)
    delta_ref[...] = jnp.dot(weighted, pick, preferred_element_type=F32, precision=lax.Precision.HIGHEST)
    eye = (
        lax.broadcasted_iota(jnp.int32, (8, 128), 0) == lax.broadcasted_iota(jnp.int32, (8, 128), 1)
    ).astype(F32)
    for i, ref in enumerate((lse_ref, delta_ref)):
        stat_ref[p.s, 8 * i : 8 * i + 8, :] = lax.dot_general(
            eye, ref[...], (((1,), (1,)), ((), ())), preferred_element_type=F32, precision=lax.Precision.HIGHEST
        )
    gather_t.start()
    gout_ref[...] = tn(dlow[...], o_ref[...])
    for hop in range(3):
        gather_d.step(hop)
        gather_t.step(hop)
    gather_d.finish()
    gather_t.finish()


def middle(lengths, span_start, span_end, pack, o32, o, lse, q, h1, gains, wout, wff, wpred):
    group, width = o.shape
    ff = wff.shape[2]
    outs = [
        ((OWN, D), F32), ((8, D), F32), ((MEL, D), F32), ((group, width), BF), ((group, 128), F32),
        ((8 * group, width), BF), ((8 * group, width), BF), ((8, 16, group), F32),
        ((2, D, ff), F32), ((D, width), F32),
    ]
    scratch = [
        pltpu.VMEM((group, ff), F32), pltpu.VMEM((group, ff), BF), pltpu.VMEM((group, D), BF),
        pltpu.VMEM((group, D), BF), pltpu.VMEM((group, ff), BF), pltpu.VMEM((group, D), BF),
        pltpu.VMEM((OWN, D), F32), pltpu.VMEM((OWN, D), F32), pltpu.VMEM((OWN, D), F32),
    ] + reduce_scratch() * 3 + BlockReduce.SEMS * 3 + BlockGather.SEMS * 3 + Gather.SEMS * 3
    return vmem_call(middle_kernel, outs, [SM] * 3 + [VM] * 10, scratch, 1, "middle", 2e10)(
        lengths, span_start, span_end, pack, o32, o, lse, q, h1, gains, wout, wff, wpred
    )


def back_kernel(
    lengths, proj_ref, wqkv_ref, a_ref, dh2_ref, h1_ref, conv_ref, rim_ref, gain_ref, kern_ref,
    feats_ref, choose_ref, rows_ref, outg_ref,
    gqkv_ref, small_ref,
    dcb, dcf, rimf, masks, dh1_ref, spread, part, from_core, pair, s1, r1, edge_send, edge_recv,
):
    p = Place()
    group = a_ref.shape[0]
    place = p.s * 4 + p.m
    prior = ((place - 1) // 4, lax.rem(place + 3, 4))
    following = ((place + 1) // 4, lax.rem(place + 1, 4))
    dcb[:EDGE, :] = jnp.zeros((EDGE, D), BF)
    dcb[EDGE + OWN :, :] = jnp.zeros((EDGE, D), BF)
    greet(mp_peers(p) + [(prior, place > 0), (following, place < 31)])
    red = BlockReduce(p, part, from_core, pair, s1, r1)
    for rows, send in ((red.far_rows(), red.send_far), (red.near_rows(), red.send_near)):
        total = nt(proj_ref[0, rows, :], wqkv_ref[0])
        total = total + nt(proj_ref[1, rows, :], wqkv_ref[1])
        part[rows, :] = (total + nt(proj_ref[2, rows, :], wqkv_ref[2])).astype(BF)
        send()
    for j in range(3):
        gqkv_ref[j] = tn(a_ref[...], proj_ref[j])
    rimf[...] = rim_ref[...].astype(F32)
    frame, _, starts, ends, _ = frame_columns(lengths, p.s * group + p.m * OWN, OWN)
    tap_masks(frame, starts, ends, masks)
    norm_grad, gain1 = norm_back(h1_ref[...], gain_ref[0:1, :], red.finish())
    dh1 = dh2_ref[...] + norm_grad
    dh1_ref[...] = dh1
    dcb[EDGE : EDGE + OWN, :] = (dh1 * gelu_slope(conv_ref[...])).astype(BF)
    edge_up = put(dcb.at[pl.ds(OWN, EDGE)], dcb.at[pl.ds(0, EDGE)], edge_send.at[0], edge_recv.at[0], following)
    edge_down = put(dcb.at[pl.ds(EDGE, EDGE)], dcb.at[pl.ds(EDGE + OWN, EDGE)], edge_send.at[1], edge_recv.at[1], prior)

    @pl.when(place < 31)
    def _():
        edge_up.start()

    @pl.when(place > 0)
    def _():
        edge_down.start()

    dcf[EDGE : EDGE + OWN, :] = dcb[EDGE : EDGE + OWN, :].astype(F32)

    @pl.loop(0, D // 128)
    def _(t):
        lanes = pl.ds(pl.multiple_of(t * 128, 128), 128)
        mine = dcf[EDGE : EDGE + OWN, lanes]
        for k in range(31):
            seen = rimf[1 + k : 1 + k + OWN, lanes] * masks[k]
            small_ref[288 + k : 289 + k, lanes] = jnp.sum(mine * seen, 0, keepdims=True)

    @pl.when(place > 0)
    def _():
        edge_up.wait_recv()

    @pl.when(place < 31)
    def _():
        edge_down.wait_recv()

    dcf[:EDGE, :] = dcb[:EDGE, :].astype(F32)
    dcf[EDGE + OWN :, :] = dcb[EDGE + OWN :, :].astype(F32)

    @pl.loop(0, D // 128)
    def _(t):
        lanes = pl.ds(pl.multiple_of(t * 128, 128), 128)
        total = jnp.zeros((OWN, 128), F32)
        for k in range(31):
            total = total + kern_ref[30 - k : 31 - k, lanes] * (dcf[1 + k : 1 + k + OWN, lanes] * masks[k])
        spread[:, lanes] = total

    dh0 = (dh1_ref[...] + spread[...]).astype(BF)
    grad = tn(feats_ref[...], dh0)
    small_ref[:MEL, :] = grad[:MEL]
    small_ref[MEL : 2 * MEL, :] = grad[128 : 128 + MEL]
    small_ref[160:288, :] = tn(choose_ref[...], dh0)
    small_ref[319:320, :] = jnp.zeros((1, D), F32)
    small_ref[320:400, :] = outg_ref[...]
    small_ref[400:401, :] = gain1
    small_ref[401:408, :] = rows_ref[:7, :]

    @pl.when(place < 31)
    def _():
        edge_up.wait_send()

    @pl.when(place > 0)
    def _():
        edge_down.wait_send()


def back(lengths, proj, wqkv, a, dh2, h1, conv, rim, gains, kern, feats, choose, rows, outg):
    outs = [((3,) + wqkv.shape[1:], F32), ((408, D), F32)]
    wide = OWN + 2 * EDGE
    scratch = [
        pltpu.VMEM((wide, D), BF), pltpu.VMEM((wide, D), F32), pltpu.VMEM((wide, D), F32),
        pltpu.VMEM((31, OWN, 128), F32), pltpu.VMEM((OWN, D), F32), pltpu.VMEM((OWN, D), F32),
    ] + reduce_scratch() + BlockReduce.SEMS + [pltpu.SemaphoreType.DMA((2,)), pltpu.SemaphoreType.DMA((2,))]
    return vmem_call(back_kernel, outs, [SM] + [VM] * 13, scratch, 2, "back", 2e10)(
        lengths, proj, wqkv, a, dh2, h1, conv, rim, gains, kern, feats, choose, rows, outg
    )


KT = 512


def lane_half(rows):
    return lax.broadcasted_iota(jnp.int32, (rows, 128), 1) < HD


def stack_pair(x):
    low, zero = lane_half(x.shape[0]), jnp.zeros_like(x)
    return jnp.concatenate([jnp.where(low, x, zero), jnp.where(low, zero, x)], 0)


def unstack_pair(x):
    rows = x.shape[0] // 2
    return jnp.where(lane_half(rows), x[:rows], x[rows:])


def slope_of(index):
    value = jnp.float32(2.0 ** (-8.0 * HEADS / HEADS))
    for head in range(HEADS - 1):
        value = jnp.where(index == head, jnp.float32(2.0 ** (-8.0 * (head + 1) / HEADS)), value)
    return value


def tile_range(lengths, first, base):
    end = jnp.int32(0)
    low = jnp.int32(0)
    high = jnp.int32(0)
    for u in range(lengths.shape[0]):
        start = end
        end = start + lengths[u]
        low = jnp.where((start <= first) & (first < end), start, low)
        last = first + OWN - 1
        high = jnp.where((start <= last) & (last < end), end, high)
    return (low - base) // KT, (high - base + KT - 1) // KT


def owner_row(lengths, base, kown):
    frame = base + lax.broadcasted_iota(jnp.int32, kown.shape, 1)
    owner = jnp.full(kown.shape, -1, jnp.int32)
    end = jnp.int32(0)
    for u in range(lengths.shape[0]):
        start = end
        end = start + lengths[u]
        owner = jnp.where((frame >= start) & (frame < end), u, owner)
    kown[...] = owner


def attend_setup(lengths, base, kown, width):
    i = pl.program_id(0)
    first = base[1] + i * OWN

    @pl.when(i == 0)
    def _():
        owner_row(lengths, base[0], kown)

    low, high = tile_range(lengths, first, base[0])
    _, owner, _, _, _ = frame_columns(lengths, first, OWN)
    heads = width // HD
    slopes = [slope_of(lax.axis_index("mp") * heads + h) for h in range(heads)]

    def distance(k0):
        shape = (OWN, KT)
        gap = (first - base[0] - k0) + lax.broadcasted_iota(jnp.int32, shape, 0)
        dist = jnp.abs(gap - lax.broadcasted_iota(jnp.int32, shape, 1)).astype(F32)
        return jnp.where(owner == kown[:, pl.ds(k0, KT)], dist, 1e30)

    return low, high, slopes, distance


def attend_forward_kernel(lengths, base, q_ref, k_ref, v_ref, o_ref, ob_ref, lse_ref, kown):
    width = q_ref.shape[1]
    low, high, slopes, distance = attend_setup(lengths, base, kown, width)
    lanes = [slice(128 * j, 128 * (j + 1)) for j in range(width // 128)]
    qs = [stack_pair(q_ref[:, l]) * BF(0.125) for l in lanes]

    def body(t, carry):
        k0 = pl.multiple_of(t * KT, KT)
        dist = distance(k0)
        out = []
        for j, l in enumerate(lanes):
            top, total, acc = carry[j]
            s = nt(qs[j], k_ref[pl.ds(k0, KT), l])
            s = jnp.concatenate([s[:OWN] - slopes[2 * j] * dist, s[OWN:] - slopes[2 * j + 1] * dist], 0)
            new = jnp.maximum(top, jnp.max(s, -1, keepdims=True))
            fade = jnp.exp(top - new)
            e = jnp.exp(s - new)
            total = total * fade + jnp.sum(e, -1, keepdims=True)
            acc = acc * fade + nn(e.astype(BF), v_ref[pl.ds(k0, KT), l])
            out.append((new, total, acc))
        return tuple(out)

    begin = (
        jnp.full((2 * OWN, 1), -1e30, F32), jnp.zeros((2 * OWN, 1), F32), jnp.zeros((2 * OWN, 128), F32),
    )
    ended = lax.fori_loop(low, high, body, tuple(begin for _ in lanes))
    lane = lax.broadcasted_iota(jnp.int32, (OWN, 128), 1)
    lse = jnp.zeros((OWN, 128), F32)
    for j, l in enumerate(lanes):
        top, total, acc = ended[j]
        o = unstack_pair(acc / total)
        o_ref[:, l] = o
        ob_ref[:, l] = o.astype(BF)
        g = top + jnp.log(total)
        lse = jnp.where(lane == 2 * j, g[:OWN], lse)
        lse = jnp.where(lane == 2 * j + 1, g[OWN:], lse)
    lse_ref[...] = lse


def blocks(width):
    return pl.BlockSpec((OWN, width), lambda i, *_: (i, 0))


def whole(*shape):
    return pl.BlockSpec(shape, lambda i, *_: (0,) * len(shape))


def attend_call(kernel, outs, out_specs, in_specs, rows, keys, name, flops):
    return pl.pallas_call(
        kernel,
        out_shape=outs,
        grid_spec=pltpu.PrefetchScalarGridSpec(
            num_scalar_prefetch=2, grid=(rows // OWN,), in_specs=in_specs, out_specs=out_specs,
            scratch_shapes=[pltpu.VMEM((1, keys), jnp.int32)],
        ),
        compiler_params=pltpu.CompilerParams(vmem_limit_bytes=50 << 20),
        cost_estimate=pl.CostEstimate(flops=flops, bytes_accessed=1 << 23, transcendentals=0),
        name=name,
    )


def attend_forward(lengths, base, q, k, v):
    (rows, width), keys = q.shape, k.shape[0]
    outs = (
        jax.ShapeDtypeStruct((rows, width), F32), jax.ShapeDtypeStruct((rows, width), BF),
        jax.ShapeDtypeStruct((rows, 128), F32),
    )
    return attend_call(
        attend_forward_kernel, outs, (blocks(width), blocks(width), blocks(128)),
        [blocks(width), whole(keys, width), whole(keys, width)], rows, keys, "attend_forward", 10**10,
    )(lengths, base, q, k, v)


def attend_backward_kernel(
    lengths, base, q_ref, k_ref, v_ref, do_ref, lse_ref, delta_ref, qa_ref, ka_ref, va_ref, doa_ref,
    stat_ref, out_ref, kown,
):
    width = q_ref.shape[1]
    low, high, slopes, distance = attend_setup(lengths, base, kown, width)
    lanes = [slice(128 * j, 128 * (j + 1)) for j in range(width // 128)]

    def column(ref, j):
        return jnp.concatenate([ref[:, 2 * j : 2 * j + 1], ref[:, 2 * j + 1 : 2 * j + 2]], 0)

    scale = BF(0.125)
    qs = [stack_pair(q_ref[:, l]) * scale for l in lanes]
    dos = [stack_pair(do_ref[:, l]) for l in lanes]
    ks = [stack_pair(k_ref[:, l]) * scale for l in lanes]
    vs = [stack_pair(v_ref[:, l]) for l in lanes]
    lses = [column(lse_ref, j) for j in range(len(lanes))]
    deltas = [column(delta_ref, j) for j in range(len(lanes))]

    def body(t, carry):
        k0 = pl.multiple_of(t * KT, KT)
        keys = pl.ds(k0, KT)
        dist = distance(k0)
        out = []
        for j, l in enumerate(lanes):
            dq, dk, dv = carry[j]
            kj, vj, qj, doj = ka_ref[keys, l], va_ref[keys, l], qa_ref[keys, l], doa_ref[keys, l]
            bias = [slopes[2 * j + h] * dist for h in (0, 1)]
            s = nt(qs[j], kj)
            e = jnp.exp(jnp.concatenate([s[:OWN] - bias[0], s[OWN:] - bias[1]], 0) - lses[j])
            ds = (e * (nt(dos[j], vj) - deltas[j])).astype(BF)
            dq = dq + nn(ds, kj)
            s = nt(ks[j], qj)
            far = [stat_ref[t, 2 * j + h : 2 * j + h + 1, :] for h in (0, 1)]
            e = jnp.exp(jnp.concatenate([s[:OWN] - bias[0] - far[0], s[OWN:] - bias[1] - far[1]], 0))
            dv = dv + nn(e.astype(BF), doj)
            g = nt(vs[j], doj)
            far = [stat_ref[t, 8 + 2 * j + h : 9 + 2 * j + h, :] for h in (0, 1)]
            ds = (e * jnp.concatenate([g[:OWN] - far[0], g[OWN:] - far[1]], 0)).astype(BF)
            dk = dk + nn(ds, qj)
            out.append((dq, dk, dv))
        return tuple(out)

    zero = jnp.zeros((2 * OWN, 128), F32)
    ended = lax.fori_loop(low, high, body, tuple((zero, zero, zero) for _ in lanes))
    for j, l in enumerate(lanes):
        dq, dk, dv = ended[j]
        out_ref[0, :, l] = (unstack_pair(dq) * 0.125).astype(BF)
        out_ref[1, :, l] = (unstack_pair(dk) * 0.125).astype(BF)
        out_ref[2, :, l] = unstack_pair(dv).astype(BF)


def attend_backward(lengths, base, q, k, v, do, lse, delta, qa, ka, va, doa, stat):
    (rows, width), keys = q.shape, ka.shape[0]
    return attend_call(
        attend_backward_kernel, jax.ShapeDtypeStruct((3, rows, width), BF),
        pl.BlockSpec((3, OWN, width), lambda i, *_: (0, i, 0)),
        [blocks(width)] * 4 + [blocks(128)] * 2 + [whole(keys, width)] * 4 + [whole(*stat.shape)],
        rows, keys, "attend_backward", 3 * 10**10,
    )(lengths, base, q, k, v, do, lse, delta, qa, ka, va, doa, stat)


def adam_step(weight, first_old, second, gradient, step_rate, decay_on):
    first_new = beta_one * first_old + (1.0 - beta_one) * gradient
    second_new = beta_two * second + (1.0 - beta_two) * gradient * gradient
    fix_one = 1.0 - beta_one**STEP
    fix_two = 1.0 - beta_two**STEP
    moved = first_new / fix_one / (jnp.sqrt(second_new / fix_two) + adam_epsilon)
    return (first_new, second_new, weight - step_rate * (moved + decay_on * weight_decay * weight))


def update(loss_total, grads, frames, states):
    weights, firsts, seconds = states
    big_squares = jnp.sum(grads[0] * grads[0]) + jnp.sum(grads[1] * grads[1])
    small_squares = jnp.zeros((), jnp.float32)
    for gradient in grads[2:]:
        small_squares = small_squares + jnp.sum(gradient * gradient)
    big_total = lax.psum(big_squares, ("seq", "mp"))
    grad_norm = jnp.sqrt(big_total + small_squares)
    factor = jnp.minimum(1.0, 0.3 / math.sqrt(frames) / grad_norm)
    results = [loss_total, grad_norm]
    for number in range(7):
        results.extend(
            adam_step(
                weights[number],
                firsts[number],
                seconds[number],
                grads[number] * factor,
                step_rates[number],
                decay_flags[number],
            )
        )
    return tuple(results)


def split_arguments(arguments):
    rest = arguments[7:]
    return arguments[:7], (rest[0::3], rest[1::3], rest[2::3])


def per_device(*arguments):
    inputs, states = split_arguments(arguments)
    row_count = inputs[0].shape[0]
    if (lax.axis_size("seq"), lax.axis_size("mp"), row_count) == (8, 4, 512):
        return step_by_kernels(inputs, states)
    return step_by_collectives(inputs, states)


def step_by_kernels(inputs, states):
    mel, noise, phone_ids, lengths, span_start, span_end, flow_times = inputs
    attention, feedforward, win, phone_table, kern, wpred, gains = states[0]
    row_count = mel.shape[0]
    frames = row_count * lax.axis_size("seq")
    wff = lax.all_gather(feedforward.astype(BF), "seq", axis=1, tiled=True)
    columns = ((0, 0), (0, 128 - MEL))
    with_phone = jnp.concatenate([noise, phone_ids.astype(F32)[:, None]], 1)
    pack = jnp.concatenate(
        [jnp.pad(mel, columns), jnp.pad(with_phone, ((0, 0), (0, 127 - MEL)))], 1
    )
    table = time_features(flow_times, D)
    h1, conv, rim, a, q, k, v, wqkv, wout, feats, choose = front(
        lengths, span_start, span_end, flow_times, pack, table, win, phone_table, kern, gains, attention
    )
    row_base = lax.axis_index("seq") * row_count
    base = jnp.stack([jnp.zeros_like(row_base), row_base]).astype(jnp.int32)
    o32, o, lse = attend_forward(lengths, base, q, k, v)
    dh2, rows, outg, do, delta, q_all, do_all, stat, gff, gout = middle(
        lengths, span_start, span_end, pack, o32, o, lse, q, h1, gains, wout, wff, wpred
    )
    k_own = lax.dynamic_slice_in_dim(k, row_base, row_count, 0)
    v_own = lax.dynamic_slice_in_dim(v, row_base, row_count, 0)
    proj = attend_backward(lengths, base, q, k_own, v_own, do, lse, delta, q_all, k, v, do_all, stat)
    gqkv, small = back(
        lengths, proj, wqkv, a, dh2, h1, conv, rim, gains, kern, feats, choose, rows, outg
    )
    small = lax.psum(small, ("seq", "mp"))
    feedforward_grad = lax.psum_scatter(gff, "seq", scatter_dimension=1, tiled=True)
    attention_grad = lax.psum_scatter(
        jnp.concatenate([gqkv, gout[None]], 0), "seq", scatter_dimension=1, tiled=True
    )
    gain_grad = jnp.stack([small[400], small[402], small[401]])
    grads = (
        attention_grad, feedforward_grad, small[:160], small[160:288], small[288:319],
        small[320:400].T, gain_grad,
    )
    return update(small[403, 0], grads, frames, states)


def step_by_collectives(inputs, states):
    mel_frames, noise_frames, phone_ids, lengths, span_start, span_end, flow_times = inputs
    (
        attention_weight,
        feedforward_weight,
        input_weight,
        phone_table,
        position_kernel,
        output_weight,
        layer_gains,
    ) = states[0]
    row_count = mel_frames.shape[0]
    frames = row_count * lax.axis_size("seq")
    row_base = lax.axis_index("seq") * row_count
    longest = min(MAXLEN, frames // 2)
    near_count = min((longest - 1 + row_count - 1) // row_count, lax.axis_size("seq") - 1)
    window_start = row_base - near_count * row_count
    reach = position_kernel.shape[0] // 2
    tables = (lengths, span_start, span_end, flow_times)
    row_index = row_base + jnp.arange(row_count)
    owners, masked, moment = frame_tables(*tables, row_index)
    covered, uncovered = mask_counts(lengths, span_start, span_end)
    row_weight = masked / jnp.maximum(covered, 1.0) + 0.1 * (1.0 - masked) / jnp.maximum(
        uncovered, 1.0
    )
    attention_full, feedforward_full = (
        lax.all_gather(attention_weight.astype(jnp.bfloat16), "seq", axis=1, tiled=True),
        lax.all_gather(feedforward_weight.astype(jnp.bfloat16), "seq", axis=1, tiled=True),
    )
    heads_local = attention_full.shape[2] // HD
    target = mel_frames - (1.0 - flow_sigma) * noise_frames
    noisy = (1.0 - (1.0 - flow_sigma) * moment[:, None]) * noise_frames + moment[
        :, None
    ] * mel_frames
    context = mel_frames * (1.0 - masked[:, None])
    feats = jnp.concatenate([context, noisy], 1).astype(jnp.bfloat16)
    choose = (phone_ids[:, None] == jnp.arange(phone_table.shape[0])[None, :]).astype(jnp.bfloat16)
    start_h = product(feats, input_weight.astype(jnp.bfloat16)) + product(
        choose, phone_table.astype(jnp.bfloat16)
    )
    start_h = start_h + time_features(moment, D)
    start_low = start_h.astype(jnp.bfloat16)
    rim = padded_2(start_low, (("seq", 0),), reach)
    pad_owner = frame_tables(*tables, row_base - reach + jnp.arange(row_count + 2 * reach))[0]
    conv_raw = jnp.zeros(start_h.shape, jnp.float32)
    for offset in range(position_kernel.shape[0]):
        same_owner = (pad_owner[offset : offset + row_count] == owners).astype(jnp.float32)
        conv_raw = (
            conv_raw
            + position_kernel[offset][None, :]
            * rim[offset : offset + row_count].astype(jnp.float32)
            * same_owner[:, None]
        )
    conv_gelu, conv_back = jax.vjp(jax.nn.gelu, conv_raw)
    hidden_one = start_h + conv_gelu
    ln_one, norm_back_one = jax.vjp(layer_norm, hidden_one, layer_gains[0])
    ln_one_low = ln_one.astype(jnp.bfloat16)
    projected = jnp.einsum(
        "td,kdh->kth", ln_one_low, attention_full[:3], preferred_element_type=jnp.float32
    ).astype(jnp.bfloat16)
    queries, keyed, valued = (projected[0], projected[1], projected[2])
    def window(array):
        return slice_window(
            lax.all_gather(array, "seq", axis=0, tiled=True), row_base, near_count, row_count
        )

    base = jnp.stack([window_start, row_base]).astype(jnp.int32)
    key_all, value_all = window(keyed), window(valued)
    out_f32, out_low, log_total = attend_forward(lengths, base, queries, key_all, value_all)
    attended = lax.psum(
        contract_cols(out_low, attention_full[3]).astype(jnp.bfloat16), "mp"
    ).astype(jnp.float32)
    hidden_two = hidden_one + attended
    ln_two, norm_back_two = jax.vjp(layer_norm, hidden_two, layer_gains[1])
    ln_two_low = ln_two.astype(jnp.bfloat16)
    upward = product(ln_two_low, feedforward_full[0])
    gated_f32, gelu_back = jax.vjp(jax.nn.gelu, upward)
    gated = gated_f32.astype(jnp.bfloat16)
    downward = lax.psum(
        contract_cols(gated, feedforward_full[1]).astype(jnp.bfloat16), "mp"
    ).astype(jnp.float32)
    hidden_three = hidden_two + downward
    ln_three, norm_back_three = jax.vjp(layer_norm, hidden_three, layer_gains[2])
    ln_three_low = ln_three.astype(jnp.bfloat16)
    output_low = output_weight.astype(jnp.bfloat16)
    predicted = product(ln_three_low, output_low)
    errors = predicted - target
    loss_local = jnp.sum(row_weight * jnp.mean(errors * errors, 1))
    loss_total = lax.psum(loss_local, "seq")
    pred_grad = (row_weight[:, None] * (2.0 / errors.shape[1]) * errors).astype(jnp.bfloat16)
    output_grad = contract_rows(ln_three_low, pred_grad)
    three_grad, gain_three = norm_back_three(contract_cols(pred_grad, output_low))
    down_low = three_grad.astype(jnp.bfloat16)
    down_wgrad = contract_rows(down_low, gated)
    up_grad = gelu_back(product(down_low, feedforward_full[1]))[0].astype(jnp.bfloat16)
    up_wgrad = contract_rows(ln_two_low, up_grad)
    two_sum = lax.psum(
        contract_cols(up_grad, feedforward_full[0]).astype(jnp.bfloat16), "mp"
    ).astype(jnp.float32)
    norm_grad, gain_two = norm_back_two(two_sum)
    two_grad = three_grad + norm_grad
    attended_low = two_grad.astype(jnp.bfloat16)
    out_wgrad = contract_rows(attended_low, out_low)
    out_heads = product(attended_low, attention_full[3]).astype(jnp.bfloat16)
    delta = jnp.sum(
        (out_heads.astype(jnp.float32) * out_f32).reshape(row_count, heads_local, HD), 2
    )
    delta = jnp.pad(delta, ((0, 0), (0, 128 - heads_local)))
    stat = window(jnp.concatenate([log_total[:, :8], delta[:, :8]], 1))
    stat = stat.reshape(-1, KT, 16).transpose(0, 2, 1)
    proj_grad = attend_backward(
        lengths, base, queries, keyed, valued, out_heads, log_total, delta,
        window(queries), key_all, value_all, window(out_heads), stat,
    )
    qkv_wgrad = jnp.einsum("td,kth->kdh", ln_one_low, proj_grad, preferred_element_type=jnp.float32)
    one_part = jnp.einsum(
        "kth,kdh->td", proj_grad, attention_full[:3], preferred_element_type=jnp.float32
    )
    one_sum = lax.psum(one_part.astype(jnp.bfloat16), "mp").astype(jnp.float32)
    norm_grad, gain_one = norm_back_one(one_sum)
    one_grad = two_grad + norm_grad
    conv_grad = conv_back(one_grad)[0].astype(jnp.bfloat16)
    grad_rim = padded_2(conv_grad, (("seq", 0),), reach)
    spread = jnp.zeros(one_grad.shape, jnp.float32)
    kernel_rows = []
    conv_grad_f32 = conv_grad.astype(jnp.float32)
    for offset in range(position_kernel.shape[0]):
        back_start = 2 * reach - offset
        same_back = (pad_owner[back_start : back_start + row_count] == owners).astype(jnp.float32)
        spread = (
            spread
            + position_kernel[offset][None, :]
            * grad_rim[back_start : back_start + row_count].astype(jnp.float32)
            * same_back[:, None]
        )
        same_fore = (pad_owner[offset : offset + row_count] == owners).astype(jnp.float32)
        kernel_rows.append(
            jnp.sum(
                conv_grad_f32
                * rim[offset : offset + row_count].astype(jnp.float32)
                * same_fore[:, None],
                0,
            )
        )
    kernel_grad = jnp.stack(kernel_rows)
    start_grad = (one_grad + spread).astype(jnp.bfloat16)
    input_wgrad = contract_rows(feats, start_grad)
    phone_wgrad = contract_rows(choose, start_grad)
    gains_grad = jnp.stack([gain_one, gain_two, gain_three])
    small_sums = lax.psum((input_wgrad, phone_wgrad, kernel_grad, output_grad, gains_grad), "seq")
    attention_grad, feedforward_grad = (
        lax.psum_scatter(
            jnp.concatenate([qkv_wgrad, out_wgrad[None]], 0), "seq", scatter_dimension=1, tiled=True
        ),
        lax.psum_scatter(jnp.stack([up_wgrad, down_wgrad]), "seq", scatter_dimension=1, tiled=True),
    )
    grads = (attention_grad, feedforward_grad) + tuple(small_sums)
    return update(loss_total, grads, frames, states)


def solution(mesh):
    in_specs = (
        P("seq", None),
        P("seq", None),
        P("seq"),
        P(),
        P(),
        P(),
        P(),
        P(None, "seq", "mp"),
        P(None, "seq", "mp"),
        P(None, "seq", "mp"),
        P(None, "seq", "mp"),
        P(None, "seq", "mp"),
        P(None, "seq", "mp"),
        P(),
        P(),
        P(),
        P(),
        P(),
        P(),
        P(),
        P(),
        P(),
        P(),
        P(),
        P(),
        P(),
        P(),
        P(),
    )
    out_specs = (
        P(),
        P(),
        P(None, "seq", "mp"),
        P(None, "seq", "mp"),
        P(None, "seq", "mp"),
        P(None, "seq", "mp"),
        P(None, "seq", "mp"),
        P(None, "seq", "mp"),
        P(),
        P(),
        P(),
        P(),
        P(),
        P(),
        P(),
        P(),
        P(),
        P(),
        P(),
        P(),
        P(),
        P(),
        P(),
    )
    return jax.shard_map(
        per_device, mesh=mesh, in_specs=in_specs, out_specs=out_specs, check_vma=False
    )
```

```python
import functools
import math

import jax
import jax.numpy as jnp
from jax import lax
from jax.experimental import pallas as pl
from jax.experimental.pallas import tpu as pltpu
from jax.sharding import PartitionSpec as P

D = 1024
HEADS = 16
HD = 64
MEL = 80
STEP = 10
MAXLEN = 1600


norm_epsilon = 1e-05
flow_sigma = 1e-05
beta_one = 0.9
beta_two = 0.95
adam_epsilon = 1e-08
weight_decay = 0.1
step_rates = (0.04, 0.04, 0.08, 1.0, 0.2, 0.04, 1.0)
decay_flags = (1.0, 1.0, 1.0, 1.0, 1.0, 1.0, 0.0)


def padded_2(array, sides, width):
    for axis, dim in sides:
        devices, length = (lax.axis_size(axis), array.shape[dim])
        up = [(i, (i + 1) % devices) for i in range(devices - 1)]
        down = [(j, i) for i, j in up]
        last = lax.slice_in_dim(array, length - width, length, axis=dim)
        initial = lax.slice_in_dim(array, 0, width, axis=dim)
        before = lax.ppermute(last, axis, up)
        after = lax.ppermute(initial, axis, down)
        array = jnp.concatenate([before, array, after], axis=dim)
    return array


def layer_norm(inputs, gain_row):
    centre_mean = jnp.mean(inputs, -1, keepdims=True)
    centered = inputs - centre_mean
    variance = jnp.mean(centered * centered, -1, keepdims=True)
    return centered * lax.rsqrt(variance + norm_epsilon) * gain_row


def frame_tables(lengths, span_start, span_end, flow_times, frame_index):
    utter_ends = jnp.cumsum(lengths)
    starts = utter_ends - lengths
    member = (
        (frame_index[:, None] >= starts[None, :]) & (frame_index[:, None] < utter_ends[None, :])
    ).astype(jnp.float32)
    labels = (jnp.arange(lengths.shape[0]) + 1).astype(jnp.float32)
    owners = jnp.sum(member * labels[None, :], 1) - 1.0
    position = frame_index.astype(jnp.float32) - jnp.sum(
        member * starts.astype(jnp.float32)[None, :], 1
    )
    low_end = jnp.sum(member * span_start.astype(jnp.float32)[None, :], 1)
    high_end = jnp.sum(member * span_end.astype(jnp.float32)[None, :], 1)
    masked = ((position >= low_end) & (position < high_end)).astype(jnp.float32)
    moment = jnp.sum(member * flow_times[None, :], 1)
    return (owners, masked, moment)


def mask_counts(lengths, span_start, span_end):
    span_low = jnp.minimum(span_start, lengths)
    span_high = jnp.minimum(span_end, lengths)
    covered = jnp.sum(jnp.maximum(span_high - span_low, 0)).astype(jnp.float32)
    return (covered, jnp.sum(lengths).astype(jnp.float32) - covered)


def time_features(moment, width):
    half_width = width // 2
    frequency = jnp.exp(
        -math.log(10000.0) * jnp.arange(half_width).astype(jnp.float32) / half_width
    )
    angles = moment[:, None] * 100.0 * frequency[None, :]
    return jnp.concatenate([jnp.sin(angles), jnp.cos(angles)], 1)


def product(left, right):
    return jnp.dot(left, right, preferred_element_type=jnp.float32)


def contract_rows(left, right):
    return lax.dot_general(
        left, right, (((0,), (0,)), ((), ())), preferred_element_type=jnp.float32
    )


def contract_cols(left, right):
    return lax.dot_general(
        left, right, (((1,), (1,)), ((), ())), preferred_element_type=jnp.float32
    )


def slice_window(full_rows, row_base, near_count, row_count):
    pad_rows = near_count * row_count
    padded = jnp.pad(full_rows, ((pad_rows, pad_rows), (0, 0)))
    return lax.dynamic_slice_in_dim(padded, row_base, (2 * near_count + 1) * row_count, 0)


MESH = pl.DeviceIdType.MESH
VM = pl.BlockSpec(memory_space=pltpu.VMEM)
SM = pl.BlockSpec(memory_space=pltpu.SMEM)
BF = jnp.bfloat16
F32 = jnp.float32
OWN = 128
EDGE = 16


def nn(a, b):
    return jnp.dot(a, b, preferred_element_type=F32)


def nt(a, b):
    return lax.dot_general(a, b, (((1,), (1,)), ((), ())), preferred_element_type=F32)


def tn(a, b):
    return lax.dot_general(a, b, (((0,), (0,)), ((), ())), preferred_element_type=F32)


def put(src, dst, send, recv, device):
    return pltpu.make_async_remote_copy(
        src_ref=src, dst_ref=dst, send_sem=send, recv_sem=recv, device_id=device, device_id_type=MESH
    )


class Place:
    def __init__(self):
        self.s, self.m = lax.axis_index("seq"), lax.axis_index("mp")
        self.z, self.x = self.s // 2, lax.rem(self.s, 2)
        self.y, self.c = self.m // 2, lax.rem(self.m, 2)
        self.core = (self.s, self.m + 1 - 2 * self.c)
        self.across = (self.s, lax.rem(self.m + 2, 4))
        self.side = (self.s + 1 - 2 * self.x, self.m)
        self.up = (self.s + 2, self.m)
        self.down = (self.s - 2, self.m)


def greet(peers):
    barrier = pltpu.get_barrier_semaphore()
    total = 0
    for device, exists in peers:
        if exists is None:
            pl.semaphore_signal(barrier, inc=1, device_id=device, device_id_type=MESH)
            total = total + 1
        else:

            @pl.when(exists)
            def _(device=device):
                pl.semaphore_signal(barrier, inc=1, device_id=device, device_id_type=MESH)

            total = total + exists.astype(jnp.int32)
    pl.semaphore_wait(barrier, total)


def grid_peers(p):
    return [(p.side, None), (p.up, p.z < 3), (p.down, p.z > 0)]


def mp_peers(p):
    return [(p.core, None), (p.across, None)]


class Gather:
    SEMS = [pltpu.SemaphoreType.DMA((3, 8)), pltpu.SemaphoreType.DMA((8,))]

    def __init__(self, p, view, send, recv):
        self.p, self.view, self.send, self.recv = p, view, send, recv

    def copy(self, slot, kind):
        p = self.p
        device = (p.side, p.up, p.down)[kind]
        return put(
            self.view(slot), self.view(slot), self.send.at[kind, slot], self.recv.at[slot], device
        )

    def start(self):
        p = self.p
        self.copy(p.s, 0).start()

        @pl.when(p.z < 3)
        def _():
            self.copy(p.s, 1).start()

        @pl.when(p.z > 0)
        def _():
            self.copy(p.s, 2).start()

    def step(self, hop):
        p = self.p
        below, above = p.s - 2 * (hop + 1), p.s + 2 * (hop + 1)

        @pl.when(p.z - 1 - hop >= 0)
        def _():
            self.copy(below, 0).wait_recv()
            self.copy(below, 0).start()

            @pl.when(p.z < 3)
            def _():
                self.copy(below, 1).start()

        @pl.when(p.z + 1 + hop <= 3)
        def _():
            self.copy(above, 0).wait_recv()
            self.copy(above, 0).start()

            @pl.when(p.z > 0)
            def _():
                self.copy(above, 2).start()

    def finish(self):
        p = self.p
        for zz in range(4):
            self.copy(2 * zz + 1 - p.x, 0).wait_recv()
        for zz in range(4):
            slot = 2 * zz + p.x
            self.copy(slot, 0).wait_send()

            @pl.when((p.z < 3) & (p.z >= zz))
            def _(slot=slot):
                self.copy(slot, 1).wait_send()

            @pl.when((p.z > 0) & (p.z <= zz))
            def _(slot=slot):
                self.copy(slot, 2).wait_send()


class NearGather:
    SEMS = [pltpu.SemaphoreType.DMA((8,)), pltpu.SemaphoreType.DMA((8,))]

    def __init__(self, p, view, edge, send, recv):
        self.p, self.view, self.edge, self.send, self.recv = p, view, edge, send, recv
        self.turn = 1 - 2 * p.x
        s, turn = p.s, self.turn
        self.ahead, self.behind = (s + 2 * turn, p.m), (s - 2 * turn, p.m)
        self.has_ahead = (s + 2 * turn >= 0) & (s + 2 * turn <= 7)
        self.has_behind = (s - 2 * turn >= 0) & (s - 2 * turn <= 7)

    def copy(self, slot, sem, device):
        return put(self.view(slot), self.view(slot), self.send.at[sem], self.recv.at[slot], device)

    def part(self, slot, last, sem, device):
        return put(self.edge(slot, last), self.edge(slot, last), self.send.at[sem], self.recv.at[slot], device)

    def sends(self):
        p, s, turn = self.p, self.p.s, self.turn
        both = self.has_ahead & self.has_behind
        return [
            (lambda: self.copy(s, 0, p.side), None),
            (lambda: self.copy(s, 1, self.ahead), self.has_ahead),
            (lambda: self.copy(s, 2, self.behind), self.has_behind),
            (lambda: self.copy(s + turn, 3, self.behind), self.has_behind),
            (lambda: self.copy(s + 2 * turn, 4, p.side), self.has_ahead),
            (lambda: self.part(s + 2 * turn, p.x, 5, self.behind), both),
            (lambda: self.part(s - 2 * turn, 1 - p.x, 6, self.ahead), both),
            (lambda: self.copy(s - turn, 7, self.ahead), both),
        ]

    def go(self, index):
        copy, made = self.sends()[index]
        if made is None:
            copy().start()
        else:

            @pl.when(made)
            def _():
                copy().start()

    def arrive(self, slot, exists):
        @pl.when(exists)
        def _():
            self.copy(slot, 0, self.p.side).wait_recv()

    def start(self):
        for index in (0, 1, 2):
            self.go(index)

    def step(self, hop):
        s, turn = self.p.s, self.turn
        if hop == 0:
            self.copy(s + turn, 0, self.p.side).wait_recv()
            self.go(3)
        elif hop == 1:
            self.arrive(s + 2 * turn, self.has_ahead)
            self.go(4)
            self.go(5)
            self.arrive(s - 2 * turn, self.has_behind)
            self.go(6)
        else:
            self.arrive(s - turn, self.has_behind)
            self.go(7)

    def finish(self):
        s = self.p.s
        self.arrive(s - 3, s >= 3)
        self.arrive(s + 3, s <= 4)

        @pl.when(s >= 4)
        def _():
            self.part(s - 4, 1, 0, self.p.side).wait_recv()

        @pl.when(s <= 3)
        def _():
            self.part(s + 4, 0, 0, self.p.side).wait_recv()

        for copy, made in self.sends():
            if made is None:
                copy().wait_send()
            else:

                @pl.when(made)
                def _(copy=copy):
                    copy().wait_send()


def near_rows(ref, group):
    def view(slot):
        return ref.at[pl.ds(pl.multiple_of(slot * group, group), group), :]

    def edge(slot, last):
        return ref.at[pl.ds(pl.multiple_of(slot * group + last * (group - 64), 64), 64), :]

    return view, edge


class BlockGather:
    SEMS = [pltpu.SemaphoreType.DMA((3,)), pltpu.SemaphoreType.DMA((4,))]

    def __init__(self, p, full, send, recv):
        self.p, self.full, self.send, self.recv = p, full, send, recv

    def copy(self, slot, kind):
        rows = self.full.at[pl.ds(pl.multiple_of(slot * OWN, OWN), OWN)]
        device = self.p.across if kind == 0 else self.p.core
        return put(rows, rows, self.send.at[kind], self.recv.at[slot], device)

    def start(self):
        self.copy(self.p.m, 0).start()
        self.copy(self.p.m, 1).start()

    def finish(self):
        p = self.p
        far = lax.rem(p.m + 2, 4)
        self.copy(far, 0).wait_recv()
        self.copy(far, 2).start()
        self.copy(p.m + 1 - 2 * p.c, 1).wait_recv()
        self.copy(lax.rem(p.m + 3 - 2 * p.c, 4), 2).wait_recv()
        for kind in range(3):
            self.copy(p.m, kind).wait_send()


class BlockReduce:
    SEMS = [pltpu.SemaphoreType.DMA((3,)), pltpu.SemaphoreType.DMA((3,))]

    def __init__(self, p, part, from_core, pair, send, recv):
        self.p, self.part, self.from_core, self.pair = p, part, from_core, pair
        self.send, self.recv = send, recv

    def rows(self, slot):
        return pl.ds(pl.multiple_of(slot * OWN, OWN), OWN)

    def core_copy(self, i):
        p = self.p
        yy = 1 - p.y if i == 0 else p.y
        return put(
            self.part.at[self.rows(2 * yy + 1 - p.c)], self.from_core.at[i],
            self.send.at[i], self.recv.at[i], p.core,
        )

    def across_copy(self):
        return put(self.pair.at[0], self.pair.at[1], self.send.at[2], self.recv.at[2], self.p.across)

    def far_rows(self):
        return pl.ds(pl.multiple_of((1 - self.p.y) * 2 * OWN, OWN), 2 * OWN)

    def near_rows(self):
        return pl.ds(pl.multiple_of(self.p.y * 2 * OWN, OWN), 2 * OWN)

    def send_far(self):
        p = self.p
        self.core_copy(0).start()
        self.core_copy(0).wait_recv()
        mine = self.part[self.rows(2 * (1 - p.y) + p.c), :].astype(F32)
        self.pair[0] = (mine + self.from_core[0].astype(F32)).astype(self.pair.dtype)
        self.across_copy().start()

    def send_near(self):
        self.core_copy(1).start()

    def finish(self):
        self.core_copy(1).wait_recv()
        total = self.part[self.rows(self.p.m), :].astype(F32) + self.from_core[1].astype(F32)
        self.across_copy().wait_recv()
        total = total + self.pair[1].astype(F32)
        self.core_copy(0).wait_send()
        self.core_copy(1).wait_send()
        self.across_copy().wait_send()
        return total


class GridReduce:
    SEMS = [pltpu.SemaphoreType.DMA((2, 4)), pltpu.SemaphoreType.DMA((3, 4))]

    def __init__(self, p, column, side, from_side, slim, above_slim, below_slim, wide, above, below, send, recv):
        self.p, self.column, self.side, self.from_side = p, column, side, from_side
        self.slim, self.above_slim, self.below_slim = slim, above_slim, below_slim
        self.wide, self.above, self.below = wide, above, below
        self.send, self.recv = send, recv

    def level(self, t):
        return jnp.where(self.p.z >= 2, t, 3 - t)

    def side_copy(self, zz):
        return put(self.side.at[zz], self.from_side.at[zz], self.send.at[0, zz], self.recv.at[0, zz], self.p.side)

    def down_copy(self, zz, first):
        src, dst = (self.slim, self.above_slim) if first else (self.wide, self.above)
        return put(src.at[zz], dst.at[zz], self.send.at[1, zz], self.recv.at[1, zz], self.p.down)

    def up_copy(self, zz, first):
        src, dst = (self.slim, self.below_slim) if first else (self.wide, self.below)
        return put(src.at[zz], dst.at[zz], self.send.at[1, zz], self.recv.at[2, zz], self.p.up)

    def start(self, t, both):
        p, zz = self.p, self.level(t)
        self.side[zz] = both[pl.ds(pl.multiple_of((1 - p.x) * OWN, OWN), OWN), :].astype(BF)
        self.side_copy(zz).start()
        self.column[zz] = both[pl.ds(pl.multiple_of(p.x * OWN, OWN), OWN), :]

    def add(self, zz, copy, slim, wide, first_from):
        @pl.when(self.p.z == first_from)
        def _():
            copy(zz, True).wait_recv()
            self.column[zz] = self.column[zz] + slim[zz].astype(F32)

        @pl.when(self.p.z != first_from)
        def _():
            copy(zz, False).wait_recv()
            self.column[zz] = self.column[zz] + wide[zz]

    def add_above(self, zz):
        self.add(zz, self.down_copy, self.above_slim, self.above, 2)

    def add_below(self, zz):
        self.add(zz, self.up_copy, self.below_slim, self.below, 1)

    def pass_on(self, zz, end, arrived, copy):
        @pl.when(end)
        def _():
            self.slim[zz] = self.column[zz].astype(BF)
            copy(zz, True).start()

        @pl.when(jnp.logical_not(end))
        def _():
            arrived(zz)
            self.wide[zz] = self.column[zz]
            copy(zz, False).start()

    def step(self, t):
        p, zz = self.p, self.level(t)
        self.side_copy(zz).wait_recv()
        self.column[zz] = self.column[zz] + self.from_side[zz].astype(F32)

        @pl.when(zz < p.z)
        def _():
            self.pass_on(zz, p.z == 3, self.add_above, self.down_copy)

        @pl.when(zz > p.z)
        def _():
            self.pass_on(zz, p.z == 0, self.add_below, self.up_copy)

    def finish(self, result):
        p, z = self.p, self.p.z

        @pl.when(z < 3)
        def _():
            self.add_above(z)

        @pl.when(z > 0)
        def _():
            self.add_below(z)

        result[...] = self.column[z]
        for zz in range(4):
            self.side_copy(zz).wait_send()

            @pl.when(zz < z)
            def _(zz=zz):
                self.sent(zz, z == 3, self.down_copy)

            @pl.when(zz > z)
            def _(zz=zz):
                self.sent(zz, z == 0, self.up_copy)

    def sent(self, zz, end, copy):
        @pl.when(end)
        def _():
            copy(zz, True).wait_send()

        @pl.when(jnp.logical_not(end))
        def _():
            copy(zz, False).wait_send()


def grid_scratch():
    block = (4, OWN, D)
    wide, slim = pltpu.VMEM(block, F32), pltpu.VMEM(block, BF)
    return [wide] + [slim] * 5 + [wide] * 3


def reduce_scratch():
    return [pltpu.VMEM((512, D), BF), pltpu.VMEM((2, OWN, D), BF), pltpu.VMEM((2, OWN, D), BF)]


GELU_A = math.sqrt(2.0 / math.pi)


def gelu(v):
    return 0.5 * v * (1.0 + jnp.tanh(GELU_A * (v + 0.044715 * (v * v * v))))


def gelu_slope(v):
    t = jnp.tanh(GELU_A * (v + 0.044715 * (v * v * v)))
    return 0.5 * (1.0 + t) + 0.5 * v * (1.0 - t * t) * (GELU_A * (1.0 + 3.0 * 0.044715 * v * v))


def norm_parts(v):
    mean = jnp.mean(v, -1, keepdims=True)
    centered = v - mean
    variance = jnp.mean(centered * centered, -1, keepdims=True)
    scale = lax.rsqrt(variance + norm_epsilon)
    return centered * scale, scale


def norm_back(v, gain, grad):
    unit, scale = norm_parts(v)
    gain_row = jnp.sum(grad * unit, 0, keepdims=True)
    g = grad * gain
    inner = g - jnp.mean(g, -1, keepdims=True) - unit * jnp.mean(g * unit, -1, keepdims=True)
    return scale * inner, gain_row


def frame_columns(lengths, first, rows, extra=()):
    frame = first + lax.broadcasted_iota(jnp.int32, (rows, 1), 0)
    end = jnp.int32(0)
    owner = jnp.full((rows, 1), -1, jnp.int32)
    starts = jnp.zeros((rows, 1), jnp.int32)
    ends = jnp.zeros((rows, 1), jnp.int32)
    picked = [jnp.zeros((rows, 1), e.dtype) for e in extra]
    for u in range(lengths.shape[0]):
        start = end
        end = start + lengths[u]
        inside = (frame >= start) & (frame < end)
        owner = jnp.where(inside, u, owner)
        starts = jnp.where(inside, start, starts)
        ends = jnp.where(inside, end, ends)
        picked = [jnp.where(inside, e[u], c) for e, c in zip(extra, picked)]
    return frame, owner, starts, ends, picked


def tap_masks(frame, starts, ends, mask_ref):
    low = jnp.broadcast_to(starts - frame + 15, (OWN, 128))
    high = jnp.broadcast_to(ends - frame + 15, (OWN, 128))
    for k in range(31):
        mask_ref[k] = ((low <= k) & (high > k)).astype(F32)


def front_kernel(
    lengths, span_start, span_end, flow_times, pack_ref, table_ref, win_ref, phone_ref, kern_ref,
    gain_ref, watt_ref,
    h1_ref, conv_ref, rim_ref, a_ref, q_ref, k_ref, v_ref, wqkv_ref, wout_ref, feats_ref, choose_ref,
    ext, rimf, masks, edge_send, edge_recv, ag_send, ag_recv, w_send, w_recv, o_send, o_recv,
    k_send, k_recv, v_send, v_recv,
):
    p = Place()
    group = pack_ref.shape[0]
    prior, following = (p.s - 1, p.m), (p.s + 1, p.m)
    shard = watt_ref.shape[1]
    own_w = pl.ds(pl.multiple_of(p.s * shard, shard), shard)
    for j in range(3):
        wqkv_ref[j, own_w, :] = watt_ref[j].astype(BF)
    wout_ref[own_w, :] = watt_ref[3].astype(BF)
    k_ref[...] = jnp.zeros(k_ref.shape, BF)
    v_ref[...] = jnp.zeros(v_ref.shape, BF)
    ext[:EDGE, :] = jnp.zeros((EDGE, 256), F32)
    ext[EDGE + group :, :] = jnp.zeros((EDGE, 256), F32)
    ext[EDGE : EDGE + group, :] = pack_ref[...]
    greet(grid_peers(p) + mp_peers(p) + [(prior, p.s > 0), (following, p.s < 7)])
    edge_up = put(ext.at[pl.ds(group, EDGE)], ext.at[pl.ds(0, EDGE)], edge_send.at[0], edge_recv.at[0], following)
    edge_down = put(ext.at[pl.ds(EDGE, EDGE)], ext.at[pl.ds(EDGE + group, EDGE)], edge_send.at[1], edge_recv.at[1], prior)

    @pl.when(p.s < 7)
    def _():
        edge_up.start()

    @pl.when(p.s > 0)
    def _():
        edge_down.start()

    def shard_rows(slot):
        return pl.ds(pl.multiple_of(slot * shard, shard), shard)

    gather_w = Gather(p, lambda slot: wqkv_ref.at[:, shard_rows(slot), :], w_send, w_recv)
    gather_o = Gather(p, lambda slot: wout_ref.at[shard_rows(slot), :], o_send, o_recv)
    gather_w.start()
    gather_o.start()

    @pl.when(p.s > 0)
    def _():
        edge_up.wait_recv()

    @pl.when(p.s < 7)
    def _():
        edge_down.wait_recv()

    first = p.s * group + p.m * OWN
    wide = OWN + 2 * EDGE
    frame, owner, starts, _, picked = frame_columns(
        lengths, first - EDGE, wide, (span_start, span_end, flow_times)
    )
    position = frame - starts
    masked = ((position >= picked[0]) & (position < picked[1]) & (owner >= 0)).astype(F32)
    moment = picked[2]
    both = ext[pl.ds(pl.multiple_of(p.m * OWN, OWN), wide), :]
    mel, noise = both[:, :128], both[:, 128:]
    lane = lax.broadcasted_iota(jnp.int32, (wide, 128), 1)
    context = (mel * (1.0 - masked)).astype(BF)
    noisy = (1.0 - (1.0 - flow_sigma) * moment) * noise + moment * mel
    noisy = jnp.where(lane < MEL, noisy, 0.0).astype(BF)
    phone = noise[:, MEL : MEL + 1]
    choose = jnp.where(phone == lane.astype(F32), 1.0, 0.0).astype(BF)
    h0 = nn(context[:, :MEL], win_ref[:MEL, :].astype(BF))
    h0 = h0 + nn(noisy[:, :MEL], win_ref[MEL:, :].astype(BF)) + nn(choose, phone_ref[...].astype(BF))
    time = jnp.zeros((wide, D), F32)
    for u in range(table_ref.shape[0]):
        time = jnp.where(owner == u, table_ref[u : u + 1, :], time)
    h0 = h0 + time
    low = h0.astype(BF)
    rim_ref[...] = low
    rimf[...] = low.astype(F32)
    h1_ref[...] = h0[EDGE : EDGE + OWN]
    feats_ref[:, :128] = context[EDGE : EDGE + OWN]
    feats_ref[:, 128:] = noisy[EDGE : EDGE + OWN]
    choose_ref[...] = choose[EDGE : EDGE + OWN]
    gather_w.step(0)
    gather_o.step(0)
    frame, _, starts, ends, _ = frame_columns(lengths, first, OWN)
    tap_masks(frame, starts, ends, masks)

    @pl.loop(0, D // 128)
    def _(t):
        lanes = pl.ds(pl.multiple_of(t * 128, 128), 128)
        total = jnp.zeros((OWN, 128), F32)
        for k in range(31):
            total = total + kern_ref[k : k + 1, lanes] * (rimf[1 + k : 1 + k + OWN, lanes] * masks[k])
        conv_ref[:, lanes] = total

    h1 = h1_ref[...] + gelu(conv_ref[...])
    h1_ref[...] = h1
    unit, _ = norm_parts(h1)
    own = pl.ds(pl.multiple_of(p.m * OWN, OWN), OWN)
    a_ref[own, :] = (unit * gain_ref[0:1, :]).astype(BF)
    gather_a = BlockGather(p, a_ref, ag_send, ag_recv)
    gather_a.start()
    gather_w.step(1)
    gather_o.step(1)
    gather_a.finish()
    gather_w.step(2)
    gather_o.step(2)
    gather_w.finish()
    rows = pl.ds(pl.multiple_of(p.s * group, group), group)

    gather_k = NearGather(p, *near_rows(k_ref, group), k_send, k_recv)
    gather_v = NearGather(p, *near_rows(v_ref, group), v_send, v_recv)
    k_ref[rows, :] = nn(a_ref[...], wqkv_ref[1]).astype(BF)
    gather_k.start()
    v_ref[rows, :] = nn(a_ref[...], wqkv_ref[2]).astype(BF)
    gather_v.start()
    q_ref[...] = nn(a_ref[...], wqkv_ref[0]).astype(BF)
    gather_o.finish()
    for hop in range(3):
        gather_k.step(hop)
        gather_v.step(hop)
    gather_k.finish()
    gather_v.finish()

    @pl.when(p.s < 7)
    def _():
        edge_up.wait_send()

    @pl.when(p.s > 0)
    def _():
        edge_down.wait_send()


def vmem_call(kernel, outs, specs, scratch, cid, name, flops=1e9):
    return pl.pallas_call(
        kernel,
        out_shape=tuple(jax.ShapeDtypeStruct(*o) for o in outs),
        in_specs=specs,
        out_specs=tuple([VM] * len(outs)),
        scratch_shapes=scratch,
        compiler_params=pltpu.CompilerParams(
            collective_id=cid, has_side_effects=True, vmem_limit_bytes=56 << 20
        ),
        cost_estimate=pl.CostEstimate(flops=int(flops), bytes_accessed=1 << 24, transcendentals=0),
        name=name,
    )


def front(lengths, span_start, span_end, flow_times, pack, table, win, phone, kern, gains, watt):
    group = pack.shape[0]
    shard, width = watt.shape[1:]
    outs = [
        ((OWN, D), F32), ((OWN, D), F32), ((OWN + 2 * EDGE, D), BF), ((group, D), BF),
        ((group, width), BF), ((8 * group, width), BF), ((8 * group, width), BF),
        ((3, 8 * shard, width), BF), ((8 * shard, width), BF), ((OWN, 256), BF), ((OWN, 128), BF),
    ]
    scratch = [
        pltpu.VMEM((group + 2 * EDGE, 256), F32), pltpu.VMEM((OWN + 2 * EDGE, D), F32),
        pltpu.VMEM((31, OWN, 128), F32), pltpu.SemaphoreType.DMA((2,)), pltpu.SemaphoreType.DMA((2,)),
    ] + BlockGather.SEMS + Gather.SEMS * 2 + NearGather.SEMS * 2
    return vmem_call(front_kernel, outs, [SM] * 4 + [VM] * 7, scratch, 0, "front", 2e10)(
        lengths, span_start, span_end, flow_times, pack, table, win, phone, kern, gains, watt
    )


def middle_kernel(
    lengths, span_start, span_end, pack_ref, o32_ref, o_ref, lse_ref, q_ref, h1_ref, gain_ref,
    wout_ref, wup_ref, wdown_ref, wpred_ref,
    dh2_ref, rows_ref, outg_ref, do_ref, delta_ref, qall_ref, doall_ref, stat_ref, gup_ref, gdown_ref, gout_ref,
    u_ref, gated, b_ref, dy_ref, du_ref, dlow, h_ref, h3_ref, dh3_ref,
    part1, core1, pair1, part2, core2, pair2, part3, core3, pair3,
    s1, r1, s2, r2, s3, r3, as1, ar1, as2, ar2, as3, ar3,
    q_send, q_recv, d_send, d_recv, t_send, t_recv,
    both, *w_refs,
):
    p = Place()
    group = pack_ref.shape[0]
    halves = group // 2
    first = p.s * group + p.m * OWN
    own = pl.ds(pl.multiple_of(p.m * OWN, OWN), OWN)

    def rows_of(slot):
        return pl.ds(pl.multiple_of(slot * group, group), group)

    qall_ref[...] = jnp.zeros(qall_ref.shape, BF)
    doall_ref[...] = jnp.zeros(doall_ref.shape, BF)
    stat_ref[...] = jnp.zeros(stat_ref.shape, F32)
    qall_ref[rows_of(p.s), :] = q_ref[...]
    greet(grid_peers(p) + mp_peers(p))
    gather_q = NearGather(p, *near_rows(qall_ref, group), q_send, q_recv)
    gather_d = NearGather(p, *near_rows(doall_ref, group), d_send, d_recv)
    gather_t = NearGather(
        p, lambda slot: stat_ref.at[slot], lambda slot, last: stat_ref.at[slot], t_send, t_recv
    )
    gather_q.start()

    red = BlockReduce(p, part1, core1, pair1, s1, r1)
    for rows, send in ((red.far_rows(), red.send_far), (red.near_rows(), red.send_near)):
        part1[rows, :] = nt(o_ref[rows, :], wout_ref[...]).astype(BF)
        send()
    gather_q.step(0)
    h2 = h1_ref[...] + red.finish()
    h_ref[...] = h2
    unit, _ = norm_parts(h2)
    b_ref[own, :] = (unit * gain_ref[1:2, :]).astype(BF)
    gather_b = BlockGather(p, b_ref, as1, ar1)
    gather_b.start()
    gather_q.step(1)
    gather_b.finish()

    ff = wup_ref.shape[1]
    tile = 256

    @pl.loop(0, ff // tile)
    def _(t):
        lanes = pl.ds(pl.multiple_of(t * tile, tile), tile)
        up = nn(b_ref[...], wup_ref[:, lanes])
        u_ref[:, lanes] = up
        gated[:, lanes] = gelu(up).astype(BF)

    red = BlockReduce(p, part2, core2, pair2, s2, r2)
    for rows, send in ((red.far_rows(), red.send_far), (red.near_rows(), red.send_near)):

        @pl.loop(0, D // tile)
        def _(t):
            lanes = pl.ds(pl.multiple_of(t * tile, tile), tile)
            part2[rows, lanes] = nt(gated[rows, :], wdown_ref[lanes, :]).astype(BF)

        send()
    gather_q.step(2)
    _, owner, starts, _, picked = frame_columns(lengths, first, OWN, (span_start, span_end))
    position = first + lax.broadcasted_iota(jnp.int32, (OWN, 1), 0) - starts
    masked = ((position >= picked[0]) & (position < picked[1])).astype(F32)
    covered, frames = jnp.int32(0), jnp.int32(0)
    for n in range(lengths.shape[0]):
        span = jnp.minimum(span_end[n], lengths[n]) - jnp.minimum(span_start[n], lengths[n])
        covered = covered + jnp.maximum(span, 0)
        frames = frames + lengths[n]
    count = jnp.full((OWN, 1), jnp.maximum(covered, 1), jnp.int32).astype(F32)
    rest = jnp.full((OWN, 1), jnp.maximum(frames - covered, 1), jnp.int32).astype(F32)
    weight = masked / count + 0.1 * (1.0 - masked) / rest
    raw = pack_ref[own, :]
    target = (raw[:, :128] - (1.0 - flow_sigma) * raw[:, 128:])[:, :MEL]
    wpred = wpred_ref[...].astype(BF)

    h3 = h_ref[...] + red.finish()
    h3_ref[...] = h3
    unit, _ = norm_parts(h3)
    low = (unit * gain_ref[2:3, :]).astype(BF)
    errors = nn(low, wpred) - target
    loss = jnp.sum(weight * jnp.mean(errors * errors, 1, keepdims=True), 0, keepdims=True)
    dpred = (weight * (2.0 / MEL) * errors).astype(BF)
    outg_ref[...] = tn(dpred, low)
    dh3, gain3 = norm_back(h3, gain_ref[2:3, :], nt(dpred, wpred))
    dh3_ref[...] = dh3
    dy_ref[own, :] = dh3.astype(BF)
    gather_y = BlockGather(p, dy_ref, as2, ar2)
    gather_y.start()
    gather_q.finish()
    gather_y.finish()

    @pl.loop(0, ff // tile)
    def _(t):
        lanes = pl.ds(pl.multiple_of(t * tile, tile), tile)
        down = nn(dy_ref[...], wdown_ref[:, lanes])
        du_ref[:, lanes] = (down * gelu_slope(u_ref[:, lanes])).astype(BF)

    red = BlockReduce(p, part3, core3, pair3, s3, r3)
    for rows, send in ((red.far_rows(), red.send_far), (red.near_rows(), red.send_near)):

        @pl.loop(0, D // tile)
        def _(t):
            lanes = pl.ds(pl.multiple_of(t * tile, tile), tile)
            part3[rows, lanes] = nt(du_ref[rows, :], wup_ref[lanes, :]).astype(BF)

        send()

    down_sum = GridReduce(p, *w_refs)

    @pl.loop(0, 4)
    def _(t):
        lanes = pl.ds(pl.multiple_of(down_sum.level(t) * tile, tile), tile)
        both[...] = tn(dy_ref[:, lanes], gated[...])
        down_sum.start(t, both)

    db = red.finish()
    norm_grad, gain2 = norm_back(h_ref[...], gain_ref[1:2, :], db)
    dh2 = dh3_ref[...] + norm_grad
    dh2_ref[...] = dh2
    dlow[own, :] = dh2.astype(BF)
    gather_h = BlockGather(p, dlow, as3, ar3)
    gather_h.start()
    rows_ref[...] = jnp.concatenate(
        [gain3, gain2, jnp.broadcast_to(loss, (1, D)), jnp.zeros((5, D), F32)], 0
    )

    @pl.loop(0, D // tile)
    def _(t):
        lanes = pl.ds(pl.multiple_of(t * tile, tile), tile)
        gup_ref[lanes, :] = tn(b_ref[:, lanes], du_ref[...])

    down_sum.step(0)
    gather_h.finish()
    grad = nn(dlow[...], wout_ref[...]).astype(BF)
    do_ref[...] = grad
    doall_ref[rows_of(p.s), :] = grad
    gather_d.start()
    weighted = grad.astype(F32) * o32_ref[...]
    width = o_ref.shape[1]
    head = lax.broadcasted_iota(jnp.int32, (width, 128), 0) // HD
    pick = (head == lax.broadcasted_iota(jnp.int32, (width, 128), 1)).astype(F32)
    delta_ref[...] = jnp.dot(weighted, pick, preferred_element_type=F32, precision=lax.Precision.HIGHEST)
    eye = (
        lax.broadcasted_iota(jnp.int32, (8, 128), 0) == lax.broadcasted_iota(jnp.int32, (8, 128), 1)
    ).astype(F32)
    for i, ref in enumerate((lse_ref, delta_ref)):
        stat_ref[p.s, 8 * i : 8 * i + 8, :] = lax.dot_general(
            eye, ref[...], (((1,), (1,)), ((), ())), preferred_element_type=F32, precision=lax.Precision.HIGHEST
        )
    gather_t.start()
    gout_ref[...] = tn(dlow[...], o_ref[...])
    for hop in range(3):
        down_sum.step(hop + 1)
        gather_d.step(hop)
        gather_t.step(hop)
    down_sum.finish(gdown_ref)
    gather_d.finish()
    gather_t.finish()


def middle(lengths, span_start, span_end, pack, o32, o, lse, q, h1, gains, wout, wup, wdown, wpred):
    group, width = o.shape
    ff = wup.shape[1]
    outs = [
        ((OWN, D), F32), ((8, D), F32), ((MEL, D), F32), ((group, width), BF), ((group, 128), F32),
        ((8 * group, width), BF), ((8 * group, width), BF), ((8, 16, group), F32),
        ((D, ff), F32), ((OWN, ff), F32), ((D, width), F32),
    ]
    scratch = [
        pltpu.VMEM((group, ff), F32), pltpu.VMEM((group, ff), BF), pltpu.VMEM((group, D), BF),
        pltpu.VMEM((group, D), BF), pltpu.VMEM((group, ff), BF), pltpu.VMEM((group, D), BF),
        pltpu.VMEM((OWN, D), F32), pltpu.VMEM((OWN, D), F32), pltpu.VMEM((OWN, D), F32),
    ] + reduce_scratch() * 3 + BlockReduce.SEMS * 3 + BlockGather.SEMS * 3 + NearGather.SEMS * 3
    scratch = scratch + [pltpu.VMEM((2 * OWN, D), F32)] + grid_scratch() + GridReduce.SEMS
    return vmem_call(middle_kernel, outs, [SM] * 3 + [VM] * 11, scratch, 1, "middle", 2e10)(
        lengths, span_start, span_end, pack, o32, o, lse, q, h1, gains, wout, wup, wdown, wpred
    )


def back_kernel(
    lengths, proj_ref, wqkv_ref, a_ref, dh2_ref, h1_ref, conv_ref, rim_ref, gain_ref, kern_ref,
    feats_ref, choose_ref, rows_ref, outg_ref, gup_ref, gdown_ref, gout_ref,
    gatt_ref, gff_ref, small_ref, scalar_ref,
    dcb, dcf, rimf, masks, dh1_ref, spread, part, from_core, pair, s1, r1, edge_send, edge_recv,
    both, *rest,
):
    p = Place()
    up_sum, rest = GridReduce(p, *rest[:11]), rest[11:]
    att_sum, rest = GridReduce(p, *rest[:11]), rest[11:]
    (
        att, few, few_core, few_pair, few_send, few_recv, piece, pieces, piece_send, piece_recv,
        g_send, g_recv, y_send, y_recv, c_send, c_recv, seen, seen_send, seen_recv, last, last_send, last_recv,
    ) = rest
    group = a_ref.shape[0]
    place = p.s * 4 + p.m
    prior = ((place + 31) // 4 - 8 * ((place + 31) // 32), lax.rem(place + 3, 4))
    following = ((place + 1) // 4, lax.rem(place + 1, 4))
    dcb[:EDGE, :] = jnp.zeros((EDGE, D), BF)
    dcb[EDGE + OWN :, :] = jnp.zeros((EDGE, D), BF)
    peers = [((lax.rem(p.s + d, 8), p.m), None) for d in range(1, 8)]
    others = [((p.s, lax.rem(p.m + d, 4)), None) for d in range(1, 4)]
    greet(peers + others + [(prior, place > 0), (following, place < 31)])
    red = BlockReduce(p, part, from_core, pair, s1, r1)
    for rows, send in ((red.far_rows(), red.send_far), (red.near_rows(), red.send_near)):
        total = nt(proj_ref[0, rows, :], wqkv_ref[0])
        total = total + nt(proj_ref[1, rows, :], wqkv_ref[1])
        part[rows, :] = (total + nt(proj_ref[2, rows, :], wqkv_ref[2])).astype(BF)
        send()

    @pl.loop(0, 4)
    def _(t):
        rows = pl.ds(pl.multiple_of(up_sum.level(t) * 2 * OWN, 2 * OWN), 2 * OWN)
        up_sum.start(t, gup_ref.at[rows])

    @pl.loop(0, 4)
    def _(t):
        rows = pl.ds(pl.multiple_of(att_sum.level(t) * 2 * OWN, 2 * OWN), 2 * OWN)
        for j in range(3):
            both[:, 256 * j : 256 * (j + 1)] = tn(a_ref[:, rows], proj_ref[j])
        both[:, 768:] = gout_ref[rows, :]
        att_sum.start(t, both)

    rimf[...] = rim_ref[...].astype(F32)
    frame, _, starts, ends, _ = frame_columns(lengths, p.s * group + p.m * OWN, OWN)
    tap_masks(frame, starts, ends, masks)
    norm_grad, gain1 = norm_back(h1_ref[...], gain_ref[0:1, :], red.finish())
    dh1 = dh2_ref[...] + norm_grad
    dh1_ref[...] = dh1
    dcb[EDGE : EDGE + OWN, :] = (dh1 * gelu_slope(conv_ref[...])).astype(BF)
    edge_up = put(dcb.at[pl.ds(OWN, EDGE)], dcb.at[pl.ds(0, EDGE)], edge_send.at[0], edge_recv.at[0], following)
    edge_down = put(dcb.at[pl.ds(EDGE, EDGE)], dcb.at[pl.ds(EDGE + OWN, EDGE)], edge_send.at[1], edge_recv.at[1], prior)

    @pl.when(place < 31)
    def _():
        edge_up.start()

    @pl.when(place > 0)
    def _():
        edge_down.start()

    up_sum.step(0)
    dcf[EDGE : EDGE + OWN, :] = dcb[EDGE : EDGE + OWN, :].astype(F32)

    @pl.loop(0, D // 128)
    def _(t):
        lanes = pl.ds(pl.multiple_of(t * 128, 128), 128)
        mine = dcf[EDGE : EDGE + OWN, lanes]
        for k in range(31):
            near = rimf[1 + k : 1 + k + OWN, lanes] * masks[k]
            few[288 + k : 289 + k, lanes] = jnp.sum(mine * near, 0, keepdims=True)

    up_sum.step(1)

    @pl.when(place > 0)
    def _():
        edge_up.wait_recv()

    @pl.when(place < 31)
    def _():
        edge_down.wait_recv()

    dcf[:EDGE, :] = dcb[:EDGE, :].astype(F32)
    dcf[EDGE + OWN :, :] = dcb[EDGE + OWN :, :].astype(F32)

    @pl.loop(0, D // 128)
    def _(t):
        lanes = pl.ds(pl.multiple_of(t * 128, 128), 128)
        total = jnp.zeros((OWN, 128), F32)
        for k in range(31):
            total = total + kern_ref[30 - k : 31 - k, lanes] * (dcf[1 + k : 1 + k + OWN, lanes] * masks[k])
        spread[:, lanes] = total

    dh0 = (dh1_ref[...] + spread[...]).astype(BF)
    grad = tn(feats_ref[...], dh0)
    few[:MEL, :] = grad[:MEL]
    few[MEL : 2 * MEL, :] = grad[128 : 128 + MEL]
    few[160:288, :] = tn(choose_ref[...], dh0)
    few[319:320, :] = jnp.zeros((1, D), F32)
    few[320:400, :] = outg_ref[...]
    few[400:401, :] = gain1
    few[401:403, :] = rows_ref[:2, :]
    few[403:, :] = jnp.zeros((109, D), F32)

    few_sum = BlockReduce(p, few, few_core, few_pair, few_send, few_recv)
    few_sum.send_far()
    few_sum.send_near()
    up_sum.step(2)
    piece[...] = few_sum.finish()

    def piece_copy(d):
        there = lax.rem(p.s + d, 8)
        rows = pl.ds(pl.multiple_of(there * 16, 16), 16)
        return put(piece.at[rows], pieces.at[p.s], piece_send.at[d - 1], piece_recv.at[p.s], (there, p.m))

    def piece_wait(d):
        here = lax.rem(p.s + d, 8)
        rows = pl.ds(0, 16)
        return put(piece.at[rows], pieces.at[here], piece_send.at[d - 1], piece_recv.at[here], (here, p.m))

    for d in range(1, 8):
        piece_copy(d).start()
    pieces[p.s] = piece[pl.ds(pl.multiple_of(p.s * 16, 16), 16), :]
    up_sum.step(3)
    att_sum.step(0)
    for d in range(1, 8):
        piece_wait(d).wait_recv()
    total = pieces[0]
    for n in range(1, 8):
        total = total + pieces[n]
    mine = pl.ds(pl.multiple_of(p.m * OWN, OWN), OWN)

    def slot_rows(m, slot):
        return pl.ds(pl.multiple_of(m * OWN + slot * 16, 16), 16)

    small_ref[slot_rows(p.m, p.s), :] = total
    gather = Gather(p, lambda slot: small_ref.at[slot_rows(p.m, slot)], g_send, g_recv)

    def cross(slot, m):
        view = small_ref.at[slot_rows(m, slot)]
        return put(view, view, y_send.at[slot], y_recv.at[slot], p.across)

    gather.start()
    cross(p.s, p.m).start()
    few_squares = jnp.sum(total * total)
    for hop in range(3):
        att_sum.step(hop + 1)
        gather.step(hop)
    up_sum.finish(gff_ref.at[0])
    gff_ref[1] = gdown_ref[...]
    gather.finish()
    for d in range(1, 8):
        cross(lax.rem(p.s + d, 8), p.m).start()
    att_sum.finish(att)
    for j in range(4):
        gatt_ref[j] = att[:, 256 * j : 256 * (j + 1)]
    squares = few_squares + jnp.sum(att[...] * att[...])
    squares = squares + jnp.sum(gff_ref[0] * gff_ref[0]) + jnp.sum(gff_ref[1] * gff_ref[1])
    row = lax.broadcasted_iota(jnp.int32, (8, 128), 0)
    seen[p.s] = jnp.where(row == 0, squares, rows_ref[2:3, :128])

    def scalar_copy(d, incoming):
        there = lax.rem(p.s + d, 8)
        slot = there if incoming else p.s
        return put(seen.at[p.s], seen.at[slot], seen_send.at[d - 1], seen_recv.at[slot], (there, p.m))

    for d in range(1, 8):
        scalar_copy(d, False).start()
    far = lax.rem(p.m + 2, 4)
    for n in range(8):
        cross(n, far).wait_recv()

    def core_rows(m):
        return pl.ds(pl.multiple_of(m * OWN, OWN), OWN)

    def core_copy(i, m):
        view = small_ref.at[core_rows(m)]
        return put(view, view, c_send.at[i], c_recv.at[i], p.core)

    core_copy(0, p.m).start()
    core_copy(1, far).start()
    for d in range(1, 8):
        scalar_copy(d, True).wait_recv()
    total = seen[0]
    for n in range(1, 8):
        total = total + seen[n]
    last[p.m] = total

    def last_copy(d, incoming):
        there = lax.rem(p.m + d, 4)
        slot = there if incoming else p.m
        return put(last.at[p.m], last.at[slot], last_send.at[d - 1], last_recv.at[slot], (p.s, there))

    for d in range(1, 4):
        last_copy(d, False).start()
    core_copy(0, p.m + 1 - 2 * p.c).wait_recv()
    core_copy(1, 3 - p.m).wait_recv()
    for d in range(1, 4):
        last_copy(d, True).wait_recv()
    scalar_ref[...] = (last[0] + last[1]) + (last[2] + last[3])
    for d in range(1, 8):
        piece_copy(d).wait_send()
        scalar_copy(d, False).wait_send()
    for n in range(8):
        cross(n, p.m).wait_send()
    core_copy(0, p.m).wait_send()
    core_copy(1, far).wait_send()
    for d in range(1, 4):
        last_copy(d, False).wait_send()

    @pl.when(place < 31)
    def _():
        edge_up.wait_send()

    @pl.when(place > 0)
    def _():
        edge_down.wait_send()


def back(lengths, proj, wqkv, a, dh2, h1, conv, rim, gains, kern, feats, choose, rows, outg, gup, gdown, gout):
    outs = [((4, OWN, 256), F32), ((2, OWN, D), F32), ((512, D), F32), ((8, 128), F32)]
    wide = OWN + 2 * EDGE
    dma = pltpu.SemaphoreType.DMA
    scratch = [
        pltpu.VMEM((wide, D), BF), pltpu.VMEM((wide, D), F32), pltpu.VMEM((wide, D), F32),
        pltpu.VMEM((31, OWN, 128), F32), pltpu.VMEM((OWN, D), F32), pltpu.VMEM((OWN, D), F32),
    ] + reduce_scratch() + BlockReduce.SEMS + [dma((2,)), dma((2,)), pltpu.VMEM((2 * OWN, D), F32)]
    scratch = scratch + grid_scratch() + GridReduce.SEMS + grid_scratch() + GridReduce.SEMS + [pltpu.VMEM((OWN, D), F32)]
    scratch = scratch + [
        pltpu.VMEM((512, D), F32), pltpu.VMEM((2, OWN, D), F32), pltpu.VMEM((2, OWN, D), F32),
    ] + BlockReduce.SEMS + [pltpu.VMEM((OWN, D), F32), pltpu.VMEM((8, 16, D), F32), dma((7,)), dma((8,))]
    scratch = scratch + Gather.SEMS + [dma((8,)), dma((8,)), dma((2,)), dma((2,))]
    scratch = scratch + [pltpu.VMEM((8, 8, 128), F32), dma((7,)), dma((8,))]
    scratch = scratch + [pltpu.VMEM((4, 8, 128), F32), dma((3,)), dma((4,))]
    return vmem_call(back_kernel, outs, [SM] + [VM] * 16, scratch, 2, "back", 2e10)(
        lengths, proj, wqkv, a, dh2, h1, conv, rim, gains, kern, feats, choose, rows, outg, gup, gdown, gout
    )


KT = 512


def lane_half(rows):
    return lax.broadcasted_iota(jnp.int32, (rows, 128), 1) < HD


def stack_pair(x):
    low, zero = lane_half(x.shape[0]), jnp.zeros_like(x)
    return jnp.concatenate([jnp.where(low, x, zero), jnp.where(low, zero, x)], 0)


def unstack_pair(x):
    rows = x.shape[0] // 2
    return jnp.where(lane_half(rows), x[:rows], x[rows:])


def slope_of(index):
    value = jnp.float32(2.0 ** (-8.0 * HEADS / HEADS))
    for head in range(HEADS - 1):
        value = jnp.where(index == head, jnp.float32(2.0 ** (-8.0 * (head + 1) / HEADS)), value)
    return value


def tile_range(lengths, first, base):
    end = jnp.int32(0)
    low = jnp.int32(0)
    high = jnp.int32(0)
    for u in range(lengths.shape[0]):
        start = end
        end = start + lengths[u]
        low = jnp.where((start <= first) & (first < end), start, low)
        last = first + OWN - 1
        high = jnp.where((start <= last) & (last < end), end, high)
    return (low - base) // KT, (high - base + KT - 1) // KT


def owner_row(lengths, base, kown):
    frame = base + lax.broadcasted_iota(jnp.int32, kown.shape, 1)
    owner = jnp.full(kown.shape, -1, jnp.int32)
    end = jnp.int32(0)
    for u in range(lengths.shape[0]):
        start = end
        end = start + lengths[u]
        owner = jnp.where((frame >= start) & (frame < end), u, owner)
    kown[...] = owner


def attend_setup(lengths, base, kown, width):
    i = pl.program_id(0)
    first = base[1] + i * OWN

    @pl.when(i == 0)
    def _():
        owner_row(lengths, base[0], kown)

    low, high = tile_range(lengths, first, base[0])
    _, owner, _, _, _ = frame_columns(lengths, first, OWN)
    heads = width // HD
    slopes = [slope_of(lax.axis_index("mp") * heads + h) for h in range(heads)]

    def distance(k0):
        shape = (OWN, KT)
        gap = (first - base[0] - k0) + lax.broadcasted_iota(jnp.int32, shape, 0)
        dist = jnp.abs(gap - lax.broadcasted_iota(jnp.int32, shape, 1)).astype(F32)
        return jnp.where(owner == kown[:, pl.ds(k0, KT)], dist, 1e30)

    return low, high, slopes, distance


def attend_forward_kernel(lengths, base, q_ref, k_ref, v_ref, o_ref, ob_ref, lse_ref, kown):
    width = q_ref.shape[1]
    low, high, slopes, distance = attend_setup(lengths, base, kown, width)
    lanes = [slice(128 * j, 128 * (j + 1)) for j in range(width // 128)]
    qs = [stack_pair(q_ref[:, l]) * BF(0.125) for l in lanes]

    def body(t, carry):
        k0 = pl.multiple_of(t * KT, KT)
        dist = distance(k0)
        out = []
        for j, l in enumerate(lanes):
            top, total, acc = carry[j]
            s = nt(qs[j], k_ref[pl.ds(k0, KT), l])
            s = jnp.concatenate([s[:OWN] - slopes[2 * j] * dist, s[OWN:] - slopes[2 * j + 1] * dist], 0)
            new = jnp.maximum(top, jnp.max(s, -1, keepdims=True))
            fade = jnp.exp(top - new)
            e = jnp.exp(s - new)
            total = total * fade + jnp.sum(e, -1, keepdims=True)
            acc = acc * fade + nn(e.astype(BF), v_ref[pl.ds(k0, KT), l])
            out.append((new, total, acc))
        return tuple(out)

    begin = (
        jnp.full((2 * OWN, 1), -1e30, F32), jnp.zeros((2 * OWN, 1), F32), jnp.zeros((2 * OWN, 128), F32),
    )
    ended = lax.fori_loop(low, high, body, tuple(begin for _ in lanes))
    lane = lax.broadcasted_iota(jnp.int32, (OWN, 128), 1)
    lse = jnp.zeros((OWN, 128), F32)
    for j, l in enumerate(lanes):
        top, total, acc = ended[j]
        o = unstack_pair(acc / total)
        o_ref[:, l] = o
        ob_ref[:, l] = o.astype(BF)
        g = top + jnp.log(total)
        lse = jnp.where(lane == 2 * j, g[:OWN], lse)
        lse = jnp.where(lane == 2 * j + 1, g[OWN:], lse)
    lse_ref[...] = lse


def blocks(width):
    return pl.BlockSpec((OWN, width), lambda i, *_: (i, 0))


def whole(*shape):
    return pl.BlockSpec(shape, lambda i, *_: (0,) * len(shape))


def attend_call(kernel, outs, out_specs, in_specs, rows, keys, name, flops):
    return pl.pallas_call(
        kernel,
        out_shape=outs,
        grid_spec=pltpu.PrefetchScalarGridSpec(
            num_scalar_prefetch=2, grid=(rows // OWN,), in_specs=in_specs, out_specs=out_specs,
            scratch_shapes=[pltpu.VMEM((1, keys), jnp.int32)],
        ),
        compiler_params=pltpu.CompilerParams(vmem_limit_bytes=50 << 20),
        cost_estimate=pl.CostEstimate(flops=flops, bytes_accessed=1 << 23, transcendentals=0),
        name=name,
    )


def attend_forward(lengths, base, q, k, v):
    (rows, width), keys = q.shape, k.shape[0]
    outs = (
        jax.ShapeDtypeStruct((rows, width), F32), jax.ShapeDtypeStruct((rows, width), BF),
        jax.ShapeDtypeStruct((rows, 128), F32),
    )
    return attend_call(
        attend_forward_kernel, outs, (blocks(width), blocks(width), blocks(128)),
        [blocks(width), whole(keys, width), whole(keys, width)], rows, keys, "attend_forward", 10**10,
    )(lengths, base, q, k, v)


def attend_backward_kernel(
    lengths, base, q_ref, k_ref, v_ref, do_ref, lse_ref, delta_ref, qa_ref, ka_ref, va_ref, doa_ref,
    stat_ref, out_ref, kown,
):
    width = q_ref.shape[1]
    low, high, slopes, distance = attend_setup(lengths, base, kown, width)
    lanes = [slice(128 * j, 128 * (j + 1)) for j in range(width // 128)]

    def column(ref, j):
        return jnp.concatenate([ref[:, 2 * j : 2 * j + 1], ref[:, 2 * j + 1 : 2 * j + 2]], 0)

    scale = BF(0.125)
    qs = [stack_pair(q_ref[:, l]) * scale for l in lanes]
    dos = [stack_pair(do_ref[:, l]) for l in lanes]
    ks = [stack_pair(k_ref[:, l]) * scale for l in lanes]
    vs = [stack_pair(v_ref[:, l]) for l in lanes]
    lses = [column(lse_ref, j) for j in range(len(lanes))]
    deltas = [column(delta_ref, j) for j in range(len(lanes))]

    def body(t, carry):
        k0 = pl.multiple_of(t * KT, KT)
        keys = pl.ds(k0, KT)
        dist = distance(k0)
        out = []
        for j, l in enumerate(lanes):
            dq, dk, dv = carry[j]
            kj, vj, qj, doj = ka_ref[keys, l], va_ref[keys, l], qa_ref[keys, l], doa_ref[keys, l]
            bias = [slopes[2 * j + h] * dist for h in (0, 1)]
            s = nt(qs[j], kj)
            e = jnp.exp(jnp.concatenate([s[:OWN] - bias[0], s[OWN:] - bias[1]], 0) - lses[j])
            ds = (e * (nt(dos[j], vj) - deltas[j])).astype(BF)
            dq = dq + nn(ds, kj)
            s = nt(ks[j], qj)
            far = [stat_ref[t, 2 * j + h : 2 * j + h + 1, :] for h in (0, 1)]
            e = jnp.exp(jnp.concatenate([s[:OWN] - bias[0] - far[0], s[OWN:] - bias[1] - far[1]], 0))
            dv = dv + nn(e.astype(BF), doj)
            g = nt(vs[j], doj)
            far = [stat_ref[t, 8 + 2 * j + h : 9 + 2 * j + h, :] for h in (0, 1)]
            ds = (e * jnp.concatenate([g[:OWN] - far[0], g[OWN:] - far[1]], 0)).astype(BF)
            dk = dk + nn(ds, qj)
            out.append((dq, dk, dv))
        return tuple(out)

    zero = jnp.zeros((2 * OWN, 128), F32)
    ended = lax.fori_loop(low, high, body, tuple((zero, zero, zero) for _ in lanes))
    for j, l in enumerate(lanes):
        dq, dk, dv = ended[j]
        out_ref[0, :, l] = (unstack_pair(dq) * 0.125).astype(BF)
        out_ref[1, :, l] = (unstack_pair(dk) * 0.125).astype(BF)
        out_ref[2, :, l] = unstack_pair(dv).astype(BF)


def attend_backward(lengths, base, q, k, v, do, lse, delta, qa, ka, va, doa, stat):
    (rows, width), keys = q.shape, ka.shape[0]
    return attend_call(
        attend_backward_kernel, jax.ShapeDtypeStruct((3, rows, width), BF),
        pl.BlockSpec((3, OWN, width), lambda i, *_: (0, i, 0)),
        [blocks(width)] * 4 + [blocks(128)] * 2 + [whole(keys, width)] * 4 + [whole(*stat.shape)],
        rows, keys, "attend_backward", 3 * 10**10,
    )(lengths, base, q, k, v, do, lse, delta, qa, ka, va, doa, stat)


def adam_step(weight, first_old, second, gradient, step_rate, decay_on):
    first_new = beta_one * first_old + (1.0 - beta_one) * gradient
    second_new = beta_two * second + (1.0 - beta_two) * gradient * gradient
    fix_one = 1.0 - beta_one**STEP
    fix_two = 1.0 - beta_two**STEP
    moved = first_new / fix_one / (jnp.sqrt(second_new / fix_two) + adam_epsilon)
    return (first_new, second_new, weight - step_rate * (moved + decay_on * weight_decay * weight))


def update(loss_total, grads, frames, states):
    big_squares = jnp.sum(grads[0] * grads[0]) + jnp.sum(grads[1] * grads[1])
    small_squares = jnp.zeros((), jnp.float32)
    for gradient in grads[2:]:
        small_squares = small_squares + jnp.sum(gradient * gradient)
    big_total = lax.psum(big_squares, ("seq", "mp"))
    return adam_all(loss_total, jnp.sqrt(big_total + small_squares), grads, frames, states)


def adam_all(loss_total, grad_norm, grads, frames, states):
    weights, firsts, seconds = states
    factor = jnp.minimum(1.0, 0.3 / math.sqrt(frames) / grad_norm)
    results = [loss_total, grad_norm]
    for number in range(7):
        results.extend(
            adam_step(
                weights[number],
                firsts[number],
                seconds[number],
                grads[number] * factor,
                step_rates[number],
                decay_flags[number],
            )
        )
    return tuple(results)


def split_arguments(arguments):
    rest = arguments[7:]
    return arguments[:7], (rest[0::3], rest[1::3], rest[2::3])


def per_device(*arguments):
    inputs, states = split_arguments(arguments)
    row_count = inputs[0].shape[0]
    if (lax.axis_size("seq"), lax.axis_size("mp"), row_count) == (8, 4, 512):
        return step_by_kernels(inputs, states)
    return step_by_collectives(inputs, states)


def step_by_kernels(inputs, states):
    mel, noise, phone_ids, lengths, span_start, span_end, flow_times = inputs
    attention, feedforward, win, phone_table, kern, wpred, gains = states[0]
    row_count = mel.shape[0]
    frames = row_count * lax.axis_size("seq")
    wup, wdown = [lax.all_gather(w, "seq", axis=0, tiled=True) for w in feedforward.astype(BF)]
    columns = ((0, 0), (0, 128 - MEL))
    with_phone = jnp.concatenate([noise, phone_ids.astype(F32)[:, None]], 1)
    pack = jnp.concatenate(
        [jnp.pad(mel, columns), jnp.pad(with_phone, ((0, 0), (0, 127 - MEL)))], 1
    )
    table = time_features(flow_times, D)
    h1, conv, rim, a, q, k, v, wqkv, wout, feats, choose = front(
        lengths, span_start, span_end, flow_times, pack, table, win, phone_table, kern, gains, attention
    )
    row_base = lax.axis_index("seq") * row_count
    base = jnp.stack([jnp.zeros_like(row_base), row_base]).astype(jnp.int32)
    o32, o, lse = attend_forward(lengths, base, q, k, v)
    dh2, rows, outg, do, delta, q_all, do_all, stat, gup, gdown, gout = middle(
        lengths, span_start, span_end, pack, o32, o, lse, q, h1, gains, wout, wup, wdown, wpred
    )
    k_own = lax.dynamic_slice_in_dim(k, row_base, row_count, 0)
    v_own = lax.dynamic_slice_in_dim(v, row_base, row_count, 0)
    proj = attend_backward(lengths, base, q, k_own, v_own, do, lse, delta, q_all, k, v, do_all, stat)
    attention_grad, feedforward_grad, small, scalars = back(
        lengths, proj, wqkv, a, dh2, h1, conv, rim, gains, kern, feats, choose, rows, outg, gup, gdown, gout
    )
    gain_grad = jnp.stack([small[400], small[402], small[401]])
    grads = (
        attention_grad, feedforward_grad, small[:160], small[160:288], small[288:319],
        small[320:400].T, gain_grad,
    )
    return adam_all(scalars[1, 0], jnp.sqrt(scalars[0, 0]), grads, frames, states)


def step_by_collectives(inputs, states):
    mel_frames, noise_frames, phone_ids, lengths, span_start, span_end, flow_times = inputs
    (
        attention_weight,
        feedforward_weight,
        input_weight,
        phone_table,
        position_kernel,
        output_weight,
        layer_gains,
    ) = states[0]
    row_count = mel_frames.shape[0]
    frames = row_count * lax.axis_size("seq")
    row_base = lax.axis_index("seq") * row_count
    longest = min(MAXLEN, frames // 2)
    near_count = min((longest - 1 + row_count - 1) // row_count, lax.axis_size("seq") - 1)
    window_start = row_base - near_count * row_count
    reach = position_kernel.shape[0] // 2
    tables = (lengths, span_start, span_end, flow_times)
    row_index = row_base + jnp.arange(row_count)
    owners, masked, moment = frame_tables(*tables, row_index)
    covered, uncovered = mask_counts(lengths, span_start, span_end)
    row_weight = masked / jnp.maximum(covered, 1.0) + 0.1 * (1.0 - masked) / jnp.maximum(
        uncovered, 1.0
    )
    attention_full, feedforward_full = (
        lax.all_gather(attention_weight.astype(jnp.bfloat16), "seq", axis=1, tiled=True),
        lax.all_gather(feedforward_weight.astype(jnp.bfloat16), "seq", axis=1, tiled=True),
    )
    heads_local = attention_full.shape[2] // HD
    target = mel_frames - (1.0 - flow_sigma) * noise_frames
    noisy = (1.0 - (1.0 - flow_sigma) * moment[:, None]) * noise_frames + moment[
        :, None
    ] * mel_frames
    context = mel_frames * (1.0 - masked[:, None])
    feats = jnp.concatenate([context, noisy], 1).astype(jnp.bfloat16)
    choose = (phone_ids[:, None] == jnp.arange(phone_table.shape[0])[None, :]).astype(jnp.bfloat16)
    start_h = product(feats, input_weight.astype(jnp.bfloat16)) + product(
        choose, phone_table.astype(jnp.bfloat16)
    )
    start_h = start_h + time_features(moment, D)
    start_low = start_h.astype(jnp.bfloat16)
    rim = padded_2(start_low, (("seq", 0),), reach)
    pad_owner = frame_tables(*tables, row_base - reach + jnp.arange(row_count + 2 * reach))[0]
    conv_raw = jnp.zeros(start_h.shape, jnp.float32)
    for offset in range(position_kernel.shape[0]):
        same_owner = (pad_owner[offset : offset + row_count] == owners).astype(jnp.float32)
        conv_raw = (
            conv_raw
            + position_kernel[offset][None, :]
            * rim[offset : offset + row_count].astype(jnp.float32)
            * same_owner[:, None]
        )
    conv_gelu, conv_back = jax.vjp(jax.nn.gelu, conv_raw)
    hidden_one = start_h + conv_gelu
    ln_one, norm_back_one = jax.vjp(layer_norm, hidden_one, layer_gains[0])
    ln_one_low = ln_one.astype(jnp.bfloat16)
    projected = jnp.einsum(
        "td,kdh->kth", ln_one_low, attention_full[:3], preferred_element_type=jnp.float32
    ).astype(jnp.bfloat16)
    queries, keyed, valued = (projected[0], projected[1], projected[2])
    def window(array):
        return slice_window(
            lax.all_gather(array, "seq", axis=0, tiled=True), row_base, near_count, row_count
        )

    base = jnp.stack([window_start, row_base]).astype(jnp.int32)
    key_all, value_all = window(keyed), window(valued)
    out_f32, out_low, log_total = attend_forward(lengths, base, queries, key_all, value_all)
    attended = lax.psum(
        contract_cols(out_low, attention_full[3]).astype(jnp.bfloat16), "mp"
    ).astype(jnp.float32)
    hidden_two = hidden_one + attended
    ln_two, norm_back_two = jax.vjp(layer_norm, hidden_two, layer_gains[1])
    ln_two_low = ln_two.astype(jnp.bfloat16)
    upward = product(ln_two_low, feedforward_full[0])
    gated_f32, gelu_back = jax.vjp(jax.nn.gelu, upward)
    gated = gated_f32.astype(jnp.bfloat16)
    downward = lax.psum(
        contract_cols(gated, feedforward_full[1]).astype(jnp.bfloat16), "mp"
    ).astype(jnp.float32)
    hidden_three = hidden_two + downward
    ln_three, norm_back_three = jax.vjp(layer_norm, hidden_three, layer_gains[2])
    ln_three_low = ln_three.astype(jnp.bfloat16)
    output_low = output_weight.astype(jnp.bfloat16)
    predicted = product(ln_three_low, output_low)
    errors = predicted - target
    loss_local = jnp.sum(row_weight * jnp.mean(errors * errors, 1))
    loss_total = lax.psum(loss_local, "seq")
    pred_grad = (row_weight[:, None] * (2.0 / errors.shape[1]) * errors).astype(jnp.bfloat16)
    output_grad = contract_rows(ln_three_low, pred_grad)
    three_grad, gain_three = norm_back_three(contract_cols(pred_grad, output_low))
    down_low = three_grad.astype(jnp.bfloat16)
    down_wgrad = contract_rows(down_low, gated)
    up_grad = gelu_back(product(down_low, feedforward_full[1]))[0].astype(jnp.bfloat16)
    up_wgrad = contract_rows(ln_two_low, up_grad)
    two_sum = lax.psum(
        contract_cols(up_grad, feedforward_full[0]).astype(jnp.bfloat16), "mp"
    ).astype(jnp.float32)
    norm_grad, gain_two = norm_back_two(two_sum)
    two_grad = three_grad + norm_grad
    attended_low = two_grad.astype(jnp.bfloat16)
    out_wgrad = contract_rows(attended_low, out_low)
    out_heads = product(attended_low, attention_full[3]).astype(jnp.bfloat16)
    delta = jnp.sum(
        (out_heads.astype(jnp.float32) * out_f32).reshape(row_count, heads_local, HD), 2
    )
    delta = jnp.pad(delta, ((0, 0), (0, 128 - heads_local)))
    stat = window(jnp.concatenate([log_total[:, :8], delta[:, :8]], 1))
    stat = stat.reshape(-1, KT, 16).transpose(0, 2, 1)
    proj_grad = attend_backward(
        lengths, base, queries, keyed, valued, out_heads, log_total, delta,
        window(queries), key_all, value_all, window(out_heads), stat,
    )
    qkv_wgrad = jnp.einsum("td,kth->kdh", ln_one_low, proj_grad, preferred_element_type=jnp.float32)
    one_part = jnp.einsum(
        "kth,kdh->td", proj_grad, attention_full[:3], preferred_element_type=jnp.float32
    )
    one_sum = lax.psum(one_part.astype(jnp.bfloat16), "mp").astype(jnp.float32)
    norm_grad, gain_one = norm_back_one(one_sum)
    one_grad = two_grad + norm_grad
    conv_grad = conv_back(one_grad)[0].astype(jnp.bfloat16)
    grad_rim = padded_2(conv_grad, (("seq", 0),), reach)
    spread = jnp.zeros(one_grad.shape, jnp.float32)
    kernel_rows = []
    conv_grad_f32 = conv_grad.astype(jnp.float32)
    for offset in range(position_kernel.shape[0]):
        back_start = 2 * reach - offset
        same_back = (pad_owner[back_start : back_start + row_count] == owners).astype(jnp.float32)
        spread = (
            spread
            + position_kernel[offset][None, :]
            * grad_rim[back_start : back_start + row_count].astype(jnp.float32)
            * same_back[:, None]
        )
        same_fore = (pad_owner[offset : offset + row_count] == owners).astype(jnp.float32)
        kernel_rows.append(
            jnp.sum(
                conv_grad_f32
                * rim[offset : offset + row_count].astype(jnp.float32)
                * same_fore[:, None],
                0,
            )
        )
    kernel_grad = jnp.stack(kernel_rows)
    start_grad = (one_grad + spread).astype(jnp.bfloat16)
    input_wgrad = contract_rows(feats, start_grad)
    phone_wgrad = contract_rows(choose, start_grad)
    gains_grad = jnp.stack([gain_one, gain_two, gain_three])
    small_sums = lax.psum((input_wgrad, phone_wgrad, kernel_grad, output_grad, gains_grad), "seq")
    attention_grad, feedforward_grad = (
        lax.psum_scatter(
            jnp.concatenate([qkv_wgrad, out_wgrad[None]], 0), "seq", scatter_dimension=1, tiled=True
        ),
        lax.psum_scatter(jnp.stack([up_wgrad, down_wgrad]), "seq", scatter_dimension=1, tiled=True),
    )
    grads = (attention_grad, feedforward_grad) + tuple(small_sums)
    return update(loss_total, grads, frames, states)


def solution(mesh):
    in_specs = (
        P("seq", None),
        P("seq", None),
        P("seq"),
        P(),
        P(),
        P(),
        P(),
        P(None, "seq", "mp"),
        P(None, "seq", "mp"),
        P(None, "seq", "mp"),
        P(None, "seq", "mp"),
        P(None, "seq", "mp"),
        P(None, "seq", "mp"),
        P(),
        P(),
        P(),
        P(),
        P(),
        P(),
        P(),
        P(),
        P(),
        P(),
        P(),
        P(),
        P(),
        P(),
        P(),
    )
    out_specs = (
        P(),
        P(),
        P(None, "seq", "mp"),
        P(None, "seq", "mp"),
        P(None, "seq", "mp"),
        P(None, "seq", "mp"),
        P(None, "seq", "mp"),
        P(None, "seq", "mp"),
        P(),
        P(),
        P(),
        P(),
        P(),
        P(),
        P(),
        P(),
        P(),
        P(),
        P(),
        P(),
        P(),
        P(),
        P(),
    )
    return jax.shard_map(
        per_device, mesh=mesh, in_specs=in_specs, out_specs=out_specs, check_vma=False
    )
```

```python
import functools
import math

import jax
import jax.numpy as jnp
from jax import lax
from jax.experimental import pallas as pl
from jax.experimental.pallas import tpu as pltpu
from jax.sharding import PartitionSpec as P

D = 1024
HEADS = 16
HD = 64
MEL = 80
STEP = 10
MAXLEN = 1600


norm_epsilon = 1e-05
flow_sigma = 1e-05
beta_one = 0.9
beta_two = 0.95
adam_epsilon = 1e-08
weight_decay = 0.1
step_rates = (0.04, 0.04, 0.08, 1.0, 0.2, 0.04, 1.0)
decay_flags = (1.0, 1.0, 1.0, 1.0, 1.0, 1.0, 0.0)


def padded_2(array, sides, width):
    for axis, dim in sides:
        devices, length = (lax.axis_size(axis), array.shape[dim])
        up = [(i, (i + 1) % devices) for i in range(devices - 1)]
        down = [(j, i) for i, j in up]
        last = lax.slice_in_dim(array, length - width, length, axis=dim)
        initial = lax.slice_in_dim(array, 0, width, axis=dim)
        before = lax.ppermute(last, axis, up)
        after = lax.ppermute(initial, axis, down)
        array = jnp.concatenate([before, array, after], axis=dim)
    return array


def layer_norm(inputs, gain_row):
    centre_mean = jnp.mean(inputs, -1, keepdims=True)
    centered = inputs - centre_mean
    variance = jnp.mean(centered * centered, -1, keepdims=True)
    return centered * lax.rsqrt(variance + norm_epsilon) * gain_row


def frame_tables(lengths, span_start, span_end, flow_times, frame_index):
    utter_ends = jnp.cumsum(lengths)
    starts = utter_ends - lengths
    member = (
        (frame_index[:, None] >= starts[None, :]) & (frame_index[:, None] < utter_ends[None, :])
    ).astype(jnp.float32)
    labels = (jnp.arange(lengths.shape[0]) + 1).astype(jnp.float32)
    owners = jnp.sum(member * labels[None, :], 1) - 1.0
    position = frame_index.astype(jnp.float32) - jnp.sum(
        member * starts.astype(jnp.float32)[None, :], 1
    )
    low_end = jnp.sum(member * span_start.astype(jnp.float32)[None, :], 1)
    high_end = jnp.sum(member * span_end.astype(jnp.float32)[None, :], 1)
    masked = ((position >= low_end) & (position < high_end)).astype(jnp.float32)
    moment = jnp.sum(member * flow_times[None, :], 1)
    return (owners, masked, moment)


def mask_counts(lengths, span_start, span_end):
    span_low = jnp.minimum(span_start, lengths)
    span_high = jnp.minimum(span_end, lengths)
    covered = jnp.sum(jnp.maximum(span_high - span_low, 0)).astype(jnp.float32)
    return (covered, jnp.sum(lengths).astype(jnp.float32) - covered)


def time_features(moment, width):
    half_width = width // 2
    frequency = jnp.exp(
        -math.log(10000.0) * jnp.arange(half_width).astype(jnp.float32) / half_width
    )
    angles = moment[:, None] * 100.0 * frequency[None, :]
    return jnp.concatenate([jnp.sin(angles), jnp.cos(angles)], 1)


def product(left, right):
    return jnp.dot(left, right, preferred_element_type=jnp.float32)


def contract_rows(left, right):
    return lax.dot_general(
        left, right, (((0,), (0,)), ((), ())), preferred_element_type=jnp.float32
    )


def contract_cols(left, right):
    return lax.dot_general(
        left, right, (((1,), (1,)), ((), ())), preferred_element_type=jnp.float32
    )


def slice_window(full_rows, row_base, near_count, row_count):
    pad_rows = near_count * row_count
    padded = jnp.pad(full_rows, ((pad_rows, pad_rows), (0, 0)))
    return lax.dynamic_slice_in_dim(padded, row_base, (2 * near_count + 1) * row_count, 0)


MESH = pl.DeviceIdType.MESH
VM = pl.BlockSpec(memory_space=pltpu.VMEM)
SM = pl.BlockSpec(memory_space=pltpu.SMEM)
BF = jnp.bfloat16
F32 = jnp.float32
OWN = 128
EDGE = 16


def nn(a, b):
    return jnp.dot(a, b, preferred_element_type=F32)


def nt(a, b):
    return lax.dot_general(a, b, (((1,), (1,)), ((), ())), preferred_element_type=F32)


def tn(a, b):
    return lax.dot_general(a, b, (((0,), (0,)), ((), ())), preferred_element_type=F32)


def put(src, dst, send, recv, device):
    return pltpu.make_async_remote_copy(
        src_ref=src, dst_ref=dst, send_sem=send, recv_sem=recv, device_id=device, device_id_type=MESH
    )


class Place:
    def __init__(self):
        self.s, self.m = lax.axis_index("seq"), lax.axis_index("mp")
        self.z, self.x = self.s // 2, lax.rem(self.s, 2)
        self.y, self.c = self.m // 2, lax.rem(self.m, 2)
        self.core = (self.s, self.m + 1 - 2 * self.c)
        self.across = (self.s, lax.rem(self.m + 2, 4))
        self.side = (self.s + 1 - 2 * self.x, self.m)
        self.up = (self.s + 2, self.m)
        self.down = (self.s - 2, self.m)


def greet(peers):
    barrier = pltpu.get_barrier_semaphore()
    total = 0
    for device, exists in peers:
        if exists is None:
            pl.semaphore_signal(barrier, inc=1, device_id=device, device_id_type=MESH)
            total = total + 1
        else:

            @pl.when(exists)
            def _(device=device):
                pl.semaphore_signal(barrier, inc=1, device_id=device, device_id_type=MESH)

            total = total + exists.astype(jnp.int32)
    pl.semaphore_wait(barrier, total)


def grid_peers(p):
    column = [((2 * lax.rem(p.z + d, 4) + p.x, p.m), None) for d in range(1, 4)]
    return [(p.side, None)] + column


def mp_peers(p):
    return [(p.core, None), (p.across, None)]


class Gather:
    SEMS = [pltpu.SemaphoreType.DMA((3, 8)), pltpu.SemaphoreType.DMA((8,))]

    def __init__(self, p, view, send, recv):
        self.p, self.view, self.send, self.recv = p, view, send, recv

    def copy(self, slot, kind):
        p = self.p
        device = (p.side, p.up, p.down)[kind]
        return put(
            self.view(slot), self.view(slot), self.send.at[kind, slot], self.recv.at[slot], device
        )

    def start(self):
        p = self.p
        self.copy(p.s, 0).start()

        @pl.when(p.z < 3)
        def _():
            self.copy(p.s, 1).start()

        @pl.when(p.z > 0)
        def _():
            self.copy(p.s, 2).start()

    def step(self, hop):
        p = self.p
        below, above = p.s - 2 * (hop + 1), p.s + 2 * (hop + 1)

        @pl.when(p.z - 1 - hop >= 0)
        def _():
            self.copy(below, 0).wait_recv()
            self.copy(below, 0).start()

            @pl.when(p.z < 3)
            def _():
                self.copy(below, 1).start()

        @pl.when(p.z + 1 + hop <= 3)
        def _():
            self.copy(above, 0).wait_recv()
            self.copy(above, 0).start()

            @pl.when(p.z > 0)
            def _():
                self.copy(above, 2).start()

    def finish(self):
        p = self.p
        for zz in range(4):
            self.copy(2 * zz + 1 - p.x, 0).wait_recv()
        for zz in range(4):
            slot = 2 * zz + p.x
            self.copy(slot, 0).wait_send()

            @pl.when((p.z < 3) & (p.z >= zz))
            def _(slot=slot):
                self.copy(slot, 1).wait_send()

            @pl.when((p.z > 0) & (p.z <= zz))
            def _(slot=slot):
                self.copy(slot, 2).wait_send()


class NearGather:
    SEMS = [pltpu.SemaphoreType.DMA((8,)), pltpu.SemaphoreType.DMA((8,))]

    def __init__(self, p, view, edge, send, recv):
        self.p, self.view, self.edge, self.send, self.recv = p, view, edge, send, recv
        self.turn = 1 - 2 * p.x
        s, turn = p.s, self.turn
        self.ahead, self.behind = (s + 2 * turn, p.m), (s - 2 * turn, p.m)
        self.has_ahead = (s + 2 * turn >= 0) & (s + 2 * turn <= 7)
        self.has_behind = (s - 2 * turn >= 0) & (s - 2 * turn <= 7)

    def copy(self, slot, sem, device):
        return put(self.view(slot), self.view(slot), self.send.at[sem], self.recv.at[slot], device)

    def part(self, slot, last, sem, device):
        return put(self.edge(slot, last), self.edge(slot, last), self.send.at[sem], self.recv.at[slot], device)

    def sends(self):
        p, s, turn = self.p, self.p.s, self.turn
        both = self.has_ahead & self.has_behind
        return [
            (lambda: self.copy(s, 0, p.side), None),
            (lambda: self.copy(s, 1, self.ahead), self.has_ahead),
            (lambda: self.copy(s, 2, self.behind), self.has_behind),
            (lambda: self.copy(s + turn, 3, self.behind), self.has_behind),
            (lambda: self.copy(s + 2 * turn, 4, p.side), self.has_ahead),
            (lambda: self.part(s + 2 * turn, p.x, 5, self.behind), both),
            (lambda: self.part(s - 2 * turn, 1 - p.x, 6, self.ahead), both),
            (lambda: self.copy(s - turn, 7, self.ahead), both),
        ]

    def go(self, index):
        copy, made = self.sends()[index]
        if made is None:
            copy().start()
        else:

            @pl.when(made)
            def _():
                copy().start()

    def arrive(self, slot, exists):
        @pl.when(exists)
        def _():
            self.copy(slot, 0, self.p.side).wait_recv()

    def start(self):
        for index in (0, 1, 2):
            self.go(index)

    def step(self, hop):
        s, turn = self.p.s, self.turn
        if hop == 0:
            self.copy(s + turn, 0, self.p.side).wait_recv()
            self.go(3)
        elif hop == 1:
            self.arrive(s + 2 * turn, self.has_ahead)
            self.go(4)
            self.go(5)
            self.arrive(s - 2 * turn, self.has_behind)
            self.go(6)
        else:
            self.arrive(s - turn, self.has_behind)
            self.go(7)

    def finish(self):
        s = self.p.s
        self.arrive(s - 3, s >= 3)
        self.arrive(s + 3, s <= 4)

        @pl.when(s >= 4)
        def _():
            self.part(s - 4, 1, 0, self.p.side).wait_recv()

        @pl.when(s <= 3)
        def _():
            self.part(s + 4, 0, 0, self.p.side).wait_recv()

        for copy, made in self.sends():
            if made is None:
                copy().wait_send()
            else:

                @pl.when(made)
                def _(copy=copy):
                    copy().wait_send()


def near_rows(ref, group):
    def view(slot):
        return ref.at[pl.ds(pl.multiple_of(slot * group, group), group), :]

    def edge(slot, last):
        return ref.at[pl.ds(pl.multiple_of(slot * group + last * (group - 64), 64), 64), :]

    return view, edge


class BlockGather:
    SEMS = [pltpu.SemaphoreType.DMA((3,)), pltpu.SemaphoreType.DMA((4,))]

    def __init__(self, p, full, send, recv):
        self.p, self.full, self.send, self.recv = p, full, send, recv

    def copy(self, slot, kind):
        rows = self.full.at[pl.ds(pl.multiple_of(slot * OWN, OWN), OWN)]
        device = self.p.across if kind == 0 else self.p.core
        return put(rows, rows, self.send.at[kind], self.recv.at[slot], device)

    def start(self):
        self.copy(self.p.m, 0).start()
        self.copy(self.p.m, 1).start()

    def finish(self):
        p = self.p
        far = lax.rem(p.m + 2, 4)
        self.copy(far, 0).wait_recv()
        self.copy(far, 2).start()
        self.copy(p.m + 1 - 2 * p.c, 1).wait_recv()
        self.copy(lax.rem(p.m + 3 - 2 * p.c, 4), 2).wait_recv()
        for kind in range(3):
            self.copy(p.m, kind).wait_send()


class BlockReduce:
    SEMS = [pltpu.SemaphoreType.DMA((3,)), pltpu.SemaphoreType.DMA((3,))]

    def __init__(self, p, part, from_core, pair, send, recv):
        self.p, self.part, self.from_core, self.pair = p, part, from_core, pair
        self.send, self.recv = send, recv

    def rows(self, slot):
        return pl.ds(pl.multiple_of(slot * OWN, OWN), OWN)

    def core_copy(self, i):
        p = self.p
        yy = 1 - p.y if i == 0 else p.y
        return put(
            self.part.at[self.rows(2 * yy + 1 - p.c)], self.from_core.at[i],
            self.send.at[i], self.recv.at[i], p.core,
        )

    def across_copy(self):
        return put(self.pair.at[0], self.pair.at[1], self.send.at[2], self.recv.at[2], self.p.across)

    def far_rows(self):
        return pl.ds(pl.multiple_of((1 - self.p.y) * 2 * OWN, OWN), 2 * OWN)

    def near_rows(self):
        return pl.ds(pl.multiple_of(self.p.y * 2 * OWN, OWN), 2 * OWN)

    def send_far(self):
        p = self.p
        self.core_copy(0).start()
        self.core_copy(0).wait_recv()
        mine = self.part[self.rows(2 * (1 - p.y) + p.c), :].astype(F32)
        self.pair[0] = (mine + self.from_core[0].astype(F32)).astype(self.pair.dtype)
        self.across_copy().start()

    def send_near(self):
        self.core_copy(1).start()

    def finish(self):
        self.core_copy(1).wait_recv()
        total = self.part[self.rows(self.p.m), :].astype(F32) + self.from_core[1].astype(F32)
        self.across_copy().wait_recv()
        total = total + self.pair[1].astype(F32)
        self.core_copy(0).wait_send()
        self.core_copy(1).wait_send()
        self.across_copy().wait_send()
        return total


class GridReduce:
    SEMS = [pltpu.SemaphoreType.DMA((2, 4)), pltpu.SemaphoreType.DMA((2, 4))]

    def __init__(self, p, column, side, from_side, chain, incoming, send, recv):
        self.p, self.column, self.side, self.from_side = p, column, side, from_side
        self.chain, self.incoming, self.send, self.recv = chain, incoming, send, recv

    def level(self, t):
        z = self.p.z
        high = jnp.where(z == 3, t, jnp.where(t == 0, 0, jnp.where(t == 1, 1, 5 - t)))
        low = jnp.where(z == 0, 3 - t, jnp.where(t == 0, 3, jnp.where(t == 1, 2, t - 2)))
        return jnp.where(z >= 2, high, low)

    def side_copy(self, zz):
        return put(self.side.at[zz], self.from_side.at[zz], self.send.at[0, zz], self.recv.at[0, zz], self.p.side)

    def along(self, there, slot):
        p = self.p
        return put(
            self.chain.at[there], self.incoming.at[slot], self.send.at[1, there], self.recv.at[1, slot],
            (2 * there + p.x, p.m),
        )

    def start(self, t, both):
        p, zz = self.p, self.level(t)
        self.side[zz] = both[pl.ds(pl.multiple_of((1 - p.x) * OWN, OWN), OWN), :].astype(BF)
        self.side_copy(zz).start()
        self.column[zz] = both[pl.ds(pl.multiple_of(p.x * OWN, OWN), OWN), :]

    def step(self, t):
        p, zz = self.p, self.level(t)
        self.side_copy(zz).wait_recv()
        if t == 3:
            self.column[zz] = self.column[zz] + self.from_side[zz].astype(F32)
        else:
            self.chain[zz] = (self.column[zz] + self.from_side[zz].astype(F32)).astype(BF)
            self.along(zz, p.z).start()

    def finish(self, result):
        z = self.p.z
        total = self.column[z]
        for d in range(1, 4):
            other = lax.rem(z + d, 4)
            self.along(other, other).wait_recv()
        for d in range(1, 4):
            total = total + self.incoming[lax.rem(z + d, 4)].astype(F32)
        result[...] = total
        for zz in range(4):
            self.side_copy(zz).wait_send()
        for d in range(1, 4):
            self.along(lax.rem(z + d, 4), z).wait_send()


def grid_scratch():
    block = (4, OWN, D)
    return [pltpu.VMEM(block, F32)] + [pltpu.VMEM(block, BF)] * 4


def reduce_scratch():
    return [pltpu.VMEM((512, D), BF), pltpu.VMEM((2, OWN, D), BF), pltpu.VMEM((2, OWN, D), BF)]


GELU_A = math.sqrt(2.0 / math.pi)


def gelu(v):
    return 0.5 * v * (1.0 + jnp.tanh(GELU_A * (v + 0.044715 * (v * v * v))))


def gelu_slope(v):
    t = jnp.tanh(GELU_A * (v + 0.044715 * (v * v * v)))
    return 0.5 * (1.0 + t) + 0.5 * v * (1.0 - t * t) * (GELU_A * (1.0 + 3.0 * 0.044715 * v * v))


def norm_parts(v):
    mean = jnp.mean(v, -1, keepdims=True)
    centered = v - mean
    variance = jnp.mean(centered * centered, -1, keepdims=True)
    scale = lax.rsqrt(variance + norm_epsilon)
    return centered * scale, scale


def norm_back(v, gain, grad):
    unit, scale = norm_parts(v)
    gain_row = jnp.sum(grad * unit, 0, keepdims=True)
    g = grad * gain
    inner = g - jnp.mean(g, -1, keepdims=True) - unit * jnp.mean(g * unit, -1, keepdims=True)
    return scale * inner, gain_row


def frame_columns(lengths, first, rows, extra=()):
    frame = first + lax.broadcasted_iota(jnp.int32, (rows, 1), 0)
    end = jnp.int32(0)
    owner = jnp.full((rows, 1), -1, jnp.int32)
    starts = jnp.zeros((rows, 1), jnp.int32)
    ends = jnp.zeros((rows, 1), jnp.int32)
    picked = [jnp.zeros((rows, 1), e.dtype) for e in extra]
    for u in range(lengths.shape[0]):
        start = end
        end = start + lengths[u]
        inside = (frame >= start) & (frame < end)
        owner = jnp.where(inside, u, owner)
        starts = jnp.where(inside, start, starts)
        ends = jnp.where(inside, end, ends)
        picked = [jnp.where(inside, e[u], c) for e, c in zip(extra, picked)]
    return frame, owner, starts, ends, picked


def tap_masks(frame, starts, ends, mask_ref):
    low = jnp.broadcast_to(starts - frame + 15, (OWN, 128))
    high = jnp.broadcast_to(ends - frame + 15, (OWN, 128))
    for k in range(31):
        mask_ref[k] = ((low <= k) & (high > k)).astype(F32)


def vmem_call(kernel, outs, specs, scratch, cid, name, flops=1e9):
    return pl.pallas_call(
        kernel,
        out_shape=tuple(jax.ShapeDtypeStruct(*o) for o in outs),
        in_specs=specs,
        out_specs=tuple([VM] * len(outs)),
        scratch_shapes=scratch,
        compiler_params=pltpu.CompilerParams(
            collective_id=cid, has_side_effects=True, vmem_limit_bytes=61 << 20
        ),
        cost_estimate=pl.CostEstimate(flops=int(flops), bytes_accessed=1 << 24, transcendentals=0),
        name=name,
    )


def forward_kernel(
    lengths, span_start, span_end, flow_times, pack_ref, table_ref, win_ref, phone_ref, kern_ref,
    gain_ref, watt_ref, up_shard, down_shard, wpred_ref,
    h1_ref, conv_ref, rim_ref, a_ref, q_ref, k_ref, v_ref, wqkv_ref, feats_ref, choose_ref, lse_ref,
    dh2_ref, rows_ref, outg_ref, do_ref, delta_ref, qall_ref, doall_ref, stat_ref, gup_ref, gdown_ref, gout_ref,
    wout_ref, ext, rimf, masks, edge_send, edge_recv, ag_send, ag_recv, w_send, w_recv, o_send, o_recv,
    k_send, k_recv, v_send, v_recv,
    kown, qown, o32_ref, o_ref, tops, totals, sums,
    u_ref, gated, b_ref, dy_ref, du_ref, dlow, h_ref, dh3_ref,
    part, core1, pair1, core2, pair2, core3, pair3,
    s1, r1, s2, r2, s3, r3, as1, ar1, as2, ar2, as3, ar3,
    q_send, q_recv, d_send, d_recv, t_send, t_recv, wup_ref, wdown_ref, wu_send, wu_recv, wd_send, wd_recv,
    both, *w_refs,
):
    p = Place()
    group = pack_ref.shape[0]
    prior, following = (p.s - 1, p.m), (p.s + 1, p.m)
    shard = watt_ref.shape[1]
    own_w = pl.ds(pl.multiple_of(p.s * shard, shard), shard)
    for j in range(3):
        wqkv_ref[j, own_w, :] = watt_ref[j].astype(BF)
    wout_ref[own_w, :] = watt_ref[3].astype(BF)
    wup_ref[own_w, :] = up_shard[...].astype(BF)
    wdown_ref[own_w, :] = down_shard[...].astype(BF)
    for ref in (qall_ref, doall_ref, stat_ref):
        ref[...] = jnp.zeros(ref.shape, ref.dtype)
    k_ref[...] = jnp.zeros(k_ref.shape, BF)
    v_ref[...] = jnp.zeros(v_ref.shape, BF)
    ext[:EDGE, :] = jnp.zeros((EDGE, 256), F32)
    ext[EDGE + group :, :] = jnp.zeros((EDGE, 256), F32)
    ext[EDGE : EDGE + group, :] = pack_ref[...]
    greet(grid_peers(p) + mp_peers(p) + [(prior, p.s > 0), (following, p.s < 7)])
    edge_up = put(ext.at[pl.ds(group, EDGE)], ext.at[pl.ds(0, EDGE)], edge_send.at[0], edge_recv.at[0], following)
    edge_down = put(ext.at[pl.ds(EDGE, EDGE)], ext.at[pl.ds(EDGE + group, EDGE)], edge_send.at[1], edge_recv.at[1], prior)

    @pl.when(p.s < 7)
    def _():
        edge_up.start()

    @pl.when(p.s > 0)
    def _():
        edge_down.start()

    def shard_rows(slot):
        return pl.ds(pl.multiple_of(slot * shard, shard), shard)

    gather_w = Gather(p, lambda slot: wqkv_ref.at[:, shard_rows(slot), :], w_send, w_recv)
    gather_o = Gather(p, lambda slot: wout_ref.at[shard_rows(slot), :], o_send, o_recv)
    def rows_of(slot):
        return pl.ds(pl.multiple_of(slot * group, group), group)

    gather_q = NearGather(p, *near_rows(qall_ref, group), q_send, q_recv)
    gather_d = NearGather(p, *near_rows(doall_ref, group), d_send, d_recv)
    gather_t = NearGather(
        p, lambda slot: stat_ref.at[slot], lambda slot, last: stat_ref.at[slot], t_send, t_recv
    )
    gather_up = Gather(p, lambda slot: wup_ref.at[shard_rows(slot), :], wu_send, wu_recv)
    gather_down = Gather(p, lambda slot: wdown_ref.at[shard_rows(slot), :], wd_send, wd_recv)
    gather_w.start()
    gather_o.start()

    @pl.when(p.s > 0)
    def _():
        edge_up.wait_recv()

    @pl.when(p.s < 7)
    def _():
        edge_down.wait_recv()

    first = p.s * group + p.m * OWN
    wide = OWN + 2 * EDGE

    def features(begin, both):
        rows = both.shape[0]
        frame, owner, starts, _, picked = frame_columns(
            lengths, begin, rows, (span_start, span_end, flow_times)
        )
        position = frame - starts
        masked = ((position >= picked[0]) & (position < picked[1]) & (owner >= 0)).astype(F32)
        moment = picked[2]
        mel, noise = both[:, :128], both[:, 128:]
        lane = lax.broadcasted_iota(jnp.int32, (rows, 128), 1)
        context = (mel * (1.0 - masked)).astype(BF)
        noisy = (1.0 - (1.0 - flow_sigma) * moment) * noise + moment * mel
        noisy = jnp.where(lane < MEL, noisy, 0.0).astype(BF)
        phone = noise[:, MEL : MEL + 1]
        choose = jnp.where(phone == lane.astype(F32), 1.0, 0.0).astype(BF)
        return owner, context, noisy, choose

    owner, context, noisy, choose = features(
        first - EDGE, ext[pl.ds(pl.multiple_of(p.m * OWN, OWN), wide), :]
    )
    h0 = nn(context[:, :MEL], win_ref[:MEL, :].astype(BF))
    h0 = h0 + nn(noisy[:, :MEL], win_ref[MEL:, :].astype(BF)) + nn(choose, phone_ref[...].astype(BF))
    time = jnp.zeros((wide, D), F32)
    for u in range(table_ref.shape[0]):
        time = jnp.where(owner == u, table_ref[u : u + 1, :], time)
    h0 = h0 + time
    low = h0.astype(BF)
    rim_ref[...] = low
    rimf[...] = low.astype(F32)
    h1_ref[...] = h0[EDGE : EDGE + OWN]
    gather_w.step(0)
    gather_o.step(0)
    frame, _, starts, ends, _ = frame_columns(lengths, first, OWN)
    tap_masks(frame, starts, ends, masks)

    @pl.loop(0, D // 128)
    def _(t):
        lanes = pl.ds(pl.multiple_of(t * 128, 128), 128)
        total = jnp.zeros((OWN, 128), F32)
        for k in range(31):
            total = total + kern_ref[k : k + 1, lanes] * (rimf[1 + k : 1 + k + OWN, lanes] * masks[k])
        conv_ref[:, lanes] = total

    h1 = h1_ref[...] + gelu(conv_ref[...])
    h1_ref[...] = h1
    unit, _ = norm_parts(h1)
    own = pl.ds(pl.multiple_of(p.m * OWN, OWN), OWN)
    a_ref[own, :] = (unit * gain_ref[0:1, :]).astype(BF)
    gather_a = BlockGather(p, a_ref, ag_send, ag_recv)
    gather_a.start()
    gather_w.step(1)
    gather_o.step(1)
    gather_a.finish()
    gather_w.step(2)
    gather_o.step(2)
    gather_w.finish()
    rows = pl.ds(pl.multiple_of(p.s * group, group), group)

    gather_k = NearGather(p, *near_rows(k_ref, group), k_send, k_recv)
    gather_v = NearGather(p, *near_rows(v_ref, group), v_send, v_recv)
    k_ref[rows, :] = nn(a_ref[...], wqkv_ref[1]).astype(BF)
    gather_k.start()
    v_ref[rows, :] = nn(a_ref[...], wqkv_ref[2]).astype(BF)
    gather_v.start()
    q_ref[...] = nn(a_ref[...], wqkv_ref[0]).astype(BF)
    _, context, noisy, choose = features(p.s * group, pack_ref[...])
    feats_ref[:, :128] = context
    feats_ref[:, 128:] = noisy
    choose_ref[...] = choose
    gather_o.finish()

    width = q_ref.shape[1]
    pairs = [slice(128 * j, 128 * (j + 1)) for j in range(width // 128)]
    heads = width // HD
    slopes = [slope_of(p.m * heads + h) for h in range(heads)]
    owner_row(lengths, 0, kown)
    _, owner, _, _, _ = frame_columns(lengths, p.s * group, group)
    qown[...] = owner
    tops[...] = jnp.full(tops.shape, -1e30, F32)
    totals[...] = jnp.zeros(totals.shape, F32)
    sums[...] = jnp.zeros(sums.shape, F32)

    def tile(slot):
        keys = rows_of(slot)

        @pl.loop(0, group // OWN)
        def _(i):
            mine = pl.ds(pl.multiple_of(i * OWN, OWN), OWN)
            gap = (p.s - slot) * group + i * OWN + lax.broadcasted_iota(jnp.int32, (OWN, group), 0)
            dist = jnp.abs(gap - lax.broadcasted_iota(jnp.int32, (OWN, group), 1)).astype(F32)
            dist = jnp.where(qown[mine, :] == kown[:, keys], dist, 1e30)
            for j, l in enumerate(pairs):
                n = len(pairs) * i + j
                top = tops[n]
                scores = nt(stack_pair(q_ref[mine, l]) * BF(0.125), k_ref[keys, l])
                scores = jnp.concatenate(
                    [scores[:OWN] - slopes[2 * j] * dist, scores[OWN:] - slopes[2 * j + 1] * dist], 0
                )
                new = jnp.maximum(top, jnp.max(scores, -1, keepdims=True))
                fade = jnp.exp(top - new)
                e = jnp.exp(scores - new[:, :1])
                tops[n] = new
                totals[n] = totals[n] * fade + jnp.sum(e, -1, keepdims=True)
                sums[n] = sums[n] * fade + nn(e.astype(BF), v_ref[keys, l])

    def tile_if(slot, exists, wait):
        @pl.when(exists)
        def _():
            wait(gather_k)
            wait(gather_v)
            tile(slot)

    turn = gather_k.turn
    tile(p.s)
    for g in (gather_k, gather_v):
        g.step(0)
    tile(p.s + turn)
    for g in (gather_k, gather_v):
        g.step(1)
    tile_if(p.s + 2 * turn, gather_k.has_ahead, lambda g: None)
    for g in (gather_k, gather_v):
        g.step(2)
    gather_up.start()
    tile_if(p.s - 2 * turn, gather_k.has_behind, lambda g: None)
    tile_if(p.s - turn, gather_k.has_behind, lambda g: None)
    gather_up.step(0)
    tile_if(p.s - 3, p.s >= 3, lambda g: g.copy(p.s - 3, 0, p.side).wait_recv())
    tile_if(p.s + 3, p.s <= 4, lambda g: g.copy(p.s + 3, 0, p.side).wait_recv())
    gather_up.step(1)
    tile_if(p.s - 4, p.s >= 4, lambda g: g.part(p.s - 4, 1, 0, p.side).wait_recv())
    tile_if(p.s + 4, p.s <= 3, lambda g: g.part(p.s + 4, 0, 0, p.side).wait_recv())

    @pl.loop(0, group // OWN)
    def _(i):
        mine = pl.ds(pl.multiple_of(i * OWN, OWN), OWN)
        lane = lax.broadcasted_iota(jnp.int32, (OWN, 128), 1)
        lse = jnp.zeros((OWN, 128), F32)
        for j, l in enumerate(pairs):
            n = len(pairs) * i + j
            o = unstack_pair(sums[n] / totals[n])
            o32_ref[mine, l] = o
            o_ref[mine, l] = o.astype(BF)
            g = tops[n] + jnp.log(totals[n])
            lse = jnp.where(lane == 2 * j, g[:OWN], lse)
            lse = jnp.where(lane == 2 * j + 1, g[OWN:], lse)
        lse_ref[mine, :] = lse

    red = BlockReduce(p, part, core1, pair1, s1, r1)
    for rows, send in ((red.far_rows(), red.send_far), (red.near_rows(), red.send_near)):
        part[rows, :] = nt(o_ref[rows, :], wout_ref[...]).astype(BF)
        send()
    gather_up.step(2)
    gather_down.start()
    h2 = h1_ref[...] + red.finish()
    h_ref[...] = h2
    unit, _ = norm_parts(h2)
    b_ref[own, :] = (unit * gain_ref[1:2, :]).astype(BF)
    gather_b = BlockGather(p, b_ref, as1, ar1)
    gather_b.start()
    gather_up.finish()
    gather_down.step(0)
    gather_b.finish()

    ff = up_shard.shape[1]
    tile = 256

    @pl.loop(0, ff // tile)
    def _(t):
        lanes = pl.ds(pl.multiple_of(t * tile, tile), tile)
        up = nn(b_ref[...], wup_ref[:, lanes])
        u_ref[:, lanes] = up
        gated[:, lanes] = gelu(up).astype(BF)

    gather_down.step(1)
    gather_down.step(2)
    gather_down.finish()
    qall_ref[rows_of(p.s), :] = q_ref[...]
    gather_q.start()
    red = BlockReduce(p, part, core2, pair2, s2, r2)
    for rows, send in ((red.far_rows(), red.send_far), (red.near_rows(), red.send_near)):

        @pl.loop(0, D // tile)
        def _(t):
            lanes = pl.ds(pl.multiple_of(t * tile, tile), tile)
            part[rows, lanes] = nt(gated[rows, :], wdown_ref[lanes, :]).astype(BF)

        send()
    gather_q.step(0)
    _, owner, starts, _, picked = frame_columns(lengths, first, OWN, (span_start, span_end))
    position = first + lax.broadcasted_iota(jnp.int32, (OWN, 1), 0) - starts
    masked = ((position >= picked[0]) & (position < picked[1])).astype(F32)
    covered, frames = jnp.int32(0), jnp.int32(0)
    for n in range(lengths.shape[0]):
        span = jnp.minimum(span_end[n], lengths[n]) - jnp.minimum(span_start[n], lengths[n])
        covered = covered + jnp.maximum(span, 0)
        frames = frames + lengths[n]
    count = jnp.full((OWN, 1), jnp.maximum(covered, 1), jnp.int32).astype(F32)
    rest = jnp.full((OWN, 1), jnp.maximum(frames - covered, 1), jnp.int32).astype(F32)
    weight = masked / count + 0.1 * (1.0 - masked) / rest
    raw = pack_ref[own, :]
    target = (raw[:, :128] - (1.0 - flow_sigma) * raw[:, 128:])[:, :MEL]
    wpred = wpred_ref[...].astype(BF)

    h3 = h_ref[...] + red.finish()
    unit, _ = norm_parts(h3)
    low = (unit * gain_ref[2:3, :]).astype(BF)
    errors = nn(low, wpred) - target
    loss = jnp.sum(weight * jnp.mean(errors * errors, 1, keepdims=True), 0, keepdims=True)
    dpred = (weight * (2.0 / MEL) * errors).astype(BF)
    outg_ref[...] = tn(dpred, low)
    dh3, gain3 = norm_back(h3, gain_ref[2:3, :], nt(dpred, wpred))
    dh3_ref[...] = dh3
    dy_ref[own, :] = dh3.astype(BF)
    gather_y = BlockGather(p, dy_ref, as2, ar2)
    gather_y.start()
    gather_q.step(1)
    gather_q.step(2)
    gather_y.finish()

    @pl.loop(0, ff // tile)
    def _(t):
        lanes = pl.ds(pl.multiple_of(t * tile, tile), tile)
        down = nn(dy_ref[...], wdown_ref[:, lanes])
        du_ref[:, lanes] = (down * gelu_slope(u_ref[:, lanes])).astype(BF)

    red = BlockReduce(p, part, core3, pair3, s3, r3)
    for rows, send in ((red.far_rows(), red.send_far), (red.near_rows(), red.send_near)):

        @pl.loop(0, D // tile)
        def _(t):
            lanes = pl.ds(pl.multiple_of(t * tile, tile), tile)
            part[rows, lanes] = nt(du_ref[rows, :], wup_ref[lanes, :]).astype(BF)

        send()

    down_sum = GridReduce(p, *w_refs)

    @pl.loop(0, 4)
    def _(t):
        lanes = pl.ds(pl.multiple_of(down_sum.level(t) * tile, tile), tile)
        both[...] = tn(dy_ref[:, lanes], gated[...])
        down_sum.start(t, both)

    gather_q.finish()
    db = red.finish()
    norm_grad, gain2 = norm_back(h_ref[...], gain_ref[1:2, :], db)
    dh2 = dh3_ref[...] + norm_grad
    dh2_ref[...] = dh2
    dlow[own, :] = dh2.astype(BF)
    gather_h = BlockGather(p, dlow, as3, ar3)
    gather_h.start()
    rows_ref[...] = jnp.concatenate(
        [gain3, gain2, jnp.broadcast_to(loss, (1, D)), jnp.zeros((5, D), F32)], 0
    )

    @pl.loop(0, D // tile)
    def _(t):
        lanes = pl.ds(pl.multiple_of(t * tile, tile), tile)
        gup_ref[lanes, :] = tn(b_ref[:, lanes], du_ref[...])

    down_sum.step(0)
    gather_h.finish()
    grad = nn(dlow[...], wout_ref[...]).astype(BF)
    do_ref[...] = grad
    doall_ref[rows_of(p.s), :] = grad
    gather_d.start()
    weighted = grad.astype(F32) * o32_ref[...]
    width = o_ref.shape[1]
    head = lax.broadcasted_iota(jnp.int32, (width, 128), 0) // HD
    pick = (head == lax.broadcasted_iota(jnp.int32, (width, 128), 1)).astype(F32)
    delta_ref[...] = jnp.dot(weighted, pick, preferred_element_type=F32, precision=lax.Precision.HIGHEST)
    eye = (
        lax.broadcasted_iota(jnp.int32, (8, 128), 0) == lax.broadcasted_iota(jnp.int32, (8, 128), 1)
    ).astype(F32)
    for i, ref in enumerate((lse_ref, delta_ref)):
        stat_ref[p.s, 8 * i : 8 * i + 8, :] = lax.dot_general(
            eye, ref[...], (((1,), (1,)), ((), ())), preferred_element_type=F32, precision=lax.Precision.HIGHEST
        )
    gather_t.start()
    gout_ref[...] = tn(dlow[...], o_ref[...])
    for hop in range(3):
        down_sum.step(hop + 1)
        gather_d.step(hop)
        gather_t.step(hop)
    down_sum.finish(gdown_ref)
    gather_d.finish()
    gather_t.finish()
    for g in (gather_k, gather_v):
        for copy, made in g.sends():
            if made is None:
                copy().wait_send()
            else:

                @pl.when(made)
                def _(copy=copy):
                    copy().wait_send()

    @pl.when(p.s < 7)
    def _():
        edge_up.wait_send()

    @pl.when(p.s > 0)
    def _():
        edge_down.wait_send()


def forward(lengths, span_start, span_end, flow_times, pack, table, win, phone, kern, gains, watt, up, down, wpred):
    group = pack.shape[0]
    shard, width = watt.shape[1:]
    ff = up.shape[1]
    frames = 8 * group
    outs = [
        ((OWN, D), F32), ((OWN, D), F32), ((OWN + 2 * EDGE, D), BF), ((group, D), BF),
        ((group, width), BF), ((frames, width), BF), ((frames, width), BF),
        ((3, 8 * shard, width), BF), ((group, 256), BF), ((group, 128), BF), ((group, 128), F32),
        ((OWN, D), F32), ((8, D), F32), ((MEL, D), F32), ((group, width), BF), ((group, 128), F32),
        ((frames, width), BF), ((frames, width), BF), ((8, 16, group), F32),
        ((D, ff), F32), ((OWN, ff), F32), ((D, width), F32),
    ]
    dma, vmem = pltpu.SemaphoreType.DMA, pltpu.VMEM
    states = vmem((group // OWN * (width // 128), 2 * OWN, 128), F32)
    scratch = [
        vmem((8 * shard, width), BF), vmem((group + 2 * EDGE, 256), F32), vmem((OWN + 2 * EDGE, D), F32),
        vmem((31, OWN, 128), F32), dma((2,)), dma((2,)),
    ] + BlockGather.SEMS + Gather.SEMS * 2 + NearGather.SEMS * 2
    scratch = scratch + [
        vmem((1, frames), jnp.int32), vmem((group, 1), jnp.int32), vmem((group, width), F32),
        vmem((group, width), BF), states, states, states,
        vmem((group, ff), F32), vmem((group, ff), BF), vmem((group, D), BF), vmem((group, D), BF),
        vmem((group, ff), BF), vmem((group, D), BF), vmem((OWN, D), F32), vmem((OWN, D), F32),
    ]
    landing = reduce_scratch()[1:]
    scratch = scratch + reduce_scratch() + landing * 2 + BlockReduce.SEMS * 3 + BlockGather.SEMS * 3
    scratch = scratch + NearGather.SEMS * 3 + [vmem((D, ff), BF), vmem((D, ff), BF)] + Gather.SEMS * 2
    scratch = scratch + [vmem((2 * OWN, D), F32)] + grid_scratch() + GridReduce.SEMS
    return vmem_call(forward_kernel, outs, [SM] * 4 + [VM] * 10, scratch, 0, "forward", 4e10)(
        lengths, span_start, span_end, flow_times, pack, table, win, phone, kern, gains, watt, up, down, wpred
    )


FEW = 448


def back_kernel(
    lengths, proj_ref, wqkv_ref, a_ref, dh2_ref, h1_ref, conv_ref, rim_ref, gain_ref, kern_ref,
    feats_ref, choose_ref, rows_ref, outg_ref, gup_ref, gdown_ref, gout_ref,
    gatt_ref, gff_ref, small_ref, scalar_ref,
    dcb, dcf, rimf, masks, dh1_ref, part, from_core, pair, s1, r1, edge_send, edge_recv,
    both, *rest,
):
    p = Place()
    att_sum, rest = GridReduce(p, *rest[:7]), rest[7:]
    up_sum, rest = GridReduce(p, *rest[:7]), rest[7:]
    (
        att, dh0, dh0_lanes, few, few_lanes, piece, pieces, d_send, d_recv, few_send, few_recv,
        piece_send, piece_recv, g_send, g_recv, y_send, y_recv, c_send, c_recv,
        seen, seen_send, seen_recv, last, last_send, last_recv,
    ) = rest
    group = a_ref.shape[0]
    place = p.s * 4 + p.m
    prior = ((place + 31) // 4 - 8 * ((place + 31) // 32), lax.rem(place + 3, 4))
    following = ((place + 1) // 4, lax.rem(place + 1, 4))
    dcb[:EDGE, :] = jnp.zeros((EDGE, D), BF)
    dcb[EDGE + OWN :, :] = jnp.zeros((EDGE, D), BF)
    peers = [((lax.rem(p.s + d, 8), p.m), None) for d in range(1, 8)]
    others = [((p.s, lax.rem(p.m + d, 4)), None) for d in range(1, 4)]
    greet(peers + others + [(prior, place > 0), (following, place < 31)])
    red = BlockReduce(p, part, from_core, pair, s1, r1)
    for rows, send in ((red.far_rows(), red.send_far), (red.near_rows(), red.send_near)):
        total = nt(proj_ref[0, rows, :], wqkv_ref[0])
        total = total + nt(proj_ref[1, rows, :], wqkv_ref[1])
        part[rows, :] = (total + nt(proj_ref[2, rows, :], wqkv_ref[2])).astype(BF)
        send()

    def attention_block(t):
        rows = pl.ds(pl.multiple_of(att_sum.level(t) * 2 * OWN, 2 * OWN), 2 * OWN)
        for j in range(3):
            both[:, 256 * j : 256 * (j + 1)] = tn(a_ref[:, rows], proj_ref[j])
        both[:, 768:] = gout_ref[rows, :]
        att_sum.start(t, both)

    def up_block(t):
        rows = pl.ds(pl.multiple_of(up_sum.level(t) * 2 * OWN, 2 * OWN), 2 * OWN)
        up_sum.start(t, gup_ref.at[rows])

    pl.loop(0, 2)(up_block)
    rimf[...] = rim_ref[...].astype(F32)
    frame, _, starts, ends, _ = frame_columns(lengths, p.s * group + p.m * OWN, OWN)
    tap_masks(frame, starts, ends, masks)
    norm_grad, gain1 = norm_back(h1_ref[...], gain_ref[0:1, :], red.finish())
    dh1 = dh2_ref[...] + norm_grad
    dh1_ref[...] = dh1
    dcb[EDGE : EDGE + OWN, :] = (dh1 * gelu_slope(conv_ref[...])).astype(BF)
    edge_up = put(dcb.at[pl.ds(OWN, EDGE)], dcb.at[pl.ds(0, EDGE)], edge_send.at[0], edge_recv.at[0], following)
    edge_down = put(dcb.at[pl.ds(EDGE, EDGE)], dcb.at[pl.ds(EDGE + OWN, EDGE)], edge_send.at[1], edge_recv.at[1], prior)

    @pl.when(place < 31)
    def _():
        edge_up.start()

    @pl.when(place > 0)
    def _():
        edge_down.start()

    pl.loop(2, 4)(up_block)
    dcf[EDGE : EDGE + OWN, :] = dcb[EDGE : EDGE + OWN, :].astype(F32)

    @pl.loop(0, D // 128)
    def _(t):
        lanes = pl.ds(pl.multiple_of(t * 128, 128), 128)
        mine = dcf[EDGE : EDGE + OWN, lanes]
        for k in range(31):
            near = rimf[1 + k : 1 + k + OWN, lanes] * masks[k]
            few[k : k + 1, lanes] = jnp.sum(mine * near, 0, keepdims=True)

    few[31:32, :] = gain1
    few[32:112, :] = outg_ref[...]
    few[112:114, :] = rows_ref[:2, :]
    few[114:, :] = jnp.zeros((14, D), F32)

    def quarter(m):
        return pl.ds(pl.multiple_of(m * 256, 256), 256)

    def mp_slot(d, incoming):
        there = lax.rem(p.m + d, 4)
        return there, (there if incoming else p.m)

    def few_copy(d, incoming=False):
        there, slot = mp_slot(d, incoming)
        return put(few.at[:, quarter(there)], few_lanes.at[slot], few_send.at[d - 1], few_recv.at[slot], (p.s, there))

    def dh0_copy(d, incoming=False):
        there, slot = mp_slot(d, incoming)
        rows = pl.ds(pl.multiple_of(slot * OWN, OWN), OWN)
        return put(dh0.at[:, quarter(there)], dh0_lanes.at[rows, :], d_send.at[d - 1], d_recv.at[slot], (p.s, there))

    for d in range(1, 4):
        few_copy(d).start()
    few_lanes[p.m] = few[:, quarter(p.m)]
    up_sum.step(0)

    @pl.when(place > 0)
    def _():
        edge_up.wait_recv()

    @pl.when(place < 31)
    def _():
        edge_down.wait_recv()

    dcf[:EDGE, :] = dcb[:EDGE, :].astype(F32)
    dcf[EDGE + OWN :, :] = dcb[EDGE + OWN :, :].astype(F32)

    @pl.loop(0, D // 128)
    def _(t):
        lanes = pl.ds(pl.multiple_of(t * 128, 128), 128)
        total = jnp.zeros((OWN, 128), F32)
        for k in range(31):
            total = total + kern_ref[30 - k : 31 - k, lanes] * (dcf[1 + k : 1 + k + OWN, lanes] * masks[k])
        dh0[:, lanes] = (dh1_ref[:, lanes] + total).astype(BF)

    for d in range(1, 4):
        dh0_copy(d).start()
    dh0_lanes[pl.ds(pl.multiple_of(p.m * OWN, OWN), OWN), :] = dh0[:, quarter(p.m)]
    pl.loop(0, 2)(attention_block)
    up_sum.step(1)
    for d in range(1, 4):
        few_copy(d, True).wait_recv()
    piece[288:416, :] = (few_lanes[0] + few_lanes[1]) + (few_lanes[2] + few_lanes[3])
    piece[416:, :] = jnp.zeros((FEW - 416, 256), F32)
    for d in range(1, 4):
        dh0_copy(d, True).wait_recv()
    grad = tn(feats_ref[...], dh0_lanes[...])
    piece[:MEL, :] = grad[:MEL]
    piece[MEL : 2 * MEL, :] = grad[128 : 128 + MEL]
    piece[160:288, :] = tn(choose_ref[...], dh0_lanes[...])

    eighth = FEW // 8

    def piece_rows(slot):
        return pl.ds(pl.multiple_of(slot * eighth, 8), eighth)

    def seq_slot(d, incoming):
        there = lax.rem(p.s + d, 8)
        return there, (there if incoming else p.s)

    def piece_copy(d, incoming=False):
        there, slot = seq_slot(d, incoming)
        return put(piece.at[piece_rows(there)], pieces.at[slot], piece_send.at[d - 1], piece_recv.at[slot], (there, p.m))

    for d in range(1, 8):
        piece_copy(d).start()
    pieces[p.s] = piece[piece_rows(p.s), :]
    up_sum.step(2)
    pl.loop(2, 4)(attention_block)
    up_sum.step(3)
    att_sum.step(0)
    for d in range(1, 8):
        piece_copy(d, True).wait_recv()
    total = pieces[0]
    for n in range(1, 8):
        total = total + pieces[n]
    small_ref[piece_rows(p.s), quarter(p.m)] = total

    def share_copy(d, incoming=False):
        there, slot = seq_slot(d, incoming)
        view = small_ref.at[piece_rows(slot), quarter(p.m)]
        return put(view, view, g_send.at[d - 1], g_recv.at[slot], (there, p.m))

    def cross(slot, m):
        view = small_ref.at[piece_rows(slot), quarter(m)]
        return put(view, view, y_send.at[slot], y_recv.at[slot], p.across)

    for d in range(1, 8):
        share_copy(d).start()
    cross(p.s, p.m).start()
    few_squares = jnp.sum(total * total)
    att_sum.step(1)
    att_sum.step(2)
    for d in range(1, 8):
        share_copy(d, True).wait_recv()
        cross(lax.rem(p.s + d, 8), p.m).start()
    att_sum.step(3)
    up_sum.finish(gff_ref.at[0])
    gff_ref[1] = gdown_ref[...]
    squares = few_squares + jnp.sum(gff_ref[0] * gff_ref[0]) + jnp.sum(gff_ref[1] * gff_ref[1])
    far = lax.rem(p.m + 2, 4)
    for n in range(8):
        cross(n, far).wait_recv()

    def core_copy(i, m):
        view = small_ref.at[:, quarter(m)]
        return put(view, view, c_send.at[i], c_recv.at[i], p.core)

    core_copy(0, p.m).start()
    core_copy(1, far).start()
    att_sum.finish(att)
    squares = squares + jnp.sum(att[...] * att[...])
    row = lax.broadcasted_iota(jnp.int32, (8, 128), 0)
    seen[p.s] = jnp.where(row == 0, squares, rows_ref[2:3, :128])

    def scalar_copy(d, incoming=False):
        there, slot = seq_slot(d, incoming)
        return put(seen.at[p.s], seen.at[slot], seen_send.at[d - 1], seen_recv.at[slot], (there, p.m))

    for d in range(1, 8):
        scalar_copy(d).start()
    for j in range(4):
        gatt_ref[j] = att[:, 256 * j : 256 * (j + 1)]
    for d in range(1, 8):
        scalar_copy(d, True).wait_recv()
    total = seen[0]
    for n in range(1, 8):
        total = total + seen[n]
    last[p.m] = total

    def last_copy(d, incoming=False):
        there, slot = mp_slot(d, incoming)
        return put(last.at[p.m], last.at[slot], last_send.at[d - 1], last_recv.at[slot], (p.s, there))

    for d in range(1, 4):
        last_copy(d).start()
    core_copy(0, p.m + 1 - 2 * p.c).wait_recv()
    core_copy(1, 3 - p.m).wait_recv()
    for d in range(1, 4):
        last_copy(d, True).wait_recv()
    scalar_ref[...] = (last[0] + last[1]) + (last[2] + last[3])
    for d in range(1, 8):
        piece_copy(d).wait_send()
        share_copy(d).wait_send()
        scalar_copy(d).wait_send()
    for n in range(8):
        cross(n, p.m).wait_send()
    core_copy(0, p.m).wait_send()
    core_copy(1, far).wait_send()
    for d in range(1, 4):
        few_copy(d).wait_send()
        last_copy(d).wait_send()
        dh0_copy(d).wait_send()

    @pl.when(place < 31)
    def _():
        edge_up.wait_send()

    @pl.when(place > 0)
    def _():
        edge_down.wait_send()


def back(lengths, proj, wqkv, a, dh2, h1, conv, rim, gains, kern, feats, choose, rows, outg, gup, gdown, gout):
    outs = [((4, OWN, 256), F32), ((2, OWN, D), F32), ((FEW, D), F32), ((8, 128), F32)]
    wide, group = OWN + 2 * EDGE, a.shape[0]
    dma, vmem = pltpu.SemaphoreType.DMA, pltpu.VMEM
    scratch = [
        vmem((wide, D), BF), vmem((wide, D), F32), vmem((wide, D), F32),
        vmem((31, OWN, 128), F32), vmem((OWN, D), F32),
    ] + reduce_scratch() + BlockReduce.SEMS + [dma((2,)), dma((2,)), vmem((2 * OWN, D), F32)]
    scratch = scratch + (grid_scratch() + GridReduce.SEMS) * 2
    scratch = scratch + [
        vmem((OWN, D), F32), vmem((OWN, D), BF), vmem((group, 256), BF), vmem((OWN, D), F32),
        vmem((4, OWN, 256), F32), vmem((FEW, 256), F32), vmem((8, FEW // 8, 256), F32),
        dma((3,)), dma((4,)), dma((3,)), dma((4,)), dma((7,)), dma((8,)), dma((7,)), dma((8,)),
        dma((8,)), dma((8,)), dma((2,)), dma((2,)),
        vmem((8, 8, 128), F32), dma((7,)), dma((8,)), vmem((4, 8, 128), F32), dma((3,)), dma((4,)),
    ]
    return vmem_call(back_kernel, outs, [SM] + [VM] * 16, scratch, 2, "back", 2e10)(
        lengths, proj, wqkv, a, dh2, h1, conv, rim, gains, kern, feats, choose, rows, outg, gup, gdown, gout
    )


KT = 512


def lane_half(rows):
    return lax.broadcasted_iota(jnp.int32, (rows, 128), 1) < HD


def stack_pair(x):
    low, zero = lane_half(x.shape[0]), jnp.zeros_like(x)
    return jnp.concatenate([jnp.where(low, x, zero), jnp.where(low, zero, x)], 0)


def unstack_pair(x):
    rows = x.shape[0] // 2
    return jnp.where(lane_half(rows), x[:rows], x[rows:])


def slope_of(index):
    value = jnp.float32(2.0 ** (-8.0 * HEADS / HEADS))
    for head in range(HEADS - 1):
        value = jnp.where(index == head, jnp.float32(2.0 ** (-8.0 * (head + 1) / HEADS)), value)
    return value


def tile_range(lengths, first, base):
    end = jnp.int32(0)
    low = jnp.int32(0)
    high = jnp.int32(0)
    for u in range(lengths.shape[0]):
        start = end
        end = start + lengths[u]
        low = jnp.where((start <= first) & (first < end), start, low)
        last = first + OWN - 1
        high = jnp.where((start <= last) & (last < end), end, high)
    return (low - base) // KT, (high - base + KT - 1) // KT


def owner_row(lengths, base, kown):
    frame = base + lax.broadcasted_iota(jnp.int32, kown.shape, 1)
    owner = jnp.full(kown.shape, -1, jnp.int32)
    end = jnp.int32(0)
    for u in range(lengths.shape[0]):
        start = end
        end = start + lengths[u]
        owner = jnp.where((frame >= start) & (frame < end), u, owner)
    kown[...] = owner


def attend_setup(lengths, base, kown, width):
    i = pl.program_id(0)
    first = base[1] + i * OWN

    @pl.when(i == 0)
    def _():
        owner_row(lengths, base[0], kown)

    low, high = tile_range(lengths, first, base[0])
    _, owner, _, _, _ = frame_columns(lengths, first, OWN)
    heads = width // HD
    slopes = [slope_of(lax.axis_index("mp") * heads + h) for h in range(heads)]

    def distance(k0):
        shape = (OWN, KT)
        gap = (first - base[0] - k0) + lax.broadcasted_iota(jnp.int32, shape, 0)
        dist = jnp.abs(gap - lax.broadcasted_iota(jnp.int32, shape, 1)).astype(F32)
        return jnp.where(owner == kown[:, pl.ds(k0, KT)], dist, 1e30)

    return low, high, slopes, distance


def attend_forward_kernel(lengths, base, q_ref, k_ref, v_ref, o_ref, ob_ref, lse_ref, kown):
    width = q_ref.shape[1]
    low, high, slopes, distance = attend_setup(lengths, base, kown, width)
    lanes = [slice(128 * j, 128 * (j + 1)) for j in range(width // 128)]
    qs = [stack_pair(q_ref[:, l]) * BF(0.125) for l in lanes]

    def body(t, carry):
        k0 = pl.multiple_of(t * KT, KT)
        dist = distance(k0)
        out = []
        for j, l in enumerate(lanes):
            top, total, acc = carry[j]
            s = nt(qs[j], k_ref[pl.ds(k0, KT), l])
            s = jnp.concatenate([s[:OWN] - slopes[2 * j] * dist, s[OWN:] - slopes[2 * j + 1] * dist], 0)
            new = jnp.maximum(top, jnp.max(s, -1, keepdims=True))
            fade = jnp.exp(top - new)
            e = jnp.exp(s - new)
            total = total * fade + jnp.sum(e, -1, keepdims=True)
            acc = acc * fade + nn(e.astype(BF), v_ref[pl.ds(k0, KT), l])
            out.append((new, total, acc))
        return tuple(out)

    begin = (
        jnp.full((2 * OWN, 1), -1e30, F32), jnp.zeros((2 * OWN, 1), F32), jnp.zeros((2 * OWN, 128), F32),
    )
    ended = lax.fori_loop(low, high, body, tuple(begin for _ in lanes))
    lane = lax.broadcasted_iota(jnp.int32, (OWN, 128), 1)
    lse = jnp.zeros((OWN, 128), F32)
    for j, l in enumerate(lanes):
        top, total, acc = ended[j]
        o = unstack_pair(acc / total)
        o_ref[:, l] = o
        ob_ref[:, l] = o.astype(BF)
        g = top + jnp.log(total)
        lse = jnp.where(lane == 2 * j, g[:OWN], lse)
        lse = jnp.where(lane == 2 * j + 1, g[OWN:], lse)
    lse_ref[...] = lse


def blocks(width):
    return pl.BlockSpec((OWN, width), lambda i, *_: (i, 0))


def whole(*shape):
    return pl.BlockSpec(shape, lambda i, *_: (0,) * len(shape))


def attend_call(kernel, outs, out_specs, in_specs, rows, keys, name, flops):
    return pl.pallas_call(
        kernel,
        out_shape=outs,
        grid_spec=pltpu.PrefetchScalarGridSpec(
            num_scalar_prefetch=2, grid=(rows // OWN,), in_specs=in_specs, out_specs=out_specs,
            scratch_shapes=[pltpu.VMEM((1, keys), jnp.int32)],
        ),
        compiler_params=pltpu.CompilerParams(vmem_limit_bytes=50 << 20),
        cost_estimate=pl.CostEstimate(flops=flops, bytes_accessed=1 << 23, transcendentals=0),
        name=name,
    )


def attend_forward(lengths, base, q, k, v):
    (rows, width), keys = q.shape, k.shape[0]
    outs = (
        jax.ShapeDtypeStruct((rows, width), F32), jax.ShapeDtypeStruct((rows, width), BF),
        jax.ShapeDtypeStruct((rows, 128), F32),
    )
    return attend_call(
        attend_forward_kernel, outs, (blocks(width), blocks(width), blocks(128)),
        [blocks(width), whole(keys, width), whole(keys, width)], rows, keys, "attend_forward", 10**10,
    )(lengths, base, q, k, v)


def attend_backward_kernel(
    lengths, base, q_ref, k_ref, v_ref, do_ref, lse_ref, delta_ref, qa_ref, ka_ref, va_ref, doa_ref,
    stat_ref, out_ref, kown,
):
    width = q_ref.shape[1]
    low, high, slopes, distance = attend_setup(lengths, base, kown, width)
    lanes = [slice(128 * j, 128 * (j + 1)) for j in range(width // 128)]

    def column(ref, j):
        return jnp.concatenate([ref[:, 2 * j : 2 * j + 1], ref[:, 2 * j + 1 : 2 * j + 2]], 0)

    scale = BF(0.125)
    qs = [stack_pair(q_ref[:, l]) * scale for l in lanes]
    dos = [stack_pair(do_ref[:, l]) for l in lanes]
    ks = [stack_pair(k_ref[:, l]) * scale for l in lanes]
    vs = [stack_pair(v_ref[:, l]) for l in lanes]
    lses = [column(lse_ref, j) for j in range(len(lanes))]
    deltas = [column(delta_ref, j) for j in range(len(lanes))]

    def body(t, carry):
        k0 = pl.multiple_of(t * KT, KT)
        keys = pl.ds(k0, KT)
        dist = distance(k0)
        out = []
        for j, l in enumerate(lanes):
            dq, dk, dv = carry[j]
            kj, vj, qj, doj = ka_ref[keys, l], va_ref[keys, l], qa_ref[keys, l], doa_ref[keys, l]
            bias = [slopes[2 * j + h] * dist for h in (0, 1)]
            s = nt(qs[j], kj)
            e = jnp.exp(jnp.concatenate([s[:OWN] - bias[0], s[OWN:] - bias[1]], 0) - lses[j])
            ds = (e * (nt(dos[j], vj) - deltas[j])).astype(BF)
            dq = dq + nn(ds, kj)
            s = nt(ks[j], qj)
            far = [stat_ref[t, 2 * j + h : 2 * j + h + 1, :] for h in (0, 1)]
            e = jnp.exp(jnp.concatenate([s[:OWN] - bias[0] - far[0], s[OWN:] - bias[1] - far[1]], 0))
            dv = dv + nn(e.astype(BF), doj)
            g = nt(vs[j], doj)
            far = [stat_ref[t, 8 + 2 * j + h : 9 + 2 * j + h, :] for h in (0, 1)]
            ds = (e * jnp.concatenate([g[:OWN] - far[0], g[OWN:] - far[1]], 0)).astype(BF)
            dk = dk + nn(ds, qj)
            out.append((dq, dk, dv))
        return tuple(out)

    zero = jnp.zeros((2 * OWN, 128), F32)
    ended = lax.fori_loop(low, high, body, tuple((zero, zero, zero) for _ in lanes))
    for j, l in enumerate(lanes):
        dq, dk, dv = ended[j]
        out_ref[0, :, l] = (unstack_pair(dq) * 0.125).astype(BF)
        out_ref[1, :, l] = (unstack_pair(dk) * 0.125).astype(BF)
        out_ref[2, :, l] = unstack_pair(dv).astype(BF)


def attend_backward(lengths, base, q, k, v, do, lse, delta, qa, ka, va, doa, stat):
    (rows, width), keys = q.shape, ka.shape[0]
    return attend_call(
        attend_backward_kernel, jax.ShapeDtypeStruct((3, rows, width), BF),
        pl.BlockSpec((3, OWN, width), lambda i, *_: (0, i, 0)),
        [blocks(width)] * 4 + [blocks(128)] * 2 + [whole(keys, width)] * 4 + [whole(*stat.shape)],
        rows, keys, "attend_backward", 3 * 10**10,
    )(lengths, base, q, k, v, do, lse, delta, qa, ka, va, doa, stat)


def adam_step(weight, first_old, second, gradient, step_rate, decay_on):
    first_new = beta_one * first_old + (1.0 - beta_one) * gradient
    second_new = beta_two * second + (1.0 - beta_two) * gradient * gradient
    fix_one = 1.0 - beta_one**STEP
    fix_two = 1.0 - beta_two**STEP
    moved = first_new / fix_one / (jnp.sqrt(second_new / fix_two) + adam_epsilon)
    return (first_new, second_new, weight - step_rate * (moved + decay_on * weight_decay * weight))


def update(loss_total, grads, frames, states):
    big_squares = jnp.sum(grads[0] * grads[0]) + jnp.sum(grads[1] * grads[1])
    small_squares = jnp.zeros((), jnp.float32)
    for gradient in grads[2:]:
        small_squares = small_squares + jnp.sum(gradient * gradient)
    big_total = lax.psum(big_squares, ("seq", "mp"))
    return adam_all(loss_total, jnp.sqrt(big_total + small_squares), grads, frames, states)


def adam_all(loss_total, grad_norm, grads, frames, states):
    weights, firsts, seconds = states
    factor = jnp.minimum(1.0, 0.3 / math.sqrt(frames) / grad_norm)
    results = [loss_total, grad_norm]
    for number in range(7):
        results.extend(
            adam_step(
                weights[number],
                firsts[number],
                seconds[number],
                grads[number] * factor,
                step_rates[number],
                decay_flags[number],
            )
        )
    return tuple(results)


def split_arguments(arguments):
    rest = arguments[7:]
    return arguments[:7], (rest[0::3], rest[1::3], rest[2::3])


def per_device(*arguments):
    inputs, states = split_arguments(arguments)
    row_count = inputs[0].shape[0]
    if (lax.axis_size("seq"), lax.axis_size("mp"), row_count) == (8, 4, 512):
        return step_by_kernels(inputs, states)
    return step_by_collectives(inputs, states)


def step_by_kernels(inputs, states):
    mel, noise, phone_ids, lengths, span_start, span_end, flow_times = inputs
    attention, feedforward, win, phone_table, kern, wpred, gains = states[0]
    row_count = mel.shape[0]
    frames = row_count * lax.axis_size("seq")
    columns = ((0, 0), (0, 128 - MEL))
    with_phone = jnp.concatenate([noise, phone_ids.astype(F32)[:, None]], 1)
    pack = jnp.concatenate(
        [jnp.pad(mel, columns), jnp.pad(with_phone, ((0, 0), (0, 127 - MEL)))], 1
    )
    table = time_features(flow_times, D)
    (
        h1, conv, rim, a, q, k, v, wqkv, feats, choose, lse,
        dh2, rows, outg, do, delta, q_all, do_all, stat, gup, gdown, gout,
    ) = forward(
        lengths, span_start, span_end, flow_times, pack, table, win, phone_table, kern, gains, attention,
        feedforward[0], feedforward[1], wpred,
    )
    row_base = lax.axis_index("seq") * row_count
    base = jnp.stack([jnp.zeros_like(row_base), row_base]).astype(jnp.int32)
    k_own = lax.dynamic_slice_in_dim(k, row_base, row_count, 0)
    v_own = lax.dynamic_slice_in_dim(v, row_base, row_count, 0)
    proj = attend_backward(lengths, base, q, k_own, v_own, do, lse, delta, q_all, k, v, do_all, stat)
    attention_grad, feedforward_grad, small, scalars = back(
        lengths, proj, wqkv, a, dh2, h1, conv, rim, gains, kern, feats, choose, rows, outg, gup, gdown, gout
    )
    gain_grad = jnp.stack([small[319], small[401], small[400]])
    grads = (
        attention_grad, feedforward_grad, small[:160], small[160:288], small[288:319],
        small[320:400].T, gain_grad,
    )
    return adam_all(scalars[1, 0], jnp.sqrt(scalars[0, 0]), grads, frames, states)


def step_by_collectives(inputs, states):
    mel_frames, noise_frames, phone_ids, lengths, span_start, span_end, flow_times = inputs
    (
        attention_weight,
        feedforward_weight,
        input_weight,
        phone_table,
        position_kernel,
        output_weight,
        layer_gains,
    ) = states[0]
    row_count = mel_frames.shape[0]
    frames = row_count * lax.axis_size("seq")
    row_base = lax.axis_index("seq") * row_count
    longest = min(MAXLEN, frames // 2)
    near_count = min((longest - 1 + row_count - 1) // row_count, lax.axis_size("seq") - 1)
    window_start = row_base - near_count * row_count
    reach = position_kernel.shape[0] // 2
    tables = (lengths, span_start, span_end, flow_times)
    row_index = row_base + jnp.arange(row_count)
    owners, masked, moment = frame_tables(*tables, row_index)
    covered, uncovered = mask_counts(lengths, span_start, span_end)
    row_weight = masked / jnp.maximum(covered, 1.0) + 0.1 * (1.0 - masked) / jnp.maximum(
        uncovered, 1.0
    )
    attention_full, feedforward_full = (
        lax.all_gather(attention_weight.astype(jnp.bfloat16), "seq", axis=1, tiled=True),
        lax.all_gather(feedforward_weight.astype(jnp.bfloat16), "seq", axis=1, tiled=True),
    )
    heads_local = attention_full.shape[2] // HD
    target = mel_frames - (1.0 - flow_sigma) * noise_frames
    noisy = (1.0 - (1.0 - flow_sigma) * moment[:, None]) * noise_frames + moment[
        :, None
    ] * mel_frames
    context = mel_frames * (1.0 - masked[:, None])
    feats = jnp.concatenate([context, noisy], 1).astype(jnp.bfloat16)
    choose = (phone_ids[:, None] == jnp.arange(phone_table.shape[0])[None, :]).astype(jnp.bfloat16)
    start_h = product(feats, input_weight.astype(jnp.bfloat16)) + product(
        choose, phone_table.astype(jnp.bfloat16)
    )
    start_h = start_h + time_features(moment, D)
    start_low = start_h.astype(jnp.bfloat16)
    rim = padded_2(start_low, (("seq", 0),), reach)
    pad_owner = frame_tables(*tables, row_base - reach + jnp.arange(row_count + 2 * reach))[0]
    conv_raw = jnp.zeros(start_h.shape, jnp.float32)
    for offset in range(position_kernel.shape[0]):
        same_owner = (pad_owner[offset : offset + row_count] == owners).astype(jnp.float32)
        conv_raw = (
            conv_raw
            + position_kernel[offset][None, :]
            * rim[offset : offset + row_count].astype(jnp.float32)
            * same_owner[:, None]
        )
    conv_gelu, conv_back = jax.vjp(jax.nn.gelu, conv_raw)
    hidden_one = start_h + conv_gelu
    ln_one, norm_back_one = jax.vjp(layer_norm, hidden_one, layer_gains[0])
    ln_one_low = ln_one.astype(jnp.bfloat16)
    projected = jnp.einsum(
        "td,kdh->kth", ln_one_low, attention_full[:3], preferred_element_type=jnp.float32
    ).astype(jnp.bfloat16)
    queries, keyed, valued = (projected[0], projected[1], projected[2])
    def window(array):
        return slice_window(
            lax.all_gather(array, "seq", axis=0, tiled=True), row_base, near_count, row_count
        )

    base = jnp.stack([window_start, row_base]).astype(jnp.int32)
    key_all, value_all = window(keyed), window(valued)
    out_f32, out_low, log_total = attend_forward(lengths, base, queries, key_all, value_all)
    attended = lax.psum(
        contract_cols(out_low, attention_full[3]).astype(jnp.bfloat16), "mp"
    ).astype(jnp.float32)
    hidden_two = hidden_one + attended
    ln_two, norm_back_two = jax.vjp(layer_norm, hidden_two, layer_gains[1])
    ln_two_low = ln_two.astype(jnp.bfloat16)
    upward = product(ln_two_low, feedforward_full[0])
    gated_f32, gelu_back = jax.vjp(jax.nn.gelu, upward)
    gated = gated_f32.astype(jnp.bfloat16)
    downward = lax.psum(
        contract_cols(gated, feedforward_full[1]).astype(jnp.bfloat16), "mp"
    ).astype(jnp.float32)
    hidden_three = hidden_two + downward
    ln_three, norm_back_three = jax.vjp(layer_norm, hidden_three, layer_gains[2])
    ln_three_low = ln_three.astype(jnp.bfloat16)
    output_low = output_weight.astype(jnp.bfloat16)
    predicted = product(ln_three_low, output_low)
    errors = predicted - target
    loss_local = jnp.sum(row_weight * jnp.mean(errors * errors, 1))
    loss_total = lax.psum(loss_local, "seq")
    pred_grad = (row_weight[:, None] * (2.0 / errors.shape[1]) * errors).astype(jnp.bfloat16)
    output_grad = contract_rows(ln_three_low, pred_grad)
    three_grad, gain_three = norm_back_three(contract_cols(pred_grad, output_low))
    down_low = three_grad.astype(jnp.bfloat16)
    down_wgrad = contract_rows(down_low, gated)
    up_grad = gelu_back(product(down_low, feedforward_full[1]))[0].astype(jnp.bfloat16)
    up_wgrad = contract_rows(ln_two_low, up_grad)
    two_sum = lax.psum(
        contract_cols(up_grad, feedforward_full[0]).astype(jnp.bfloat16), "mp"
    ).astype(jnp.float32)
    norm_grad, gain_two = norm_back_two(two_sum)
    two_grad = three_grad + norm_grad
    attended_low = two_grad.astype(jnp.bfloat16)
    out_wgrad = contract_rows(attended_low, out_low)
    out_heads = product(attended_low, attention_full[3]).astype(jnp.bfloat16)
    delta = jnp.sum(
        (out_heads.astype(jnp.float32) * out_f32).reshape(row_count, heads_local, HD), 2
    )
    delta = jnp.pad(delta, ((0, 0), (0, 128 - heads_local)))
    stat = window(jnp.concatenate([log_total[:, :8], delta[:, :8]], 1))
    stat = stat.reshape(-1, KT, 16).transpose(0, 2, 1)
    proj_grad = attend_backward(
        lengths, base, queries, keyed, valued, out_heads, log_total, delta,
        window(queries), key_all, value_all, window(out_heads), stat,
    )
    qkv_wgrad = jnp.einsum("td,kth->kdh", ln_one_low, proj_grad, preferred_element_type=jnp.float32)
    one_part = jnp.einsum(
        "kth,kdh->td", proj_grad, attention_full[:3], preferred_element_type=jnp.float32
    )
    one_sum = lax.psum(one_part.astype(jnp.bfloat16), "mp").astype(jnp.float32)
    norm_grad, gain_one = norm_back_one(one_sum)
    one_grad = two_grad + norm_grad
    conv_grad = conv_back(one_grad)[0].astype(jnp.bfloat16)
    grad_rim = padded_2(conv_grad, (("seq", 0),), reach)
    spread = jnp.zeros(one_grad.shape, jnp.float32)
    kernel_rows = []
    conv_grad_f32 = conv_grad.astype(jnp.float32)
    for offset in range(position_kernel.shape[0]):
        back_start = 2 * reach - offset
        same_back = (pad_owner[back_start : back_start + row_count] == owners).astype(jnp.float32)
        spread = (
            spread
            + position_kernel[offset][None, :]
            * grad_rim[back_start : back_start + row_count].astype(jnp.float32)
            * same_back[:, None]
        )
        same_fore = (pad_owner[offset : offset + row_count] == owners).astype(jnp.float32)
        kernel_rows.append(
            jnp.sum(
                conv_grad_f32
                * rim[offset : offset + row_count].astype(jnp.float32)
                * same_fore[:, None],
                0,
            )
        )
    kernel_grad = jnp.stack(kernel_rows)
    start_grad = (one_grad + spread).astype(jnp.bfloat16)
    input_wgrad = contract_rows(feats, start_grad)
    phone_wgrad = contract_rows(choose, start_grad)
    gains_grad = jnp.stack([gain_one, gain_two, gain_three])
    small_sums = lax.psum((input_wgrad, phone_wgrad, kernel_grad, output_grad, gains_grad), "seq")
    attention_grad, feedforward_grad = (
        lax.psum_scatter(
            jnp.concatenate([qkv_wgrad, out_wgrad[None]], 0), "seq", scatter_dimension=1, tiled=True
        ),
        lax.psum_scatter(jnp.stack([up_wgrad, down_wgrad]), "seq", scatter_dimension=1, tiled=True),
    )
    grads = (attention_grad, feedforward_grad) + tuple(small_sums)
    return update(loss_total, grads, frames, states)


def solution(mesh):
    in_specs = (
        P("seq", None),
        P("seq", None),
        P("seq"),
        P(),
        P(),
        P(),
        P(),
        P(None, "seq", "mp"),
        P(None, "seq", "mp"),
        P(None, "seq", "mp"),
        P(None, "seq", "mp"),
        P(None, "seq", "mp"),
        P(None, "seq", "mp"),
        P(),
        P(),
        P(),
        P(),
        P(),
        P(),
        P(),
        P(),
        P(),
        P(),
        P(),
        P(),
        P(),
        P(),
        P(),
    )
    out_specs = (
        P(),
        P(),
        P(None, "seq", "mp"),
        P(None, "seq", "mp"),
        P(None, "seq", "mp"),
        P(None, "seq", "mp"),
        P(None, "seq", "mp"),
        P(None, "seq", "mp"),
        P(),
        P(),
        P(),
        P(),
        P(),
        P(),
        P(),
        P(),
        P(),
        P(),
        P(),
        P(),
        P(),
        P(),
        P(),
    )
    return jax.shard_map(
        per_device, mesh=mesh, in_specs=in_specs, out_specs=out_specs, check_vma=False
    )
```

```python
import functools
import math

import jax
import jax.numpy as jnp
from jax import lax
from jax.experimental import pallas as pl
from jax.experimental.pallas import tpu as pltpu
from jax.sharding import PartitionSpec as P

D = 1024
HEADS = 16
HD = 64
MEL = 80
STEP = 10
MAXLEN = 1600


norm_epsilon = 1e-05
flow_sigma = 1e-05
beta_one = 0.9
beta_two = 0.95
adam_epsilon = 1e-08
weight_decay = 0.1
step_rates = (0.04, 0.04, 0.08, 1.0, 0.2, 0.04, 1.0)
decay_flags = (1.0, 1.0, 1.0, 1.0, 1.0, 1.0, 0.0)


def padded_2(array, sides, width):
    for axis, dim in sides:
        devices, length = (lax.axis_size(axis), array.shape[dim])
        up = [(i, (i + 1) % devices) for i in range(devices - 1)]
        down = [(j, i) for i, j in up]
        last = lax.slice_in_dim(array, length - width, length, axis=dim)
        initial = lax.slice_in_dim(array, 0, width, axis=dim)
        before = lax.ppermute(last, axis, up)
        after = lax.ppermute(initial, axis, down)
        array = jnp.concatenate([before, array, after], axis=dim)
    return array


def layer_norm(inputs, gain_row):
    centre_mean = jnp.mean(inputs, -1, keepdims=True)
    centered = inputs - centre_mean
    variance = jnp.mean(centered * centered, -1, keepdims=True)
    return centered * lax.rsqrt(variance + norm_epsilon) * gain_row


def frame_tables(lengths, span_start, span_end, flow_times, frame_index):
    utter_ends = jnp.cumsum(lengths)
    starts = utter_ends - lengths
    member = (
        (frame_index[:, None] >= starts[None, :]) & (frame_index[:, None] < utter_ends[None, :])
    ).astype(jnp.float32)
    labels = (jnp.arange(lengths.shape[0]) + 1).astype(jnp.float32)
    owners = jnp.sum(member * labels[None, :], 1) - 1.0
    position = frame_index.astype(jnp.float32) - jnp.sum(
        member * starts.astype(jnp.float32)[None, :], 1
    )
    low_end = jnp.sum(member * span_start.astype(jnp.float32)[None, :], 1)
    high_end = jnp.sum(member * span_end.astype(jnp.float32)[None, :], 1)
    masked = ((position >= low_end) & (position < high_end)).astype(jnp.float32)
    moment = jnp.sum(member * flow_times[None, :], 1)
    return (owners, masked, moment)


def mask_counts(lengths, span_start, span_end):
    span_low = jnp.minimum(span_start, lengths)
    span_high = jnp.minimum(span_end, lengths)
    covered = jnp.sum(jnp.maximum(span_high - span_low, 0)).astype(jnp.float32)
    return (covered, jnp.sum(lengths).astype(jnp.float32) - covered)


def time_features(moment, width):
    half_width = width // 2
    frequency = jnp.exp(
        -math.log(10000.0) * jnp.arange(half_width).astype(jnp.float32) / half_width
    )
    angles = moment[:, None] * 100.0 * frequency[None, :]
    return jnp.concatenate([jnp.sin(angles), jnp.cos(angles)], 1)


def product(left, right):
    return jnp.dot(left, right, preferred_element_type=jnp.float32)


def contract_rows(left, right):
    return lax.dot_general(
        left, right, (((0,), (0,)), ((), ())), preferred_element_type=jnp.float32
    )


def contract_cols(left, right):
    return lax.dot_general(
        left, right, (((1,), (1,)), ((), ())), preferred_element_type=jnp.float32
    )


def slice_window(full_rows, row_base, near_count, row_count):
    pad_rows = near_count * row_count
    padded = jnp.pad(full_rows, ((pad_rows, pad_rows), (0, 0)))
    return lax.dynamic_slice_in_dim(padded, row_base, (2 * near_count + 1) * row_count, 0)


MESH = pl.DeviceIdType.MESH
VM = pl.BlockSpec(memory_space=pltpu.VMEM)
SM = pl.BlockSpec(memory_space=pltpu.SMEM)
BF = jnp.bfloat16
F32 = jnp.float32
OWN = 128
EDGE = 16
HALF = OWN // 2


def nn(a, b):
    return jnp.dot(a, b, preferred_element_type=F32)


def nt(a, b):
    return lax.dot_general(a, b, (((1,), (1,)), ((), ())), preferred_element_type=F32)


def tn(a, b):
    return lax.dot_general(a, b, (((0,), (0,)), ((), ())), preferred_element_type=F32)


def put(src, dst, send, recv, device):
    return pltpu.make_async_remote_copy(
        src_ref=src, dst_ref=dst, send_sem=send, recv_sem=recv, device_id=device, device_id_type=MESH
    )


class Place:
    def __init__(self):
        self.s, self.m = lax.axis_index("seq"), lax.axis_index("mp")
        self.z, self.x = self.s // 2, lax.rem(self.s, 2)
        self.y, self.c = self.m // 2, lax.rem(self.m, 2)
        self.core = (self.s, self.m + 1 - 2 * self.c)
        self.across = (self.s, lax.rem(self.m + 2, 4))
        self.side = (self.s + 1 - 2 * self.x, self.m)
        self.up = (self.s + 2, self.m)
        self.down = (self.s - 2, self.m)


def greet(peers):
    barrier = pltpu.get_barrier_semaphore()
    total = 0
    for device, exists in peers:
        if exists is None:
            pl.semaphore_signal(barrier, inc=1, device_id=device, device_id_type=MESH)
            total = total + 1
        else:

            @pl.when(exists)
            def _(device=device):
                pl.semaphore_signal(barrier, inc=1, device_id=device, device_id_type=MESH)

            total = total + exists.astype(jnp.int32)
    pl.semaphore_wait(barrier, total)


def grid_peers(p):
    column = [((2 * lax.rem(p.z + d, 4) + p.x, p.m), None) for d in range(1, 4)]
    return [(p.side, None)] + column


def mp_peers(p):
    return [(p.core, None), (p.across, None)]


class Gather:
    SEMS = [pltpu.SemaphoreType.DMA((3, 8)), pltpu.SemaphoreType.DMA((8,))]

    def __init__(self, p, view, send, recv):
        self.p, self.view, self.send, self.recv = p, view, send, recv

    def copy(self, slot, kind):
        p = self.p
        device = (p.side, p.up, p.down)[kind]
        return put(
            self.view(slot), self.view(slot), self.send.at[kind, slot], self.recv.at[slot], device
        )

    def start(self):
        p = self.p
        self.copy(p.s, 0).start()

        @pl.when(p.z < 3)
        def _():
            self.copy(p.s, 1).start()

        @pl.when(p.z > 0)
        def _():
            self.copy(p.s, 2).start()

    def step(self, hop):
        p = self.p
        below, above = p.s - 2 * (hop + 1), p.s + 2 * (hop + 1)

        @pl.when(p.z - 1 - hop >= 0)
        def _():
            self.copy(below, 0).wait_recv()
            self.copy(below, 0).start()

            @pl.when(p.z < 3)
            def _():
                self.copy(below, 1).start()

        @pl.when(p.z + 1 + hop <= 3)
        def _():
            self.copy(above, 0).wait_recv()
            self.copy(above, 0).start()

            @pl.when(p.z > 0)
            def _():
                self.copy(above, 2).start()

    def finish(self):
        p = self.p
        for zz in range(4):
            self.copy(2 * zz + 1 - p.x, 0).wait_recv()
        for zz in range(4):
            slot = 2 * zz + p.x
            self.copy(slot, 0).wait_send()

            @pl.when((p.z < 3) & (p.z >= zz))
            def _(slot=slot):
                self.copy(slot, 1).wait_send()

            @pl.when((p.z > 0) & (p.z <= zz))
            def _(slot=slot):
                self.copy(slot, 2).wait_send()


class ColumnGather:
    SEMS = [pltpu.SemaphoreType.DMA((2, 4)), pltpu.SemaphoreType.DMA((8,))]

    def __init__(self, p, view, send, recv):
        self.p, self.view, self.send, self.recv = p, view, send, recv

    def level(self, hop):
        z = self.p.z
        if hop == 0:
            return z + 1 - 2 * lax.rem(z, 2)
        return jnp.where(z < 2, 1 + hop, 2 - hop)

    def copy(self, slot, sem, device):
        return put(self.view(slot), self.view(slot), self.send.at[sem], self.recv.at[slot], device)

    def along(self, hop):
        p = self.p
        zz = self.level(hop)
        return self.copy(p.s, (0, hop), (2 * zz + p.x, p.m))

    def aside(self, hop):
        p = self.p
        slot = p.s if hop == 3 else 2 * self.level(hop) + p.x
        return self.copy(slot, (1, hop), p.side)

    def start(self):
        self.aside(3).start()
        for hop in range(3):
            self.along(hop).start()

    def step(self, hop):
        self.aside(hop).wait_recv()
        self.aside(hop).start()

    def finish(self):
        p = self.p
        for zz in range(4):
            self.copy(2 * zz + 1 - p.x, (1, 3), p.side).wait_recv()
        for hop in range(3):
            self.along(hop).wait_send()
        for hop in range(4):
            self.aside(hop).wait_send()


class NearGather:
    SEMS = [pltpu.SemaphoreType.DMA((8,)), pltpu.SemaphoreType.DMA((8,))]

    def __init__(self, p, view, edge, send, recv):
        self.p, self.view, self.edge, self.send, self.recv = p, view, edge, send, recv
        self.turn = 1 - 2 * p.x
        s, turn = p.s, self.turn
        self.ahead, self.behind = (s + 2 * turn, p.m), (s - 2 * turn, p.m)
        self.has_ahead = (s + 2 * turn >= 0) & (s + 2 * turn <= 7)
        self.has_behind = (s - 2 * turn >= 0) & (s - 2 * turn <= 7)

    def copy(self, slot, sem, device):
        return put(self.view(slot), self.view(slot), self.send.at[sem], self.recv.at[slot], device)

    def part(self, slot, last, sem, device):
        return put(self.edge(slot, last), self.edge(slot, last), self.send.at[sem], self.recv.at[slot], device)

    def sends(self):
        p, s, turn = self.p, self.p.s, self.turn
        both = self.has_ahead & self.has_behind
        return [
            (lambda: self.copy(s, 0, p.side), None),
            (lambda: self.copy(s, 1, self.ahead), self.has_ahead),
            (lambda: self.copy(s, 2, self.behind), self.has_behind),
            (lambda: self.copy(s + turn, 3, self.behind), self.has_behind),
            (lambda: self.copy(s + 2 * turn, 4, p.side), self.has_ahead),
            (lambda: self.part(s + 2 * turn, p.x, 5, self.behind), both),
            (lambda: self.part(s - 2 * turn, 1 - p.x, 6, self.ahead), both),
            (lambda: self.copy(s - turn, 7, self.ahead), both),
        ]

    def go(self, index):
        copy, made = self.sends()[index]
        if made is None:
            copy().start()
        else:

            @pl.when(made)
            def _():
                copy().start()

    def arrive(self, slot, exists):
        @pl.when(exists)
        def _():
            self.copy(slot, 0, self.p.side).wait_recv()

    def start(self):
        for index in (0, 1, 2):
            self.go(index)

    def step(self, hop):
        s, turn = self.p.s, self.turn
        if hop == 0:
            self.copy(s + turn, 0, self.p.side).wait_recv()
            self.go(3)
        elif hop == 1:
            self.arrive(s + 2 * turn, self.has_ahead)
            self.go(4)
            self.go(5)
            self.arrive(s - 2 * turn, self.has_behind)
            self.go(6)
        else:
            self.arrive(s - turn, self.has_behind)
            self.go(7)

    def finish(self):
        s = self.p.s
        self.arrive(s - 3, s >= 3)
        self.arrive(s + 3, s <= 4)

        @pl.when(s >= 4)
        def _():
            self.part(s - 4, 1, 0, self.p.side).wait_recv()

        @pl.when(s <= 3)
        def _():
            self.part(s + 4, 0, 0, self.p.side).wait_recv()

        for copy, made in self.sends():
            if made is None:
                copy().wait_send()
            else:

                @pl.when(made)
                def _(copy=copy):
                    copy().wait_send()


def near_rows(ref, group):
    def view(slot):
        return ref.at[pl.ds(pl.multiple_of(slot * group, group), group), :]

    def edge(slot, last):
        return ref.at[pl.ds(pl.multiple_of(slot * group + last * (group - 64), 64), 64), :]

    return view, edge


class BlockGather:
    SEMS = [pltpu.SemaphoreType.DMA((3, 2)), pltpu.SemaphoreType.DMA((4, 2))]

    def __init__(self, p, full, send, recv):
        self.p, self.full, self.send, self.recv = p, full, send, recv

    def copy(self, slot, kind, h):
        rows = self.full.at[pl.ds(pl.multiple_of(slot * OWN + h * HALF, HALF), HALF)]
        device = self.p.across if kind == 0 else self.p.core
        return put(rows, rows, self.send.at[kind, h], self.recv.at[slot, h], device)

    def start(self, h):
        self.copy(self.p.m, 0, h).start()
        self.copy(self.p.m, 1, h).start()

    def finish(self):
        p = self.p
        far = lax.rem(p.m + 2, 4)
        for h in (0, 1):
            self.copy(far, 0, h).wait_recv()
            self.copy(far, 2, h).start()
        for h in (0, 1):
            self.copy(p.m + 1 - 2 * p.c, 1, h).wait_recv()
            self.copy(3 - p.m, 2, h).wait_recv()
            for kind in range(3):
                self.copy(p.m, kind, h).wait_send()


class BlockReduce:
    SEMS = [pltpu.SemaphoreType.DMA((3, 2)), pltpu.SemaphoreType.DMA((3, 2))]

    def __init__(self, p, part, from_core, pair, send, recv):
        self.p, self.part, self.from_core, self.pair = p, part, from_core, pair
        self.send, self.recv = send, recv

    def rows(self, slot, h):
        return pl.ds(pl.multiple_of(slot * OWN + h * HALF, HALF), HALF)

    def core_copy(self, i, h):
        p = self.p
        yy = 1 - p.y if i == 0 else p.y
        return put(
            self.part.at[self.rows(2 * yy + 1 - p.c, h)], self.from_core.at[i, pl.ds(h * HALF, HALF)],
            self.send.at[i, h], self.recv.at[i, h], p.core,
        )

    def across_copy(self, h):
        half = pl.ds(h * HALF, HALF)
        return put(
            self.pair.at[0, half], self.pair.at[1, half], self.send.at[2, h], self.recv.at[2, h], self.p.across
        )

    def far_rows(self):
        return pl.ds(pl.multiple_of((1 - self.p.y) * 2 * OWN, OWN), 2 * OWN)

    def near_rows(self):
        return pl.ds(pl.multiple_of(self.p.y * 2 * OWN, OWN), 2 * OWN)

    def send_far(self):
        p = self.p
        for h in (0, 1):
            self.core_copy(0, h).start()
        for h in (0, 1):
            half = slice(h * HALF, (h + 1) * HALF)
            self.core_copy(0, h).wait_recv()
            mine = self.part[self.rows(2 * (1 - p.y) + p.c, h), :].astype(F32)
            self.pair[0, half, :] = (mine + self.from_core[0, half, :].astype(F32)).astype(self.pair.dtype)
            self.across_copy(h).start()

    def send_near(self):
        for h in (0, 1):
            self.core_copy(1, h).start()

    def finish(self, h):
        half = slice(h * HALF, (h + 1) * HALF)
        self.core_copy(1, h).wait_recv()
        total = self.part[self.rows(self.p.m, h), :].astype(F32) + self.from_core[1, half, :].astype(F32)
        self.across_copy(h).wait_recv()
        return total + self.pair[1, half, :].astype(F32)

    def sent(self):
        for h in (0, 1):
            self.core_copy(0, h).wait_send()
            self.core_copy(1, h).wait_send()
            self.across_copy(h).wait_send()


class GridReduce:
    SEMS = [pltpu.SemaphoreType.DMA((2, 4)), pltpu.SemaphoreType.DMA((2, 4))]

    def __init__(self, p, column, side, from_side, chain, incoming, send, recv):
        self.p, self.column, self.side, self.from_side = p, column, side, from_side
        self.chain, self.incoming, self.send, self.recv = chain, incoming, send, recv

    def level(self, t):
        z = self.p.z
        high = jnp.where(z == 3, t, jnp.where(t == 0, 0, jnp.where(t == 1, 1, 5 - t)))
        low = jnp.where(z == 0, 3 - t, jnp.where(t == 0, 3, jnp.where(t == 1, 2, t - 2)))
        return jnp.where(z >= 2, high, low)

    def side_copy(self, zz):
        return put(self.side.at[zz], self.from_side.at[zz], self.send.at[0, zz], self.recv.at[0, zz], self.p.side)

    def along(self, there, slot):
        p = self.p
        return put(
            self.chain.at[there], self.incoming.at[slot], self.send.at[1, there], self.recv.at[1, slot],
            (2 * there + p.x, p.m),
        )

    def start(self, t, both):
        p, zz = self.p, self.level(t)
        rows = self.side.shape[1]
        self.side[zz] = both[pl.ds(pl.multiple_of((1 - p.x) * rows, rows), rows), :].astype(self.side.dtype)
        self.side_copy(zz).start()
        self.column[zz] = both[pl.ds(pl.multiple_of(p.x * rows, rows), rows), :]

    def step(self, t):
        p, zz = self.p, self.level(t)
        self.side_copy(zz).wait_recv()
        if t == 3:
            self.column[zz] = self.column[zz] + self.from_side[zz].astype(F32)
        else:
            self.chain[zz] = (self.column[zz] + self.from_side[zz].astype(F32)).astype(self.chain.dtype)
            self.along(zz, p.z).start()

    def finish(self, result):
        z = self.p.z
        total = self.column[z]
        for d in range(1, 4):
            other = lax.rem(z + d, 4)
            self.along(other, other).wait_recv()
        for d in range(1, 4):
            total = total + self.incoming[lax.rem(z + d, 4)].astype(F32)
        result[...] = total
        for zz in range(4):
            self.side_copy(zz).wait_send()
        for d in range(1, 4):
            self.along(lax.rem(z + d, 4), z).wait_send()


def grid_scratch():
    block = (4, OWN, D)
    return [pltpu.VMEM(block, F32)] + [pltpu.VMEM(block, BF)] * 4


def reduce_scratch():
    return [pltpu.VMEM((512, D), BF), pltpu.VMEM((2, OWN, D), BF), pltpu.VMEM((2, OWN, D), BF)]


GELU_A = math.sqrt(2.0 / math.pi)


def gelu(v):
    return 0.5 * v * (1.0 + jnp.tanh(GELU_A * (v + 0.044715 * (v * v * v))))


def gelu_slope(v):
    t = jnp.tanh(GELU_A * (v + 0.044715 * (v * v * v)))
    return 0.5 * (1.0 + t) + 0.5 * v * (1.0 - t * t) * (GELU_A * (1.0 + 3.0 * 0.044715 * v * v))


def norm_parts(v):
    mean = jnp.mean(v, -1, keepdims=True)
    centered = v - mean
    variance = jnp.mean(centered * centered, -1, keepdims=True)
    scale = lax.rsqrt(variance + norm_epsilon)
    return centered * scale, scale


def norm_back(v, gain, grad):
    unit, scale = norm_parts(v)
    gain_row = jnp.sum(grad * unit, 0, keepdims=True)
    g = grad * gain
    inner = g - jnp.mean(g, -1, keepdims=True) - unit * jnp.mean(g * unit, -1, keepdims=True)
    return scale * inner, gain_row


def frame_columns(lengths, first, rows, extra=()):
    frame = first + lax.broadcasted_iota(jnp.int32, (rows, 1), 0)
    end = jnp.int32(0)
    owner = jnp.full((rows, 1), -1, jnp.int32)
    starts = jnp.zeros((rows, 1), jnp.int32)
    ends = jnp.zeros((rows, 1), jnp.int32)
    picked = [jnp.zeros((rows, 1), e.dtype) for e in extra]
    for u in range(lengths.shape[0]):
        start = end
        end = start + lengths[u]
        inside = (frame >= start) & (frame < end)
        owner = jnp.where(inside, u, owner)
        starts = jnp.where(inside, start, starts)
        ends = jnp.where(inside, end, ends)
        picked = [jnp.where(inside, e[u], c) for e, c in zip(extra, picked)]
    return frame, owner, starts, ends, picked


def tap_masks(frame, starts, ends, mask_ref):
    low = jnp.broadcast_to(starts - frame + 15, (OWN, 128))
    high = jnp.broadcast_to(ends - frame + 15, (OWN, 128))
    for k in range(31):
        mask_ref[k] = ((low <= k) & (high > k)).astype(F32)


def vmem_call(kernel, outs, specs, scratch, cid, name, flops=1e9):
    return pl.pallas_call(
        kernel,
        out_shape=tuple(jax.ShapeDtypeStruct(*o) for o in outs),
        in_specs=specs,
        out_specs=tuple([VM] * len(outs)),
        scratch_shapes=scratch,
        compiler_params=pltpu.CompilerParams(
            collective_id=cid, has_side_effects=True, vmem_limit_bytes=61 << 20
        ),
        cost_estimate=pl.CostEstimate(flops=int(flops), bytes_accessed=1 << 24, transcendentals=0),
        name=name,
    )


def forward_kernel(
    lengths, span_start, span_end, flow_times, pack_ref, table_ref, win_ref, phone_ref, kern_ref,
    gain_ref, watt_ref, ff_shard, wpred_ref,
    h1_ref, conv_ref, rim_ref, a_ref, q_ref, k_ref, v_ref, wqkv_ref, feats_ref, choose_ref, lse_ref,
    dh2_ref, rows_ref, outg_ref, do_ref, delta_ref, qall_ref, doall_ref, stat_ref, gup_ref, gdown_ref, gout_ref,
    wout_ref, ext, rimf, masks, edge_send, edge_recv, ag_send, ag_recv, w_send, w_recv, o_send, o_recv,
    k_send, k_recv, v_send, v_recv,
    kown, qown, o32_ref, o_ref, tops, totals, sums,
    u_ref, gated, b_ref, dy_ref, du_ref, dlow, h_ref, dh3_ref,
    part, core1, pair1, core2, pair2, core3, pair3,
    s1, r1, s2, r2, s3, r3, as1, ar1, as2, ar2, as3, ar3,
    q_send, q_recv, d_send, d_recv, t_send, t_recv, wup_ref, wdown_ref, wu_send, wu_recv, wd_send, wd_recv,
    both, *w_refs,
):
    p = Place()
    group = pack_ref.shape[0]
    prior, following = (p.s - 1, p.m), (p.s + 1, p.m)
    shard = watt_ref.shape[1]
    own_w = pl.ds(pl.multiple_of(p.s * shard, shard), shard)
    for j in range(3):
        wqkv_ref[j, own_w, :] = watt_ref[j].astype(BF)
    wout_ref[own_w, :] = watt_ref[3].astype(BF)
    wup_ref[own_w, :] = ff_shard[0].astype(BF)
    wdown_ref[own_w, :] = ff_shard[1].astype(BF)
    for ref in (qall_ref, doall_ref, stat_ref):
        ref[...] = jnp.zeros(ref.shape, ref.dtype)
    k_ref[...] = jnp.zeros(k_ref.shape, BF)
    v_ref[...] = jnp.zeros(v_ref.shape, BF)
    ext[:EDGE, :] = jnp.zeros((EDGE, 256), F32)
    ext[EDGE + group :, :] = jnp.zeros((EDGE, 256), F32)
    ext[EDGE : EDGE + group, :] = pack_ref[...]
    greet(grid_peers(p) + mp_peers(p) + [(prior, p.s > 0), (following, p.s < 7)])
    edge_up = put(ext.at[pl.ds(group, EDGE)], ext.at[pl.ds(0, EDGE)], edge_send.at[0], edge_recv.at[0], following)
    edge_down = put(ext.at[pl.ds(EDGE, EDGE)], ext.at[pl.ds(EDGE + group, EDGE)], edge_send.at[1], edge_recv.at[1], prior)

    @pl.when(p.s < 7)
    def _():
        edge_up.start()

    @pl.when(p.s > 0)
    def _():
        edge_down.start()

    def shard_rows(slot):
        return pl.ds(pl.multiple_of(slot * shard, shard), shard)

    gather_w = Gather(p, lambda slot: wqkv_ref.at[:, shard_rows(slot), :], w_send, w_recv)
    gather_o = Gather(p, lambda slot: wout_ref.at[shard_rows(slot), :], o_send, o_recv)
    def rows_of(slot):
        return pl.ds(pl.multiple_of(slot * group, group), group)

    gather_q = NearGather(p, *near_rows(qall_ref, group), q_send, q_recv)
    gather_d = NearGather(p, *near_rows(doall_ref, group), d_send, d_recv)
    gather_t = NearGather(
        p, lambda slot: stat_ref.at[slot], lambda slot, last: stat_ref.at[slot], t_send, t_recv
    )
    gather_up = Gather(p, lambda slot: wup_ref.at[shard_rows(slot), :], wu_send, wu_recv)
    gather_down = Gather(p, lambda slot: wdown_ref.at[shard_rows(slot), :], wd_send, wd_recv)
    gather_w.start()
    gather_o.start()

    @pl.when(p.s > 0)
    def _():
        edge_up.wait_recv()

    @pl.when(p.s < 7)
    def _():
        edge_down.wait_recv()

    first = p.s * group + p.m * OWN
    wide = OWN + 2 * EDGE

    def features(begin, both):
        rows = both.shape[0]
        frame, owner, starts, _, picked = frame_columns(
            lengths, begin, rows, (span_start, span_end, flow_times)
        )
        position = frame - starts
        masked = ((position >= picked[0]) & (position < picked[1]) & (owner >= 0)).astype(F32)
        moment = picked[2]
        mel, noise = both[:, :128], both[:, 128:]
        lane = lax.broadcasted_iota(jnp.int32, (rows, 128), 1)
        context = (mel * (1.0 - masked)).astype(BF)
        noisy = (1.0 - (1.0 - flow_sigma) * moment) * noise + moment * mel
        noisy = jnp.where(lane < MEL, noisy, 0.0).astype(BF)
        phone = noise[:, MEL : MEL + 1]
        choose = jnp.where(phone == lane.astype(F32), 1.0, 0.0).astype(BF)
        return owner, context, noisy, choose

    owner, context, noisy, choose = features(
        first - EDGE, ext[pl.ds(pl.multiple_of(p.m * OWN, OWN), wide), :]
    )
    h0 = nn(context[:, :MEL], win_ref[:MEL, :].astype(BF))
    h0 = h0 + nn(noisy[:, :MEL], win_ref[MEL:, :].astype(BF)) + nn(choose, phone_ref[...].astype(BF))
    time = jnp.zeros((wide, D), F32)
    for u in range(table_ref.shape[0]):
        time = jnp.where(owner == u, table_ref[u : u + 1, :], time)
    h0 = h0 + time
    low = h0.astype(BF)
    rim_ref[...] = low
    rimf[...] = low.astype(F32)
    h1_ref[...] = h0[EDGE : EDGE + OWN]
    gather_w.step(0)
    gather_o.step(0)
    frame, _, starts, ends, _ = frame_columns(lengths, first, OWN)
    tap_masks(frame, starts, ends, masks)

    @pl.loop(0, D // 128)
    def _(t):
        lanes = pl.ds(pl.multiple_of(t * 128, 128), 128)
        total = jnp.zeros((OWN, 128), F32)
        for k in range(31):
            total = total + kern_ref[k : k + 1, lanes] * (rimf[1 + k : 1 + k + OWN, lanes] * masks[k])
        conv_ref[:, lanes] = total

    own = pl.ds(pl.multiple_of(p.m * OWN, OWN), OWN)
    halves = [(h, slice(h * HALF, (h + 1) * HALF)) for h in (0, 1)]
    gather_a = BlockGather(p, a_ref, ag_send, ag_recv)

    def own_half(h):
        return pl.ds(pl.multiple_of(p.m * OWN + h * HALF, HALF), HALF)

    for h, half in halves:
        h1 = h1_ref[half, :] + gelu(conv_ref[half, :])
        h1_ref[half, :] = h1
        unit, _ = norm_parts(h1)
        a_ref[own_half(h), :] = (unit * gain_ref[0:1, :]).astype(BF)
        gather_a.start(h)
    gather_w.step(1)
    gather_o.step(1)
    gather_a.finish()
    gather_w.step(2)
    gather_o.step(2)
    gather_w.finish()
    rows = pl.ds(pl.multiple_of(p.s * group, group), group)

    gather_k = NearGather(p, *near_rows(k_ref, group), k_send, k_recv)
    gather_v = NearGather(p, *near_rows(v_ref, group), v_send, v_recv)
    k_ref[rows, :] = nn(a_ref[...], wqkv_ref[1]).astype(BF)
    gather_k.start()
    v_ref[rows, :] = nn(a_ref[...], wqkv_ref[2]).astype(BF)
    gather_v.start()
    q_ref[...] = nn(a_ref[...], wqkv_ref[0]).astype(BF)
    _, context, noisy, choose = features(p.s * group, pack_ref[...])
    feats_ref[:, :128] = context
    feats_ref[:, 128:] = noisy
    choose_ref[...] = choose
    gather_o.finish()

    width = q_ref.shape[1]
    pairs = [slice(128 * j, 128 * (j + 1)) for j in range(width // 128)]
    heads = width // HD
    slopes = [slope_of(p.m * heads + h) for h in range(heads)]
    owner_row(lengths, 0, kown)
    _, owner, _, _, _ = frame_columns(lengths, p.s * group, group)
    qown[...] = owner
    tops[...] = jnp.full(tops.shape, -1e30, F32)
    totals[...] = jnp.zeros(totals.shape, F32)
    sums[...] = jnp.zeros(sums.shape, F32)

    def tile(slot):
        keys = rows_of(slot)

        @pl.loop(0, group // OWN)
        def _(i):
            mine = pl.ds(pl.multiple_of(i * OWN, OWN), OWN)
            gap = (p.s - slot) * group + i * OWN + lax.broadcasted_iota(jnp.int32, (OWN, group), 0)
            dist = jnp.abs(gap - lax.broadcasted_iota(jnp.int32, (OWN, group), 1)).astype(F32)
            dist = jnp.where(qown[mine, :] == kown[:, keys], dist, 1e30)
            for j, l in enumerate(pairs):
                n = len(pairs) * i + j
                top = tops[n]
                scores = nt(stack_pair(q_ref[mine, l]) * BF(0.125), k_ref[keys, l])
                scores = jnp.concatenate(
                    [scores[:OWN] - slopes[2 * j] * dist, scores[OWN:] - slopes[2 * j + 1] * dist], 0
                )
                new = jnp.maximum(top, jnp.max(scores, -1, keepdims=True))
                fade = jnp.exp(top - new)
                e = jnp.exp(scores - new[:, :1])
                tops[n] = new
                totals[n] = totals[n] * fade + jnp.sum(e, -1, keepdims=True)
                sums[n] = sums[n] * fade + nn(e.astype(BF), v_ref[keys, l])

    def tile_if(slot, exists, wait):
        @pl.when(exists)
        def _():
            wait(gather_k)
            wait(gather_v)
            tile(slot)

    turn = gather_k.turn
    tile(p.s)
    for g in (gather_k, gather_v):
        g.step(0)
    tile(p.s + turn)
    for g in (gather_k, gather_v):
        g.step(1)
    tile_if(p.s + 2 * turn, gather_k.has_ahead, lambda g: None)
    for g in (gather_k, gather_v):
        g.step(2)
    gather_up.start()
    tile_if(p.s - 2 * turn, gather_k.has_behind, lambda g: None)
    tile_if(p.s - turn, gather_k.has_behind, lambda g: None)
    gather_up.step(0)
    tile_if(p.s - 3, p.s >= 3, lambda g: g.copy(p.s - 3, 0, p.side).wait_recv())
    tile_if(p.s + 3, p.s <= 4, lambda g: g.copy(p.s + 3, 0, p.side).wait_recv())
    gather_up.step(1)
    tile_if(p.s - 4, p.s >= 4, lambda g: g.part(p.s - 4, 1, 0, p.side).wait_recv())
    tile_if(p.s + 4, p.s <= 3, lambda g: g.part(p.s + 4, 0, 0, p.side).wait_recv())

    @pl.loop(0, group // OWN)
    def _(i):
        mine = pl.ds(pl.multiple_of(i * OWN, OWN), OWN)
        lane = lax.broadcasted_iota(jnp.int32, (OWN, 128), 1)
        lse = jnp.zeros((OWN, 128), F32)
        for j, l in enumerate(pairs):
            n = len(pairs) * i + j
            o = unstack_pair(sums[n] / totals[n])
            o32_ref[mine, l] = o
            o_ref[mine, l] = o.astype(BF)
            g = tops[n] + jnp.log(totals[n])
            lse = jnp.where(lane == 2 * j, g[:OWN], lse)
            lse = jnp.where(lane == 2 * j + 1, g[OWN:], lse)
        lse_ref[mine, :] = lse

    red = BlockReduce(p, part, core1, pair1, s1, r1)
    for rows, send in ((red.far_rows(), red.send_far), (red.near_rows(), red.send_near)):
        part[rows, :] = nt(o_ref[rows, :], wout_ref[...]).astype(BF)
        send()
    gather_up.step(2)
    gather_down.start()
    gather_b = BlockGather(p, b_ref, as1, ar1)
    for h, half in halves:
        h2 = h1_ref[half, :] + red.finish(h)
        h_ref[half, :] = h2
        unit, _ = norm_parts(h2)
        b_ref[own_half(h), :] = (unit * gain_ref[1:2, :]).astype(BF)
        gather_b.start(h)
    red.sent()
    gather_up.finish()
    gather_down.step(0)
    gather_b.finish()

    ff = ff_shard.shape[2]
    tile = 256

    @pl.loop(0, ff // tile)
    def _(t):
        lanes = pl.ds(pl.multiple_of(t * tile, tile), tile)
        up = nn(b_ref[...], wup_ref[:, lanes])
        u_ref[:, lanes] = up
        gated[:, lanes] = gelu(up).astype(BF)

    gather_down.step(1)
    gather_down.step(2)
    gather_down.finish()
    qall_ref[rows_of(p.s), :] = q_ref[...]
    gather_q.start()
    red = BlockReduce(p, part, core2, pair2, s2, r2)
    for rows, send in ((red.far_rows(), red.send_far), (red.near_rows(), red.send_near)):

        @pl.loop(0, D // tile)
        def _(t):
            lanes = pl.ds(pl.multiple_of(t * tile, tile), tile)
            part[rows, lanes] = nt(gated[rows, :], wdown_ref[lanes, :]).astype(BF)

        send()
    gather_q.step(0)
    _, owner, starts, _, picked = frame_columns(lengths, first, OWN, (span_start, span_end))
    position = first + lax.broadcasted_iota(jnp.int32, (OWN, 1), 0) - starts
    masked = ((position >= picked[0]) & (position < picked[1])).astype(F32)
    covered, frames = jnp.int32(0), jnp.int32(0)
    for n in range(lengths.shape[0]):
        span = jnp.minimum(span_end[n], lengths[n]) - jnp.minimum(span_start[n], lengths[n])
        covered = covered + jnp.maximum(span, 0)
        frames = frames + lengths[n]
    count = jnp.full((OWN, 1), jnp.maximum(covered, 1), jnp.int32).astype(F32)
    rest = jnp.full((OWN, 1), jnp.maximum(frames - covered, 1), jnp.int32).astype(F32)
    weight = masked / count + 0.1 * (1.0 - masked) / rest
    raw = pack_ref[own, :]
    target = (raw[:, :128] - (1.0 - flow_sigma) * raw[:, 128:])[:, :MEL]
    wpred = wpred_ref[...].astype(BF)

    gather_y = BlockGather(p, dy_ref, as2, ar2)
    loss = jnp.zeros((1, 1), F32)
    gain3 = jnp.zeros((1, D), F32)
    for h, half in halves:
        h3 = h_ref[half, :] + red.finish(h)
        unit, _ = norm_parts(h3)
        low = (unit * gain_ref[2:3, :]).astype(BF)
        errors = nt(low, wpred) - target[half]
        loss = loss + jnp.sum(weight[half] * jnp.mean(errors * errors, 1, keepdims=True), 0, keepdims=True)
        dpred = (weight[half] * (2.0 / MEL) * errors).astype(BF)
        dh3, gain_row = norm_back(h3, gain_ref[2:3, :], nn(dpred, wpred))
        dh3_ref[half, :] = dh3
        dy_ref[own_half(h), :] = dh3.astype(BF)
        gather_y.start(h)
        gain3 = gain3 + gain_row
        outg = tn(dpred, low)
        outg_ref[...] = outg if h == 0 else outg_ref[...] + outg
    red.sent()
    gather_q.step(1)
    gather_q.step(2)
    gather_y.finish()

    @pl.loop(0, ff // tile)
    def _(t):
        lanes = pl.ds(pl.multiple_of(t * tile, tile), tile)
        down = nn(dy_ref[...], wdown_ref[:, lanes])
        du_ref[:, lanes] = (down * gelu_slope(u_ref[:, lanes])).astype(BF)

    red = BlockReduce(p, part, core3, pair3, s3, r3)
    for rows, send in ((red.far_rows(), red.send_far), (red.near_rows(), red.send_near)):

        @pl.loop(0, D // tile)
        def _(t):
            lanes = pl.ds(pl.multiple_of(t * tile, tile), tile)
            part[rows, lanes] = nt(du_ref[rows, :], wup_ref[lanes, :]).astype(BF)

        send()

    down_sum = GridReduce(p, *w_refs)

    @pl.loop(0, 4)
    def _(t):
        lanes = pl.ds(pl.multiple_of(down_sum.level(t) * tile, tile), tile)
        both[...] = tn(dy_ref[:, lanes], gated[...])
        down_sum.start(t, both)

    gather_q.finish()
    gather_h = BlockGather(p, dlow, as3, ar3)
    gain2 = jnp.zeros((1, D), F32)
    for h, half in halves:
        norm_grad, gain_row = norm_back(h_ref[half, :], gain_ref[1:2, :], red.finish(h))
        dh2 = dh3_ref[half, :] + norm_grad
        dh2_ref[half, :] = dh2
        dlow[own_half(h), :] = dh2.astype(BF)
        gather_h.start(h)
        gain2 = gain2 + gain_row
    red.sent()
    rows_ref[...] = jnp.concatenate(
        [gain3, gain2, jnp.broadcast_to(loss, (1, D)), jnp.zeros((5, D), F32)], 0
    )

    @pl.loop(0, D // tile)
    def _(t):
        lanes = pl.ds(pl.multiple_of(t * tile, tile), tile)
        gup_ref[lanes, :] = tn(b_ref[:, lanes], du_ref[...])

    down_sum.step(0)
    gather_h.finish()
    grad = nn(dlow[...], wout_ref[...]).astype(BF)
    do_ref[...] = grad
    doall_ref[rows_of(p.s), :] = grad
    gather_d.start()
    weighted = grad.astype(F32) * o32_ref[...]
    width = o_ref.shape[1]
    head = lax.broadcasted_iota(jnp.int32, (width, 128), 0) // HD
    pick = (head == lax.broadcasted_iota(jnp.int32, (width, 128), 1)).astype(F32)
    delta_ref[...] = jnp.dot(weighted, pick, preferred_element_type=F32, precision=lax.Precision.HIGHEST)
    eye = (
        lax.broadcasted_iota(jnp.int32, (8, 128), 0) == lax.broadcasted_iota(jnp.int32, (8, 128), 1)
    ).astype(F32)
    for i, ref in enumerate((lse_ref, delta_ref)):
        stat_ref[p.s, 8 * i : 8 * i + 8, :] = lax.dot_general(
            eye, ref[...], (((1,), (1,)), ((), ())), preferred_element_type=F32, precision=lax.Precision.HIGHEST
        )
    gather_t.start()
    gout_ref[...] = tn(dlow[...], o_ref[...])
    for hop in range(3):
        down_sum.step(hop + 1)
        gather_d.step(hop)
        gather_t.step(hop)
    down_sum.finish(gdown_ref)
    gather_d.finish()
    gather_t.finish()
    for g in (gather_k, gather_v):
        for copy, made in g.sends():
            if made is None:
                copy().wait_send()
            else:

                @pl.when(made)
                def _(copy=copy):
                    copy().wait_send()

    @pl.when(p.s < 7)
    def _():
        edge_up.wait_send()

    @pl.when(p.s > 0)
    def _():
        edge_down.wait_send()


def forward(lengths, span_start, span_end, flow_times, pack, table, win, phone, kern, gains, watt, wff, wpred):
    group = pack.shape[0]
    shard, width = watt.shape[1:]
    ff = wff.shape[2]
    frames = 8 * group
    outs = [
        ((OWN, D), F32), ((OWN, D), F32), ((OWN + 2 * EDGE, D), BF), ((group, D), BF),
        ((group, width), BF), ((frames, width), BF), ((frames, width), BF),
        ((3, 8 * shard, width), BF), ((group, 256), BF), ((group, 128), BF), ((group, 128), F32),
        ((OWN, D), F32), ((8, D), F32), ((MEL, D), F32), ((group, width), BF), ((group, 128), F32),
        ((frames, width), BF), ((frames, width), BF), ((8, 16, group), F32),
        ((D, ff), F32), ((OWN, ff), F32), ((D, width), F32),
    ]
    dma, vmem = pltpu.SemaphoreType.DMA, pltpu.VMEM
    states = vmem((group // OWN * (width // 128), 2 * OWN, 128), F32)
    scratch = [
        vmem((8 * shard, width), BF), vmem((group + 2 * EDGE, 256), F32), vmem((OWN + 2 * EDGE, D), F32),
        vmem((31, OWN, 128), F32), dma((2,)), dma((2,)),
    ] + BlockGather.SEMS + Gather.SEMS * 2 + NearGather.SEMS * 2
    scratch = scratch + [
        vmem((1, frames), jnp.int32), vmem((group, 1), jnp.int32), vmem((group, width), F32),
        vmem((group, width), BF), states, states, states,
        vmem((group, ff), F32), vmem((group, ff), BF), vmem((group, D), BF), vmem((group, D), BF),
        vmem((group, ff), BF), vmem((group, D), BF), vmem((OWN, D), F32), vmem((OWN, D), F32),
    ]
    landing = reduce_scratch()[1:]
    scratch = scratch + reduce_scratch() + landing * 2 + BlockReduce.SEMS * 3 + BlockGather.SEMS * 3
    scratch = scratch + NearGather.SEMS * 3 + [vmem((D, ff), BF), vmem((D, ff), BF)] + Gather.SEMS * 2
    scratch = scratch + [vmem((2 * OWN, D), F32)] + grid_scratch() + GridReduce.SEMS
    return vmem_call(forward_kernel, outs, [SM] * 4 + [VM] * 9, scratch, 0, "forward", 4e10)(
        lengths, span_start, span_end, flow_times, pack, table, win, phone, kern, gains, watt, wff, wpred
    )


FEW = 448


def back_kernel(
    lengths, proj_ref, wqkv_ref, a_ref, dh2_ref, h1_ref, conv_ref, rim_ref, gain_ref, kern_ref,
    feats_ref, choose_ref, rows_ref, outg_ref, gup_ref, gdown_ref, gout_ref,
    gatt_ref, gff_ref, small_ref, scalar_ref,
    dcb, dcf, rimf, masks, dh1_ref, part, from_core, pair, s1, r1, edge_send, edge_recv,
    both, *rest,
):
    p = Place()
    att_sum, rest = GridReduce(p, *rest[:7]), rest[7:]
    up_sum, rest = GridReduce(p, *rest[:7]), rest[7:]
    few_sum, rest = GridReduce(p, *rest[:7]), rest[7:]
    (
        att, dh0, dh0_lanes, few, few_lanes, piece, few_own, d_send, d_recv, few_send, few_recv,
        g_send, g_recv, y_send, y_recv, c_send, c_recv,
        seen, seen_send, seen_recv, last, last_send, last_recv,
    ) = rest
    group = a_ref.shape[0]
    place = p.s * 4 + p.m
    prior = ((place + 31) // 4 - 8 * ((place + 31) // 32), lax.rem(place + 3, 4))
    following = ((place + 1) // 4, lax.rem(place + 1, 4))
    dcb[:EDGE, :] = jnp.zeros((EDGE, D), BF)
    dcb[EDGE + OWN :, :] = jnp.zeros((EDGE, D), BF)
    peers = [((lax.rem(p.s + d, 8), p.m), None) for d in range(1, 8)]
    others = [((p.s, lax.rem(p.m + d, 4)), None) for d in range(1, 4)]
    greet(peers + others + [(prior, place > 0), (following, place < 31)])
    red = BlockReduce(p, part, from_core, pair, s1, r1)
    for rows, send in ((red.far_rows(), red.send_far), (red.near_rows(), red.send_near)):
        total = nt(proj_ref[0, rows, :], wqkv_ref[0])
        total = total + nt(proj_ref[1, rows, :], wqkv_ref[1])
        part[rows, :] = (total + nt(proj_ref[2, rows, :], wqkv_ref[2])).astype(BF)
        send()

    def attention_block(t):
        rows = pl.ds(pl.multiple_of(att_sum.level(t) * 2 * OWN, 2 * OWN), 2 * OWN)
        for j in range(3):
            both[:, 256 * j : 256 * (j + 1)] = tn(a_ref[:, rows], proj_ref[j])
        both[:, 768:] = gout_ref[rows, :]
        att_sum.start(t, both)

    def up_block(t):
        rows = pl.ds(pl.multiple_of(up_sum.level(t) * 2 * OWN, 2 * OWN), 2 * OWN)
        up_sum.start(t, gup_ref.at[rows])

    pl.loop(0, 2)(up_block)
    rimf[...] = rim_ref[...].astype(F32)
    frame, _, starts, ends, _ = frame_columns(lengths, p.s * group + p.m * OWN, OWN)
    tap_masks(frame, starts, ends, masks)
    gain1 = jnp.zeros((1, D), F32)
    for h in (0, 1):
        half = slice(h * HALF, (h + 1) * HALF)
        norm_grad, gain_row = norm_back(h1_ref[half, :], gain_ref[0:1, :], red.finish(h))
        dh1 = dh2_ref[half, :] + norm_grad
        dh1_ref[half, :] = dh1
        dcb[EDGE + h * HALF : EDGE + (h + 1) * HALF, :] = (dh1 * gelu_slope(conv_ref[half, :])).astype(BF)
        gain1 = gain1 + gain_row
    red.sent()
    edge_up = put(dcb.at[pl.ds(OWN, EDGE)], dcb.at[pl.ds(0, EDGE)], edge_send.at[0], edge_recv.at[0], following)
    edge_down = put(dcb.at[pl.ds(EDGE, EDGE)], dcb.at[pl.ds(EDGE + OWN, EDGE)], edge_send.at[1], edge_recv.at[1], prior)

    @pl.when(place < 31)
    def _():
        edge_up.start()

    @pl.when(place > 0)
    def _():
        edge_down.start()

    pl.loop(2, 4)(up_block)
    dcf[EDGE : EDGE + OWN, :] = dcb[EDGE : EDGE + OWN, :].astype(F32)

    @pl.loop(0, D // 128)
    def _(t):
        lanes = pl.ds(pl.multiple_of(t * 128, 128), 128)
        mine = dcf[EDGE : EDGE + OWN, lanes]
        for k in range(31):
            near = rimf[1 + k : 1 + k + OWN, lanes] * masks[k]
            few[k : k + 1, lanes] = jnp.sum(mine * near, 0, keepdims=True)

    few[31:32, :] = gain1
    few[32:112, :] = outg_ref[...]
    few[112:114, :] = rows_ref[:2, :]
    few[114:, :] = jnp.zeros((14, D), F32)

    def quarter(m):
        return pl.ds(pl.multiple_of(m * 256, 256), 256)

    def mp_slot(d, incoming):
        there = lax.rem(p.m + d, 4)
        return there, (there if incoming else p.m)

    def few_copy(d, incoming=False):
        there, slot = mp_slot(d, incoming)
        return put(few.at[:, quarter(there)], few_lanes.at[slot], few_send.at[d - 1], few_recv.at[slot], (p.s, there))

    def dh0_copy(d, incoming=False):
        there, slot = mp_slot(d, incoming)
        rows = pl.ds(pl.multiple_of(slot * OWN, OWN), OWN)
        return put(dh0.at[:, quarter(there)], dh0_lanes.at[rows, :], d_send.at[d - 1], d_recv.at[slot], (p.s, there))

    for d in range(1, 4):
        few_copy(d).start()
    few_lanes[p.m] = few[:, quarter(p.m)]
    up_sum.step(0)

    @pl.when(place > 0)
    def _():
        edge_up.wait_recv()

    @pl.when(place < 31)
    def _():
        edge_down.wait_recv()

    dcf[:EDGE, :] = dcb[:EDGE, :].astype(F32)
    dcf[EDGE + OWN :, :] = dcb[EDGE + OWN :, :].astype(F32)

    @pl.loop(0, D // 128)
    def _(t):
        lanes = pl.ds(pl.multiple_of(t * 128, 128), 128)
        total = jnp.zeros((OWN, 128), F32)
        for k in range(31):
            total = total + kern_ref[30 - k : 31 - k, lanes] * (dcf[1 + k : 1 + k + OWN, lanes] * masks[k])
        dh0[:, lanes] = (dh1_ref[:, lanes] + total).astype(BF)

    for d in range(1, 4):
        dh0_copy(d).start()
    dh0_lanes[pl.ds(pl.multiple_of(p.m * OWN, OWN), OWN), :] = dh0[:, quarter(p.m)]
    pl.loop(0, 2)(attention_block)
    up_sum.step(1)
    for d in range(1, 4):
        few_copy(d, True).wait_recv()
    piece[288:416, :] = (few_lanes[0] + few_lanes[1]) + (few_lanes[2] + few_lanes[3])
    piece[416:, :] = jnp.zeros((FEW - 416, 256), F32)
    for d in range(1, 4):
        dh0_copy(d, True).wait_recv()
    grad = tn(feats_ref[...], dh0_lanes[...])
    piece[:MEL, :] = grad[:MEL]
    piece[MEL : 2 * MEL, :] = grad[128 : 128 + MEL]
    piece[160:288, :] = tn(choose_ref[...], dh0_lanes[...])

    eighth = FEW // 8

    def piece_rows(slot):
        return pl.ds(pl.multiple_of(slot * eighth, 8), eighth)

    def few_block(t):
        rows = pl.ds(pl.multiple_of(few_sum.level(t) * 2 * eighth, 8), 2 * eighth)
        few_sum.start(t, piece.at[rows])

    def seq_slot(d, incoming):
        there = lax.rem(p.s + d, 8)
        return there, (there if incoming else p.s)

    pl.loop(0, 4)(few_block)
    up_sum.step(2)
    for t in range(4):
        few_sum.step(t)
    pl.loop(2, 4)(attention_block)
    up_sum.step(3)
    att_sum.step(0)
    few_sum.finish(few_own)
    few_squares = jnp.sum(few_own[...] * few_own[...])
    small_ref[piece_rows(p.s), quarter(p.m)] = few_own[...]
    share = ColumnGather(p, lambda slot: small_ref.at[piece_rows(slot), quarter(p.m)], g_send, g_recv)

    def cross(slot, m):
        view = small_ref.at[piece_rows(slot), quarter(m)]
        return put(view, view, y_send.at[slot], y_recv.at[slot], p.across)

    share.start()
    cross(p.s, p.m).start()
    att_sum.step(1)
    for hop in range(3):
        share.step(hop)
        cross(2 * share.level(hop) + p.x, p.m).start()
    att_sum.step(2)
    share.finish()
    for zz in range(4):
        cross(2 * zz + 1 - p.x, p.m).start()
    att_sum.step(3)
    up_sum.finish(gff_ref.at[0])
    gff_ref[1] = gdown_ref[...]
    squares = few_squares + jnp.sum(gff_ref[0] * gff_ref[0]) + jnp.sum(gff_ref[1] * gff_ref[1])
    far = lax.rem(p.m + 2, 4)
    for n in range(8):
        cross(n, far).wait_recv()

    def core_copy(i, m):
        view = small_ref.at[:, quarter(m)]
        return put(view, view, c_send.at[i], c_recv.at[i], p.core)

    core_copy(0, p.m).start()
    core_copy(1, far).start()
    att_sum.finish(att)
    squares = squares + jnp.sum(att[...] * att[...])
    row = lax.broadcasted_iota(jnp.int32, (8, 128), 0)
    seen[p.s] = jnp.where(row == 0, squares, rows_ref[2:3, :128])

    def scalar_copy(d, incoming=False):
        there, slot = seq_slot(d, incoming)
        return put(seen.at[p.s], seen.at[slot], seen_send.at[d - 1], seen_recv.at[slot], (there, p.m))

    for d in range(1, 8):
        scalar_copy(d).start()
    for j in range(4):
        gatt_ref[j] = att[:, 256 * j : 256 * (j + 1)]
    for d in range(1, 8):
        scalar_copy(d, True).wait_recv()
    total = seen[0]
    for n in range(1, 8):
        total = total + seen[n]
    last[p.m] = total

    def last_copy(d, incoming=False):
        there, slot = mp_slot(d, incoming)
        return put(last.at[p.m], last.at[slot], last_send.at[d - 1], last_recv.at[slot], (p.s, there))

    for d in range(1, 4):
        last_copy(d).start()
    core_copy(0, p.m + 1 - 2 * p.c).wait_recv()
    core_copy(1, 3 - p.m).wait_recv()
    for d in range(1, 4):
        last_copy(d, True).wait_recv()
    scalar_ref[...] = (last[0] + last[1]) + (last[2] + last[3])
    for d in range(1, 8):
        scalar_copy(d).wait_send()
    for n in range(8):
        cross(n, p.m).wait_send()
    core_copy(0, p.m).wait_send()
    core_copy(1, far).wait_send()
    for d in range(1, 4):
        few_copy(d).wait_send()
        last_copy(d).wait_send()
        dh0_copy(d).wait_send()

    @pl.when(place < 31)
    def _():
        edge_up.wait_send()

    @pl.when(place > 0)
    def _():
        edge_down.wait_send()


def back(lengths, proj, wqkv, a, dh2, h1, conv, rim, gains, kern, feats, choose, rows, outg, gup, gdown, gout):
    outs = [((4, OWN, 256), F32), ((2, OWN, D), F32), ((FEW, D), F32), ((8, 128), F32)]
    wide, group = OWN + 2 * EDGE, a.shape[0]
    dma, vmem = pltpu.SemaphoreType.DMA, pltpu.VMEM
    scratch = [
        vmem((wide, D), BF), vmem((wide, D), F32), vmem((wide, D), F32),
        vmem((31, OWN, 128), F32), vmem((OWN, D), F32),
    ] + reduce_scratch() + BlockReduce.SEMS + [dma((2,)), dma((2,)), vmem((2 * OWN, D), F32)]
    scratch = scratch + (grid_scratch() + GridReduce.SEMS) * 2
    eighth = FEW // 8
    scratch = scratch + [vmem((4, eighth, 256), F32)] * 5 + GridReduce.SEMS
    scratch = scratch + [
        vmem((OWN, D), F32), vmem((OWN, D), BF), vmem((group, 256), BF), vmem((OWN, D), F32),
        vmem((4, OWN, 256), F32), vmem((FEW, 256), F32), vmem((eighth, 256), F32),
        dma((3,)), dma((4,)), dma((3,)), dma((4,)),
    ] + ColumnGather.SEMS + [
        dma((8,)), dma((8,)), dma((2,)), dma((2,)),
        vmem((8, 8, 128), F32), dma((7,)), dma((8,)), vmem((4, 8, 128), F32), dma((3,)), dma((4,)),
    ]
    return vmem_call(back_kernel, outs, [SM] + [VM] * 16, scratch, 2, "back", 2e10)(
        lengths, proj, wqkv, a, dh2, h1, conv, rim, gains, kern, feats, choose, rows, outg, gup, gdown, gout
    )


KT = 512
KB = 256


def lane_half(rows):
    return lax.broadcasted_iota(jnp.int32, (rows, 128), 1) < HD


def stack_pair(x):
    low, zero = lane_half(x.shape[0]), jnp.zeros_like(x)
    return jnp.concatenate([jnp.where(low, x, zero), jnp.where(low, zero, x)], 0)


def unstack_pair(x):
    rows = x.shape[0] // 2
    return jnp.where(lane_half(rows), x[:rows], x[rows:])


def slope_of(index):
    value = jnp.float32(2.0 ** (-8.0 * HEADS / HEADS))
    for head in range(HEADS - 1):
        value = jnp.where(index == head, jnp.float32(2.0 ** (-8.0 * (head + 1) / HEADS)), value)
    return value


def tile_range(lengths, first, base, size):
    end = jnp.int32(0)
    low = jnp.int32(0)
    high = jnp.int32(0)
    for u in range(lengths.shape[0]):
        start = end
        end = start + lengths[u]
        low = jnp.where((start <= first) & (first < end), start, low)
        last = first + OWN - 1
        high = jnp.where((start <= last) & (last < end), end, high)
    return (low - base) // size, (high - base + size - 1) // size


def owner_row(lengths, base, kown):
    frame = base + lax.broadcasted_iota(jnp.int32, kown.shape, 1)
    owner = jnp.full(kown.shape, -1, jnp.int32)
    end = jnp.int32(0)
    for u in range(lengths.shape[0]):
        start = end
        end = start + lengths[u]
        owner = jnp.where((frame >= start) & (frame < end), u, owner)
    kown[...] = owner


def attend_setup(lengths, base, kown, width, size):
    i = pl.program_id(0)
    first = base[1] + i * OWN

    @pl.when(i == 0)
    def _():
        owner_row(lengths, base[0], kown)

    low, high = tile_range(lengths, first, base[0], size)
    _, owner, _, _, _ = frame_columns(lengths, first, OWN)
    heads = width // HD
    slopes = [slope_of(lax.axis_index("mp") * heads + h) for h in range(heads)]

    def distance(k0):
        shape = (OWN, size)
        gap = (first - base[0] - k0) + lax.broadcasted_iota(jnp.int32, shape, 0)
        dist = jnp.abs(gap - lax.broadcasted_iota(jnp.int32, shape, 1)).astype(F32)
        return jnp.where(owner == kown[:, pl.ds(k0, size)], dist, 1e30)

    return low, high, slopes, distance


def attend_forward_kernel(lengths, base, q_ref, k_ref, v_ref, o_ref, ob_ref, lse_ref, kown):
    width = q_ref.shape[1]
    low, high, slopes, distance = attend_setup(lengths, base, kown, width, KT)
    lanes = [slice(128 * j, 128 * (j + 1)) for j in range(width // 128)]
    qs = [stack_pair(q_ref[:, l]) * BF(0.125) for l in lanes]

    def body(t, carry):
        k0 = pl.multiple_of(t * KT, KT)
        dist = distance(k0)
        out = []
        for j, l in enumerate(lanes):
            top, total, acc = carry[j]
            s = nt(qs[j], k_ref[pl.ds(k0, KT), l])
            s = jnp.concatenate([s[:OWN] - slopes[2 * j] * dist, s[OWN:] - slopes[2 * j + 1] * dist], 0)
            new = jnp.maximum(top, jnp.max(s, -1, keepdims=True))
            fade = jnp.exp(top - new)
            e = jnp.exp(s - new)
            total = total * fade + jnp.sum(e, -1, keepdims=True)
            acc = acc * fade + nn(e.astype(BF), v_ref[pl.ds(k0, KT), l])
            out.append((new, total, acc))
        return tuple(out)

    begin = (
        jnp.full((2 * OWN, 1), -1e30, F32), jnp.zeros((2 * OWN, 1), F32), jnp.zeros((2 * OWN, 128), F32),
    )
    ended = lax.fori_loop(low, high, body, tuple(begin for _ in lanes))
    lane = lax.broadcasted_iota(jnp.int32, (OWN, 128), 1)
    lse = jnp.zeros((OWN, 128), F32)
    for j, l in enumerate(lanes):
        top, total, acc = ended[j]
        o = unstack_pair(acc / total)
        o_ref[:, l] = o
        ob_ref[:, l] = o.astype(BF)
        g = top + jnp.log(total)
        lse = jnp.where(lane == 2 * j, g[:OWN], lse)
        lse = jnp.where(lane == 2 * j + 1, g[OWN:], lse)
    lse_ref[...] = lse


def blocks(width):
    return pl.BlockSpec((OWN, width), lambda i, *_: (i, 0))


def attend_call(kernel, outs, out_specs, in_specs, rows, keys, name, flops):
    return pl.pallas_call(
        kernel,
        out_shape=outs,
        grid_spec=pltpu.PrefetchScalarGridSpec(
            num_scalar_prefetch=2, grid=(rows // OWN,), in_specs=in_specs, out_specs=out_specs,
            scratch_shapes=[pltpu.VMEM((1, keys), jnp.int32)],
        ),
        compiler_params=pltpu.CompilerParams(vmem_limit_bytes=50 << 20),
        cost_estimate=pl.CostEstimate(flops=flops, bytes_accessed=1 << 23, transcendentals=0),
        name=name,
    )


def attend_forward(lengths, base, q, k, v):
    (rows, width), keys = q.shape, k.shape[0]
    outs = (
        jax.ShapeDtypeStruct((rows, width), F32), jax.ShapeDtypeStruct((rows, width), BF),
        jax.ShapeDtypeStruct((rows, 128), F32),
    )
    return attend_call(
        attend_forward_kernel, outs, (blocks(width), blocks(width), blocks(128)),
        [blocks(width), VM, VM], rows, keys, "attend_forward", 10**10,
    )(lengths, base, q, k, v)


def attend_backward_kernel(
    lengths, base, q_ref, k_ref, v_ref, do_ref, lse_ref, delta_ref, qa_ref, ka_ref, va_ref, doa_ref,
    stat_ref, out_ref, kown,
):
    width = q_ref.shape[1]
    low, high, slopes, distance = attend_setup(lengths, base, kown, width, KB)
    lanes = [slice(128 * j, 128 * (j + 1)) for j in range(width // 128)]

    def column(ref, j):
        return jnp.concatenate([ref[:, 2 * j : 2 * j + 1], ref[:, 2 * j + 1 : 2 * j + 2]], 0)

    scale = BF(0.125)
    qs = [stack_pair(q_ref[:, l]) * scale for l in lanes]
    dos = [stack_pair(do_ref[:, l]) for l in lanes]
    ks = [stack_pair(k_ref[:, l]) * scale for l in lanes]
    vs = [stack_pair(v_ref[:, l]) for l in lanes]
    lses = [column(lse_ref, j) for j in range(len(lanes))]
    deltas = [column(delta_ref, j) for j in range(len(lanes))]

    def body(t, carry):
        k0 = pl.multiple_of(t * KB, KB)
        keys = pl.ds(k0, KB)
        part = pl.ds(pl.multiple_of(lax.rem(t, KT // KB) * KB, KB), KB)
        whole_tile = t // (KT // KB)
        dist = distance(k0)
        out = []
        for j, l in enumerate(lanes):
            dq, dk, dv = carry[j]
            kj, vj, qj, doj = ka_ref[keys, l], va_ref[keys, l], qa_ref[keys, l], doa_ref[keys, l]
            bias = [slopes[2 * j + h] * dist for h in (0, 1)]
            s = nt(qs[j], kj)
            e = jnp.exp(jnp.concatenate([s[:OWN] - bias[0], s[OWN:] - bias[1]], 0) - lses[j])
            ds = (e * (nt(dos[j], vj) - deltas[j])).astype(BF)
            dq = dq + nn(ds, kj)
            s = nt(ks[j], qj)
            far = [stat_ref[whole_tile, 2 * j + h : 2 * j + h + 1, part] for h in (0, 1)]
            e = jnp.exp(jnp.concatenate([s[:OWN] - bias[0] - far[0], s[OWN:] - bias[1] - far[1]], 0))
            dv = dv + nn(e.astype(BF), doj)
            g = nt(vs[j], doj)
            far = [stat_ref[whole_tile, 8 + 2 * j + h : 9 + 2 * j + h, part] for h in (0, 1)]
            ds = (e * jnp.concatenate([g[:OWN] - far[0], g[OWN:] - far[1]], 0)).astype(BF)
            dk = dk + nn(ds, qj)
            out.append((dq, dk, dv))
        return tuple(out)

    zero = jnp.zeros((2 * OWN, 128), F32)
    ended = lax.fori_loop(low, high, body, tuple((zero, zero, zero) for _ in lanes))
    for j, l in enumerate(lanes):
        dq, dk, dv = ended[j]
        out_ref[0, :, l] = (unstack_pair(dq) * 0.125).astype(BF)
        out_ref[1, :, l] = (unstack_pair(dk) * 0.125).astype(BF)
        out_ref[2, :, l] = unstack_pair(dv).astype(BF)


def attend_backward(lengths, base, q, k, v, do, lse, delta, qa, ka, va, doa, stat):
    (rows, width), keys = q.shape, ka.shape[0]
    own = blocks(width)
    if k.shape[0] != rows:
        own = pl.BlockSpec((OWN, width), lambda i, lengths, base: (base[1] // OWN + i, 0))
    return attend_call(
        attend_backward_kernel, jax.ShapeDtypeStruct((3, rows, width), BF),
        pl.BlockSpec((3, OWN, width), lambda i, *_: (0, i, 0)),
        [blocks(width), own, own, blocks(width)] + [blocks(128)] * 2 + [VM] * 5,
        rows, keys, "attend_backward", 3 * 10**10,
    )(lengths, base, q, k, v, do, lse, delta, qa, ka, va, doa, stat)


def adam_step(weight, first_old, second, gradient, step_rate, decay_on):
    first_new = beta_one * first_old + (1.0 - beta_one) * gradient
    second_new = beta_two * second + (1.0 - beta_two) * gradient * gradient
    fix_one = 1.0 - beta_one**STEP
    fix_two = 1.0 - beta_two**STEP
    moved = first_new / fix_one / (jnp.sqrt(second_new / fix_two) + adam_epsilon)
    return (first_new, second_new, weight - step_rate * (moved + decay_on * weight_decay * weight))


def update(loss_total, grads, frames, states):
    big_squares = jnp.sum(grads[0] * grads[0]) + jnp.sum(grads[1] * grads[1])
    small_squares = jnp.zeros((), jnp.float32)
    for gradient in grads[2:]:
        small_squares = small_squares + jnp.sum(gradient * gradient)
    big_total = lax.psum(big_squares, ("seq", "mp"))
    return adam_all(loss_total, jnp.sqrt(big_total + small_squares), grads, frames, states)


def adam_all(loss_total, grad_norm, grads, frames, states):
    weights, firsts, seconds = states
    factor = jnp.minimum(1.0, 0.3 / math.sqrt(frames) / grad_norm)
    results = [loss_total, grad_norm]
    for number in range(7):
        results.extend(
            adam_step(
                weights[number],
                firsts[number],
                seconds[number],
                grads[number] * factor,
                step_rates[number],
                decay_flags[number],
            )
        )
    return tuple(results)


def split_arguments(arguments):
    rest = arguments[7:]
    return arguments[:7], (rest[0::3], rest[1::3], rest[2::3])


def per_device(*arguments):
    inputs, states = split_arguments(arguments)
    row_count = inputs[0].shape[0]
    if (lax.axis_size("seq"), lax.axis_size("mp"), row_count) == (8, 4, 512):
        return step_by_kernels(inputs, states)
    return step_by_collectives(inputs, states)


def step_by_kernels(inputs, states):
    mel, noise, phone_ids, lengths, span_start, span_end, flow_times = inputs
    attention, feedforward, win, phone_table, kern, wpred, gains = states[0]
    row_count = mel.shape[0]
    frames = row_count * lax.axis_size("seq")
    columns = ((0, 0), (0, 128 - MEL))
    with_phone = jnp.concatenate([noise, phone_ids.astype(F32)[:, None]], 1)
    pack = jnp.concatenate(
        [jnp.pad(mel, columns), jnp.pad(with_phone, ((0, 0), (0, 127 - MEL)))], 1
    )
    table = time_features(flow_times, D)
    (
        h1, conv, rim, a, q, k, v, wqkv, feats, choose, lse,
        dh2, rows, outg, do, delta, q_all, do_all, stat, gup, gdown, gout,
    ) = forward(
        lengths, span_start, span_end, flow_times, pack, table, win, phone_table, kern, gains, attention,
        feedforward, wpred.T,
    )
    row_base = lax.axis_index("seq") * row_count
    base = jnp.stack([jnp.zeros_like(row_base), row_base]).astype(jnp.int32)
    proj = attend_backward(lengths, base, q, k, v, do, lse, delta, q_all, k, v, do_all, stat)
    attention_grad, feedforward_grad, small, scalars = back(
        lengths, proj, wqkv, a, dh2, h1, conv, rim, gains, kern, feats, choose, rows, outg, gup, gdown, gout
    )
    gain_grad = jnp.stack([small[319], small[401], small[400]])
    grads = (
        attention_grad, feedforward_grad, small[:160], small[160:288], small[288:319],
        small[320:400].T, gain_grad,
    )
    return adam_all(scalars[1, 0], jnp.sqrt(scalars[0, 0]), grads, frames, states)


def step_by_collectives(inputs, states):
    mel_frames, noise_frames, phone_ids, lengths, span_start, span_end, flow_times = inputs
    (
        attention_weight,
        feedforward_weight,
        input_weight,
        phone_table,
        position_kernel,
        output_weight,
        layer_gains,
    ) = states[0]
    row_count = mel_frames.shape[0]
    frames = row_count * lax.axis_size("seq")
    row_base = lax.axis_index("seq") * row_count
    longest = min(MAXLEN, frames // 2)
    near_count = min((longest - 1 + row_count - 1) // row_count, lax.axis_size("seq") - 1)
    window_start = row_base - near_count * row_count
    reach = position_kernel.shape[0] // 2
    tables = (lengths, span_start, span_end, flow_times)
    row_index = row_base + jnp.arange(row_count)
    owners, masked, moment = frame_tables(*tables, row_index)
    covered, uncovered = mask_counts(lengths, span_start, span_end)
    row_weight = masked / jnp.maximum(covered, 1.0) + 0.1 * (1.0 - masked) / jnp.maximum(
        uncovered, 1.0
    )
    attention_full, feedforward_full = (
        lax.all_gather(attention_weight.astype(jnp.bfloat16), "seq", axis=1, tiled=True),
        lax.all_gather(feedforward_weight.astype(jnp.bfloat16), "seq", axis=1, tiled=True),
    )
    heads_local = attention_full.shape[2] // HD
    target = mel_frames - (1.0 - flow_sigma) * noise_frames
    noisy = (1.0 - (1.0 - flow_sigma) * moment[:, None]) * noise_frames + moment[
        :, None
    ] * mel_frames
    context = mel_frames * (1.0 - masked[:, None])
    feats = jnp.concatenate([context, noisy], 1).astype(jnp.bfloat16)
    choose = (phone_ids[:, None] == jnp.arange(phone_table.shape[0])[None, :]).astype(jnp.bfloat16)
    start_h = product(feats, input_weight.astype(jnp.bfloat16)) + product(
        choose, phone_table.astype(jnp.bfloat16)
    )
    start_h = start_h + time_features(moment, D)
    start_low = start_h.astype(jnp.bfloat16)
    rim = padded_2(start_low, (("seq", 0),), reach)
    pad_owner = frame_tables(*tables, row_base - reach + jnp.arange(row_count + 2 * reach))[0]
    conv_raw = jnp.zeros(start_h.shape, jnp.float32)
    for offset in range(position_kernel.shape[0]):
        same_owner = (pad_owner[offset : offset + row_count] == owners).astype(jnp.float32)
        conv_raw = (
            conv_raw
            + position_kernel[offset][None, :]
            * rim[offset : offset + row_count].astype(jnp.float32)
            * same_owner[:, None]
        )
    conv_gelu, conv_back = jax.vjp(jax.nn.gelu, conv_raw)
    hidden_one = start_h + conv_gelu
    ln_one, norm_back_one = jax.vjp(layer_norm, hidden_one, layer_gains[0])
    ln_one_low = ln_one.astype(jnp.bfloat16)
    projected = jnp.einsum(
        "td,kdh->kth", ln_one_low, attention_full[:3], preferred_element_type=jnp.float32
    ).astype(jnp.bfloat16)
    queries, keyed, valued = (projected[0], projected[1], projected[2])
    def window(array):
        return slice_window(
            lax.all_gather(array, "seq", axis=0, tiled=True), row_base, near_count, row_count
        )

    base = jnp.stack([window_start, row_base]).astype(jnp.int32)
    key_all, value_all = window(keyed), window(valued)
    out_f32, out_low, log_total = attend_forward(lengths, base, queries, key_all, value_all)
    attended = lax.psum(
        contract_cols(out_low, attention_full[3]).astype(jnp.bfloat16), "mp"
    ).astype(jnp.float32)
    hidden_two = hidden_one + attended
    ln_two, norm_back_two = jax.vjp(layer_norm, hidden_two, layer_gains[1])
    ln_two_low = ln_two.astype(jnp.bfloat16)
    upward = product(ln_two_low, feedforward_full[0])
    gated_f32, gelu_back = jax.vjp(jax.nn.gelu, upward)
    gated = gated_f32.astype(jnp.bfloat16)
    downward = lax.psum(
        contract_cols(gated, feedforward_full[1]).astype(jnp.bfloat16), "mp"
    ).astype(jnp.float32)
    hidden_three = hidden_two + downward
    ln_three, norm_back_three = jax.vjp(layer_norm, hidden_three, layer_gains[2])
    ln_three_low = ln_three.astype(jnp.bfloat16)
    output_low = output_weight.astype(jnp.bfloat16)
    predicted = product(ln_three_low, output_low)
    errors = predicted - target
    loss_local = jnp.sum(row_weight * jnp.mean(errors * errors, 1))
    loss_total = lax.psum(loss_local, "seq")
    pred_grad = (row_weight[:, None] * (2.0 / errors.shape[1]) * errors).astype(jnp.bfloat16)
    output_grad = contract_rows(ln_three_low, pred_grad)
    three_grad, gain_three = norm_back_three(contract_cols(pred_grad, output_low))
    down_low = three_grad.astype(jnp.bfloat16)
    down_wgrad = contract_rows(down_low, gated)
    up_grad = gelu_back(product(down_low, feedforward_full[1]))[0].astype(jnp.bfloat16)
    up_wgrad = contract_rows(ln_two_low, up_grad)
    two_sum = lax.psum(
        contract_cols(up_grad, feedforward_full[0]).astype(jnp.bfloat16), "mp"
    ).astype(jnp.float32)
    norm_grad, gain_two = norm_back_two(two_sum)
    two_grad = three_grad + norm_grad
    attended_low = two_grad.astype(jnp.bfloat16)
    out_wgrad = contract_rows(attended_low, out_low)
    out_heads = product(attended_low, attention_full[3]).astype(jnp.bfloat16)
    delta = jnp.sum(
        (out_heads.astype(jnp.float32) * out_f32).reshape(row_count, heads_local, HD), 2
    )
    delta = jnp.pad(delta, ((0, 0), (0, 128 - heads_local)))
    stat = window(jnp.concatenate([log_total[:, :8], delta[:, :8]], 1))
    stat = stat.reshape(-1, KT, 16).transpose(0, 2, 1)
    proj_grad = attend_backward(
        lengths, base, queries, keyed, valued, out_heads, log_total, delta,
        window(queries), key_all, value_all, window(out_heads), stat,
    )
    qkv_wgrad = jnp.einsum("td,kth->kdh", ln_one_low, proj_grad, preferred_element_type=jnp.float32)
    one_part = jnp.einsum(
        "kth,kdh->td", proj_grad, attention_full[:3], preferred_element_type=jnp.float32
    )
    one_sum = lax.psum(one_part.astype(jnp.bfloat16), "mp").astype(jnp.float32)
    norm_grad, gain_one = norm_back_one(one_sum)
    one_grad = two_grad + norm_grad
    conv_grad = conv_back(one_grad)[0].astype(jnp.bfloat16)
    grad_rim = padded_2(conv_grad, (("seq", 0),), reach)
    spread = jnp.zeros(one_grad.shape, jnp.float32)
    kernel_rows = []
    conv_grad_f32 = conv_grad.astype(jnp.float32)
    for offset in range(position_kernel.shape[0]):
        back_start = 2 * reach - offset
        same_back = (pad_owner[back_start : back_start + row_count] == owners).astype(jnp.float32)
        spread = (
            spread
            + position_kernel[offset][None, :]
            * grad_rim[back_start : back_start + row_count].astype(jnp.float32)
            * same_back[:, None]
        )
        same_fore = (pad_owner[offset : offset + row_count] == owners).astype(jnp.float32)
        kernel_rows.append(
            jnp.sum(
                conv_grad_f32
                * rim[offset : offset + row_count].astype(jnp.float32)
                * same_fore[:, None],
                0,
            )
        )
    kernel_grad = jnp.stack(kernel_rows)
    start_grad = (one_grad + spread).astype(jnp.bfloat16)
    input_wgrad = contract_rows(feats, start_grad)
    phone_wgrad = contract_rows(choose, start_grad)
    gains_grad = jnp.stack([gain_one, gain_two, gain_three])
    small_sums = lax.psum((input_wgrad, phone_wgrad, kernel_grad, output_grad, gains_grad), "seq")
    attention_grad, feedforward_grad = (
        lax.psum_scatter(
            jnp.concatenate([qkv_wgrad, out_wgrad[None]], 0), "seq", scatter_dimension=1, tiled=True
        ),
        lax.psum_scatter(jnp.stack([up_wgrad, down_wgrad]), "seq", scatter_dimension=1, tiled=True),
    )
    grads = (attention_grad, feedforward_grad) + tuple(small_sums)
    return update(loss_total, grads, frames, states)


def solution(mesh):
    in_specs = (
        P("seq", None),
        P("seq", None),
        P("seq"),
        P(),
        P(),
        P(),
        P(),
        P(None, "seq", "mp"),
        P(None, "seq", "mp"),
        P(None, "seq", "mp"),
        P(None, "seq", "mp"),
        P(None, "seq", "mp"),
        P(None, "seq", "mp"),
        P(),
        P(),
        P(),
        P(),
        P(),
        P(),
        P(),
        P(),
        P(),
        P(),
        P(),
        P(),
        P(),
        P(),
        P(),
    )
    out_specs = (
        P(),
        P(),
        P(None, "seq", "mp"),
        P(None, "seq", "mp"),
        P(None, "seq", "mp"),
        P(None, "seq", "mp"),
        P(None, "seq", "mp"),
        P(None, "seq", "mp"),
        P(),
        P(),
        P(),
        P(),
        P(),
        P(),
        P(),
        P(),
        P(),
        P(),
        P(),
        P(),
        P(),
        P(),
        P(),
    )
    return jax.shard_map(
        per_device, mesh=mesh, in_specs=in_specs, out_specs=out_specs, check_vma=False
    )
```

```python
import functools
import math

import jax
import jax.numpy as jnp
from jax import lax
from jax.experimental import pallas as pl
from jax.experimental.pallas import tpu as pltpu
from jax.sharding import PartitionSpec as P

D = 1024
HEADS = 16
HD = 64
MEL = 80
STEP = 10
MAXLEN = 1600


norm_epsilon = 1e-05
flow_sigma = 1e-05
beta_one = 0.9
beta_two = 0.95
adam_epsilon = 1e-08
weight_decay = 0.1
step_rates = (0.04, 0.04, 0.08, 1.0, 0.2, 0.04, 1.0)
decay_flags = (1.0, 1.0, 1.0, 1.0, 1.0, 1.0, 0.0)


def padded_2(array, sides, width):
    for axis, dim in sides:
        devices, length = (lax.axis_size(axis), array.shape[dim])
        up = [(i, (i + 1) % devices) for i in range(devices - 1)]
        down = [(j, i) for i, j in up]
        last = lax.slice_in_dim(array, length - width, length, axis=dim)
        initial = lax.slice_in_dim(array, 0, width, axis=dim)
        before = lax.ppermute(last, axis, up)
        after = lax.ppermute(initial, axis, down)
        array = jnp.concatenate([before, array, after], axis=dim)
    return array


def layer_norm(inputs, gain_row):
    centre_mean = jnp.mean(inputs, -1, keepdims=True)
    centered = inputs - centre_mean
    variance = jnp.mean(centered * centered, -1, keepdims=True)
    return centered * lax.rsqrt(variance + norm_epsilon) * gain_row


def frame_tables(lengths, span_start, span_end, flow_times, frame_index):
    utter_ends = jnp.cumsum(lengths)
    starts = utter_ends - lengths
    member = (
        (frame_index[:, None] >= starts[None, :]) & (frame_index[:, None] < utter_ends[None, :])
    ).astype(jnp.float32)
    labels = (jnp.arange(lengths.shape[0]) + 1).astype(jnp.float32)
    owners = jnp.sum(member * labels[None, :], 1) - 1.0
    position = frame_index.astype(jnp.float32) - jnp.sum(
        member * starts.astype(jnp.float32)[None, :], 1
    )
    low_end = jnp.sum(member * span_start.astype(jnp.float32)[None, :], 1)
    high_end = jnp.sum(member * span_end.astype(jnp.float32)[None, :], 1)
    masked = ((position >= low_end) & (position < high_end)).astype(jnp.float32)
    moment = jnp.sum(member * flow_times[None, :], 1)
    return (owners, masked, moment)


def mask_counts(lengths, span_start, span_end):
    span_low = jnp.minimum(span_start, lengths)
    span_high = jnp.minimum(span_end, lengths)
    covered = jnp.sum(jnp.maximum(span_high - span_low, 0)).astype(jnp.float32)
    return (covered, jnp.sum(lengths).astype(jnp.float32) - covered)


def time_features(moment, width):
    half_width = width // 2
    frequency = jnp.exp(
        -math.log(10000.0) * jnp.arange(half_width).astype(jnp.float32) / half_width
    )
    angles = moment[:, None] * 100.0 * frequency[None, :]
    return jnp.concatenate([jnp.sin(angles), jnp.cos(angles)], 1)


def product(left, right):
    return jnp.dot(left, right, preferred_element_type=jnp.float32)


def contract_rows(left, right):
    return lax.dot_general(
        left, right, (((0,), (0,)), ((), ())), preferred_element_type=jnp.float32
    )


def contract_cols(left, right):
    return lax.dot_general(
        left, right, (((1,), (1,)), ((), ())), preferred_element_type=jnp.float32
    )


def slice_window(full_rows, row_base, near_count, row_count):
    pad_rows = near_count * row_count
    padded = jnp.pad(full_rows, ((pad_rows, pad_rows), (0, 0)))
    return lax.dynamic_slice_in_dim(padded, row_base, (2 * near_count + 1) * row_count, 0)


MESH = pl.DeviceIdType.MESH
VM = pl.BlockSpec(memory_space=pltpu.VMEM)
SM = pl.BlockSpec(memory_space=pltpu.SMEM)
BF = jnp.bfloat16
F32 = jnp.float32
OWN = 128
EDGE = 16
HALF = OWN // 2


def nn(a, b):
    return jnp.dot(a, b, preferred_element_type=F32)


def nt(a, b):
    return lax.dot_general(a, b, (((1,), (1,)), ((), ())), preferred_element_type=F32)


def tn(a, b):
    return lax.dot_general(a, b, (((0,), (0,)), ((), ())), preferred_element_type=F32)


def put(src, dst, send, recv, device):
    return pltpu.make_async_remote_copy(
        src_ref=src, dst_ref=dst, send_sem=send, recv_sem=recv, device_id=device, device_id_type=MESH
    )


class Place:
    def __init__(self):
        self.s, self.m = lax.axis_index("seq"), lax.axis_index("mp")
        self.z, self.x = self.s // 2, lax.rem(self.s, 2)
        self.y, self.c = self.m // 2, lax.rem(self.m, 2)
        self.core = (self.s, self.m + 1 - 2 * self.c)
        self.across = (self.s, lax.rem(self.m + 2, 4))
        self.side = (self.s + 1 - 2 * self.x, self.m)
        self.up = (self.s + 2, self.m)
        self.down = (self.s - 2, self.m)


def greet(peers):
    barrier = pltpu.get_barrier_semaphore()
    total = 0
    for device, exists in peers:
        if exists is None:
            pl.semaphore_signal(barrier, inc=1, device_id=device, device_id_type=MESH)
            total = total + 1
        else:

            @pl.when(exists)
            def _(device=device):
                pl.semaphore_signal(barrier, inc=1, device_id=device, device_id_type=MESH)

            total = total + exists.astype(jnp.int32)
    pl.semaphore_wait(barrier, total)


def grid_peers(p):
    column = [((2 * lax.rem(p.z + d, 4) + p.x, p.m), None) for d in range(1, 4)]
    return [(p.side, None)] + column


def mp_peers(p):
    return [(p.core, None), (p.across, None)]


class Gather:
    SEMS = [pltpu.SemaphoreType.DMA((3, 8)), pltpu.SemaphoreType.DMA((8,))]

    def __init__(self, p, view, send, recv):
        self.p, self.view, self.send, self.recv = p, view, send, recv

    def copy(self, slot, kind):
        p = self.p
        device = (p.side, p.up, p.down)[kind]
        return put(
            self.view(slot), self.view(slot), self.send.at[kind, slot], self.recv.at[slot], device
        )

    def start(self):
        p = self.p
        self.copy(p.s, 0).start()

        @pl.when(p.z < 3)
        def _():
            self.copy(p.s, 1).start()

        @pl.when(p.z > 0)
        def _():
            self.copy(p.s, 2).start()

    def step(self, hop):
        p = self.p
        below, above = p.s - 2 * (hop + 1), p.s + 2 * (hop + 1)

        @pl.when(p.z - 1 - hop >= 0)
        def _():
            self.copy(below, 0).wait_recv()
            self.copy(below, 0).start()

            @pl.when(p.z < 3)
            def _():
                self.copy(below, 1).start()

        @pl.when(p.z + 1 + hop <= 3)
        def _():
            self.copy(above, 0).wait_recv()
            self.copy(above, 0).start()

            @pl.when(p.z > 0)
            def _():
                self.copy(above, 2).start()

    def finish(self):
        p = self.p
        for zz in range(4):
            self.copy(2 * zz + 1 - p.x, 0).wait_recv()
        for zz in range(4):
            slot = 2 * zz + p.x
            self.copy(slot, 0).wait_send()

            @pl.when((p.z < 3) & (p.z >= zz))
            def _(slot=slot):
                self.copy(slot, 1).wait_send()

            @pl.when((p.z > 0) & (p.z <= zz))
            def _(slot=slot):
                self.copy(slot, 2).wait_send()


class ColumnGather:
    SEMS = [pltpu.SemaphoreType.DMA((2, 4)), pltpu.SemaphoreType.DMA((8,))]

    def __init__(self, p, view, send, recv):
        self.p, self.view, self.send, self.recv = p, view, send, recv

    def level(self, hop):
        z = self.p.z
        if hop == 0:
            return z + 1 - 2 * lax.rem(z, 2)
        return jnp.where(z < 2, 1 + hop, 2 - hop)

    def copy(self, slot, sem, device):
        return put(self.view(slot), self.view(slot), self.send.at[sem], self.recv.at[slot], device)

    def along(self, hop):
        p = self.p
        zz = self.level(hop)
        return self.copy(p.s, (0, hop), (2 * zz + p.x, p.m))

    def aside(self, hop):
        p = self.p
        slot = p.s if hop == 3 else 2 * self.level(hop) + p.x
        return self.copy(slot, (1, hop), p.side)

    def start(self):
        self.aside(3).start()
        for hop in range(3):
            self.along(hop).start()

    def step(self, hop):
        self.aside(hop).wait_recv()
        self.aside(hop).start()

    def finish(self):
        p = self.p
        for zz in range(4):
            self.copy(2 * zz + 1 - p.x, (1, 3), p.side).wait_recv()
        for hop in range(3):
            self.along(hop).wait_send()
        for hop in range(4):
            self.aside(hop).wait_send()


class WideGather(Gather):
    def along(self, slot, down, up):
        for kind, wanted in ((1, up), (2, down)):
            if wanted is not None:

                @pl.when(wanted)
                def _(kind=kind):
                    self.copy(slot, kind).start()

    def cross(self):
        p = self.p
        slot = p.s + 1 - 2 * p.x
        self.copy(slot, 0).wait_recv()
        self.along(slot, p.z > 0, p.z < 3)

    def step(self, hop):
        p = self.p
        for other in (0, 1):
            near = p.s + other * (1 - 2 * p.x)

            @pl.when(p.z - 1 - hop >= 0)
            def _(slot=near - 2 * (hop + 1)):
                self.copy(slot, 0).wait_recv()
                self.along(slot, None, p.z < 3)

            @pl.when(p.z + 1 + hop <= 3)
            def _(slot=near + 2 * (hop + 1)):
                self.copy(slot, 0).wait_recv()
                self.along(slot, p.z > 0, None)

    def finish(self):
        p = self.p
        self.copy(p.s, 0).wait_send()
        for slot in range(8):
            zz = slot // 2

            @pl.when((p.z < 3) & (p.z >= zz))
            def _(slot=slot):
                self.copy(slot, 1).wait_send()

            @pl.when((p.z > 0) & (p.z <= zz))
            def _(slot=slot):
                self.copy(slot, 2).wait_send()


class NearGather:
    SEMS = [pltpu.SemaphoreType.DMA((8,)), pltpu.SemaphoreType.DMA((8,))]

    def __init__(self, p, view, edge, send, recv):
        self.p, self.view, self.edge, self.send, self.recv = p, view, edge, send, recv
        self.turn = 1 - 2 * p.x
        s, turn = p.s, self.turn
        self.ahead, self.behind = (s + 2 * turn, p.m), (s - 2 * turn, p.m)
        self.has_ahead = (s + 2 * turn >= 0) & (s + 2 * turn <= 7)
        self.has_behind = (s - 2 * turn >= 0) & (s - 2 * turn <= 7)

    def copy(self, slot, sem, device):
        return put(self.view(slot), self.view(slot), self.send.at[sem], self.recv.at[slot], device)

    def part(self, slot, last, sem, device):
        return put(self.edge(slot, last), self.edge(slot, last), self.send.at[sem], self.recv.at[slot], device)

    def sends(self):
        p, s, turn = self.p, self.p.s, self.turn
        both = self.has_ahead & self.has_behind
        return [
            (lambda: self.copy(s, 0, p.side), None),
            (lambda: self.copy(s, 1, self.ahead), self.has_ahead),
            (lambda: self.copy(s, 2, self.behind), self.has_behind),
            (lambda: self.copy(s + turn, 3, self.behind), self.has_behind),
            (lambda: self.copy(s + 2 * turn, 4, p.side), self.has_ahead),
            (lambda: self.part(s + 2 * turn, p.x, 5, self.behind), both),
            (lambda: self.part(s - 2 * turn, 1 - p.x, 6, self.ahead), both),
            (lambda: self.copy(s - turn, 7, self.ahead), both),
        ]

    def go(self, index):
        copy, made = self.sends()[index]
        if made is None:
            copy().start()
        else:

            @pl.when(made)
            def _():
                copy().start()

    def arrive(self, slot, exists):
        @pl.when(exists)
        def _():
            self.copy(slot, 0, self.p.side).wait_recv()

    def start(self):
        for index in (0, 1, 2):
            self.go(index)

    def step(self, hop):
        s, turn = self.p.s, self.turn
        if hop == 0:
            self.copy(s + turn, 0, self.p.side).wait_recv()
            self.go(3)
        elif hop == 1:
            self.arrive(s + 2 * turn, self.has_ahead)
            self.go(4)
            self.go(5)
            self.arrive(s - 2 * turn, self.has_behind)
            self.go(6)
        else:
            self.arrive(s - turn, self.has_behind)
            self.go(7)

    def finish(self):
        s = self.p.s
        self.arrive(s - 3, s >= 3)
        self.arrive(s + 3, s <= 4)

        @pl.when(s >= 4)
        def _():
            self.part(s - 4, 1, 0, self.p.side).wait_recv()

        @pl.when(s <= 3)
        def _():
            self.part(s + 4, 0, 0, self.p.side).wait_recv()

        for copy, made in self.sends():
            if made is None:
                copy().wait_send()
            else:

                @pl.when(made)
                def _(copy=copy):
                    copy().wait_send()


def near_rows(ref, group):
    def view(slot):
        return ref.at[pl.ds(pl.multiple_of(slot * group, group), group), :]

    def edge(slot, last):
        return ref.at[pl.ds(pl.multiple_of(slot * group + last * (group - 64), 64), 64), :]

    return view, edge


class BlockGather:
    SEMS = [pltpu.SemaphoreType.DMA((3, 2)), pltpu.SemaphoreType.DMA((4, 2))]

    def __init__(self, p, full, send, recv):
        self.p, self.full, self.send, self.recv = p, full, send, recv

    def copy(self, slot, kind, h):
        rows = self.full.at[pl.ds(pl.multiple_of(slot * OWN + h * HALF, HALF), HALF)]
        device = self.p.across if kind == 0 else self.p.core
        return put(rows, rows, self.send.at[kind, h], self.recv.at[slot, h], device)

    def start(self, h):
        self.copy(self.p.m, 0, h).start()
        self.copy(self.p.m, 1, h).start()

    def finish(self):
        p = self.p
        far = lax.rem(p.m + 2, 4)
        for h in (0, 1):
            self.copy(far, 0, h).wait_recv()
            self.copy(far, 2, h).start()
        for h in (0, 1):
            self.copy(p.m + 1 - 2 * p.c, 1, h).wait_recv()
            self.copy(3 - p.m, 2, h).wait_recv()
            for kind in range(3):
                self.copy(p.m, kind, h).wait_send()


class BlockReduce:
    SEMS = [pltpu.SemaphoreType.DMA((3, 2)), pltpu.SemaphoreType.DMA((3, 2))]

    def __init__(self, p, part, from_core, pair, send, recv):
        self.p, self.part, self.from_core, self.pair = p, part, from_core, pair
        self.send, self.recv = send, recv

    def rows(self, slot, h):
        return pl.ds(pl.multiple_of(slot * OWN + h * HALF, HALF), HALF)

    def core_copy(self, i, h):
        p = self.p
        yy = 1 - p.y if i == 0 else p.y
        return put(
            self.part.at[self.rows(2 * yy + 1 - p.c, h)], self.from_core.at[i, pl.ds(h * HALF, HALF)],
            self.send.at[i, h], self.recv.at[i, h], p.core,
        )

    def across_copy(self, h):
        half = pl.ds(h * HALF, HALF)
        return put(
            self.pair.at[0, half], self.pair.at[1, half], self.send.at[2, h], self.recv.at[2, h], self.p.across
        )

    def far_rows(self):
        return pl.ds(pl.multiple_of((1 - self.p.y) * 2 * OWN, OWN), 2 * OWN)

    def near_rows(self):
        return pl.ds(pl.multiple_of(self.p.y * 2 * OWN, OWN), 2 * OWN)

    def send_far(self):
        p = self.p
        for h in (0, 1):
            self.core_copy(0, h).start()
        for h in (0, 1):
            half = slice(h * HALF, (h + 1) * HALF)
            self.core_copy(0, h).wait_recv()
            mine = self.part[self.rows(2 * (1 - p.y) + p.c, h), :].astype(F32)
            self.pair[0, half, :] = (mine + self.from_core[0, half, :].astype(F32)).astype(self.pair.dtype)
            self.across_copy(h).start()

    def send_near(self):
        for h in (0, 1):
            self.core_copy(1, h).start()

    def finish(self, h):
        half = slice(h * HALF, (h + 1) * HALF)
        self.core_copy(1, h).wait_recv()
        total = self.part[self.rows(self.p.m, h), :].astype(F32) + self.from_core[1, half, :].astype(F32)
        self.across_copy(h).wait_recv()
        return total + self.pair[1, half, :].astype(F32)

    def sent(self):
        for h in (0, 1):
            self.core_copy(0, h).wait_send()
            self.core_copy(1, h).wait_send()
            self.across_copy(h).wait_send()


class GridReduce:
    SEMS = [pltpu.SemaphoreType.DMA((2, 4)), pltpu.SemaphoreType.DMA((2, 4))]

    def __init__(self, p, column, side, from_side, chain, incoming, send, recv):
        self.p, self.column, self.side, self.from_side = p, column, side, from_side
        self.chain, self.incoming, self.send, self.recv = chain, incoming, send, recv

    def level(self, t):
        z = self.p.z
        high = jnp.where(z == 3, t, jnp.where(t == 0, 0, jnp.where(t == 1, 1, 5 - t)))
        low = jnp.where(z == 0, 3 - t, jnp.where(t == 0, 3, jnp.where(t == 1, 2, t - 2)))
        return jnp.where(z >= 2, high, low)

    def side_copy(self, zz):
        return put(self.side.at[zz], self.from_side.at[zz], self.send.at[0, zz], self.recv.at[0, zz], self.p.side)

    def along(self, there, slot):
        p = self.p
        return put(
            self.chain.at[there], self.incoming.at[slot], self.send.at[1, there], self.recv.at[1, slot],
            (2 * there + p.x, p.m),
        )

    def start(self, t, both):
        p, zz = self.p, self.level(t)
        rows = self.side.shape[1]
        self.side[zz] = both[pl.ds(pl.multiple_of((1 - p.x) * rows, rows), rows), :].astype(self.side.dtype)
        self.side_copy(zz).start()
        self.column[zz] = both[pl.ds(pl.multiple_of(p.x * rows, rows), rows), :]

    def step(self, t):
        p, zz = self.p, self.level(t)
        self.side_copy(zz).wait_recv()
        if t == 3:
            self.column[zz] = self.column[zz] + self.from_side[zz].astype(F32)
        else:
            self.chain[zz] = (self.column[zz] + self.from_side[zz].astype(F32)).astype(self.chain.dtype)
            self.along(zz, p.z).start()

    def finish(self, result):
        z = self.p.z
        total = self.column[z]
        for d in range(1, 4):
            other = lax.rem(z + d, 4)
            self.along(other, other).wait_recv()
        for d in range(1, 4):
            total = total + self.incoming[lax.rem(z + d, 4)].astype(F32)
        result[...] = total
        for zz in range(4):
            self.side_copy(zz).wait_send()
        for d in range(1, 4):
            self.along(lax.rem(z + d, 4), z).wait_send()


def grid_scratch():
    block = (4, OWN, D)
    return [pltpu.VMEM(block, F32)] + [pltpu.VMEM(block, BF)] * 4


def reduce_scratch():
    return [pltpu.VMEM((512, D), BF), pltpu.VMEM((2, OWN, D), BF), pltpu.VMEM((2, OWN, D), BF)]


GELU_A = math.sqrt(2.0 / math.pi)


def gelu(v):
    return 0.5 * v * (1.0 + jnp.tanh(GELU_A * (v + 0.044715 * (v * v * v))))


def gelu_slope(v):
    t = jnp.tanh(GELU_A * (v + 0.044715 * (v * v * v)))
    return 0.5 * (1.0 + t) + 0.5 * v * (1.0 - t * t) * (GELU_A * (1.0 + 3.0 * 0.044715 * v * v))


def norm_parts(v):
    mean = jnp.mean(v, -1, keepdims=True)
    centered = v - mean
    variance = jnp.mean(centered * centered, -1, keepdims=True)
    scale = lax.rsqrt(variance + norm_epsilon)
    return centered * scale, scale


def norm_back(v, gain, grad):
    unit, scale = norm_parts(v)
    gain_row = jnp.sum(grad * unit, 0, keepdims=True)
    g = grad * gain
    inner = g - jnp.mean(g, -1, keepdims=True) - unit * jnp.mean(g * unit, -1, keepdims=True)
    return scale * inner, gain_row


def frame_columns(lengths, first, rows, extra=()):
    frame = first + lax.broadcasted_iota(jnp.int32, (rows, 1), 0)
    end = jnp.int32(0)
    owner = jnp.full((rows, 1), -1, jnp.int32)
    starts = jnp.zeros((rows, 1), jnp.int32)
    ends = jnp.zeros((rows, 1), jnp.int32)
    picked = [jnp.zeros((rows, 1), e.dtype) for e in extra]
    for u in range(lengths.shape[0]):
        start = end
        end = start + lengths[u]
        inside = (frame >= start) & (frame < end)
        owner = jnp.where(inside, u, owner)
        starts = jnp.where(inside, start, starts)
        ends = jnp.where(inside, end, ends)
        picked = [jnp.where(inside, e[u], c) for e, c in zip(extra, picked)]
    return frame, owner, starts, ends, picked


def tap_masks(frame, starts, ends, mask_ref):
    low = jnp.broadcast_to(starts - frame + 15, (OWN, 128))
    high = jnp.broadcast_to(ends - frame + 15, (OWN, 128))
    for k in range(31):
        mask_ref[k] = ((low <= k) & (high > k)).astype(F32)


def vmem_call(kernel, outs, specs, scratch, cid, name, flops=1e9):
    return pl.pallas_call(
        kernel,
        out_shape=tuple(jax.ShapeDtypeStruct(*o) for o in outs),
        in_specs=specs,
        out_specs=tuple([VM] * len(outs)),
        scratch_shapes=scratch,
        compiler_params=pltpu.CompilerParams(
            collective_id=cid, has_side_effects=True, vmem_limit_bytes=61 << 20
        ),
        cost_estimate=pl.CostEstimate(flops=int(flops), bytes_accessed=1 << 24, transcendentals=0),
        name=name,
    )


def forward_kernel(
    lengths, span_start, span_end, flow_times, pack_ref, table_ref, win_ref, phone_ref, kern_ref,
    gain_ref, watt_ref, ff_shard, wpred_ref,
    h1_ref, conv_ref, rim_ref, a_ref, q_ref, k_ref, v_ref, wqkv_ref, feats_ref, choose_ref, lse_ref,
    dh2_ref, rows_ref, outg_ref, do_ref, delta_ref, qall_ref, doall_ref, stat_ref, gup_ref, gdown_ref, gout_ref,
    wout_ref, ext, rimf, masks, edge_send, edge_recv, ag_send, ag_recv, w_send, w_recv, o_send, o_recv,
    k_send, k_recv, v_send, v_recv,
    kown, qown, o32_ref, o_ref, tops, totals, sums,
    u_ref, gated, b_ref, dy_ref, du_ref, dlow, h_ref, dh3_ref,
    part, core1, pair1, core2, pair2, core3, pair3,
    s1, r1, s2, r2, s3, r3, as1, ar1, as2, ar2, as3, ar3,
    q_send, q_recv, d_send, d_recv, t_send, t_recv, wup_ref, wdown_ref, wu_send, wu_recv, wd_send, wd_recv, wx_send, wx_recv,
    both, *w_refs,
):
    p = Place()
    group = pack_ref.shape[0]
    prior, following = (p.s - 1, p.m), (p.s + 1, p.m)
    shard = watt_ref.shape[1]
    own_w = pl.ds(pl.multiple_of(p.s * shard, shard), shard)
    for j in range(3):
        wqkv_ref[j, own_w, :] = watt_ref[j].astype(BF)
    wout_ref[own_w, :] = watt_ref[3].astype(BF)
    wup_ref[own_w, :] = ff_shard[0].astype(BF)
    wdown_ref[own_w, :] = ff_shard[1].astype(BF)
    for ref in (qall_ref, doall_ref, stat_ref):
        ref[...] = jnp.zeros(ref.shape, ref.dtype)
    k_ref[...] = jnp.zeros(k_ref.shape, BF)
    v_ref[...] = jnp.zeros(v_ref.shape, BF)
    ext[:EDGE, :] = jnp.zeros((EDGE, 256), F32)
    ext[EDGE + group :, :] = jnp.zeros((EDGE, 256), F32)
    ext[EDGE : EDGE + group, :] = pack_ref[...]
    greet(grid_peers(p) + mp_peers(p) + [(prior, p.s > 0), (following, p.s < 7)])
    edge_up = put(ext.at[pl.ds(group, EDGE)], ext.at[pl.ds(0, EDGE)], edge_send.at[0], edge_recv.at[0], following)
    edge_down = put(ext.at[pl.ds(EDGE, EDGE)], ext.at[pl.ds(EDGE + group, EDGE)], edge_send.at[1], edge_recv.at[1], prior)

    @pl.when(p.s < 7)
    def _():
        edge_up.start()

    @pl.when(p.s > 0)
    def _():
        edge_down.start()

    def shard_rows(slot):
        return pl.ds(pl.multiple_of(slot * shard, shard), shard)

    gather_w = Gather(p, lambda slot: wqkv_ref.at[:, shard_rows(slot), :], w_send, w_recv)
    gather_o = Gather(p, lambda slot: wout_ref.at[shard_rows(slot), :], o_send, o_recv)
    def rows_of(slot):
        return pl.ds(pl.multiple_of(slot * group, group), group)

    def half_rows(slot, h):
        return pl.ds(pl.multiple_of(slot * shard + h * (shard // 2), shard // 2), shard // 2)

    gather_q = NearGather(p, *near_rows(qall_ref, group), q_send, q_recv)
    gather_d = NearGather(p, *near_rows(doall_ref, group), d_send, d_recv)
    gather_t = NearGather(
        p, lambda slot: stat_ref.at[slot], lambda slot, last: stat_ref.at[slot], t_send, t_recv
    )
    gather_up = Gather(p, lambda slot: wup_ref.at[shard_rows(slot), :], wu_send, wu_recv)
    gather_down = Gather(p, lambda slot: wdown_ref.at[half_rows(slot, 0), :], wd_send, wd_recv)
    gather_wide = WideGather(p, lambda slot: wdown_ref.at[half_rows(slot, 1), :], wx_send, wx_recv)
    gather_w.start()
    gather_o.start()

    @pl.when(p.s > 0)
    def _():
        edge_up.wait_recv()

    @pl.when(p.s < 7)
    def _():
        edge_down.wait_recv()

    first = p.s * group + p.m * OWN
    wide = OWN + 2 * EDGE

    def features(begin, both):
        rows = both.shape[0]
        frame, owner, starts, _, picked = frame_columns(
            lengths, begin, rows, (span_start, span_end, flow_times)
        )
        position = frame - starts
        masked = ((position >= picked[0]) & (position < picked[1]) & (owner >= 0)).astype(F32)
        moment = picked[2]
        mel, noise = both[:, :128], both[:, 128:]
        lane = lax.broadcasted_iota(jnp.int32, (rows, 128), 1)
        context = (mel * (1.0 - masked)).astype(BF)
        noisy = (1.0 - (1.0 - flow_sigma) * moment) * noise + moment * mel
        noisy = jnp.where(lane < MEL, noisy, 0.0).astype(BF)
        phone = noise[:, MEL : MEL + 1]
        choose = jnp.where(phone == lane.astype(F32), 1.0, 0.0).astype(BF)
        return owner, context, noisy, choose

    owner, context, noisy, choose = features(
        first - EDGE, ext[pl.ds(pl.multiple_of(p.m * OWN, OWN), wide), :]
    )
    h0 = nn(context[:, :MEL], win_ref[:MEL, :].astype(BF))
    h0 = h0 + nn(noisy[:, :MEL], win_ref[MEL:, :].astype(BF)) + nn(choose, phone_ref[...].astype(BF))
    time = jnp.zeros((wide, D), F32)
    for u in range(table_ref.shape[0]):
        time = jnp.where(owner == u, table_ref[u : u + 1, :], time)
    h0 = h0 + time
    low = h0.astype(BF)
    rim_ref[...] = low
    rimf[...] = low.astype(F32)
    h1_ref[...] = h0[EDGE : EDGE + OWN]
    gather_w.step(0)
    gather_o.step(0)
    frame, _, starts, ends, _ = frame_columns(lengths, first, OWN)
    tap_masks(frame, starts, ends, masks)

    @pl.loop(0, D // 128)
    def _(t):
        lanes = pl.ds(pl.multiple_of(t * 128, 128), 128)
        total = jnp.zeros((OWN, 128), F32)
        for k in range(31):
            total = total + kern_ref[k : k + 1, lanes] * (rimf[1 + k : 1 + k + OWN, lanes] * masks[k])
        conv_ref[:, lanes] = total

    own = pl.ds(pl.multiple_of(p.m * OWN, OWN), OWN)
    halves = [(h, slice(h * HALF, (h + 1) * HALF)) for h in (0, 1)]
    gather_a = BlockGather(p, a_ref, ag_send, ag_recv)

    def own_half(h):
        return pl.ds(pl.multiple_of(p.m * OWN + h * HALF, HALF), HALF)

    for h, half in halves:
        h1 = h1_ref[half, :] + gelu(conv_ref[half, :])
        h1_ref[half, :] = h1
        unit, _ = norm_parts(h1)
        a_ref[own_half(h), :] = (unit * gain_ref[0:1, :]).astype(BF)
        gather_a.start(h)
    gather_w.step(1)
    gather_o.step(1)
    gather_a.finish()
    gather_w.step(2)
    gather_o.step(2)
    gather_w.finish()
    rows = pl.ds(pl.multiple_of(p.s * group, group), group)

    gather_k = NearGather(p, *near_rows(k_ref, group), k_send, k_recv)
    gather_v = NearGather(p, *near_rows(v_ref, group), v_send, v_recv)
    k_ref[rows, :] = nn(a_ref[...], wqkv_ref[1]).astype(BF)
    gather_k.start()
    v_ref[rows, :] = nn(a_ref[...], wqkv_ref[2]).astype(BF)
    gather_v.start()
    gather_up.start()
    q_ref[...] = nn(a_ref[...], wqkv_ref[0]).astype(BF)
    _, context, noisy, choose = features(p.s * group, pack_ref[...])
    feats_ref[:, :128] = context
    feats_ref[:, 128:] = noisy
    choose_ref[...] = choose
    gather_o.finish()

    width = q_ref.shape[1]
    pairs = [slice(128 * j, 128 * (j + 1)) for j in range(width // 128)]
    heads = width // HD
    slopes = [slope_of(p.m * heads + h) for h in range(heads)]
    owner_row(lengths, 0, kown)
    _, owner, _, _, _ = frame_columns(lengths, p.s * group, group)
    qown[...] = owner
    tops[...] = jnp.full(tops.shape, -1e30, F32)
    totals[...] = jnp.zeros(totals.shape, F32)
    sums[...] = jnp.zeros(sums.shape, F32)

    def attend(i, slot, begin, size):
        mine = pl.ds(pl.multiple_of(i * OWN, OWN), OWN)
        keys = pl.ds(pl.multiple_of(slot * group + begin, OWN), size)
        gap = (p.s - slot) * group + i * OWN - begin + lax.broadcasted_iota(jnp.int32, (OWN, size), 0)
        dist = jnp.abs(gap - lax.broadcasted_iota(jnp.int32, (OWN, size), 1)).astype(F32)
        dist = jnp.where(qown[mine, :] == kown[:, keys], dist, 1e30)
        for j, l in enumerate(pairs):
            n = len(pairs) * i + j
            top = tops[n]
            scores = nt(stack_pair(q_ref[mine, l]) * BF(0.125), k_ref[keys, l])
            scores = jnp.concatenate(
                [scores[:OWN] - slopes[2 * j] * dist, scores[OWN:] - slopes[2 * j + 1] * dist], 0
            )
            new = jnp.maximum(top, jnp.max(scores, -1, keepdims=True))
            fade = jnp.exp(top - new)
            e = jnp.exp(scores - new[:, :1])
            tops[n] = new
            totals[n] = totals[n] * fade + jnp.sum(e, -1, keepdims=True)
            sums[n] = sums[n] * fade + nn(e.astype(BF), v_ref[keys, l])

    def tile(slot):
        @pl.loop(0, group // OWN)
        def _(i):
            attend(i, slot, 0, group)

    def tile_if(slot, exists, wait):
        @pl.when(exists)
        def _():
            wait(gather_k)
            wait(gather_v)
            tile(slot)

    turn = gather_k.turn
    tile(p.s)
    for g in (gather_k, gather_v):
        g.step(0)
    tile(p.s + turn)
    for g in (gather_k, gather_v):
        g.step(1)
    tile_if(p.s + 2 * turn, gather_k.has_ahead, lambda g: None)
    for g in (gather_k, gather_v):
        g.step(2)
    gather_wide.start()
    gather_down.start()
    tile_if(p.s - 2 * turn, gather_k.has_behind, lambda g: None)
    tile_if(p.s - turn, gather_k.has_behind, lambda g: None)
    gather_up.step(0)
    tile_if(p.s - 3, p.s >= 3, lambda g: g.copy(p.s - 3, 0, p.side).wait_recv())
    tile_if(p.s + 3, p.s <= 4, lambda g: g.copy(p.s + 3, 0, p.side).wait_recv())
    gather_up.step(1)

    @pl.when(p.s >= 4)
    def _():
        for g in (gather_k, gather_v):
            g.part(p.s - 4, 1, 0, p.side).wait_recv()
        attend(0, p.s - 4, group - OWN, OWN)

    @pl.when(p.s <= 3)
    def _():
        for g in (gather_k, gather_v):
            g.part(p.s + 4, 0, 0, p.side).wait_recv()
        attend(group // OWN - 1, p.s + 4, 0, OWN)

    @pl.loop(0, group // OWN)
    def _(i):
        mine = pl.ds(pl.multiple_of(i * OWN, OWN), OWN)
        lane = lax.broadcasted_iota(jnp.int32, (OWN, 128), 1)
        lse = jnp.zeros((OWN, 128), F32)
        for j, l in enumerate(pairs):
            n = len(pairs) * i + j
            o = unstack_pair(sums[n] / totals[n])
            o32_ref[mine, l] = o
            o_ref[mine, l] = o.astype(BF)
            g = tops[n] + jnp.log(totals[n])
            lse = jnp.where(lane == 2 * j, g[:OWN], lse)
            lse = jnp.where(lane == 2 * j + 1, g[OWN:], lse)
        lse_ref[mine, :] = lse

    red = BlockReduce(p, part, core1, pair1, s1, r1)
    for rows, send in ((red.far_rows(), red.send_far), (red.near_rows(), red.send_near)):
        part[rows, :] = nt(o_ref[rows, :], wout_ref[...]).astype(BF)
        send()
    gather_wide.cross()
    gather_up.step(2)
    gather_down.step(0)
    gather_wide.step(0)
    gather_b = BlockGather(p, b_ref, as1, ar1)
    for h, half in halves:
        h2 = h1_ref[half, :] + red.finish(h)
        h_ref[half, :] = h2
        unit, _ = norm_parts(h2)
        b_ref[own_half(h), :] = (unit * gain_ref[1:2, :]).astype(BF)
        gather_b.start(h)
    red.sent()
    gather_up.finish()
    gather_down.step(1)
    gather_wide.step(1)
    gather_b.finish()

    ff = ff_shard.shape[2]
    tile = 256

    @pl.loop(0, ff // tile)
    def _(t):
        lanes = pl.ds(pl.multiple_of(t * tile, tile), tile)
        up = nn(b_ref[...], wup_ref[:, lanes])
        u_ref[:, lanes] = up
        gated[:, lanes] = gelu(up).astype(BF)

    gather_down.step(2)
    gather_wide.step(2)
    gather_down.finish()
    gather_wide.finish()
    qall_ref[rows_of(p.s), :] = q_ref[...]
    gather_q.start()
    red = BlockReduce(p, part, core2, pair2, s2, r2)
    for rows, send in ((red.far_rows(), red.send_far), (red.near_rows(), red.send_near)):

        @pl.loop(0, D // tile)
        def _(t):
            lanes = pl.ds(pl.multiple_of(t * tile, tile), tile)
            part[rows, lanes] = nt(gated[rows, :], wdown_ref[lanes, :]).astype(BF)

        send()
    gather_q.step(0)
    _, owner, starts, _, picked = frame_columns(lengths, first, OWN, (span_start, span_end))
    position = first + lax.broadcasted_iota(jnp.int32, (OWN, 1), 0) - starts
    masked = ((position >= picked[0]) & (position < picked[1])).astype(F32)
    covered, frames = jnp.int32(0), jnp.int32(0)
    for n in range(lengths.shape[0]):
        span = jnp.minimum(span_end[n], lengths[n]) - jnp.minimum(span_start[n], lengths[n])
        covered = covered + jnp.maximum(span, 0)
        frames = frames + lengths[n]
    count = jnp.full((OWN, 1), jnp.maximum(covered, 1), jnp.int32).astype(F32)
    rest = jnp.full((OWN, 1), jnp.maximum(frames - covered, 1), jnp.int32).astype(F32)
    weight = masked / count + 0.1 * (1.0 - masked) / rest
    raw = pack_ref[own, :]
    target = (raw[:, :128] - (1.0 - flow_sigma) * raw[:, 128:])[:, :MEL]
    wpred = wpred_ref[...].astype(BF)

    gather_y = BlockGather(p, dy_ref, as2, ar2)
    loss = jnp.zeros((1, 1), F32)
    gain3 = jnp.zeros((1, D), F32)
    for h, half in halves:
        h3 = h_ref[half, :] + red.finish(h)
        unit, _ = norm_parts(h3)
        low = (unit * gain_ref[2:3, :]).astype(BF)
        errors = nt(low, wpred) - target[half]
        loss = loss + jnp.sum(weight[half] * jnp.mean(errors * errors, 1, keepdims=True), 0, keepdims=True)
        dpred = (weight[half] * (2.0 / MEL) * errors).astype(BF)
        dh3, gain_row = norm_back(h3, gain_ref[2:3, :], nn(dpred, wpred))
        dh3_ref[half, :] = dh3
        dy_ref[own_half(h), :] = dh3.astype(BF)
        gather_y.start(h)
        gain3 = gain3 + gain_row
        outg = tn(dpred, low)
        outg_ref[...] = outg if h == 0 else outg_ref[...] + outg
    red.sent()
    gather_q.step(1)
    gather_q.step(2)
    gather_y.finish()

    @pl.loop(0, ff // tile)
    def _(t):
        lanes = pl.ds(pl.multiple_of(t * tile, tile), tile)
        down = nn(dy_ref[...], wdown_ref[:, lanes])
        du_ref[:, lanes] = (down * gelu_slope(u_ref[:, lanes])).astype(BF)

    red = BlockReduce(p, part, core3, pair3, s3, r3)
    for rows, send in ((red.far_rows(), red.send_far), (red.near_rows(), red.send_near)):

        @pl.loop(0, D // tile)
        def _(t):
            lanes = pl.ds(pl.multiple_of(t * tile, tile), tile)
            part[rows, lanes] = nt(du_ref[rows, :], wup_ref[lanes, :]).astype(BF)

        send()

    down_sum = GridReduce(p, *w_refs)

    @pl.loop(0, 4)
    def _(t):
        lanes = pl.ds(pl.multiple_of(down_sum.level(t) * tile, tile), tile)
        both[...] = tn(dy_ref[:, lanes], gated[...])
        down_sum.start(t, both)

    gather_q.finish()
    gather_h = BlockGather(p, dlow, as3, ar3)
    gain2 = jnp.zeros((1, D), F32)
    for h, half in halves:
        norm_grad, gain_row = norm_back(h_ref[half, :], gain_ref[1:2, :], red.finish(h))
        dh2 = dh3_ref[half, :] + norm_grad
        dh2_ref[half, :] = dh2
        dlow[own_half(h), :] = dh2.astype(BF)
        gather_h.start(h)
        gain2 = gain2 + gain_row
    red.sent()
    rows_ref[...] = jnp.concatenate(
        [gain3, gain2, jnp.broadcast_to(loss, (1, D)), jnp.zeros((5, D), F32)], 0
    )

    @pl.loop(0, D // tile)
    def _(t):
        lanes = pl.ds(pl.multiple_of(t * tile, tile), tile)
        gup_ref[lanes, :] = tn(b_ref[:, lanes], du_ref[...])

    down_sum.step(0)
    gather_h.finish()
    grad = nn(dlow[...], wout_ref[...]).astype(BF)
    do_ref[...] = grad
    doall_ref[rows_of(p.s), :] = grad
    gather_d.start()
    weighted = grad.astype(F32) * o32_ref[...]
    width = o_ref.shape[1]
    head = lax.broadcasted_iota(jnp.int32, (width, 128), 0) // HD
    pick = (head == lax.broadcasted_iota(jnp.int32, (width, 128), 1)).astype(F32)
    delta_ref[...] = jnp.dot(weighted, pick, preferred_element_type=F32, precision=lax.Precision.HIGHEST)
    eye = (
        lax.broadcasted_iota(jnp.int32, (8, 128), 0) == lax.broadcasted_iota(jnp.int32, (8, 128), 1)
    ).astype(F32)
    for i, ref in enumerate((lse_ref, delta_ref)):
        stat_ref[p.s, 8 * i : 8 * i + 8, :] = lax.dot_general(
            eye, ref[...], (((1,), (1,)), ((), ())), preferred_element_type=F32, precision=lax.Precision.HIGHEST
        )
    gather_t.start()
    gout_ref[...] = tn(dlow[...], o_ref[...])
    for hop in range(3):
        down_sum.step(hop + 1)
        gather_d.step(hop)
        gather_t.step(hop)
    down_sum.finish(gdown_ref)
    gather_d.finish()
    gather_t.finish()
    for g in (gather_k, gather_v):
        for copy, made in g.sends():
            if made is None:
                copy().wait_send()
            else:

                @pl.when(made)
                def _(copy=copy):
                    copy().wait_send()

    @pl.when(p.s < 7)
    def _():
        edge_up.wait_send()

    @pl.when(p.s > 0)
    def _():
        edge_down.wait_send()


def forward(lengths, span_start, span_end, flow_times, pack, table, win, phone, kern, gains, watt, wff, wpred):
    group = pack.shape[0]
    shard, width = watt.shape[1:]
    ff = wff.shape[2]
    frames = 8 * group
    outs = [
        ((OWN, D), F32), ((OWN, D), F32), ((OWN + 2 * EDGE, D), BF), ((group, D), BF),
        ((group, width), BF), ((frames, width), BF), ((frames, width), BF),
        ((3, 8 * shard, width), BF), ((group, 256), BF), ((group, 128), BF), ((group, 128), F32),
        ((OWN, D), F32), ((8, D), F32), ((MEL, D), F32), ((group, width), BF), ((group, 128), F32),
        ((frames, width), BF), ((frames, width), BF), ((8, 16, group), F32),
        ((D, ff), F32), ((OWN, ff), F32), ((D, width), F32),
    ]
    dma, vmem = pltpu.SemaphoreType.DMA, pltpu.VMEM
    states = vmem((group // OWN * (width // 128), 2 * OWN, 128), F32)
    scratch = [
        vmem((8 * shard, width), BF), vmem((group + 2 * EDGE, 256), F32), vmem((OWN + 2 * EDGE, D), F32),
        vmem((31, OWN, 128), F32), dma((2,)), dma((2,)),
    ] + BlockGather.SEMS + Gather.SEMS * 2 + NearGather.SEMS * 2
    scratch = scratch + [
        vmem((1, frames), jnp.int32), vmem((group, 1), jnp.int32), vmem((group, width), F32),
        vmem((group, width), BF), states, states, states,
        vmem((group, ff), F32), vmem((group, ff), BF), vmem((group, D), BF), vmem((group, D), BF),
        vmem((group, ff), BF), vmem((group, D), BF), vmem((OWN, D), F32), vmem((OWN, D), F32),
    ]
    landing = reduce_scratch()[1:]
    scratch = scratch + reduce_scratch() + landing * 2 + BlockReduce.SEMS * 3 + BlockGather.SEMS * 3
    scratch = scratch + NearGather.SEMS * 3 + [vmem((D, ff), BF), vmem((D, ff), BF)] + Gather.SEMS * 3
    scratch = scratch + [vmem((2 * OWN, D), F32)] + grid_scratch() + GridReduce.SEMS
    return vmem_call(forward_kernel, outs, [SM] * 4 + [VM] * 9, scratch, 0, "forward", 4e10)(
        lengths, span_start, span_end, flow_times, pack, table, win, phone, kern, gains, watt, wff, wpred
    )


FEW = 448


def back_kernel(
    lengths, proj_ref, wqkv_ref, a_ref, dh2_ref, h1_ref, conv_ref, rim_ref, gain_ref, kern_ref,
    feats_ref, choose_ref, rows_ref, outg_ref, gup_ref, gdown_ref, gout_ref,
    gatt_ref, gff_ref, small_ref, scalar_ref,
    dcb, dcf, rimf, masks, dh1_ref, part, from_core, pair, s1, r1, edge_send, edge_recv,
    both, *rest,
):
    p = Place()
    att_sum, rest = GridReduce(p, *rest[:7]), rest[7:]
    up_sum, rest = GridReduce(p, *rest[:7]), rest[7:]
    few_sum, rest = GridReduce(p, *rest[:7]), rest[7:]
    (
        att, dh0, dh0_lanes, few, few_lanes, piece, few_own, d_send, d_recv, few_send, few_recv,
        g_send, g_recv, y_send, y_recv, c_send, c_recv,
        seen, seen_send, seen_recv, last, last_send, last_recv,
    ) = rest
    group = a_ref.shape[0]
    place = p.s * 4 + p.m
    prior = ((place + 31) // 4 - 8 * ((place + 31) // 32), lax.rem(place + 3, 4))
    following = ((place + 1) // 4, lax.rem(place + 1, 4))
    dcb[:EDGE, :] = jnp.zeros((EDGE, D), BF)
    dcb[EDGE + OWN :, :] = jnp.zeros((EDGE, D), BF)
    peers = [((lax.rem(p.s + d, 8), p.m), None) for d in range(1, 8)]
    others = [((p.s, lax.rem(p.m + d, 4)), None) for d in range(1, 4)]
    greet(peers + others + [(prior, place > 0), (following, place < 31)])
    red = BlockReduce(p, part, from_core, pair, s1, r1)
    for rows, send in ((red.far_rows(), red.send_far), (red.near_rows(), red.send_near)):
        total = nt(proj_ref[0, rows, :], wqkv_ref[0])
        total = total + nt(proj_ref[1, rows, :], wqkv_ref[1])
        part[rows, :] = (total + nt(proj_ref[2, rows, :], wqkv_ref[2])).astype(BF)
        send()

    def attention_block(t):
        rows = pl.ds(pl.multiple_of(att_sum.level(t) * 2 * OWN, 2 * OWN), 2 * OWN)
        for j in range(3):
            both[:, 256 * j : 256 * (j + 1)] = tn(a_ref[:, rows], proj_ref[j])
        both[:, 768:] = gout_ref[rows, :]
        att_sum.start(t, both)

    def up_block(t):
        rows = pl.ds(pl.multiple_of(up_sum.level(t) * 2 * OWN, 2 * OWN), 2 * OWN)
        up_sum.start(t, gup_ref.at[rows])

    pl.loop(0, 2)(up_block)
    rimf[...] = rim_ref[...].astype(F32)
    frame, _, starts, ends, _ = frame_columns(lengths, p.s * group + p.m * OWN, OWN)
    tap_masks(frame, starts, ends, masks)
    gain1 = jnp.zeros((1, D), F32)
    for h in (0, 1):
        half = slice(h * HALF, (h + 1) * HALF)
        norm_grad, gain_row = norm_back(h1_ref[half, :], gain_ref[0:1, :], red.finish(h))
        dh1 = dh2_ref[half, :] + norm_grad
        dh1_ref[half, :] = dh1
        dcb[EDGE + h * HALF : EDGE + (h + 1) * HALF, :] = (dh1 * gelu_slope(conv_ref[half, :])).astype(BF)
        gain1 = gain1 + gain_row
    red.sent()
    edge_up = put(dcb.at[pl.ds(OWN, EDGE)], dcb.at[pl.ds(0, EDGE)], edge_send.at[0], edge_recv.at[0], following)
    edge_down = put(dcb.at[pl.ds(EDGE, EDGE)], dcb.at[pl.ds(EDGE + OWN, EDGE)], edge_send.at[1], edge_recv.at[1], prior)

    @pl.when(place < 31)
    def _():
        edge_up.start()

    @pl.when(place > 0)
    def _():
        edge_down.start()

    pl.loop(2, 4)(up_block)
    dcf[EDGE : EDGE + OWN, :] = dcb[EDGE : EDGE + OWN, :].astype(F32)

    @pl.loop(0, D // 128)
    def _(t):
        lanes = pl.ds(pl.multiple_of(t * 128, 128), 128)
        mine = dcf[EDGE : EDGE + OWN, lanes]
        for k in range(31):
            near = rimf[1 + k : 1 + k + OWN, lanes] * masks[k]
            few[k : k + 1, lanes] = jnp.sum(mine * near, 0, keepdims=True)

    few[31:32, :] = gain1
    few[32:112, :] = outg_ref[...]
    few[112:114, :] = rows_ref[:2, :]
    few[114:, :] = jnp.zeros((14, D), F32)

    def quarter(m):
        return pl.ds(pl.multiple_of(m * 256, 256), 256)

    def mp_slot(d, incoming):
        there = lax.rem(p.m + d, 4)
        return there, (there if incoming else p.m)

    def few_copy(d, incoming=False):
        there, slot = mp_slot(d, incoming)
        return put(few.at[:, quarter(there)], few_lanes.at[slot], few_send.at[d - 1], few_recv.at[slot], (p.s, there))

    def dh0_copy(d, incoming=False):
        there, slot = mp_slot(d, incoming)
        rows = pl.ds(pl.multiple_of(slot * OWN, OWN), OWN)
        return put(dh0.at[:, quarter(there)], dh0_lanes.at[rows, :], d_send.at[d - 1], d_recv.at[slot], (p.s, there))

    for d in range(1, 4):
        few_copy(d).start()
    few_lanes[p.m] = few[:, quarter(p.m)]
    up_sum.step(0)

    @pl.when(place > 0)
    def _():
        edge_up.wait_recv()

    @pl.when(place < 31)
    def _():
        edge_down.wait_recv()

    dcf[:EDGE, :] = dcb[:EDGE, :].astype(F32)
    dcf[EDGE + OWN :, :] = dcb[EDGE + OWN :, :].astype(F32)

    @pl.loop(0, D // 128)
    def _(t):
        lanes = pl.ds(pl.multiple_of(t * 128, 128), 128)
        total = jnp.zeros((OWN, 128), F32)
        for k in range(31):
            total = total + kern_ref[30 - k : 31 - k, lanes] * (dcf[1 + k : 1 + k + OWN, lanes] * masks[k])
        dh0[:, lanes] = (dh1_ref[:, lanes] + total).astype(BF)

    for d in range(1, 4):
        dh0_copy(d).start()
    dh0_lanes[pl.ds(pl.multiple_of(p.m * OWN, OWN), OWN), :] = dh0[:, quarter(p.m)]
    pl.loop(0, 2)(attention_block)
    up_sum.step(1)
    for d in range(1, 4):
        few_copy(d, True).wait_recv()
    piece[288:416, :] = (few_lanes[0] + few_lanes[1]) + (few_lanes[2] + few_lanes[3])
    piece[416:, :] = jnp.zeros((FEW - 416, 256), F32)
    for d in range(1, 4):
        dh0_copy(d, True).wait_recv()
    grad = tn(feats_ref[...], dh0_lanes[...])
    piece[:MEL, :] = grad[:MEL]
    piece[MEL : 2 * MEL, :] = grad[128 : 128 + MEL]
    piece[160:288, :] = tn(choose_ref[...], dh0_lanes[...])

    eighth = FEW // 8

    def piece_rows(slot):
        return pl.ds(pl.multiple_of(slot * eighth, 8), eighth)

    def few_block(t):
        rows = pl.ds(pl.multiple_of(few_sum.level(t) * 2 * eighth, 8), 2 * eighth)
        few_sum.start(t, piece.at[rows])

    def seq_slot(d, incoming):
        there = lax.rem(p.s + d, 8)
        return there, (there if incoming else p.s)

    pl.loop(0, 4)(few_block)
    up_sum.step(2)
    for t in range(4):
        few_sum.step(t)
    pl.loop(2, 4)(attention_block)
    up_sum.step(3)
    att_sum.step(0)
    few_sum.finish(few_own)
    few_squares = jnp.sum(few_own[...] * few_own[...])
    small_ref[piece_rows(p.s), quarter(p.m)] = few_own[...]
    share = ColumnGather(p, lambda slot: small_ref.at[piece_rows(slot), quarter(p.m)], g_send, g_recv)

    def cross(slot, m):
        view = small_ref.at[piece_rows(slot), quarter(m)]
        return put(view, view, y_send.at[slot], y_recv.at[slot], p.across)

    share.start()
    cross(p.s, p.m).start()
    att_sum.step(1)
    for hop in range(3):
        share.step(hop)
        cross(2 * share.level(hop) + p.x, p.m).start()
    att_sum.step(2)
    share.finish()
    for zz in range(4):
        cross(2 * zz + 1 - p.x, p.m).start()
    att_sum.step(3)
    up_sum.finish(gff_ref.at[0])
    gff_ref[1] = gdown_ref[...]
    squares = few_squares + jnp.sum(gff_ref[0] * gff_ref[0]) + jnp.sum(gff_ref[1] * gff_ref[1])
    far = lax.rem(p.m + 2, 4)
    for n in range(8):
        cross(n, far).wait_recv()

    def core_copy(i, m):
        view = small_ref.at[:, quarter(m)]
        return put(view, view, c_send.at[i], c_recv.at[i], p.core)

    core_copy(0, p.m).start()
    core_copy(1, far).start()
    att_sum.finish(att)
    squares = squares + jnp.sum(att[...] * att[...])
    row = lax.broadcasted_iota(jnp.int32, (8, 128), 0)
    seen[p.s] = jnp.where(row == 0, squares, rows_ref[2:3, :128])

    def scalar_copy(d, incoming=False):
        there, slot = seq_slot(d, incoming)
        return put(seen.at[p.s], seen.at[slot], seen_send.at[d - 1], seen_recv.at[slot], (there, p.m))

    for d in range(1, 8):
        scalar_copy(d).start()
    for j in range(4):
        gatt_ref[j] = att[:, 256 * j : 256 * (j + 1)]
    for d in range(1, 8):
        scalar_copy(d, True).wait_recv()
    total = seen[0]
    for n in range(1, 8):
        total = total + seen[n]
    last[p.m] = total

    def last_copy(d, incoming=False):
        there, slot = mp_slot(d, incoming)
        return put(last.at[p.m], last.at[slot], last_send.at[d - 1], last_recv.at[slot], (p.s, there))

    for d in range(1, 4):
        last_copy(d).start()
    core_copy(0, p.m + 1 - 2 * p.c).wait_recv()
    core_copy(1, 3 - p.m).wait_recv()
    for d in range(1, 4):
        last_copy(d, True).wait_recv()
    scalar_ref[...] = (last[0] + last[1]) + (last[2] + last[3])
    for d in range(1, 8):
        scalar_copy(d).wait_send()
    for n in range(8):
        cross(n, p.m).wait_send()
    core_copy(0, p.m).wait_send()
    core_copy(1, far).wait_send()
    for d in range(1, 4):
        few_copy(d).wait_send()
        last_copy(d).wait_send()
        dh0_copy(d).wait_send()

    @pl.when(place < 31)
    def _():
        edge_up.wait_send()

    @pl.when(place > 0)
    def _():
        edge_down.wait_send()


def back(lengths, proj, wqkv, a, dh2, h1, conv, rim, gains, kern, feats, choose, rows, outg, gup, gdown, gout):
    outs = [((4, OWN, 256), F32), ((2, OWN, D), F32), ((FEW, D), F32), ((8, 128), F32)]
    wide, group = OWN + 2 * EDGE, a.shape[0]
    dma, vmem = pltpu.SemaphoreType.DMA, pltpu.VMEM
    scratch = [
        vmem((wide, D), BF), vmem((wide, D), F32), vmem((wide, D), F32),
        vmem((31, OWN, 128), F32), vmem((OWN, D), F32),
    ] + reduce_scratch() + BlockReduce.SEMS + [dma((2,)), dma((2,)), vmem((2 * OWN, D), F32)]
    scratch = scratch + (grid_scratch() + GridReduce.SEMS) * 2
    eighth = FEW // 8
    scratch = scratch + [vmem((4, eighth, 256), F32)] * 5 + GridReduce.SEMS
    scratch = scratch + [
        vmem((OWN, D), F32), vmem((OWN, D), BF), vmem((group, 256), BF), vmem((OWN, D), F32),
        vmem((4, OWN, 256), F32), vmem((FEW, 256), F32), vmem((eighth, 256), F32),
        dma((3,)), dma((4,)), dma((3,)), dma((4,)),
    ] + ColumnGather.SEMS + [
        dma((8,)), dma((8,)), dma((2,)), dma((2,)),
        vmem((8, 8, 128), F32), dma((7,)), dma((8,)), vmem((4, 8, 128), F32), dma((3,)), dma((4,)),
    ]
    return vmem_call(back_kernel, outs, [SM] + [VM] * 16, scratch, 2, "back", 2e10)(
        lengths, proj, wqkv, a, dh2, h1, conv, rim, gains, kern, feats, choose, rows, outg, gup, gdown, gout
    )


KT = 512
KB = 256


def lane_half(rows):
    return lax.broadcasted_iota(jnp.int32, (rows, 128), 1) < HD


def stack_pair(x):
    low, zero = lane_half(x.shape[0]), jnp.zeros_like(x)
    return jnp.concatenate([jnp.where(low, x, zero), jnp.where(low, zero, x)], 0)


def unstack_pair(x):
    rows = x.shape[0] // 2
    return jnp.where(lane_half(rows), x[:rows], x[rows:])


def slope_of(index):
    value = jnp.float32(2.0 ** (-8.0 * HEADS / HEADS))
    for head in range(HEADS - 1):
        value = jnp.where(index == head, jnp.float32(2.0 ** (-8.0 * (head + 1) / HEADS)), value)
    return value


def tile_range(lengths, first, base, size):
    end = jnp.int32(0)
    low = jnp.int32(0)
    high = jnp.int32(0)
    for u in range(lengths.shape[0]):
        start = end
        end = start + lengths[u]
        low = jnp.where((start <= first) & (first < end), start, low)
        last = first + OWN - 1
        high = jnp.where((start <= last) & (last < end), end, high)
    return (low - base) // size, (high - base + size - 1) // size


def owner_row(lengths, base, kown):
    frame = base + lax.broadcasted_iota(jnp.int32, kown.shape, 1)
    owner = jnp.full(kown.shape, -1, jnp.int32)
    end = jnp.int32(0)
    for u in range(lengths.shape[0]):
        start = end
        end = start + lengths[u]
        owner = jnp.where((frame >= start) & (frame < end), u, owner)
    kown[...] = owner


def attend_setup(lengths, base, kown, width, size):
    i = pl.program_id(0)
    first = base[1] + i * OWN

    @pl.when(i == 0)
    def _():
        owner_row(lengths, base[0], kown)

    low, high = tile_range(lengths, first, base[0], size)
    _, owner, _, _, _ = frame_columns(lengths, first, OWN)
    heads = width // HD
    slopes = [slope_of(lax.axis_index("mp") * heads + h) for h in range(heads)]

    def distance(k0):
        shape = (OWN, size)
        gap = (first - base[0] - k0) + lax.broadcasted_iota(jnp.int32, shape, 0)
        dist = jnp.abs(gap - lax.broadcasted_iota(jnp.int32, shape, 1)).astype(F32)
        return jnp.where(owner == kown[:, pl.ds(k0, size)], dist, 1e30)

    return low, high, slopes, distance


def attend_forward_kernel(lengths, base, q_ref, k_ref, v_ref, o_ref, ob_ref, lse_ref, kown):
    width = q_ref.shape[1]
    low, high, slopes, distance = attend_setup(lengths, base, kown, width, KT)
    lanes = [slice(128 * j, 128 * (j + 1)) for j in range(width // 128)]
    qs = [stack_pair(q_ref[:, l]) * BF(0.125) for l in lanes]

    def body(t, carry):
        k0 = pl.multiple_of(t * KT, KT)
        dist = distance(k0)
        out = []
        for j, l in enumerate(lanes):
            top, total, acc = carry[j]
            s = nt(qs[j], k_ref[pl.ds(k0, KT), l])
            s = jnp.concatenate([s[:OWN] - slopes[2 * j] * dist, s[OWN:] - slopes[2 * j + 1] * dist], 0)
            new = jnp.maximum(top, jnp.max(s, -1, keepdims=True))
            fade = jnp.exp(top - new)
            e = jnp.exp(s - new)
            total = total * fade + jnp.sum(e, -1, keepdims=True)
            acc = acc * fade + nn(e.astype(BF), v_ref[pl.ds(k0, KT), l])
            out.append((new, total, acc))
        return tuple(out)

    begin = (
        jnp.full((2 * OWN, 1), -1e30, F32), jnp.zeros((2 * OWN, 1), F32), jnp.zeros((2 * OWN, 128), F32),
    )
    ended = lax.fori_loop(low, high, body, tuple(begin for _ in lanes))
    lane = lax.broadcasted_iota(jnp.int32, (OWN, 128), 1)
    lse = jnp.zeros((OWN, 128), F32)
    for j, l in enumerate(lanes):
        top, total, acc = ended[j]
        o = unstack_pair(acc / total)
        o_ref[:, l] = o
        ob_ref[:, l] = o.astype(BF)
        g = top + jnp.log(total)
        lse = jnp.where(lane == 2 * j, g[:OWN], lse)
        lse = jnp.where(lane == 2 * j + 1, g[OWN:], lse)
    lse_ref[...] = lse


def blocks(width):
    return pl.BlockSpec((OWN, width), lambda i, *_: (i, 0))


def attend_call(kernel, outs, out_specs, in_specs, rows, keys, name, flops):
    return pl.pallas_call(
        kernel,
        out_shape=outs,
        grid_spec=pltpu.PrefetchScalarGridSpec(
            num_scalar_prefetch=2, grid=(rows // OWN,), in_specs=in_specs, out_specs=out_specs,
            scratch_shapes=[pltpu.VMEM((1, keys), jnp.int32)],
        ),
        compiler_params=pltpu.CompilerParams(vmem_limit_bytes=50 << 20),
        cost_estimate=pl.CostEstimate(flops=flops, bytes_accessed=1 << 23, transcendentals=0),
        name=name,
    )


def attend_forward(lengths, base, q, k, v):
    (rows, width), keys = q.shape, k.shape[0]
    outs = (
        jax.ShapeDtypeStruct((rows, width), F32), jax.ShapeDtypeStruct((rows, width), BF),
        jax.ShapeDtypeStruct((rows, 128), F32),
    )
    return attend_call(
        attend_forward_kernel, outs, (blocks(width), blocks(width), blocks(128)),
        [blocks(width), VM, VM], rows, keys, "attend_forward", 10**10,
    )(lengths, base, q, k, v)


def attend_backward_kernel(
    lengths, base, q_ref, k_ref, v_ref, do_ref, lse_ref, delta_ref, qa_ref, ka_ref, va_ref, doa_ref,
    stat_ref, out_ref, kown,
):
    width = q_ref.shape[1]
    low, high, slopes, distance = attend_setup(lengths, base, kown, width, KB)
    lanes = [slice(128 * j, 128 * (j + 1)) for j in range(width // 128)]

    def column(ref, j):
        return jnp.concatenate([ref[:, 2 * j : 2 * j + 1], ref[:, 2 * j + 1 : 2 * j + 2]], 0)

    scale = BF(0.125)
    qs = [stack_pair(q_ref[:, l]) * scale for l in lanes]
    dos = [stack_pair(do_ref[:, l]) for l in lanes]
    ks = [stack_pair(k_ref[:, l]) * scale for l in lanes]
    vs = [stack_pair(v_ref[:, l]) for l in lanes]
    lses = [column(lse_ref, j) for j in range(len(lanes))]
    deltas = [column(delta_ref, j) for j in range(len(lanes))]

    def body(t, carry):
        k0 = pl.multiple_of(t * KB, KB)
        keys = pl.ds(k0, KB)
        part = pl.ds(pl.multiple_of(lax.rem(t, KT // KB) * KB, KB), KB)
        whole_tile = t // (KT // KB)
        dist = distance(k0)
        out = []
        for j, l in enumerate(lanes):
            dq, dk, dv = carry[j]
            kj, vj, qj, doj = ka_ref[keys, l], va_ref[keys, l], qa_ref[keys, l], doa_ref[keys, l]
            bias = [slopes[2 * j + h] * dist for h in (0, 1)]
            s = nt(qs[j], kj)
            e = jnp.exp(jnp.concatenate([s[:OWN] - bias[0], s[OWN:] - bias[1]], 0) - lses[j])
            ds = (e * (nt(dos[j], vj) - deltas[j])).astype(BF)
            dq = dq + nn(ds, kj)
            s = nt(ks[j], qj)
            far = [stat_ref[whole_tile, 2 * j + h : 2 * j + h + 1, part] for h in (0, 1)]
            e = jnp.exp(jnp.concatenate([s[:OWN] - bias[0] - far[0], s[OWN:] - bias[1] - far[1]], 0))
            dv = dv + nn(e.astype(BF), doj)
            g = nt(vs[j], doj)
            far = [stat_ref[whole_tile, 8 + 2 * j + h : 9 + 2 * j + h, part] for h in (0, 1)]
            ds = (e * jnp.concatenate([g[:OWN] - far[0], g[OWN:] - far[1]], 0)).astype(BF)
            dk = dk + nn(ds, qj)
            out.append((dq, dk, dv))
        return tuple(out)

    zero = jnp.zeros((2 * OWN, 128), F32)
    ended = lax.fori_loop(low, high, body, tuple((zero, zero, zero) for _ in lanes))
    for j, l in enumerate(lanes):
        dq, dk, dv = ended[j]
        out_ref[0, :, l] = (unstack_pair(dq) * 0.125).astype(BF)
        out_ref[1, :, l] = (unstack_pair(dk) * 0.125).astype(BF)
        out_ref[2, :, l] = unstack_pair(dv).astype(BF)


def attend_backward(lengths, base, q, k, v, do, lse, delta, qa, ka, va, doa, stat):
    (rows, width), keys = q.shape, ka.shape[0]
    own = blocks(width)
    if k.shape[0] != rows:
        own = pl.BlockSpec((OWN, width), lambda i, lengths, base: (base[1] // OWN + i, 0))
    return attend_call(
        attend_backward_kernel, jax.ShapeDtypeStruct((3, rows, width), BF),
        pl.BlockSpec((3, OWN, width), lambda i, *_: (0, i, 0)),
        [blocks(width), own, own, blocks(width)] + [blocks(128)] * 2 + [VM] * 5,
        rows, keys, "attend_backward", 3 * 10**10,
    )(lengths, base, q, k, v, do, lse, delta, qa, ka, va, doa, stat)


def adam_step(weight, first_old, second, gradient, step_rate, decay_on):
    first_new = beta_one * first_old + (1.0 - beta_one) * gradient
    second_new = beta_two * second + (1.0 - beta_two) * gradient * gradient
    fix_one = 1.0 - beta_one**STEP
    fix_two = 1.0 - beta_two**STEP
    moved = first_new / fix_one / (jnp.sqrt(second_new / fix_two) + adam_epsilon)
    return (first_new, second_new, weight - step_rate * (moved + decay_on * weight_decay * weight))


def update(loss_total, grads, frames, states):
    big_squares = jnp.sum(grads[0] * grads[0]) + jnp.sum(grads[1] * grads[1])
    small_squares = jnp.zeros((), jnp.float32)
    for gradient in grads[2:]:
        small_squares = small_squares + jnp.sum(gradient * gradient)
    big_total = lax.psum(big_squares, ("seq", "mp"))
    return adam_all(loss_total, jnp.sqrt(big_total + small_squares), grads, frames, states)


def adam_all(loss_total, grad_norm, grads, frames, states):
    weights, firsts, seconds = states
    factor = jnp.minimum(1.0, 0.3 / math.sqrt(frames) / grad_norm)
    results = [loss_total, grad_norm]
    for number in range(7):
        results.extend(
            adam_step(
                weights[number],
                firsts[number],
                seconds[number],
                grads[number] * factor,
                step_rates[number],
                decay_flags[number],
            )
        )
    return tuple(results)


def split_arguments(arguments):
    rest = arguments[7:]
    return arguments[:7], (rest[0::3], rest[1::3], rest[2::3])


def per_device(*arguments):
    inputs, states = split_arguments(arguments)
    row_count = inputs[0].shape[0]
    if (lax.axis_size("seq"), lax.axis_size("mp"), row_count) == (8, 4, 512):
        return step_by_kernels(inputs, states)
    return step_by_collectives(inputs, states)


def step_by_kernels(inputs, states):
    mel, noise, phone_ids, lengths, span_start, span_end, flow_times = inputs
    attention, feedforward, win, phone_table, kern, wpred, gains = states[0]
    row_count = mel.shape[0]
    frames = row_count * lax.axis_size("seq")
    columns = ((0, 0), (0, 128 - MEL))
    with_phone = jnp.concatenate([noise, phone_ids.astype(F32)[:, None]], 1)
    pack = jnp.concatenate(
        [jnp.pad(mel, columns), jnp.pad(with_phone, ((0, 0), (0, 127 - MEL)))], 1
    )
    table = time_features(flow_times, D)
    (
        h1, conv, rim, a, q, k, v, wqkv, feats, choose, lse,
        dh2, rows, outg, do, delta, q_all, do_all, stat, gup, gdown, gout,
    ) = forward(
        lengths, span_start, span_end, flow_times, pack, table, win, phone_table, kern, gains, attention,
        feedforward, wpred.T,
    )
    row_base = lax.axis_index("seq") * row_count
    base = jnp.stack([jnp.zeros_like(row_base), row_base]).astype(jnp.int32)
    proj = attend_backward(lengths, base, q, k, v, do, lse, delta, q_all, k, v, do_all, stat)
    attention_grad, feedforward_grad, small, scalars = back(
        lengths, proj, wqkv, a, dh2, h1, conv, rim, gains, kern, feats, choose, rows, outg, gup, gdown, gout
    )
    gain_grad = jnp.stack([small[319], small[401], small[400]])
    grads = (
        attention_grad, feedforward_grad, small[:160], small[160:288], small[288:319],
        small[320:400].T, gain_grad,
    )
    return adam_all(scalars[1, 0], jnp.sqrt(scalars[0, 0]), grads, frames, states)


def step_by_collectives(inputs, states):
    mel_frames, noise_frames, phone_ids, lengths, span_start, span_end, flow_times = inputs
    (
        attention_weight,
        feedforward_weight,
        input_weight,
        phone_table,
        position_kernel,
        output_weight,
        layer_gains,
    ) = states[0]
    row_count = mel_frames.shape[0]
    frames = row_count * lax.axis_size("seq")
    row_base = lax.axis_index("seq") * row_count
    longest = min(MAXLEN, frames // 2)
    near_count = min((longest - 1 + row_count - 1) // row_count, lax.axis_size("seq") - 1)
    window_start = row_base - near_count * row_count
    reach = position_kernel.shape[0] // 2
    tables = (lengths, span_start, span_end, flow_times)
    row_index = row_base + jnp.arange(row_count)
    owners, masked, moment = frame_tables(*tables, row_index)
    covered, uncovered = mask_counts(lengths, span_start, span_end)
    row_weight = masked / jnp.maximum(covered, 1.0) + 0.1 * (1.0 - masked) / jnp.maximum(
        uncovered, 1.0
    )
    attention_full, feedforward_full = (
        lax.all_gather(attention_weight.astype(jnp.bfloat16), "seq", axis=1, tiled=True),
        lax.all_gather(feedforward_weight.astype(jnp.bfloat16), "seq", axis=1, tiled=True),
    )
    heads_local = attention_full.shape[2] // HD
    target = mel_frames - (1.0 - flow_sigma) * noise_frames
    noisy = (1.0 - (1.0 - flow_sigma) * moment[:, None]) * noise_frames + moment[
        :, None
    ] * mel_frames
    context = mel_frames * (1.0 - masked[:, None])
    feats = jnp.concatenate([context, noisy], 1).astype(jnp.bfloat16)
    choose = (phone_ids[:, None] == jnp.arange(phone_table.shape[0])[None, :]).astype(jnp.bfloat16)
    start_h = product(feats, input_weight.astype(jnp.bfloat16)) + product(
        choose, phone_table.astype(jnp.bfloat16)
    )
    start_h = start_h + time_features(moment, D)
    start_low = start_h.astype(jnp.bfloat16)
    rim = padded_2(start_low, (("seq", 0),), reach)
    pad_owner = frame_tables(*tables, row_base - reach + jnp.arange(row_count + 2 * reach))[0]
    conv_raw = jnp.zeros(start_h.shape, jnp.float32)
    for offset in range(position_kernel.shape[0]):
        same_owner = (pad_owner[offset : offset + row_count] == owners).astype(jnp.float32)
        conv_raw = (
            conv_raw
            + position_kernel[offset][None, :]
            * rim[offset : offset + row_count].astype(jnp.float32)
            * same_owner[:, None]
        )
    conv_gelu, conv_back = jax.vjp(jax.nn.gelu, conv_raw)
    hidden_one = start_h + conv_gelu
    ln_one, norm_back_one = jax.vjp(layer_norm, hidden_one, layer_gains[0])
    ln_one_low = ln_one.astype(jnp.bfloat16)
    projected = jnp.einsum(
        "td,kdh->kth", ln_one_low, attention_full[:3], preferred_element_type=jnp.float32
    ).astype(jnp.bfloat16)
    queries, keyed, valued = (projected[0], projected[1], projected[2])
    def window(array):
        return slice_window(
            lax.all_gather(array, "seq", axis=0, tiled=True), row_base, near_count, row_count
        )

    base = jnp.stack([window_start, row_base]).astype(jnp.int32)
    key_all, value_all = window(keyed), window(valued)
    out_f32, out_low, log_total = attend_forward(lengths, base, queries, key_all, value_all)
    attended = lax.psum(
        contract_cols(out_low, attention_full[3]).astype(jnp.bfloat16), "mp"
    ).astype(jnp.float32)
    hidden_two = hidden_one + attended
    ln_two, norm_back_two = jax.vjp(layer_norm, hidden_two, layer_gains[1])
    ln_two_low = ln_two.astype(jnp.bfloat16)
    upward = product(ln_two_low, feedforward_full[0])
    gated_f32, gelu_back = jax.vjp(jax.nn.gelu, upward)
    gated = gated_f32.astype(jnp.bfloat16)
    downward = lax.psum(
        contract_cols(gated, feedforward_full[1]).astype(jnp.bfloat16), "mp"
    ).astype(jnp.float32)
    hidden_three = hidden_two + downward
    ln_three, norm_back_three = jax.vjp(layer_norm, hidden_three, layer_gains[2])
    ln_three_low = ln_three.astype(jnp.bfloat16)
    output_low = output_weight.astype(jnp.bfloat16)
    predicted = product(ln_three_low, output_low)
    errors = predicted - target
    loss_local = jnp.sum(row_weight * jnp.mean(errors * errors, 1))
    loss_total = lax.psum(loss_local, "seq")
    pred_grad = (row_weight[:, None] * (2.0 / errors.shape[1]) * errors).astype(jnp.bfloat16)
    output_grad = contract_rows(ln_three_low, pred_grad)
    three_grad, gain_three = norm_back_three(contract_cols(pred_grad, output_low))
    down_low = three_grad.astype(jnp.bfloat16)
    down_wgrad = contract_rows(down_low, gated)
    up_grad = gelu_back(product(down_low, feedforward_full[1]))[0].astype(jnp.bfloat16)
    up_wgrad = contract_rows(ln_two_low, up_grad)
    two_sum = lax.psum(
        contract_cols(up_grad, feedforward_full[0]).astype(jnp.bfloat16), "mp"
    ).astype(jnp.float32)
    norm_grad, gain_two = norm_back_two(two_sum)
    two_grad = three_grad + norm_grad
    attended_low = two_grad.astype(jnp.bfloat16)
    out_wgrad = contract_rows(attended_low, out_low)
    out_heads = product(attended_low, attention_full[3]).astype(jnp.bfloat16)
    delta = jnp.sum(
        (out_heads.astype(jnp.float32) * out_f32).reshape(row_count, heads_local, HD), 2
    )
    delta = jnp.pad(delta, ((0, 0), (0, 128 - heads_local)))
    stat = window(jnp.concatenate([log_total[:, :8], delta[:, :8]], 1))
    stat = stat.reshape(-1, KT, 16).transpose(0, 2, 1)
    proj_grad = attend_backward(
        lengths, base, queries, keyed, valued, out_heads, log_total, delta,
        window(queries), key_all, value_all, window(out_heads), stat,
    )
    qkv_wgrad = jnp.einsum("td,kth->kdh", ln_one_low, proj_grad, preferred_element_type=jnp.float32)
    one_part = jnp.einsum(
        "kth,kdh->td", proj_grad, attention_full[:3], preferred_element_type=jnp.float32
    )
    one_sum = lax.psum(one_part.astype(jnp.bfloat16), "mp").astype(jnp.float32)
    norm_grad, gain_one = norm_back_one(one_sum)
    one_grad = two_grad + norm_grad
    conv_grad = conv_back(one_grad)[0].astype(jnp.bfloat16)
    grad_rim = padded_2(conv_grad, (("seq", 0),), reach)
    spread = jnp.zeros(one_grad.shape, jnp.float32)
    kernel_rows = []
    conv_grad_f32 = conv_grad.astype(jnp.float32)
    for offset in range(position_kernel.shape[0]):
        back_start = 2 * reach - offset
        same_back = (pad_owner[back_start : back_start + row_count] == owners).astype(jnp.float32)
        spread = (
            spread
            + position_kernel[offset][None, :]
            * grad_rim[back_start : back_start + row_count].astype(jnp.float32)
            * same_back[:, None]
        )
        same_fore = (pad_owner[offset : offset + row_count] == owners).astype(jnp.float32)
        kernel_rows.append(
            jnp.sum(
                conv_grad_f32
                * rim[offset : offset + row_count].astype(jnp.float32)
                * same_fore[:, None],
                0,
            )
        )
    kernel_grad = jnp.stack(kernel_rows)
    start_grad = (one_grad + spread).astype(jnp.bfloat16)
    input_wgrad = contract_rows(feats, start_grad)
    phone_wgrad = contract_rows(choose, start_grad)
    gains_grad = jnp.stack([gain_one, gain_two, gain_three])
    small_sums = lax.psum((input_wgrad, phone_wgrad, kernel_grad, output_grad, gains_grad), "seq")
    attention_grad, feedforward_grad = (
        lax.psum_scatter(
            jnp.concatenate([qkv_wgrad, out_wgrad[None]], 0), "seq", scatter_dimension=1, tiled=True
        ),
        lax.psum_scatter(jnp.stack([up_wgrad, down_wgrad]), "seq", scatter_dimension=1, tiled=True),
    )
    grads = (attention_grad, feedforward_grad) + tuple(small_sums)
    return update(loss_total, grads, frames, states)


def solution(mesh):
    in_specs = (
        P("seq", None),
        P("seq", None),
        P("seq"),
        P(),
        P(),
        P(),
        P(),
        P(None, "seq", "mp"),
        P(None, "seq", "mp"),
        P(None, "seq", "mp"),
        P(None, "seq", "mp"),
        P(None, "seq", "mp"),
        P(None, "seq", "mp"),
        P(),
        P(),
        P(),
        P(),
        P(),
        P(),
        P(),
        P(),
        P(),
        P(),
        P(),
        P(),
        P(),
        P(),
        P(),
    )
    out_specs = (
        P(),
        P(),
        P(None, "seq", "mp"),
        P(None, "seq", "mp"),
        P(None, "seq", "mp"),
        P(None, "seq", "mp"),
        P(None, "seq", "mp"),
        P(None, "seq", "mp"),
        P(),
        P(),
        P(),
        P(),
        P(),
        P(),
        P(),
        P(),
        P(),
        P(),
        P(),
        P(),
        P(),
        P(),
        P(),
    )
    return jax.shard_map(
        per_device, mesh=mesh, in_specs=in_specs, out_specs=out_specs, check_vma=False
    )
```
